32 devices in a mesh: seq: 8 (over y, x, core), mp: 4 (over z).
Axes of the slice: x: 2, y: 2, z: 4, core: 2. Of those that a mesh axis runs over, the one named last changes fastest.
Arguments:
- tokens: bfloat16 [2048, 2048], P('seq'), may hold values from -6 to 6
- lengths: int32 [5], replicated, may hold values from 1 to 1792, as said below
- out_grad: bfloat16 [2048, 2048], P('seq'), may hold values from -6 to 6
- mixer_gain: float32 [2048], replicated, may hold values from 0.5 to 1.5
- mixer_value: bfloat16 [2048, 4096], P('seq', 'mp'), may hold values from -0.125 to 0.125
- mixer_gate: bfloat16 [2048, 4096], P('seq', 'mp'), may hold values from -0.125 to 0.125
- conv_weight: float32 [4, 4096], P(None, 'mp'), may hold values from -3 to 3
- conv_bias: float32 [4096], P('mp'), may hold values from -3 to 3
- select_proj: bfloat16 [160, 4096], P(None, 'mp'), may hold values from -0.375 to 0.375
- step_proj: bfloat16 [128, 4096], P(None, 'mp'), may hold values from -0.5 to 0.5
- step_bias: float32 [4096], P('mp'), may hold values from -10 to -2
- decay_log: float32 [16, 4096], P(None, 'mp'), may hold values from 0 to 2.77
- skip_gain: float32 [4096], P('mp'), may hold values from 0.5 to 1.5
- mixer_out: bfloat16 [4096, 2048], P('mp', 'seq'), may hold values from -0.1875 to 0.1875
- first_gain: float32 [2048], replicated, may hold values from 0.5 to 1.5
- first_gate: bfloat16 [2048, 8192], P('seq', 'mp'), may hold values from -0.125 to 0.125
- first_lift: bfloat16 [2048, 8192], P('seq', 'mp'), may hold values from -0.125 to 0.125
- first_down: bfloat16 [8192, 2048], P('mp', 'seq'), may hold values from -0.0625 to 0.0625
- attend_gain: float32 [2048], replicated, may hold values from 0.5 to 1.5
- query_proj: bfloat16 [2048, 2048], P('seq', 'mp'), may hold values from -0.125 to 0.125
- key_proj: bfloat16 [2048, 2048], P('seq', 'mp'), may hold values from -0.125 to 0.125
- value_proj: bfloat16 [2048, 2048], P('seq', 'mp'), may hold values from -0.125 to 0.125
- attend_out: bfloat16 [2048, 2048], P('mp', 'seq'), may hold values from -2 to 2
- second_gain: float32 [2048], replicated, may hold values from 0.5 to 1.5
- second_gate: bfloat16 [2048, 8192], P('seq', 'mp'), may hold values from -0.125 to 0.125
- second_lift: bfloat16 [2048, 8192], P('seq', 'mp'), may hold values from -0.125 to 0.125
- second_down: bfloat16 [8192, 2048], P('mp', 'seq'), may hold values from -0.0625 to 0.0625
Outputs:
- mixed: bfloat16 [2048, 2048], P('seq')
- tokens_grad: float32 [2048, 2048], P('seq')
- mixer_gain_grad: float32 [2048], replicated
- mixer_value_grad: float32 [2048, 4096], P('seq', 'mp')
- mixer_gate_grad: float32 [2048, 4096], P('seq', 'mp')
- conv_weight_grad: float32 [4, 4096], P(None, 'mp')
- conv_bias_grad: float32 [4096], P('mp')
- select_proj_grad: float32 [160, 4096], P(None, 'mp')
- step_proj_grad: float32 [128, 4096], P(None, 'mp')
- step_bias_grad: float32 [4096], P('mp')
- decay_log_grad: float32 [16, 4096], P(None, 'mp')
- skip_gain_grad: float32 [4096], P('mp')
- mixer_out_grad: float32 [4096, 2048], P('mp', 'seq')
- first_gain_grad: float32 [2048], replicated
- first_gate_grad: float32 [2048, 8192], P('seq', 'mp')
- first_lift_grad: float32 [2048, 8192], P('seq', 'mp')
- first_down_grad: float32 [8192, 2048], P('mp', 'seq')
- attend_gain_grad: float32 [2048], replicated
- query_proj_grad: float32 [2048, 2048], P('seq', 'mp')
- key_proj_grad: float32 [2048, 2048], P('seq', 'mp')
- value_proj_grad: float32 [2048, 2048], P('seq', 'mp')
- attend_out_grad: float32 [2048, 2048], P('mp', 'seq')
- second_gain_grad: float32 [2048], replicated
- second_gate_grad: float32 [2048, 8192], P('seq', 'mp')
- second_lift_grad: float32 [2048, 8192], P('seq', 'mp')
- second_down_grad: float32 [8192, 2048], P('mp', 'seq')
The draws below stay inside these ranges and needn't reach their ends.
Inputs may be any that keep to these rules, and one draw needn't show every extreme that they name: lengths lists the items in slot order: two ragged items, the long item, two ragged items. A ragged item has 1 to 64 tokens and one of them has exactly 64; the long item has 1792 tokens and fills its slot; pads fill the rest of each slot.
All inputs are finite; a program needn't handle non-finite values.
Results may differ from the reference program's by a relative error of at most 0.025.
Values may be sent and summed in bfloat16 or wider, within the bound.
A program may use at most 320 MiB of HBM per device.

```python
import math
import jax
import jax.numpy as jnp
from jax import lax

D = 2048
INNER = 4096
STATE = 16
CONV = 4
DT_RANK = 128
FF = 8192
HEAD_DIM = 128
WINDOW = 2048
RB = 160
SLOT = 64
TOKENS = 2048
LONG_SLOT = 1792


def draw_lengths(key, part):
    key = jax.random.fold_in(key, 7)
    first_key, second_key = jax.random.split(key)
    ragged = jax.random.randint(first_key, (4,), 1, SLOT + 1, dtype=jnp.int32)
    chosen = jax.random.randint(second_key, (), 0, 4, dtype=jnp.int32)
    ragged = jnp.where(jnp.arange(4, dtype=jnp.int32) == chosen, SLOT, ragged).astype(jnp.int32)
    return jnp.concatenate([ragged[:2], jnp.full((1,), LONG_SLOT, jnp.int32), ragged[2:]])


def shard_levels(own_key, extent, shards, smallest, top_value):
    loudness = 1.0
    for dim, shards_of in shards:
        heights = jax.random.uniform(jax.random.fold_in(jax.random.fold_in(own_key, 6), dim), (shards_of,), jnp.float32, smallest / len(shards), top_value / len(shards))
        loudness = loudness * jnp.repeat(jnp.exp(heights), extent[dim] // shards_of).reshape((-1,) + (1,) * (len(extent) - 1 - dim))
    return loudness


def scatter_about(rng, extent, spread, most, cuts=(), kind=jnp.bfloat16):
    values = jax.random.normal(rng, extent, jnp.float32) * spread
    if len(cuts) > 0:
        values = shard_levels(rng, extent, cuts, -0.22, 0.18) * values
    return jnp.clip(values, min=-most, max=most).astype(kind)


def setup_inputs(seed: int = 0) -> dict:
    streams_of = jax.random.split(jax.random.key(seed), 28)
    tokens = scatter_about(streams_of[0], (TOKENS, D), 1.0, 6.0, ((0, 8),))
    lengths = draw_lengths(jax.random.fold_in(streams_of[27], 71), 0)
    out_grad = scatter_about(streams_of[2], (TOKENS, D), 1.0, 6.0, ((0, 8),))
    mixer_gain = jnp.clip(1.0 + 0.1 * jax.random.normal(streams_of[3], (D,), jnp.float32), 0.5, 1.5)
    mixer_value = scatter_about(streams_of[4], (D, INNER), D ** -0.5, 0.125, ((0, 8), (1, 4)))
    mixer_gate = scatter_about(streams_of[5], (D, INNER), D ** -0.5, 0.125, ((0, 8), (1, 4)))
    conv_weight = scatter_about(streams_of[6], (CONV, INNER), CONV ** -0.5, 3.0, ((1, 4),), jnp.float32)
    conv_bias = scatter_about(streams_of[7], (INNER,), 0.5, 3.0, ((0, 4),), jnp.float32)
    select_proj = scatter_about(streams_of[8], (RB, INNER), (INNER // 16) ** -0.5, 0.375, ((1, 4),))
    step_proj = scatter_about(streams_of[9], (DT_RANK, INNER), DT_RANK ** -0.5, 0.5, ((1, 4),))
    step_bias = jnp.clip(-10.0 + 8.0 * jax.random.uniform(streams_of[10], (INNER,), jnp.float32) ** shard_levels(streams_of[10], (INNER,), ((0, 4),), -0.2, 0.2), -10.0, -2.0)
    decay_log = jnp.clip(2.77 * jax.random.uniform(streams_of[11], (STATE, INNER), jnp.float32) ** shard_levels(streams_of[11], (STATE, INNER), ((1, 4),), -0.2, 0.2), 0.0, 2.77)
    skip_gain = jnp.clip(0.5 + 1.0 * jax.random.uniform(streams_of[12], (INNER,), jnp.float32) ** shard_levels(streams_of[12], (INNER,), ((0, 4),), -0.2, 0.2), 0.5, 1.5)
    mixer_out = scatter_about(streams_of[13], (INNER, D), (INNER // 4) ** -0.5, 0.1875, ((0, 4), (1, 8)))
    first_gain = jnp.clip(1.0 + 0.1 * jax.random.normal(streams_of[14], (D,), jnp.float32), 0.5, 1.5)
    first_gate = scatter_about(streams_of[15], (D, FF), D ** -0.5, 0.125, ((0, 8), (1, 4)))
    first_lift = scatter_about(streams_of[16], (D, FF), D ** -0.5, 0.125, ((0, 8), (1, 4)))
    first_down = scatter_about(streams_of[17], (FF, D), FF ** -0.5, 0.0625, ((0, 4), (1, 8)))
    attend_gain = jnp.clip(1.0 + 0.1 * jax.random.normal(streams_of[18], (D,), jnp.float32), 0.5, 1.5)
    query_proj = scatter_about(streams_of[19], (D, D), D ** -0.5, 0.125, ((0, 8), (1, 4)))
    key_proj = scatter_about(streams_of[20], (D, D), D ** -0.5, 0.125, ((0, 8), (1, 4)))
    value_proj = scatter_about(streams_of[21], (D, D), D ** -0.5, 0.125, ((0, 8), (1, 4)))
    attend_out = scatter_about(streams_of[22], (D, D), (max(D // 256, 1)) ** -0.5, 2.0, ((0, 4), (1, 8)))
    second_gain = jnp.clip(1.0 + 0.1 * jax.random.normal(streams_of[23], (D,), jnp.float32), 0.5, 1.5)
    second_gate = scatter_about(streams_of[24], (D, FF), D ** -0.5, 0.125, ((0, 8), (1, 4)))
    second_lift = scatter_about(streams_of[25], (D, FF), D ** -0.5, 0.125, ((0, 8), (1, 4)))
    second_down = scatter_about(streams_of[26], (FF, D), FF ** -0.5, 0.0625, ((0, 4), (1, 8)))
    return {"tokens": tokens, "lengths": lengths, "out_grad": out_grad, "mixer_gain": mixer_gain, "mixer_value": mixer_value, "mixer_gate": mixer_gate, "conv_weight": conv_weight, "conv_bias": conv_bias, "select_proj": select_proj, "step_proj": step_proj, "step_bias": step_bias, "decay_log": decay_log, "skip_gain": skip_gain, "mixer_out": mixer_out, "first_gain": first_gain, "first_gate": first_gate, "first_lift": first_lift, "first_down": first_down, "attend_gain": attend_gain, "query_proj": query_proj, "key_proj": key_proj, "value_proj": value_proj, "attend_out": attend_out, "second_gain": second_gain, "second_gate": second_gate, "second_lift": second_lift, "second_down": second_down}


@jax.custom_vjp
def low(v):
    return lax.optimization_barrier(v.astype(jnp.bfloat16)).astype(jnp.float32)

@jax.custom_vjp
def low_back(v):
    return v

def low_keep(v):
    return (low(v), None)

def low_pass(kept, grad):
    return (grad,)

def back_keep(v):
    return (v, None)

def back_low(kept, grad):
    return (low(grad),)
low.defvjp(low_keep, low_pass)
low_back.defvjp(back_keep, back_low)
EPS = 1e-05
HIGH = lax.Precision.HIGHEST

def matmul(left, right):
    return jnp.dot(left, right, precision=HIGH, preferred_element_type=jnp.float32)

def layout(lengths, positions, slot, total):
    starts = jnp.array([0, slot, 2 * slot, total - 2 * slot, total - slot], jnp.int32)
    seg = lax.optimization_barrier(jnp.sum((positions[:, None] >= starts[None, :]).astype(jnp.int32), axis=1)) - 1
    which = (seg[:, None] == jnp.arange(5, dtype=jnp.int32)[None, :]).astype(jnp.int32)
    start_of = lax.optimization_barrier(jnp.sum(which * starts[None, :], axis=1))
    length_of = lax.optimization_barrier(jnp.sum(which * lengths[None, :], axis=1))
    keep = (positions - start_of < length_of).astype(jnp.float32)
    first = (positions == start_of).astype(jnp.float32)
    return (seg, keep, first)

def rms_norm(value, gain):
    scale = lax.rsqrt(lax.optimization_barrier(jnp.mean(value * value, axis=-1, keepdims=True)) + EPS)
    return value * scale * gain

def shift_rows(value, amount, fill):
    pad = jnp.full((amount,) + value.shape[1:], fill, value.dtype)
    return jnp.concatenate([pad, value[:value.shape[0] - amount]], axis=0)

def ssm_ref(step, signal, in_gate, out_gate, first, rates):
    total = step.shape[0]
    block = 64 if total % 64 == 0 else total
    count = total // block

    def token(state, row):
        delta, sig, bvec, cvec, start = row
        decay = jnp.exp(delta[None, :] * rates) * (1.0 - start)
        state = decay * state + (delta * sig)[None, :] * bvec[:, None]
        return (state, lax.optimization_barrier(jnp.sum(cvec[:, None] * state, axis=0)))

    def run(state, rows):
        return lax.scan(token, state, rows)
    rows = tuple((item.reshape((count, block) + item.shape[1:]) for item in (step, signal, in_gate, out_gate, first)))
    init = jnp.zeros(rates.shape, jnp.float32)
    _, outputs = lax.scan(jax.checkpoint(run), init, rows)
    return outputs.reshape(total, -1)

def mixer_ref(x, seg, first, gain, value_w, gate_w, conv_w, conv_b, select_w, step_w, step_b, decay_log, skip, out_w):
    normed = low(rms_norm(x, gain))
    inner = low_back(matmul(normed, value_w))
    gate = low_back(matmul(normed, gate_w))
    conv = conv_b[None, :] + conv_w[CONV - 1][None, :] * inner
    for back in range(1, CONV):
        same = (shift_rows(seg, back, -1) == seg).astype(jnp.float32)
        conv = conv + conv_w[CONV - 1 - back][None, :] * shift_rows(inner, back, 0.0) * same[:, None]
    signal = low(jax.nn.silu(conv))
    select = low_back(matmul(signal, select_w.T))
    step_low = low(select[:, :DT_RANK])
    in_gate = select[:, DT_RANK:DT_RANK + STATE]
    out_gate = select[:, DT_RANK + STATE:]
    step = jax.nn.softplus(low_back(matmul(step_low, step_w)) + step_b[None, :])
    rates = -jnp.exp(decay_log)
    states = ssm_ref(step, signal, in_gate, out_gate, first, rates)
    output = states + skip[None, :] * signal
    mixed = low(output * jax.nn.silu(gate))
    return low_back(matmul(mixed, out_w))

def ffn_ref(x, gain, gate_w, lift_w, down_w):
    normed = low(rms_norm(x, gain))
    gate = low_back(matmul(normed, gate_w))
    lift = low_back(matmul(normed, lift_w))
    hidden = low(jax.nn.silu(gate) * lift)
    return low_back(matmul(hidden, down_w))

def attend_ref(x, seg, gain, query_w, key_w, value_w, out_w):
    normed = low(rms_norm(x, gain))
    query = low(low_back(matmul(normed, query_w)))
    keys = low(low_back(matmul(normed, key_w)))
    values = low(low_back(matmul(normed, value_w)))
    total = x.shape[0]
    block = 512 if total % 512 == 0 else total
    heads = query_w.shape[1] // HEAD_DIM
    factor = 1.0 / math.sqrt(HEAD_DIM)
    key_pad = jnp.pad(keys, ((WINDOW, 0), (0, 0)))
    value_pad = jnp.pad(values, ((WINDOW, 0), (0, 0)))
    seg_pad = jnp.concatenate([jnp.full((WINDOW,), -1, jnp.int32), seg])

    def one(start):
        qrows = lax.dynamic_slice_in_dim(query, start, block).reshape(block, heads, HEAD_DIM)
        krows = lax.dynamic_slice_in_dim(key_pad, start, block + WINDOW).reshape(block + WINDOW, heads, HEAD_DIM)
        vrows = lax.dynamic_slice_in_dim(value_pad, start, block + WINDOW).reshape(block + WINDOW, heads, HEAD_DIM)
        qseg = lax.dynamic_slice_in_dim(seg, start, block)
        kseg = lax.dynamic_slice_in_dim(seg_pad, start, block + WINDOW)
        gap = jnp.arange(block, dtype=jnp.int32)[:, None] + WINDOW - jnp.arange(block + WINDOW, dtype=jnp.int32)[None, :]
        allowed = (qseg[:, None] == kseg[None, :]) & (gap >= 0) & (gap < WINDOW)
        scores = low_back(jnp.einsum('qhd,khd->hqk', qrows, krows, precision=HIGH) * factor)
        scores = jnp.where(allowed[None], scores, -1e+30)
        probs = low(jax.nn.softmax(scores, axis=-1))
        mixed = jnp.einsum('hqk,khd->qhd', probs, vrows, precision=HIGH).reshape(block, -1)
        return low(low_back(mixed))
    starts = jnp.arange(total // block, dtype=jnp.int32) * block
    mixed = lax.map(jax.checkpoint(one), starts).reshape(total, -1)
    return low_back(matmul(mixed, out_w))

def reference(tokens, lengths, out_grad, mixer_gain, mixer_value, mixer_gate, conv_weight, conv_bias, select_proj, step_proj, step_bias, decay_log, skip_gain, mixer_out, first_gain, first_gate, first_lift, first_down, attend_gain, query_proj, key_proj, value_proj, attend_out, second_gain, second_gate, second_lift, second_down):
    total = tokens.shape[0]
    positions = jnp.arange(total, dtype=jnp.int32)
    seg, keep, first = layout(lengths, positions, SLOT, total)
    keep = keep[:, None]

    def forward(x, m_gain, m_value, m_gate, c_weight, c_bias, s_proj, t_proj, t_bias, d_log, s_gain, m_out, f_gain, f_gate, f_lift, f_down, a_gain, q_proj, k_proj, v_proj, a_out, s2_gain, s2_gate, s2_lift, s2_down):
        hidden = x + keep * mixer_ref(x, seg, first, m_gain, m_value, m_gate, c_weight, c_bias, s_proj, t_proj, t_bias, d_log, s_gain, m_out)
        hidden = hidden + keep * ffn_ref(hidden, f_gain, f_gate, f_lift, f_down)
        hidden = hidden + keep * attend_ref(hidden, seg, a_gain, q_proj, k_proj, v_proj, a_out)
        return hidden + keep * ffn_ref(hidden, s2_gain, s2_gate, s2_lift, s2_down)
    floats = tuple((item.astype(jnp.float32) for item in (tokens, mixer_gain, mixer_value, mixer_gate, conv_weight, conv_bias, select_proj, step_proj, step_bias, decay_log, skip_gain, mixer_out, first_gain, first_gate, first_lift, first_down, attend_gain, query_proj, key_proj, value_proj, attend_out, second_gain, second_gate, second_lift, second_down)))
    result, pull = jax.vjp(forward, *floats)
    g_tokens, g_mgain, g_mvalue, g_mgate, g_cweight, g_cbias, g_select, g_step, g_sbias, g_decay, g_skip, g_mout, g_fgain, g_fgate, g_flift, g_fdown, g_again, g_query, g_key, g_value, g_aout, g_sgain, g_sgate, g_slift, g_sdown = pull(out_grad.astype(jnp.float32))
    return (result.astype(jnp.bfloat16), g_tokens, g_mgain, g_mvalue, g_mgate, g_cweight, g_cbias, g_select, g_step, g_sbias, g_decay, g_skip, g_mout, g_fgain, g_fgate, g_flift, g_fdown, g_again, g_query, g_key, g_value, g_aout, g_sgain, g_sgate, g_slift, g_sdown)
```

```python
import functools
import math

import jax
import jax.numpy as jnp
from jax import lax
from jax.experimental import pallas as pl
from jax.experimental.pallas import tpu as pltpu
from jax.sharding import PartitionSpec as P

STATE = 16
CONV = 4
DT_RANK = 128
HEAD_DIM = 128
WINDOW = 2048
EPS = 1e-05
CHUNKS = 8
LANES = 128
LOG2E = 1.4426950408889634
VMEM = 48 * 1024 * 1024
MESH = pl.DeviceIdType.MESH


def chunk_scan(p, q, reverse):
    rows = p.shape[0]
    at = lax.broadcasted_iota(jnp.int32, p.shape, 0)
    d = 1
    while d < rows:
        move = (rows - d) if reverse else d
        ok = (at < rows - d) if reverse else (at >= d)
        ps = jnp.where(ok, pltpu.roll(p, move, 0), 1.0)
        qs = jnp.where(ok, pltpu.roll(q, move, 0), 0.0)
        q = p * qs + q
        p = p * ps
        d *= 2
    move = (rows - 1) if reverse else 1
    ok = (at < rows - 1) if reverse else (at >= 1)
    return p, q, jnp.where(ok, pltpu.roll(p, move, 0), 1.0), jnp.where(ok, pltpu.roll(q, move, 0), 0.0)

def spread(row, like):
    return jnp.broadcast_to(row, like.shape)

def ssm_summary(dt_ref, dx_ref, in_ref, rate_ref, keep_ref, thr_ref, off_ref, sum_ref):
    steps = dt_ref.shape[0]
    zero = jnp.zeros(dt_ref.shape[1:], jnp.float32)
    rates = [spread(rate_ref[n:n + 1, :], zero) for n in range(STATE)]
    def step(t, carry):
        total, states = carry
        dt, dx = dt_ref[t], dx_ref[t]
        states = tuple(jnp.exp2(dt * rates[n]) * states[n] + in_ref[t, n] * dx for n in range(STATE))
        return total + dt, states
    total, states = lax.fori_loop(0, steps, step, (zero, (zero,) * STATE), unroll=4)
    keep = keep_ref[...]
    reach, thru = [], []
    for n in range(STATE):
        p, q, pe, qe = chunk_scan(jnp.exp2(total * rates[n]) * keep, states[n], False)
        thr_ref[n] = pe * keep
        off_ref[n] = qe * keep
        reach.append(q[q.shape[0] - 1:, :])
        thru.append(p[p.shape[0] - 1:, :])
    sum_ref[...] = jnp.concatenate(reach + thru, axis=0).astype(sum_ref.dtype)

def entering_state(all_ref, pick_ref, backwards):
    count = all_ref.shape[0]
    running = jnp.zeros((STATE, LANES), jnp.float32)
    for k in range(count):
        j = count - 1 - k if backwards else k
        both = all_ref[j].astype(jnp.float32)
        new = both[STATE:] * running + both[:STATE]
        running = jnp.where(pick_ref[j] > 0, new, running)
    return running

def ssm_states(dt_ref, dx_ref, in_ref, out_ref, rate_ref, thr_ref, off_ref, all_ref, pick_ref, y_ref, enter_ref):
    steps = dt_ref.shape[0]
    zero = jnp.zeros(dt_ref.shape[1:], jnp.float32)
    rates = [spread(rate_ref[n:n + 1, :], zero) for n in range(STATE)]
    running = entering_state(all_ref, pick_ref, False)
    start = []
    for n in range(STATE):
        e = thr_ref[n] * spread(running[n:n + 1, :], zero) + off_ref[n]
        enter_ref[n] = e
        start.append(e)
    def step(t, states):
        dt, dx = dt_ref[t], dx_ref[t]
        states = tuple(jnp.exp2(dt * rates[n]) * states[n] + in_ref[t, n] * dx for n in range(STATE))
        parts = [out_ref[t, n] * states[n] for n in range(STATE)]
        while len(parts) > 1:
            parts = [a + b for a, b in zip(parts[::2], parts[1::2])]
        y_ref[t] = parts[0]
        return states
    lax.fori_loop(0, steps, step, tuple(start), unroll=4)

def ssm_back_summary(dt_ref, dy_ref, out_ref, rate_ref, keep_ref, thr_ref, off_ref, sum_ref):
    steps = dt_ref.shape[0]
    zero = jnp.zeros(dt_ref.shape[1:], jnp.float32)
    rates = [spread(rate_ref[n:n + 1, :], zero) for n in range(STATE)]
    def step(k, carry):
        t = steps - 1 - k
        total, back = carry
        dt, dy = dt_ref[t], dy_ref[t]
        back = tuple(jnp.exp2(dt * rates[n]) * (back[n] + out_ref[t, n] * dy) for n in range(STATE))
        return total + dt, back
    total, back = lax.fori_loop(0, steps, step, (zero, (zero,) * STATE), unroll=4)
    keep = keep_ref[...]
    reach, thru = [], []
    for n in range(STATE):
        p, q, pe, qe = chunk_scan(jnp.exp2(total * rates[n]) * keep, back[n] * keep, True)
        thr_ref[n] = pe
        off_ref[n] = qe
        reach.append(q[0:1, :])
        thru.append(p[0:1, :])
    sum_ref[...] = jnp.concatenate(reach + thru, axis=0).astype(sum_ref.dtype)

def ssm_grads(dt_ref, dx_ref, dy_ref, in_ref, out_ref, rate_ref, true_ref, enter_ref, thr_ref, off_ref, all_ref, pick_ref,
              ddt_ref, prod_ref, ing_ref, outg_ref, log_ref, h_ref, a_ref):
    steps = dt_ref.shape[0]
    zero = jnp.zeros(dt_ref.shape[1:], jnp.float32)
    rates = [spread(rate_ref[n:n + 1, :], zero) for n in range(STATE)]
    @pl.when(pl.program_id(0) == 0)
    def _():
        ing_ref[...] = jnp.zeros_like(ing_ref)
        outg_ref[...] = jnp.zeros_like(outg_ref)
    def forward(t, states):
        dt, dx, dy = dt_ref[t], dx_ref[t], dy_ref[t]
        new = []
        for n in range(STATE):
            h_ref[t, n] = states[n]
            a = jnp.exp2(dt * rates[n])
            a_ref[t, n] = a
            h = a * states[n] + in_ref[t, n] * dx
            outg_ref[t, n] += dy * h
            new.append(h)
        return tuple(new)
    lax.fori_loop(0, steps, forward, tuple(enter_ref[n] for n in range(STATE)), unroll=2)
    running = entering_state(all_ref, pick_ref, True)
    start = tuple(thr_ref[n] * spread(running[n:n + 1, :], zero) + off_ref[n] for n in range(STATE))
    true = [spread(true_ref[n:n + 1, :], zero) for n in range(STATE)]
    log_ref[...] = jnp.zeros_like(log_ref)
    def backward(k, back):
        t = steps - 1 - k
        dt, dx, dy = dt_ref[t], dx_ref[t], dy_ref[t]
        new, ddt, prod = [], [], []
        for n in range(STATE):
            lam = back[n] + out_ref[t, n] * dy
            q = lam * a_ref[t, n]
            dea = q * h_ref[t, n]
            ddt.append(dea * true[n])
            log_ref[n] += dea * dt
            prod.append(lam * in_ref[t, n])
            ing_ref[t, n] += lam * dx
            new.append(q)
        while len(ddt) > 1:
            ddt = [a + b for a, b in zip(ddt[::2], ddt[1::2])]
            prod = [a + b for a, b in zip(prod[::2], prod[1::2])]
        ddt_ref[t] = ddt[0]
        prod_ref[t] = prod[0]
        return tuple(new)
    lax.fori_loop(0, steps, backward, start, unroll=2)


def specs(steps, rows):
    chan = pl.BlockSpec((steps, rows, LANES), lambda i: (0, 0, i))
    wide = pl.BlockSpec((steps, STATE, rows, LANES), lambda i: (0, 0, 0, 0))
    rate = pl.BlockSpec((STATE, LANES), lambda i: (0, i))
    per = pl.BlockSpec((STATE, rows, LANES), lambda i: (0, 0, i))
    summ = pl.BlockSpec((2 * STATE, LANES), lambda i: (0, i))
    keep = pl.BlockSpec((rows, LANES), lambda i: (0, 0))
    return chan, wide, rate, per, summ, keep

def params():
    return pltpu.CompilerParams(vmem_limit_bytes=VMEM, dimension_semantics=("arbitrary",))

def run_summary(dt, src, gates, rate2, keep, backwards):
    steps, rows, width = dt.shape
    chan, wide, rate, per, summ, kp = specs(steps, rows)
    f = jnp.float32
    return pl.pallas_call(
        ssm_back_summary if backwards else ssm_summary,
        grid=(width // LANES,),
        in_specs=[chan, chan, wide, rate, kp],
        out_specs=[per, per, summ],
        out_shape=[jax.ShapeDtypeStruct((STATE, rows, width), f)] * 2 + [jax.ShapeDtypeStruct((2 * STATE, width), jnp.bfloat16)],
        compiler_params=params(), name="ssm_back_summary" if backwards else "ssm_summary",
    )(dt, src, gates, rate2, keep)

def run_states(dt, dx, ins, outs, rate2, thr, off, everyone, pick):
    steps, rows, width = dt.shape
    chan, wide, rate, per, summ, kp = specs(steps, rows)
    count = everyone.shape[0]
    alls = pl.BlockSpec((count, 2 * STATE, LANES), lambda i: (0, 0, i))
    f = jnp.float32
    return pl.pallas_call(
        ssm_states, grid=(width // LANES,),
        in_specs=[chan, chan, wide, wide, rate, per, per, alls, pl.BlockSpec(memory_space=pltpu.SMEM)],
        out_specs=[chan, per],
        out_shape=[jax.ShapeDtypeStruct((steps, rows, width), f), jax.ShapeDtypeStruct((STATE, rows, width), f)],
        compiler_params=params(), name="ssm_states",
    )(dt, dx, ins, outs, rate2, thr, off, everyone, pick)

def run_grads(dt, dx, dy, ins, outs, rate2, rates, enter, thr, off, everyone, pick):
    steps, rows, width = dt.shape
    chan, wide, rate, per, summ, kp = specs(steps, rows)
    count = everyone.shape[0]
    alls = pl.BlockSpec((count, 2 * STATE, LANES), lambda i: (0, 0, i))
    f = jnp.float32
    s = jax.ShapeDtypeStruct
    return pl.pallas_call(
        ssm_grads, grid=(width // LANES,),
        in_specs=[chan, chan, chan, wide, wide, rate, rate, per, per, per, alls, pl.BlockSpec(memory_space=pltpu.SMEM)],
        out_specs=[chan, chan, wide, wide, per],
        out_shape=[s((steps, rows, width), f)] * 2 + [s((steps, STATE, rows, LANES), f)] * 2 + [s((STATE, rows, width), f)],
        scratch_shapes=[pltpu.VMEM((steps, STATE, rows, LANES), f)] * 2,
        compiler_params=params(), name="ssm_grads",
    )(dt, dx, dy, ins, outs, rate2, rates, enter, thr, off, everyone, pick)


def conv_back_kernel(prod_ref, dy_ref, dt_ref, more_ref, conv_ref, padded_ref, skip_ref, dconv_ref, sums_ref):
    steps = conv_ref.shape[0]
    zero = jnp.zeros(conv_ref.shape[1:], jnp.float32)
    skip = spread(skip_ref[...], zero)

    def step(t, sums):
        value = conv_ref[t]
        sigma = jax.nn.sigmoid(value)
        grad = prod_ref[t] * dt_ref[t] + dy_ref[t] * skip + more_ref[t]
        grad = grad * (sigma * (1.0 + value * (1.0 - sigma)))
        dconv_ref[t] = grad
        taps = tuple(sums[k] + grad * padded_ref[t + k] for k in range(CONV))
        return taps + (sums[CONV] + grad,)

    sums = lax.fori_loop(0, steps, step, (zero,) * (CONV + 1), unroll=2)
    sums_ref[...] = jnp.zeros_like(sums_ref)
    for k in range(CONV + 1):
        sums_ref[k : k + 1, :] = jnp.sum(sums[k], axis=0, keepdims=True)


def conv_back(prod, dys, dt, more, conv, padded, skip):
    steps, rows, width = conv.shape
    chan = pl.BlockSpec((steps, rows, LANES), lambda i: (0, 0, i))
    longer = pl.BlockSpec((padded.shape[0], rows, LANES), lambda i: (0, 0, i))
    f32 = jnp.float32
    return pl.pallas_call(
        conv_back_kernel,
        grid=(width // LANES,),
        in_specs=[chan] * 5 + [longer, pl.BlockSpec((1, LANES), lambda i: (0, i))],
        out_specs=[chan, pl.BlockSpec((8, LANES), lambda i: (0, i))],
        out_shape=[
            jax.ShapeDtypeStruct((steps, rows, width), f32), jax.ShapeDtypeStruct((8, width), f32)
        ],
        compiler_params=params(),
        name="conv_back",
    )(prod, dys, dt, more, conv, padded, skip[None])


class Ring:
    def __init__(self, count):
        self.count = count
        self.chips = count // 2
        self.side = math.isqrt(self.chips)
        self.long = self.chips // 2
        self.short = self.chips - 1 - self.long
        self.me = lax.axis_index("seq")
        self.core = self.me % 2
        self.way = 1 - 2 * self.core
        self.at = self.flip(self.me // 2)
        self.partner = self.me + self.way
        self.long_next = self.device(1, self.core)
        self.short_next = self.device(-1, self.core)

    def flip(self, chip):
        row, column = chip // self.side, chip % self.side
        return row * self.side + column + (row % 2) * (self.side - 1 - 2 * column)

    def device(self, hops, core):
        place = (self.at + hops * self.way + 2 * self.chips) % self.chips
        return self.flip(place) * 2 + core


def remote(source, target, send_sem, recv_sem, axis, to):
    return pltpu.make_async_remote_copy(
        src_ref=source,
        dst_ref=target,
        send_sem=send_sem,
        recv_sem=recv_sem,
        device_id={axis: to},
        device_id_type=MESH,
    )


def greet(axis, devices):
    barrier = pltpu.get_barrier_semaphore()
    for to in devices:
        pl.semaphore_signal(barrier, inc=1, device_id={axis: to}, device_id_type=MESH)
    return len(devices)


def others_of(axis, count):
    me = lax.axis_index(axis)
    return [lax.rem(me + d, count) for d in range(1, count)]


class Gather:
    def __init__(self, ring, shard, full, by_rows, send_sem, recv_sem, own_sem):
        self.ring, self.shard, self.full, self.by_rows = ring, shard, full, by_rows
        self.send_sem, self.recv_sem = send_sem, recv_sem
        self.size = shard.shape[0 if by_rows else 1]
        self.own = pltpu.make_async_copy(shard, self.slot(ring.me), own_sem)
        self.sent = []

    def slot(self, device):
        part = pl.ds(pl.multiple_of(device * self.size, self.size), self.size)
        return self.full.at[part] if self.by_rows else self.full.at[:, part]

    def send(self, source, device, sem, to):
        copy = remote(
            source, self.slot(device), self.send_sem.at[len(self.sent)], self.recv_sem.at[sem],
            "seq", to,
        )
        copy.start()
        self.sent.append(copy)

    def wait(self, device, sem):
        slot = self.slot(device)
        remote(
            slot, slot, self.send_sem.at[0], self.recv_sem.at[sem], "seq", self.ring.partner
        ).wait_recv()

    def start(self):
        ring = self.ring
        self.send(self.shard, ring.me, 0, ring.long_next)
        if ring.short:
            self.send(self.shard, ring.me, ring.long, ring.short_next)
        self.send(self.shard, ring.me, ring.long + ring.short, ring.partner)
        self.own.start()

    def hop(self, i):
        ring = self.ring
        base = ring.long + ring.short + 1
        if i <= ring.long:
            device = ring.device(-i, ring.core)
            self.wait(device, i - 1)
            if i < ring.long:
                self.send(self.slot(device), device, i, ring.long_next)
            self.send(self.slot(device), device, base + i - 1, ring.partner)
        if i <= ring.short:
            device = ring.device(i, ring.core)
            self.wait(device, ring.long + i - 1)
            if i < ring.short:
                self.send(self.slot(device), device, ring.long + i, ring.short_next)
            self.send(self.slot(device), device, base + ring.long + i - 1, ring.partner)

    def finish(self):
        ring = self.ring
        base = ring.long + ring.short + 1
        other = 1 - ring.core
        self.wait(ring.partner, base - 1)
        for i in range(1, ring.long + 1):
            self.wait(ring.device(i, other), base + i - 1)
        for i in range(1, ring.short + 1):
            self.wait(ring.device(-i, other), base + ring.long + i - 1)
        self.own.wait()
        for copy in self.sent:
            copy.wait_send()


class Swap:
    def __init__(self, count, source, target, send_sem, recv_sem, own_sem):
        self.count, self.source, self.target = count, source, target
        self.send_sem, self.recv_sem = send_sem, recv_sem
        self.me = lax.axis_index("seq")
        self.rows = target.shape[0] // count
        self.width = target.shape[1]
        self.own = pltpu.make_async_copy(self.block(self.me), self.slot(self.me), own_sem)
        self.sent = []

    def block(self, to):
        if len(self.source.shape) == 3:
            return self.source.at[to]
        return self.source.at[:, pl.ds(pl.multiple_of(to * self.width, self.width), self.width)]

    def slot(self, device):
        return self.target.at[pl.ds(pl.multiple_of(device * self.rows, self.rows), self.rows)]

    def start(self):
        for d in range(1, self.count):
            to = lax.rem(self.me + d, self.count)
            copy = remote(
                self.block(to), self.slot(self.me), self.send_sem.at[d - 1],
                self.recv_sem.at[d - 1], "seq", to,
            )
            copy.start()
            self.sent.append(copy)
        self.own.start()

    def finish(self):
        for d in range(1, self.count):
            slot = self.slot(lax.rem(self.me + self.count - d, self.count))
            remote(
                slot, slot, self.send_sem.at[0], self.recv_sem.at[d - 1], "seq",
                lax.rem(self.me + d, self.count),
            ).wait_recv()
        self.own.wait()
        for copy in self.sent:
            copy.wait_send()


def rms_scale(x):
    return lax.rsqrt(jnp.mean(x * x, axis=-1, keepdims=True) + EPS)


def forward_local(ins, outs, total):
    x_ref, keep_ref, gain_ref = ins
    new = x_ref[...] + keep_ref[:, 0:1] * total
    outs[0][...] = new
    return new * rms_scale(new) * gain_ref[...], None


def norm_back(ins, total):
    x_ref, keep_ref, gain_ref, grad_ref = ins[:4]
    x = x_ref[...]
    scale = rms_scale(x)
    weighted = gain_ref[...] * total
    middle = jnp.mean(weighted * x, axis=-1, keepdims=True)
    row = jnp.sum(total * x * scale, axis=0, keepdims=True)
    return grad_ref[...] + scale * weighted - x * (scale * scale * scale) * middle, row


def backward_local(ins, outs, total):
    new, row = norm_back(ins, total)
    outs[0][...] = new
    outs[1][...] = row
    return ins[1][:, 0:1] * new, None


def last_backward_local(ins, outs, total):
    return norm_back(ins, total)


def sum_local(ins, outs, total):
    return total, None


class Spread:
    def __init__(self, count, source, target, send_sem, recv_sem, own_sem):
        self.count, self.source, self.target = count, source, target
        self.send_sem, self.recv_sem = send_sem, recv_sem
        self.me = lax.axis_index("seq")
        self.own = pltpu.make_async_copy(source, target.at[self.me], own_sem)
        self.sent = []

    def start(self):
        for d in range(1, self.count):
            copy = remote(
                self.source, self.target.at[self.me], self.send_sem.at[d - 1],
                self.recv_sem.at[d - 1], "seq", lax.rem(self.me + d, self.count),
            )
            copy.start()
            self.sent.append(copy)
        self.own.start()

    def finish(self):
        for d in range(1, self.count):
            slot = self.target.at[lax.rem(self.me + self.count - d, self.count)]
            remote(
                slot, slot, self.send_sem.at[0], self.recv_sem.at[d - 1], "seq",
                lax.rem(self.me + d, self.count),
            ).wait_recv()
        self.own.wait()
        for copy in self.sent:
            copy.wait_send()


class PlaneScatter:
    def __init__(self, planes, part, target, got, send_sem, recv_sem):
        self.planes, self.part, self.target, self.got = planes, part, target, got
        self.send_sem, self.recv_sem = send_sem, recv_sem
        self.me = lax.axis_index("mp")
        self.sent = []

    def block(self, to):
        rows = self.part.shape[0] // self.planes
        return pl.ds(pl.multiple_of(to * rows, rows), rows)

    def start(self):
        for d in range(1, self.planes):
            to = lax.rem(self.me + d, self.planes)
            copy = remote(
                self.part.at[self.block(to)], self.got.at[d - 1], self.send_sem.at[d - 1],
                self.recv_sem.at[d - 1], "mp", to,
            )
            copy.start()
            self.sent.append(copy)

    def total(self):
        total = self.part[self.block(self.me), :].astype(jnp.float32)
        for d in range(1, self.planes):
            self.sent[d - 1].wait_recv()
            total = total + self.got[d - 1].astype(jnp.float32)
        return total

    def finish(self):
        self.target[...] = self.total()
        for copy in self.sent:
            copy.wait_send()


class PlaneCollect:
    def __init__(self, planes, source, target, send_sem, recv_sem):
        self.planes, self.source, self.target = planes, source, target
        self.send_sem, self.recv_sem = send_sem, recv_sem
        self.me = lax.axis_index("mp")
        rows = source.shape[0]
        self.own = target.at[pl.ds(pl.multiple_of(self.me * rows, rows), rows)]
        self.sent = []

    def start(self):
        for d in range(1, self.planes):
            copy = remote(
                self.source, self.own, self.send_sem.at[d - 1], self.recv_sem.at[d - 1],
                "mp", lax.rem(self.me + d, self.planes),
            )
            copy.start()
            self.sent.append(copy)
        self.own[...] = self.source[...]

    def finish(self):
        for copy in self.sent:
            copy.wait_recv()
        for copy in self.sent:
            copy.wait_send()


class SeqSum:
    def __init__(self, count, parts, out, low, got, mine, send_sem, recv_sem):
        self.count, self.parts, self.out = count, parts, out
        self.low, self.got, self.mine = low, got, mine
        self.send_sem, self.recv_sem = send_sem, recv_sem
        self.me = lax.axis_index("seq")
        self.rows = low.shape[0] // count
        self.first, self.second = [], []

    def block(self, device):
        return pl.ds(pl.multiple_of(device * self.rows, self.rows), self.rows)

    def start(self):
        at = 0
        for part in self.parts:
            size = part.shape[0]
            self.low[at : at + size, :] = part[...].astype(self.low.dtype)
            at += size
        if at < self.low.shape[0]:
            self.low[at:, :] = jnp.zeros((self.low.shape[0] - at, self.low.shape[1]), self.low.dtype)
        for d in range(1, self.count):
            to = lax.rem(self.me + d, self.count)
            copy = remote(
                self.low.at[self.block(to)], self.got.at[d - 1],
                self.send_sem.at[d - 1], self.recv_sem.at[d - 1], "seq", to,
            )
            copy.start()
            self.first.append(copy)

    def middle(self):
        own = self.block(self.me)
        total = self.low[own, :].astype(jnp.float32)
        for d in range(1, self.count):
            self.first[d - 1].wait_recv()
            total = total + self.got[d - 1].astype(jnp.float32)
        self.mine[...] = total.astype(self.mine.dtype)
        for d in range(1, self.count):
            copy = remote(
                self.mine, self.out.at[own], self.send_sem.at[self.count + d - 1],
                self.recv_sem.at[self.count + d - 1], "seq", lax.rem(self.me + d, self.count),
            )
            copy.start()
            self.second.append(copy)
        self.out[own, :] = self.mine[...]

    def finish(self):
        for d in range(1, self.count):
            slot = self.out.at[self.block(lax.rem(self.me + self.count - d, self.count))]
            remote(
                slot, slot, self.send_sem.at[self.count], self.recv_sem.at[self.count + d - 1],
                "seq", lax.rem(self.me + d, self.count),
            ).wait_recv()
        for copy in self.first + self.second:
            copy.wait_send()


class GainSum:
    def __init__(self, planes, count, rows, out, across, along, sems):
        self.planes, self.count, self.rows, self.out = planes, count, rows, out
        self.across, self.along, self.sems = across, along, sems
        self.me, self.plane = lax.axis_index("seq"), lax.axis_index("mp")
        self.first, self.second = [], []

    def start(self, row):
        held = self.rows.shape[0]
        self.out[...] = self.rows[...]
        self.out[held - 1 : held, :] = row
        for d in range(1, self.planes):
            copy = remote(
                self.out, self.across.at[d - 1], self.sems[0].at[d - 1], self.sems[1].at[d - 1],
                "mp", lax.rem(self.plane + d, self.planes),
            )
            copy.start()
            self.first.append(copy)

    def middle(self):
        total = self.out[...]
        for d in range(1, self.planes):
            self.first[d - 1].wait_recv()
            total = total + self.across[d - 1]
        for copy in self.first:
            copy.wait_send()
        self.out[...] = total
        for d in range(1, self.count):
            copy = remote(
                self.out, self.along.at[d - 1], self.sems[2].at[d - 1], self.sems[3].at[d - 1],
                "seq", lax.rem(self.me + d, self.count),
            )
            copy.start()
            self.second.append(copy)

    def finish(self):
        total = self.out[...]
        for d in range(1, self.count):
            self.second[d - 1].wait_recv()
            total = total + self.along[d - 1]
        for copy in self.second:
            copy.wait_send()
        self.out[...] = total


class Plan:
    def __init__(self, gathers=(), swaps=(), spreads=(), sums=()):
        self.count = lax.axis_size("seq")
        count = self.count
        vmem = pl.BlockSpec(memory_space=pltpu.VMEM)
        hbm = pl.BlockSpec(memory_space=pl.ANY)
        shape = jax.ShapeDtypeStruct
        self.sources, self.in_specs, self.shapes, self.out_specs, self.scratch = [], [], [], [], []
        self.kinds, self.after = [], []
        sems = [
            pltpu.SemaphoreType.DMA((2 * count,)), pltpu.SemaphoreType.DMA((2 * count,)),
            pltpu.SemaphoreType.DMA,
        ]
        for array, rows in gathers:
            height, width = array.shape
            by_rows = rows or width % LANES != 0
            self.add("rows" if by_rows else "columns", [array], hbm, hbm, sems, shape(
                (count * height, width) if by_rows else (height, count * width), array.dtype
            ))
            self.after[-1] = (height, width) if by_rows and not rows else None
        for array in swaps:
            height, width = array.shape[0], array.shape[1] // count
            if width % LANES:
                array = array.reshape(height, count, width).swapaxes(0, 1)
            self.add("swap", [array], hbm, hbm, sems, shape((count * height, width), array.dtype))
        for array in spreads:
            self.add("spread", [array], vmem, vmem, sems, shape((count,) + array.shape, array.dtype))
        for parts in sums:
            have, width = sum(part.shape[0] for part in parts), parts[0].shape[1]
            rows = -(-have // (16 * count)) * 16
            bf16 = jnp.bfloat16
            self.add("sum", list(parts), vmem, vmem, sems + [
                pltpu.VMEM((rows * count, width), bf16),
                pltpu.VMEM((count - 1, rows, width), bf16),
                pltpu.VMEM((rows, width), bf16),
            ], shape((rows * count, width), bf16))

    def add(self, kind, arrays, in_spec, out_spec, scratch, shape):
        self.kinds.append((kind, len(arrays), len(scratch)))
        self.sources += arrays
        self.in_specs += [in_spec] * len(arrays)
        self.shapes.append(shape)
        self.out_specs.append(out_spec)
        self.scratch += scratch
        self.after.append(None)

    def results(self, targets):
        return [
            t if cut is None
            else t.reshape((self.count,) + cut).swapaxes(0, 1).reshape(cut[0], self.count * cut[1])
            for t, cut in zip(targets, self.after)
        ]

    def bind(self, sources, targets, scratch):
        count = self.count
        self.ring = None
        self.items = []
        self.wide = False
        for (kind, many, held), target in zip(self.kinds, targets):
            mine, sources = sources[:many], sources[many:]
            sems, scratch = scratch[:held], scratch[held:]
            if kind in ("rows", "columns"):
                if self.ring is None:
                    self.ring = Ring(count)
                self.items.append(Gather(self.ring, mine[0], target, kind == "rows", *sems))
                continue
            self.wide = True
            if kind == "swap":
                self.items.append(Swap(count, mine[0], target, *sems))
            elif kind == "spread":
                self.items.append(Spread(count, mine[0], target, *sems))
            else:
                self.items.append(SeqSum(count, mine, target, *sems[3:], *sems[:2]))

    def greet(self, wide=False):
        if self.wide or wide:
            return greet("seq", others_of("seq", self.count))
        if self.ring is not None:
            near = [self.ring.long_next, self.ring.partner]
            if self.ring.short:
                near.append(self.ring.short_next)
            return greet("seq", near)
        return 0

    def start(self):
        for item in self.items:
            item.start()

    def hops(self):
        gathers = [item for item in self.items if isinstance(item, Gather)]
        if gathers:
            for i in range(1, self.ring.long + 1):
                for item in gathers:
                    item.hop(i)
        for item in self.items:
            if isinstance(item, SeqSum):
                item.middle()

    def finish(self):
        for item in self.items:
            item.finish()


def step_kernel(planes, plan, local, n_ins, n_outs, gain_at, *refs):
    part_ref, refs = refs[0], refs[1:]
    ins, refs = refs[:n_ins], refs[n_ins:]
    sources, refs = refs[: len(plan.sources)], refs[len(plan.sources) :]
    full_ref, refs = refs[0], refs[1:]
    outs, refs = refs[:n_outs], refs[n_outs:]
    targets, refs = refs[: len(plan.shapes)], refs[len(plan.shapes) :]
    got, mine = refs[:2]
    sems, refs = refs[2:6], refs[6:]
    plan.bind(sources, targets, refs[: len(plan.scratch)])
    refs = refs[len(plan.scratch) :]
    gains = None
    if gain_at is not None:
        gains = GainSum(planes, plan.count, ins[gain_at], outs[0], refs[0], refs[1], refs[2:])
    greeted = greet("mp", others_of("mp", planes)) + plan.greet(gains is not None)
    pl.semaphore_wait(pltpu.get_barrier_semaphore(), greeted)
    scatter = PlaneScatter(planes, part_ref, None, got, sems[0], sems[1])
    scatter.start()
    plan.start()
    value, row = local(ins, outs, scatter.total())
    mine[...] = value.astype(mine.dtype)
    if gains is not None:
        gains.start(row)
    collect = PlaneCollect(planes, mine, full_ref, sems[2], sems[3])
    collect.start()
    plan.hops()
    if gains is not None:
        gains.middle()
    collect.finish()
    plan.finish()
    if gains is not None:
        gains.finish()
    for copy in scatter.sent:
        copy.wait_send()


def remote_params(cid):
    return pltpu.CompilerParams(
        collective_id=cid, has_side_effects=True, vmem_limit_bytes=VMEM
    )


def z_step(name, cid, local, part, others, extra, out_dtype=jnp.bfloat16, gain_at=None, **carried):
    planes = lax.axis_size("mp")
    plan = Plan(**carried)
    rows, width = part.shape
    share = rows // planes
    f32 = jnp.float32
    shape = jax.ShapeDtypeStruct
    held = 0 if gain_at is None else others[gain_at].shape[0]
    kinds = {
        "share": shape((share, width), f32),
        "gain": shape((1, width), f32),
        "gains": shape((held, width), f32),
    }
    gain_scratch = [] if gain_at is None else [
        pltpu.VMEM((planes - 1, held, width), f32),
        pltpu.VMEM((plan.count - 1, held, width), f32),
        pltpu.SemaphoreType.DMA((planes,)),
        pltpu.SemaphoreType.DMA((planes,)),
        pltpu.SemaphoreType.DMA((plan.count,)),
        pltpu.SemaphoreType.DMA((plan.count,)),
    ]
    vmem = pl.BlockSpec(memory_space=pltpu.VMEM)
    result = pl.pallas_call(
        functools.partial(step_kernel, planes, plan, local, len(others), len(extra), gain_at),
        out_shape=[shape((rows, width), out_dtype)] + [kinds[kind] for kind in extra] + plan.shapes,
        in_specs=[vmem] * (1 + len(others)) + plan.in_specs,
        out_specs=[vmem] * (1 + len(extra)) + plan.out_specs,
        scratch_shapes=[
            pltpu.VMEM((planes - 1, share, width), part.dtype),
            pltpu.VMEM((share, width), out_dtype),
        ]
        + [pltpu.SemaphoreType.DMA((planes,))] * 4
        + plan.scratch + gain_scratch,
        compiler_params=remote_params(cid),
        name=name,
    )(part, *others, *plan.sources)
    cut = 1 + len(extra)
    return list(result[:cut]) + [plan.results(result[cut:])]


def carry_kernel(planes, plan, scatters, collects, *refs):
    sources, refs = refs[: len(plan.sources)], refs[len(plan.sources) :]
    parts, refs = refs[:scatters], refs[scatters:]
    shares, refs = refs[:collects], refs[collects:]
    targets, refs = refs[: len(plan.shapes)], refs[len(plan.shapes) :]
    sums, refs = refs[:scatters], refs[scatters:]
    fulls, refs = refs[:collects], refs[collects:]
    plan.bind(sources, targets, refs[: len(plan.scratch)])
    refs = refs[len(plan.scratch) :]
    items = []
    for part, total in zip(parts, sums):
        items.append(PlaneScatter(planes, part, total, *refs[:3]))
        refs = refs[3:]
    for share, full in zip(shares, fulls):
        items.append(PlaneCollect(planes, share, full, *refs[:2]))
        refs = refs[2:]
    greeted = plan.greet()
    if items:
        greeted += greet("mp", others_of("mp", planes))
    pl.semaphore_wait(pltpu.get_barrier_semaphore(), greeted)
    plan.start()
    for item in items:
        item.start()
    plan.hops()
    plan.finish()
    for item in items:
        item.finish()


def carry(name, cid, scatters=(), collects=(), **carried):
    planes = lax.axis_size("mp")
    plan = Plan(**carried)
    vmem = pl.BlockSpec(memory_space=pltpu.VMEM)
    shape = jax.ShapeDtypeStruct
    sems = [pltpu.SemaphoreType.DMA((planes,))] * 2
    shapes, scratch = [], []
    for part in scatters:
        share = (part.shape[0] // planes, part.shape[1])
        shapes.append(shape(share, jnp.float32))
        scratch += [pltpu.VMEM((planes - 1,) + share, part.dtype)] + sems
    for part in collects:
        shapes.append(shape((part.shape[0] * planes, part.shape[1]), part.dtype))
        scratch += sems
    result = pl.pallas_call(
        functools.partial(carry_kernel, planes, plan, len(scatters), len(collects)),
        out_shape=plan.shapes + shapes,
        in_specs=plan.in_specs + [vmem] * (len(scatters) + len(collects)),
        out_specs=plan.out_specs + [vmem] * len(shapes),
        scratch_shapes=plan.scratch + scratch,
        compiler_params=remote_params(cid),
        name=name,
    )(*plan.sources, *scatters, *collects)
    cut = len(plan.shapes)
    return plan.results(result[:cut]) + list(result[cut:])


SCALE = 1.0 / math.sqrt(HEAD_DIM)


def nt(left, right):
    return lax.dot_general(
        left, right, (((1,), (1,)), ((), ())), preferred_element_type=jnp.float32
    )


def nn(left, right):
    return jnp.dot(left, right, preferred_element_type=jnp.float32)


def attend_kernel(q_ref, k_ref, v_ref, low_ref, high_ref, pos_ref, out_ref, lse_ref):
    scores = nt(q_ref[...], k_ref[...]) * SCALE
    pos = pos_ref[...]
    scores = jnp.where((pos >= low_ref[...]) & (pos <= high_ref[...]), scores, -1e30)
    top = jnp.max(scores, axis=-1, keepdims=True)
    expo = jnp.exp(scores - top)
    mass = jnp.sum(expo, axis=-1, keepdims=True)
    probs = (expo / mass).astype(jnp.bfloat16)
    out_ref[...] = nn(probs, v_ref[...]).astype(jnp.bfloat16)
    lse_ref[0] = top + jnp.log(mass)


def query_back_kernel(q_ref, k_ref, v_ref, g_ref, low_ref, high_ref, pos_ref, lse_ref, dq_ref, mid_ref):
    keys = k_ref[...]
    scores = nt(q_ref[...], keys) * SCALE
    pos = pos_ref[...]
    scores = jnp.where((pos >= low_ref[...]) & (pos <= high_ref[...]), scores, -1e30)
    probs = jnp.exp(scores - lse_ref[0])
    prob_grad = nt(g_ref[...], v_ref[...])
    middle = jnp.sum(probs * prob_grad, axis=-1, keepdims=True)
    score_grad = (probs * (prob_grad - middle)).astype(jnp.bfloat16)
    dq_ref[...] = (nn(score_grad, keys) * SCALE).astype(jnp.bfloat16)
    mid_ref[0] = middle


def key_back_kernel(k_ref, v_ref, q_ref, g_ref, pos_ref, low_ref, high_ref, lse_ref, mid_ref, dk_ref, dv_ref):
    queries, grads = q_ref[...], g_ref[...]
    scores = nt(k_ref[...], queries) * SCALE
    pos = pos_ref[...]
    scores = jnp.where((pos >= low_ref[...]) & (pos <= high_ref[...]), scores, -1e30)
    probs = jnp.exp(scores - lse_ref[0])
    prob_grad = nt(v_ref[...], grads)
    score_grad = (probs * (prob_grad - mid_ref[0])).astype(jnp.bfloat16)
    dk_ref[...] = (nn(score_grad, queries) * SCALE).astype(jnp.bfloat16)
    dv_ref[...] = nn(probs.astype(jnp.bfloat16), grads).astype(jnp.bfloat16)


def head_block(rows, first):
    return pl.BlockSpec((rows, HEAD_DIM), lambda h: (0, first + h))


def whole_block(*shape):
    return pl.BlockSpec(shape, lambda h: (0,) * len(shape))


def attend_params():
    return pltpu.CompilerParams(vmem_limit_bytes=VMEM, dimension_semantics=("arbitrary",))


def attend_call(q, pair, low, high, pos, heads):
    rows, keys = q.shape[0], pair.shape[0]
    return pl.pallas_call(
        attend_kernel,
        grid=(heads,),
        in_specs=[
            head_block(rows, 0), head_block(keys, 0), head_block(keys, heads),
            whole_block(rows, 1), whole_block(rows, 1), whole_block(1, keys),
        ],
        out_specs=[head_block(rows, 0), pl.BlockSpec((1, rows, 1), lambda h: (h, 0, 0))],
        out_shape=[
            jax.ShapeDtypeStruct(q.shape, jnp.bfloat16),
            jax.ShapeDtypeStruct((heads, rows, 1), jnp.float32),
        ],
        compiler_params=attend_params(),
        name="attend",
    )(q, pair, pair, low, high, pos)


def query_back_call(q, pair, grad, low, high, pos, lse, heads):
    rows, keys = q.shape[0], pair.shape[0]
    stat = pl.BlockSpec((1, rows, 1), lambda h: (h, 0, 0))
    return pl.pallas_call(
        query_back_kernel,
        grid=(heads,),
        in_specs=[
            head_block(rows, 0), head_block(keys, 0), head_block(keys, heads),
            head_block(rows, 0),
            whole_block(rows, 1), whole_block(rows, 1), whole_block(1, keys), stat,
        ],
        out_specs=[head_block(rows, 0), stat],
        out_shape=[
            jax.ShapeDtypeStruct(q.shape, jnp.bfloat16),
            jax.ShapeDtypeStruct((heads, rows, 1), jnp.float32),
        ],
        compiler_params=attend_params(),
        name="query_back",
    )(q, pair, pair, grad, low, high, pos, lse)


def key_back_call(pair, queries, grads, pos, low, high, lse, mid, heads):
    rows, many = pair.shape[0], queries.shape[0]
    stat = pl.BlockSpec((1, 1, many), lambda h: (h, 0, 0))
    shape = jax.ShapeDtypeStruct((rows, heads * HEAD_DIM), jnp.bfloat16)
    return pl.pallas_call(
        key_back_kernel,
        grid=(heads,),
        in_specs=[
            head_block(rows, 0), head_block(rows, heads), head_block(many, 0), head_block(many, 0),
            whole_block(rows, 1), whole_block(1, many), whole_block(1, many), stat, stat,
        ],
        out_specs=[head_block(rows, 0)] * 2,
        out_shape=[shape, shape],
        compiler_params=attend_params(),
        name="key_back",
    )(pair, pair, queries, grads, pos, low, high, lse, mid)


def shifted(value, axis, steps):
    count = lax.axis_size(axis)
    leading, last = (max(0, -steps), min(count, count - steps))
    return lax.ppermute(value, axis, [(source, source + steps) for source in range(leading, last)])


def matmul(left, right):
    return jnp.dot(left, right, preferred_element_type=jnp.float32)


def matmul_tn(left, right):
    return lax.dot_general(
        left, right, (((0,), (0,)), ((), ())), preferred_element_type=jnp.float32
    )


def matmul_nt(left, right):
    return lax.dot_general(
        left, right, (((1,), (1,)), ((), ())), preferred_element_type=jnp.float32
    )


def layout(lengths, positions, slot, total):
    starts = jnp.array([0, slot, 2 * slot, total - 2 * slot, total - slot], jnp.int32)
    seg = jnp.sum((positions[:, None] >= starts[None, :]).astype(jnp.int32), axis=1) - 1
    which = (seg[:, None] == jnp.arange(5, dtype=jnp.int32)[None, :]).astype(jnp.int32)
    start_of = jnp.sum(which * starts[None, :], axis=1)
    length_of = jnp.sum(which * lengths[None, :], axis=1)
    keep = (positions - start_of < length_of).astype(jnp.float32)
    first = (positions == start_of).astype(jnp.float32)
    return (start_of, keep, first)


def silu_slope(value):
    sigma = jax.nn.sigmoid(value)
    return sigma * (1.0 + value * (1.0 - sigma))


def gather_rows(array):
    return lax.all_gather(array, "seq", axis=0, tiled=True)


def gather_columns(array):
    return lax.all_gather(array, "seq", axis=1, tiled=True)


def after(value, *earlier):
    return lax.optimization_barrier((value,) + earlier)[0]


def by_chunk(value):
    rows = value.shape[0]
    return value.reshape((CHUNKS, rows // CHUNKS) + value.shape[1:]).swapaxes(0, 1)


def by_token(value):
    steps = value.shape[0]
    return value.swapaxes(0, 1).reshape((CHUNKS * steps,) + value.shape[2:])


def widened(gates, steps):
    gates = gates.reshape(STATE, steps, CHUNKS).swapaxes(0, 1)
    return jnp.broadcast_to(gates[..., None], (steps, STATE, CHUNKS, LANES))


def ffn_forward(normed, both_w):
    hidden_width = both_w.shape[1] // 2
    gate = matmul(normed, both_w[:, :hidden_width])
    lift = matmul(normed, both_w[:, hidden_width:])
    hidden = (jax.nn.silu(gate) * lift).astype(jnp.bfloat16)
    return (gate, lift, hidden)


def ffn_backward(out_low, both_w, down_w, gate, lift):
    hidden_grad = matmul_nt(out_low, down_w)
    gate_low = (hidden_grad * lift * silu_slope(gate)).astype(jnp.bfloat16)
    lift_low = (hidden_grad * jax.nn.silu(gate)).astype(jnp.bfloat16)
    both = jnp.concatenate([gate_low, lift_low], axis=1)
    return (matmul_nt(both, both_w).astype(jnp.bfloat16), both)


def body(
    tokens,
    lengths,
    out_grad,
    mixer_gain,
    mixer_value,
    mixer_gate,
    conv_weight,
    conv_bias,
    select_proj,
    step_proj,
    step_bias,
    decay_log,
    skip_gain,
    mixer_out,
    first_gain,
    first_gate,
    first_lift,
    first_down,
    attend_gain,
    query_proj,
    key_proj,
    value_proj,
    attend_out,
    second_gain,
    second_gate,
    second_lift,
    second_down,
):
    f32, bf16 = jnp.float32, jnp.bfloat16
    length = tokens.shape[0]
    shards, planes = lax.axis_size("seq"), lax.axis_size("mp")
    me, plane = lax.axis_index("seq"), lax.axis_index("mp")
    total = length * shards
    slot = length // 4
    steps = length // CHUNKS
    share = length // planes
    positions = me * length + jnp.arange(length, dtype=jnp.int32)
    start_of, keep, first = layout(lengths, positions, slot, total)

    def mine(rows):
        return lax.dynamic_slice_in_dim(rows, plane * share, share)

    keep = keep[:, None]
    keep_share = jnp.broadcast_to(mine(keep), (share, LANES))
    x0 = tokens.astype(f32)
    x0_share = mine(x0)

    few = total <= tokens.shape[1]

    def collect(rows):
        return gather_rows(rows) if few else rows

    def hosted(*items):
        return list(items) if few else []

    def row_grad(normed, grads):
        result = matmul_tn(normed, grads)
        if few:
            return result
        return lax.psum_scatter(
            result.astype(bf16), "seq", scatter_dimension=0, tiled=True
        ).astype(f32)

    def column_grad(hidden, grads):
        result = matmul_tn(hidden, grads)
        if few:
            return result
        return lax.psum_scatter(
            result.astype(bf16), "seq", scatter_dimension=1, tiled=True
        ).astype(f32)

    (value_w,) = carry("value_weights", 1, gathers=[(mixer_value, True)])
    gate_w = gather_rows(mixer_gate)
    first_both = gather_rows(after(jnp.concatenate([first_gate, first_lift], axis=1), value_w))

    u1 = by_chunk((x0 * rms_scale(x0) * mixer_gain).astype(bf16)).reshape(length, -1)
    inner = matmul(u1, value_w).reshape(steps, CHUNKS, -1)
    width = inner.shape[-1]
    zg = matmul(u1, gate_w)
    joined = 1.0 - first.reshape(CHUNKS, steps)[:, 0]
    prior = shifted(inner[steps - (CONV - 1) :, CHUNKS - 1], "seq", 1)
    halo = jnp.concatenate([prior[:, None], inner[steps - (CONV - 1) :, : CHUNKS - 1]], axis=1)
    padded = jnp.concatenate([halo * joined[None, :, None], inner], axis=0)
    conv = conv_bias[None, None, :]
    for tap in range(CONV):
        conv = conv + conv_weight[tap][None, None, :] * padded[tap : tap + steps]
    signal = jax.nn.silu(conv).astype(bf16)
    flat_signal = signal.reshape(length, width)
    select, (out_w,) = z_step(
        "select_sum", 2, sum_local, matmul_nt(select_proj, flat_signal), (), (), f32,
        gathers=[(mixer_out, False)],
    )
    step_low = select[:DT_RANK].astype(bf16)
    qkv_w = gather_rows(
        after(jnp.concatenate([query_proj, key_proj, value_proj], axis=1), select)
    )
    raised = (matmul_tn(step_low, step_proj) + step_bias[None, :]).reshape(steps, CHUNKS, width)
    dt = jax.nn.softplus(raised)
    signal_wide = signal.astype(f32)
    dx = dt * signal_wide
    rates = -jnp.exp(decay_log)
    rates2 = rates * LOG2E
    keep_chunk = jnp.broadcast_to(joined[:, None], (CHUNKS, LANES))
    ins = widened(select[DT_RANK : DT_RANK + STATE], steps)
    outs = widened(select[DT_RANK + STATE :], steps)
    order = jnp.arange(shards, dtype=jnp.int32)
    thr, off, summary = run_summary(dt, dx, ins, rates2, keep_chunk, False)
    (everyone,) = carry("state_spread", 3, spreads=[summary])
    states, enter = run_states(
        dt, dx, ins, outs, rates2, thr, off, everyone, (order < me).astype(jnp.int32)
    )
    ys = states + skip_gain[None, None, :] * signal_wide
    zg = zg.reshape(steps, CHUNKS, width)
    mix = by_token((ys * jax.nn.silu(zg)).astype(bf16))
    u2, x1_share, (first_w,) = z_step(
        "mixer_join", 4, forward_local, matmul(mix, out_w).astype(bf16),
        (x0_share, keep_share, first_gain[None]), ("share",), gathers=[(first_down, False)],
    )

    second_both = gather_rows(after(jnp.concatenate([second_gate, second_lift], axis=1), u2))

    gate1, lift1, hidden1 = ffn_forward(u2, first_both)
    u3, x2_share, (attend_w,) = z_step(
        "first_join", 5, forward_local, matmul(hidden1, first_w).astype(bf16),
        (x1_share, keep_share, attend_gain[None]), ("share",),
        gathers=[(attend_out, False)],
    )

    head_width = query_proj.shape[1]
    qkv = matmul(u3, qkv_w).astype(bf16)
    query, pair = qkv[:, :head_width], qkv[:, head_width:]
    (pairs,) = carry("keys_values", 6, gathers=[(pair, True)])
    heads = query.shape[1] // HEAD_DIM
    span = min(shards, WINDOW // length + 1) * length
    key_from = jnp.clip(positions[0] + length - span, 0, total - span)
    near_pairs = lax.dynamic_slice_in_dim(pairs, key_from, span)
    key_pos = (key_from + jnp.arange(span, dtype=jnp.int32))[None, :]
    low = jnp.maximum(start_of, positions - (WINDOW - 1))[:, None]
    high = positions[:, None]
    att, lse = attend_call(query, near_pairs, low, high, key_pos, heads)
    u4, x3_share, (queries, second_w) = z_step(
        "attend_join", 7, forward_local, matmul(att, attend_w).astype(bf16),
        (x2_share, keep_share, second_gain[None]), ("share",),
        gathers=[(query, True), (second_down, False)],
    )
    early = jnp.concatenate([mix, hidden1, att], axis=1)
    early_all = collect(after(early, u4))

    gate2, lift2, hidden2 = ffn_forward(u4, second_both)
    wide_grad = out_grad.astype(f32)
    e4 = (keep * wide_grad).astype(bf16)
    du4, dboth2 = ffn_backward(e4, second_both, second_w, gate2, lift2)
    e3, g3_share, second_gain_part, ue4_all = z_step(
        "second_back", 8, backward_local, du4,
        (x3_share, keep_share, second_gain[None], mine(wide_grad)), ("share", "gain"),
        swaps=hosted(u4, e4),
    )
    late = jnp.concatenate([hidden2, dboth2], axis=1)
    late_all = collect(late)
    part4 = matmul(hidden2, second_w).astype(bf16)

    datt = matmul_nt(e3, attend_w).astype(bf16)
    dq, middle = query_back_call(query, near_pairs, datt, low, high, key_pos, lse, heads)
    stats = jnp.concatenate([lse, middle], axis=0).reshape(2 * heads, length)
    datts, all_stats, sum4 = carry(
        "query_grads", 9, gathers=[(datt, True), (stats, True)], scatters=[part4]
    )
    all_stats = all_stats.reshape(shards, 2 * heads, length).swapaxes(0, 1).reshape(2 * heads, total)
    query_from = jnp.clip(positions[0], 0, total - span)
    every_pos = query_from + jnp.arange(span, dtype=jnp.int32)
    every_start, _, _ = layout(lengths, every_pos, slot, total)
    every_low = jnp.maximum(every_start, every_pos - (WINDOW - 1))[None, :]
    near_stats = lax.dynamic_slice_in_dim(all_stats, query_from, span, axis=1)[:, None]
    dk, dv = key_back_call(
        pair,
        lax.dynamic_slice_in_dim(queries, query_from, span),
        lax.dynamic_slice_in_dim(datts, query_from, span),
        high, every_low, every_pos[None, :], near_stats[:heads], near_stats[heads:], heads,
    )
    dqkv = jnp.concatenate([dq, dk, dv], axis=1)
    du3 = matmul_nt(dqkv, qkv_w)
    e2, g2_share, attend_gain_part, _ = z_step(
        "attend_back", 10, backward_local, after(du3.astype(bf16), early_all),
        (x2_share, keep_share, attend_gain[None], g3_share), ("share", "gain"),
    )

    du2, dboth1 = ffn_backward(e2, first_both, first_w, gate1, lift1)
    e1, g1_share, first_gain_part, ue3_all = z_step(
        "first_back", 11, backward_local, after(du2, late_all),
        (x1_share, keep_share, first_gain[None], g2_share), ("share", "gain"), swaps=hosted(u3, e3),
    )
    dlater = jnp.concatenate([dboth1, dqkv], axis=1)
    dlater_all = collect(dlater)

    dmix = matmul_nt(by_chunk(e1).reshape(length, -1), out_w).reshape(steps, CHUNKS, width)
    dys = dmix * jax.nn.silu(zg)
    dzg = (dmix * ys * silu_slope(zg)).astype(bf16).reshape(length, width)
    dzg_all = collect(dzg)
    skip_grad = jnp.sum(dys * signal_wide, axis=(0, 1))
    thr, off, summary = run_summary(dt, dys, outs, rates2, keep_chunk, True)
    *ue2_all, everyone, mixed = carry(
        "grad_spread", 13, swaps=hosted(u2, e2), spreads=[summary],
        collects=[(x3_share + keep_share[:, 0:1] * sum4).astype(bf16)],
    )
    ddt, prod, in_wide, out_wide, log_wide = run_grads(
        dt, dx, dys, ins, outs, rates2, rates, enter, thr, off, everyone,
        (order > me).astype(jnp.int32),
    )
    dpre = (ddt + prod * signal_wide) * jax.nn.sigmoid(raised)
    step_bias_grad = jnp.sum(dpre, axis=(0, 1))
    dpr = dpre.astype(bf16).reshape(length, width)
    step_grad = matmul(step_low, dpr)
    dsel, ue1_all = z_step(
        "select_back", 14, sum_local,
        jnp.concatenate(
            [
                matmul_nt(step_proj, dpr),
                jnp.sum(in_wide, axis=-1).swapaxes(0, 1).reshape(STATE, length),
                jnp.sum(out_wide, axis=-1).swapaxes(0, 1).reshape(STATE, length),
            ]
        ),
        (), (), f32, swaps=hosted(u1, e1),
    )
    dsel = dsel.astype(bf16)
    select_grad = matmul(dsel, flat_signal)
    more = matmul_tn(dsel, select_proj).reshape(steps, CHUNKS, width)
    dconv, conv_sums = conv_back(prod, dys, dt, more, conv, padded, skip_gain)
    head = dconv[: CONV - 1] * joined[None, :, None]
    later = shifted(head[:, 0], "seq", -1)
    tail = jnp.concatenate([head[:, 1:], later[:, None]], axis=1)
    extended = jnp.concatenate([dconv, tail], axis=0)
    dxin = 0.0
    for tap in range(CONV):
        lag = CONV - 1 - tap
        dxin = dxin + conv_weight[tap][None, None, :] * extended[lag : lag + steps]
    dxin = dxin.astype(bf16).reshape(length, width)
    du1 = by_token(
        (matmul_nt(dxin, value_w) + matmul_nt(dzg, gate_w)).astype(bf16).reshape(steps, CHUNKS, -1)
    )
    few_rows = jnp.concatenate(
        [
            conv_sums[: CONV + 1],
            step_bias_grad[None],
            jnp.sum(log_wide, axis=1) * rates,
            skip_grad[None],
            jnp.zeros((1, width), f32),
        ]
    )
    tokens_grad, gain_sums, (*dxin_all, small) = z_step(
        "mixer_back", 15, last_backward_local, after(du1, dlater_all, dzg_all),
        (
            x0_share, keep_share, mixer_gain[None], g1_share,
            jnp.concatenate(
                [first_gain_part, attend_gain_part, second_gain_part, jnp.zeros_like(first_gain_part)]
            ),
        ),
        ("gains",), gain_at=4,
        gathers=hosted((dxin, True)), sums=[(select_grad, step_grad, few_rows)],
    )

    if few:
        (u1_all, e1_all), (u2_all, e2_all), (u4_all, e4_all) = ue1_all, ue2_all, ue4_all
        (u3_all, e3_all), (dxin_all,) = ue3_all, dxin_all
    else:
        u1_all, u2_all, u3_all, u4_all, e4_all = u1, u2, u3, u4, e4
        e3_all, e2_all, e1_all, dxin_all = e3, e2, e1, dxin
    hidden_width = hidden1.shape[1]
    mix_all = early_all[:, :width]
    hidden1_all = early_all[:, width : width + hidden_width]
    att_all = early_all[:, width + hidden_width :]
    hidden2_all = late_all[:, :hidden_width]
    dboth2_all = late_all[:, hidden_width:]
    dboth1_all = dlater_all[:, : 2 * hidden_width]
    dqkv_all = dlater_all[:, 2 * hidden_width :]
    cuts = []
    at = 0
    for size in (2 * STATE + DT_RANK, DT_RANK, CONV, 1, 1, STATE, 1):
        cuts.append(small[at : at + size].astype(f32))
        at += size
    select_sum, step_sum, conv_w_sum, conv_b_sum, step_b_sum, decay_sum, skip_sum = cuts
    return (
        mixed,
        tokens_grad.astype(f32),
        gain_sums[3],
        row_grad(u1_all, dxin_all),
        row_grad(u1_all, dzg_all),
        conv_w_sum,
        conv_b_sum[0],
        select_sum,
        step_sum,
        step_b_sum[0],
        decay_sum,
        skip_sum[0],
        column_grad(mix_all, e1_all),
        gain_sums[0],
        row_grad(u2_all, dboth1_all[:, :hidden_width]),
        row_grad(u2_all, dboth1_all[:, hidden_width:]),
        column_grad(hidden1_all, e2_all),
        gain_sums[1],
        row_grad(u3_all, dqkv_all[:, :head_width]),
        row_grad(u3_all, dqkv_all[:, head_width : 2 * head_width]),
        row_grad(u3_all, dqkv_all[:, 2 * head_width :]),
        column_grad(att_all, e3_all),
        gain_sums[2],
        row_grad(u4_all, dboth2_all[:, :hidden_width]),
        row_grad(u4_all, dboth2_all[:, hidden_width:]),
        column_grad(hidden2_all, e4_all),
    )


def solution(mesh):
    return jax.shard_map(
        body,
        mesh=mesh,
        in_specs=(
            P("seq", None),
            P(),
            P("seq", None),
            P(),
            P("seq", "mp"),
            P("seq", "mp"),
            P(None, "mp"),
            P("mp"),
            P(None, "mp"),
            P(None, "mp"),
            P("mp"),
            P(None, "mp"),
            P("mp"),
            P("mp", "seq"),
            P(),
            P("seq", "mp"),
            P("seq", "mp"),
            P("mp", "seq"),
            P(),
            P("seq", "mp"),
            P("seq", "mp"),
            P("seq", "mp"),
            P("mp", "seq"),
            P(),
            P("seq", "mp"),
            P("seq", "mp"),
            P("mp", "seq"),
        ),
        out_specs=(
            P("seq", None),
            P("seq", None),
            P(),
            P("seq", "mp"),
            P("seq", "mp"),
            P(None, "mp"),
            P("mp"),
            P(None, "mp"),
            P(None, "mp"),
            P("mp"),
            P(None, "mp"),
            P("mp"),
            P("mp", "seq"),
            P(),
            P("seq", "mp"),
            P("seq", "mp"),
            P("mp", "seq"),
            P(),
            P("seq", "mp"),
            P("seq", "mp"),
            P("seq", "mp"),
            P("mp", "seq"),
            P(),
            P("seq", "mp"),
            P("seq", "mp"),
            P("mp", "seq"),
        ),
        check_vma=False,
    )
```

```python
import functools
import math

import jax
import jax.numpy as jnp
from jax import lax
from jax.experimental import pallas as pl
from jax.experimental.pallas import tpu as pltpu
from jax.sharding import PartitionSpec as P

STATE = 16
CONV = 4
DT_RANK = 128
HEAD_DIM = 128
WINDOW = 2048
EPS = 1e-05
CHUNKS = 8
LANES = 128
LOG2E = 1.4426950408889634

VMEM = 48 * 1024 * 1024
MESH = pl.DeviceIdType.MESH


def chunk_scan(p, q, reverse):
    rows = p.shape[0]
    at = lax.broadcasted_iota(jnp.int32, p.shape, 0)
    d = 1
    while d < rows:
        move = (rows - d) if reverse else d
        ok = (at < rows - d) if reverse else (at >= d)
        ps = jnp.where(ok, pltpu.roll(p, move, 0), 1.0)
        qs = jnp.where(ok, pltpu.roll(q, move, 0), 0.0)
        q = p * qs + q
        p = p * ps
        d *= 2
    move = (rows - 1) if reverse else 1
    ok = (at < rows - 1) if reverse else (at >= 1)
    return p, q, jnp.where(ok, pltpu.roll(p, move, 0), 1.0), jnp.where(ok, pltpu.roll(q, move, 0), 0.0)

def spread(row, like):
    return jnp.broadcast_to(row, like.shape)

def ssm_summary(dt_ref, dx_ref, in_ref, rate_ref, keep_ref, thr_ref, off_ref, sum_ref):
    steps = dt_ref.shape[0]
    zero = jnp.zeros(dt_ref.shape[1:], jnp.float32)
    rates = [spread(rate_ref[n:n + 1, :], zero) for n in range(STATE)]
    def step(t, carry):
        total, states = carry
        dt, dx = dt_ref[t], dx_ref[t]
        states = tuple(jnp.exp2(dt * rates[n]) * states[n] + in_ref[t, n] * dx for n in range(STATE))
        return total + dt, states
    total, states = lax.fori_loop(0, steps, step, (zero, (zero,) * STATE), unroll=4)
    keep = keep_ref[...]
    reach, thru = [], []
    for n in range(STATE):
        p, q, pe, qe = chunk_scan(jnp.exp2(total * rates[n]) * keep, states[n], False)
        thr_ref[n] = pe * keep
        off_ref[n] = qe * keep
        reach.append(q[q.shape[0] - 1:, :])
        thru.append(p[p.shape[0] - 1:, :])
    sum_ref[...] = jnp.concatenate(reach + thru, axis=0).astype(sum_ref.dtype)

def entering_state(all_ref, pick_ref, backwards):
    count = all_ref.shape[0]
    running = jnp.zeros((STATE, LANES), jnp.float32)
    for k in range(count):
        j = count - 1 - k if backwards else k
        both = all_ref[j].astype(jnp.float32)
        new = both[STATE:] * running + both[:STATE]
        running = jnp.where(pick_ref[j] > 0, new, running)
    return running

def ssm_states(dt_ref, dx_ref, in_ref, out_ref, rate_ref, thr_ref, off_ref, all_ref, pick_ref, y_ref, enter_ref):
    steps = dt_ref.shape[0]
    zero = jnp.zeros(dt_ref.shape[1:], jnp.float32)
    rates = [spread(rate_ref[n:n + 1, :], zero) for n in range(STATE)]
    running = entering_state(all_ref, pick_ref, False)
    start = []
    for n in range(STATE):
        e = thr_ref[n] * spread(running[n:n + 1, :], zero) + off_ref[n]
        enter_ref[n] = e
        start.append(e)
    def step(t, states):
        dt, dx = dt_ref[t], dx_ref[t]
        states = tuple(jnp.exp2(dt * rates[n]) * states[n] + in_ref[t, n] * dx for n in range(STATE))
        parts = [out_ref[t, n] * states[n] for n in range(STATE)]
        while len(parts) > 1:
            parts = [a + b for a, b in zip(parts[::2], parts[1::2])]
        y_ref[t] = parts[0]
        return states
    lax.fori_loop(0, steps, step, tuple(start), unroll=4)

def ssm_back_summary(dt_ref, dy_ref, out_ref, rate_ref, keep_ref, thr_ref, off_ref, sum_ref):
    steps = dt_ref.shape[0]
    zero = jnp.zeros(dt_ref.shape[1:], jnp.float32)
    rates = [spread(rate_ref[n:n + 1, :], zero) for n in range(STATE)]
    def step(k, carry):
        t = steps - 1 - k
        total, back = carry
        dt, dy = dt_ref[t], dy_ref[t]
        back = tuple(jnp.exp2(dt * rates[n]) * (back[n] + out_ref[t, n] * dy) for n in range(STATE))
        return total + dt, back
    total, back = lax.fori_loop(0, steps, step, (zero, (zero,) * STATE), unroll=4)
    keep = keep_ref[...]
    reach, thru = [], []
    for n in range(STATE):
        p, q, pe, qe = chunk_scan(jnp.exp2(total * rates[n]) * keep, back[n] * keep, True)
        thr_ref[n] = pe
        off_ref[n] = qe
        reach.append(q[0:1, :])
        thru.append(p[0:1, :])
    sum_ref[...] = jnp.concatenate(reach + thru, axis=0).astype(sum_ref.dtype)

def ssm_grads(dt_ref, dx_ref, dy_ref, in_ref, out_ref, rate_ref, true_ref, enter_ref, thr_ref, off_ref, all_ref, pick_ref,
              ddt_ref, prod_ref, gate_ref, log_ref, h_ref, a_ref, ing_ref, outg_ref):
    steps = dt_ref.shape[0]
    zero = jnp.zeros(dt_ref.shape[1:], jnp.float32)
    rates = [spread(rate_ref[n:n + 1, :], zero) for n in range(STATE)]
    @pl.when(pl.program_id(0) == 0)
    def _():
        ing_ref[...] = jnp.zeros_like(ing_ref)
        outg_ref[...] = jnp.zeros_like(outg_ref)
    def forward(t, states):
        dt, dx, dy = dt_ref[t], dx_ref[t], dy_ref[t]
        new = []
        for n in range(STATE):
            h_ref[t, n] = states[n]
            a = jnp.exp2(dt * rates[n])
            a_ref[t, n] = a
            h = a * states[n] + in_ref[t, n] * dx
            outg_ref[t, n] += dy * h
            new.append(h)
        return tuple(new)
    lax.fori_loop(0, steps, forward, tuple(enter_ref[n] for n in range(STATE)), unroll=2)
    running = entering_state(all_ref, pick_ref, True)
    start = tuple(thr_ref[n] * spread(running[n:n + 1, :], zero) + off_ref[n] for n in range(STATE))
    true = [spread(true_ref[n:n + 1, :], zero) for n in range(STATE)]
    log_ref[...] = jnp.zeros_like(log_ref)
    def backward(k, back):
        t = steps - 1 - k
        dt, dx, dy = dt_ref[t], dx_ref[t], dy_ref[t]
        new, ddt, prod = [], [], []
        for n in range(STATE):
            lam = back[n] + out_ref[t, n] * dy
            q = lam * a_ref[t, n]
            dea = q * h_ref[t, n]
            ddt.append(dea * true[n])
            log_ref[n] += dea * dt
            prod.append(lam * in_ref[t, n])
            ing_ref[t, n] += lam * dx
            new.append(q)
        while len(ddt) > 1:
            ddt = [a + b for a, b in zip(ddt[::2], ddt[1::2])]
            prod = [a + b for a, b in zip(prod[::2], prod[1::2])]
        ddt_ref[t] = ddt[0]
        prod_ref[t] = prod[0]
        return tuple(new)
    lax.fori_loop(0, steps, backward, start, unroll=2)
    @pl.when(pl.program_id(0) == pl.num_programs(0) - 1)
    def _():
        ones = jnp.ones((8, LANES), jnp.float32)
        rows = steps * zero.shape[0]
        for k, wide_ref in enumerate((ing_ref, outg_ref)):
            for n in range(STATE):
                sums = lax.dot_general(
                    ones, wide_ref[:, n].reshape(rows, LANES), (((1,), (1,)), ((), ())),
                    precision=lax.Precision.HIGHEST, preferred_element_type=jnp.float32,
                )
                gate_ref[k * STATE + n:k * STATE + n + 1, :] = sums[0:1, :]


def specs(steps, rows):
    chan = pl.BlockSpec((steps, rows, LANES), lambda i: (0, 0, i))
    wide = pl.BlockSpec((steps, STATE, rows, LANES), lambda i: (0, 0, 0, 0))
    rate = pl.BlockSpec((STATE, LANES), lambda i: (0, i))
    per = pl.BlockSpec((STATE, rows, LANES), lambda i: (0, 0, i))
    summ = pl.BlockSpec((2 * STATE, LANES), lambda i: (0, i))
    keep = pl.BlockSpec((rows, LANES), lambda i: (0, 0))
    return chan, wide, rate, per, summ, keep

def params():
    return pltpu.CompilerParams(vmem_limit_bytes=VMEM, dimension_semantics=("arbitrary",))

def run_summary(dt, src, gates, rate2, keep, backwards):
    steps, rows, width = dt.shape
    chan, wide, rate, per, summ, kp = specs(steps, rows)
    f = jnp.float32
    return pl.pallas_call(
        ssm_back_summary if backwards else ssm_summary,
        grid=(width // LANES,),
        in_specs=[chan, chan, wide, rate, kp],
        out_specs=[per, per, summ],
        out_shape=[jax.ShapeDtypeStruct((STATE, rows, width), f)] * 2 + [jax.ShapeDtypeStruct((2 * STATE, width), jnp.bfloat16)],
        compiler_params=params(), name="ssm_back_summary" if backwards else "ssm_summary",
    )(dt, src, gates, rate2, keep)

def run_states(dt, dx, ins, outs, rate2, thr, off, everyone, pick):
    steps, rows, width = dt.shape
    chan, wide, rate, per, summ, kp = specs(steps, rows)
    count = everyone.shape[0]
    alls = pl.BlockSpec((count, 2 * STATE, LANES), lambda i: (0, 0, i))
    f = jnp.float32
    return pl.pallas_call(
        ssm_states, grid=(width // LANES,),
        in_specs=[chan, chan, wide, wide, rate, per, per, alls, pl.BlockSpec(memory_space=pltpu.SMEM)],
        out_specs=[chan, per],
        out_shape=[jax.ShapeDtypeStruct((steps, rows, width), f), jax.ShapeDtypeStruct((STATE, rows, width), f)],
        compiler_params=params(), name="ssm_states",
    )(dt, dx, ins, outs, rate2, thr, off, everyone, pick)

def run_grads(dt, dx, dy, ins, outs, rate2, rates, enter, thr, off, everyone, pick):
    steps, rows, width = dt.shape
    chan, wide, rate, per, summ, kp = specs(steps, rows)
    count = everyone.shape[0]
    alls = pl.BlockSpec((count, 2 * STATE, LANES), lambda i: (0, 0, i))
    f = jnp.float32
    s = jax.ShapeDtypeStruct
    return pl.pallas_call(
        ssm_grads, grid=(width // LANES,),
        in_specs=[chan, chan, chan, wide, wide, rate, rate, per, per, per, alls, pl.BlockSpec(memory_space=pltpu.SMEM)],
        out_specs=[chan, chan, pl.BlockSpec((2 * STATE, steps * rows), lambda i: (0, 0)), per],
        out_shape=[s((steps, rows, width), f)] * 2 + [s((2 * STATE, steps * rows), f), s((STATE, rows, width), f)],
        scratch_shapes=[pltpu.VMEM((steps, STATE, rows, LANES), f)] * 4,
        compiler_params=params(), name="ssm_grads",
    )(dt, dx, dy, ins, outs, rate2, rates, enter, thr, off, everyone, pick)


def conv_back_kernel(prod_ref, dy_ref, dt_ref, more_ref, conv_ref, padded_ref, skip_ref, dconv_ref, sums_ref):
    steps = conv_ref.shape[0]
    zero = jnp.zeros(conv_ref.shape[1:], jnp.float32)
    skip = spread(skip_ref[...], zero)

    def step(t, sums):
        value = conv_ref[t]
        sigma = jax.nn.sigmoid(value)
        grad = prod_ref[t] * dt_ref[t] + dy_ref[t] * skip + more_ref[t]
        grad = grad * (sigma * (1.0 + value * (1.0 - sigma)))
        dconv_ref[t] = grad
        taps = tuple(sums[k] + grad * padded_ref[t + k] for k in range(CONV))
        return taps + (sums[CONV] + grad,)

    sums = lax.fori_loop(0, steps, step, (zero,) * (CONV + 1), unroll=2)
    sums_ref[...] = jnp.zeros_like(sums_ref)
    for k in range(CONV + 1):
        sums_ref[k : k + 1, :] = jnp.sum(sums[k], axis=0, keepdims=True)


def conv_back(prod, dys, dt, more, conv, padded, skip):
    steps, rows, width = conv.shape
    chan = pl.BlockSpec((steps, rows, LANES), lambda i: (0, 0, i))
    longer = pl.BlockSpec((padded.shape[0], rows, LANES), lambda i: (0, 0, i))
    f32 = jnp.float32
    return pl.pallas_call(
        conv_back_kernel,
        grid=(width // LANES,),
        in_specs=[chan] * 5 + [longer, pl.BlockSpec((1, LANES), lambda i: (0, i))],
        out_specs=[chan, pl.BlockSpec((8, LANES), lambda i: (0, i))],
        out_shape=[
            jax.ShapeDtypeStruct((steps, rows, width), f32), jax.ShapeDtypeStruct((8, width), f32)
        ],
        compiler_params=params(),
        name="conv_back",
    )(prod, dys, dt, more, conv, padded, skip[None])


FFN_TILE = 512


def mm(left, right):
    return jnp.dot(left, right, preferred_element_type=jnp.float32)


def mm_nt(left, right):
    return lax.dot_general(
        left, right, (((1,), (1,)), ((), ())), preferred_element_type=jnp.float32
    )


def ffn_forward_kernel(u_ref, gate_w_ref, lift_w_ref, down_ref, gate_ref, lift_ref, part_ref, total):
    at = pl.program_id(0)
    u = u_ref[...]
    gate = mm(u, gate_w_ref[...])
    lift = mm(u, lift_w_ref[...])
    gate_ref[...] = gate
    lift_ref[...] = lift
    hidden = (gate * jax.nn.sigmoid(gate) * lift).astype(jnp.bfloat16)
    piece = mm(hidden, down_ref[...])

    @pl.when(at == 0)
    def _():
        total[...] = piece

    @pl.when(at > 0)
    def _():
        total[...] += piece

    @pl.when(at == pl.num_programs(0) - 1)
    def _():
        part_ref[...] = total[...].astype(part_ref.dtype)


def ffn_forward_call(u, both_w, down_w):
    rows, feat = u.shape
    hidden = down_w.shape[0]
    tile = min(FFN_TILE, hidden)
    count = hidden // tile
    f32, bf16 = jnp.float32, jnp.bfloat16
    shape = jax.ShapeDtypeStruct
    whole = pl.BlockSpec((rows, feat), lambda i: (0, 0))
    act = pl.BlockSpec((rows, tile), lambda i: (0, i))
    return pl.pallas_call(
        ffn_forward_kernel,
        grid=(count,),
        in_specs=[
            whole,
            pl.BlockSpec((feat, tile), lambda i: (0, i)),
            pl.BlockSpec((feat, tile), lambda i: (0, count + i)),
            pl.BlockSpec((tile, feat), lambda i: (i, 0)),
        ],
        out_specs=[act, act, whole],
        out_shape=[shape((rows, hidden), f32), shape((rows, hidden), f32), shape((rows, feat), bf16)],
        scratch_shapes=[pltpu.VMEM((rows, feat), f32)],
        compiler_params=params(),
        name="ffn_forward",
    )(u, both_w, both_w, down_w)


def ffn_backward_kernel(e_ref, gate_w_ref, lift_w_ref, down_ref, gate_ref, lift_ref, *rest):
    *side_ref, acts_ref, part_ref, total = rest
    at = pl.program_id(0)
    tile = gate_ref.shape[1]
    grad = mm_nt(e_ref[...], down_ref[...])
    gate, lift = gate_ref[...], lift_ref[...]
    sigma = jax.nn.sigmoid(gate)
    silu = gate * sigma
    gate_low = (grad * lift * (sigma * (1.0 + gate * (1.0 - sigma)))).astype(jnp.bfloat16)
    lift_low = (grad * silu).astype(jnp.bfloat16)
    acts_ref[:, 0:tile] = (silu * lift).astype(jnp.bfloat16)
    acts_ref[:, tile : 2 * tile] = gate_low
    acts_ref[:, 2 * tile : 3 * tile] = lift_low
    if side_ref:
        acts_ref[:, 3 * tile :] = side_ref[0][...]
    piece = mm_nt(gate_low, gate_w_ref[...]) + mm_nt(lift_low, lift_w_ref[...])

    @pl.when(at == 0)
    def _():
        total[...] = piece

    @pl.when(at > 0)
    def _():
        total[...] += piece

    @pl.when(at == pl.num_programs(0) - 1)
    def _():
        part_ref[...] = total[...].astype(part_ref.dtype)


def ffn_backward_call(e, both_w, down_w, gate, lift, *side):
    more = side[0].shape[1] if side else 0
    rows, feat = e.shape
    hidden = down_w.shape[0]
    tile = min(FFN_TILE, hidden)
    count = hidden // tile
    f32, bf16 = jnp.float32, jnp.bfloat16
    shape = jax.ShapeDtypeStruct
    whole = pl.BlockSpec((rows, feat), lambda i: (0, 0))
    act = pl.BlockSpec((rows, tile), lambda i: (0, i))
    return pl.pallas_call(
        ffn_backward_kernel,
        grid=(count,),
        in_specs=[
            whole,
            pl.BlockSpec((feat, tile), lambda i: (0, i)),
            pl.BlockSpec((feat, tile), lambda i: (0, count + i)),
            pl.BlockSpec((tile, feat), lambda i: (i, 0)),
            act, act,
        ]
        + [pl.BlockSpec((rows, more // count), lambda i: (0, i)) for _ in side],
        out_specs=[pl.BlockSpec((rows, 3 * tile + more // count), lambda i: (0, i)), whole],
        out_shape=[shape((rows, 3 * hidden + more), bf16), shape((rows, feat), bf16)],
        scratch_shapes=[pltpu.VMEM((rows, feat), f32)],
        compiler_params=params(),
        name="ffn_backward",
    )(e, both_w, both_w, down_w, gate, lift, *side)


def ffn_grads_tile(u_t, e_t, acts_ref, gate_ref, lift_ref, down_ref):
    tile = gate_ref.shape[1]
    down_ref[...] = mm(e_t[...], acts_ref[:, 0:tile]).T.astype(down_ref.dtype)
    gate_ref[...] = mm(u_t[...], acts_ref[:, tile : 2 * tile]).astype(gate_ref.dtype)
    lift_ref[...] = mm(u_t[...], acts_ref[:, 2 * tile : 3 * tile]).astype(lift_ref.dtype)


def ffn_grads_specs(rows, feat, hidden, wide):
    tile = min(FFN_TILE, hidden)
    count = hidden // tile
    out = pl.BlockSpec((feat, tile), lambda i: (0, i))
    return (
        (count,), pl.BlockSpec((rows, wide // count), lambda i: (0, i)),
        [out, out, pl.BlockSpec((tile, feat), lambda i: (i, 0))],
    )


def ffn_grads_kernel(u_ref, e_ref, acts_ref, gate_ref, lift_ref, down_ref, u_t, e_t):
    @pl.when(pl.program_id(0) == 0)
    def _():
        u_t[...] = u_ref[...].T
        e_t[...] = e_ref[...].T

    ffn_grads_tile(u_t, e_t, acts_ref, gate_ref, lift_ref, down_ref)


def ffn_grads_call(u, e, acts, hidden):
    rows, feat = u.shape
    grid, block, outs = ffn_grads_specs(rows, feat, hidden, acts.shape[1])
    shape = jax.ShapeDtypeStruct
    whole = pl.BlockSpec((rows, feat), lambda i: (0, 0))
    return pl.pallas_call(
        ffn_grads_kernel,
        grid=grid,
        in_specs=[whole, whole, block],
        out_specs=outs,
        out_shape=[shape((feat, hidden), jnp.float32)] * 2 + [shape((hidden, feat), jnp.float32)],
        scratch_shapes=[pltpu.VMEM((feat, rows), u.dtype)] * 2,
        compiler_params=params(),
        name="ffn_grads",
    )(u, e, acts)


def ffn_grads_beside(sources, outs, turned):
    *sources, acts_ref = sources
    for source, target in zip(sources, turned):
        target[...] = source[...].T
    rows, feat = sources[0].shape
    grid, block, specs = ffn_grads_specs(rows, feat, outs[0].shape[1], acts_ref.shape[1])

    def tiles(acts, gate, lift, down, *side):
        ffn_grads_tile(turned[0], turned[1], acts, gate, lift, down)
        for o_t, out in zip(turned[2:], side):
            out[...] = mm(o_t[...], acts[:, acts.shape[1] - out.shape[1] :])

    specs = specs + [
        pl.BlockSpec((feat, out.shape[1] // grid[0]), lambda i: (0, i)) for out in outs[3:]
    ]
    pltpu.emit_pipeline(tiles, grid=grid, in_specs=[block], out_specs=specs)(acts_ref, *outs)


def side_grads_kernel(turned, o_ref, side_ref, out_ref, o_t):
    @pl.when(pl.program_id(0) == 0)
    def _():
        o_t[...] = o_ref[...].T

    result = mm(o_t[...], side_ref[...])
    out_ref[...] = result.T if turned else result


def side_grads_call(o, acts, hidden, turned):
    rows, feat = o.shape
    count = hidden // min(FFN_TILE, hidden)
    side = (acts.shape[1] - 3 * hidden) // count
    step = acts.shape[1] // count // side
    out = (count * side, feat) if turned else (feat, count * side)
    return pl.pallas_call(
        functools.partial(side_grads_kernel, turned),
        grid=(count,),
        in_specs=[
            pl.BlockSpec((rows, feat), lambda i: (0, 0)),
            pl.BlockSpec((rows, side), lambda i: (0, step * i + step - 1)),
        ],
        out_specs=pl.BlockSpec((side, feat), lambda i: (i, 0)) if turned
        else pl.BlockSpec((feat, side), lambda i: (0, i)),
        out_shape=jax.ShapeDtypeStruct(out, jnp.float32),
        scratch_shapes=[pltpu.VMEM((feat, rows), o.dtype)],
        compiler_params=params(),
        name="side_grads",
    )(o, acts)


class Ring:
    def __init__(self, count):
        self.count = count
        self.chips = count // 2
        self.side = math.isqrt(self.chips)
        self.long = self.chips // 2
        self.short = self.chips - 1 - self.long
        self.me = lax.axis_index("seq")
        self.core = self.me % 2
        self.way = 1 - 2 * self.core
        self.at = self.flip(self.me // 2)
        self.partner = self.me + self.way
        self.long_next = self.device(1, self.core)
        self.short_next = self.device(-1, self.core)

    def flip(self, chip):
        row, column = chip // self.side, chip % self.side
        return row * self.side + column + (row % 2) * (self.side - 1 - 2 * column)

    def device(self, hops, core):
        place = (self.at + hops * self.way + 2 * self.chips) % self.chips
        return self.flip(place) * 2 + core


def remote(source, target, send_sem, recv_sem, axis, to):
    return pltpu.make_async_remote_copy(
        src_ref=source,
        dst_ref=target,
        send_sem=send_sem,
        recv_sem=recv_sem,
        device_id={axis: to},
        device_id_type=MESH,
    )


def greet(axis, devices):
    barrier = pltpu.get_barrier_semaphore()
    for to in devices:
        pl.semaphore_signal(barrier, inc=1, device_id={axis: to}, device_id_type=MESH)
    return len(devices)


def others_of(axis, count):
    me = lax.axis_index(axis)
    return [lax.rem(me + d, count) for d in range(1, count)]


class Gather:
    def __init__(self, ring, shard, full, by_rows, send_sem, recv_sem, own_sem):
        self.ring, self.shard, self.full, self.by_rows = ring, shard, full, by_rows
        self.send_sem, self.recv_sem = send_sem, recv_sem
        self.size = shard.shape[0 if by_rows else 1]
        self.own = pltpu.make_async_copy(shard, self.slot(ring.me), own_sem)
        self.sent = []

    def slot(self, device):
        part = pl.ds(pl.multiple_of(device * self.size, self.size), self.size)
        return self.full.at[part] if self.by_rows else self.full.at[:, part]

    def send(self, source, device, sem, to):
        copy = remote(
            source, self.slot(device), self.send_sem.at[len(self.sent)], self.recv_sem.at[sem],
            "seq", to,
        )
        copy.start()
        self.sent.append(copy)

    def wait(self, device, sem):
        slot = self.slot(device)
        remote(
            slot, slot, self.send_sem.at[0], self.recv_sem.at[sem], "seq", self.ring.partner
        ).wait_recv()

    def start(self):
        ring = self.ring
        self.send(self.shard, ring.me, 0, ring.long_next)
        if ring.short:
            self.send(self.shard, ring.me, ring.long, ring.short_next)
        self.send(self.shard, ring.me, ring.long + ring.short, ring.partner)
        self.own.start()

    def hop(self, i):
        ring = self.ring
        base = ring.long + ring.short + 1
        if i <= ring.long:
            device = ring.device(-i, ring.core)
            self.wait(device, i - 1)
            if i < ring.long:
                self.send(self.slot(device), device, i, ring.long_next)
            self.send(self.slot(device), device, base + i - 1, ring.partner)
        if i <= ring.short:
            device = ring.device(i, ring.core)
            self.wait(device, ring.long + i - 1)
            if i < ring.short:
                self.send(self.slot(device), device, ring.long + i, ring.short_next)
            self.send(self.slot(device), device, base + ring.long + i - 1, ring.partner)

    def finish(self):
        ring = self.ring
        base = ring.long + ring.short + 1
        other = 1 - ring.core
        self.wait(ring.partner, base - 1)
        for i in range(1, ring.long + 1):
            self.wait(ring.device(i, other), base + i - 1)
        for i in range(1, ring.short + 1):
            self.wait(ring.device(-i, other), base + ring.long + i - 1)
        self.own.wait()
        for copy in self.sent:
            copy.wait_send()


class Swap:
    def __init__(self, count, source, target, send_sem, recv_sem, own_sem):
        self.count, self.source, self.target = count, source, target
        self.send_sem, self.recv_sem = send_sem, recv_sem
        self.me = lax.axis_index("seq")
        self.rows = target.shape[0] // count
        self.width = target.shape[1]
        self.own = pltpu.make_async_copy(self.block(self.me), self.slot(self.me), own_sem)
        self.sent = []

    def block(self, to):
        if len(self.source.shape) == 3:
            return self.source.at[to]
        return self.source.at[:, pl.ds(pl.multiple_of(to * self.width, self.width), self.width)]

    def slot(self, device):
        return self.target.at[pl.ds(pl.multiple_of(device * self.rows, self.rows), self.rows)]

    def start(self):
        for d in range(1, self.count):
            to = lax.rem(self.me + d, self.count)
            copy = remote(
                self.block(to), self.slot(self.me), self.send_sem.at[d - 1],
                self.recv_sem.at[d - 1], "seq", to,
            )
            copy.start()
            self.sent.append(copy)
        self.own.start()

    def finish(self):
        for d in range(1, self.count):
            slot = self.slot(lax.rem(self.me + self.count - d, self.count))
            remote(
                slot, slot, self.send_sem.at[0], self.recv_sem.at[d - 1], "seq",
                lax.rem(self.me + d, self.count),
            ).wait_recv()
        self.own.wait()
        for copy in self.sent:
            copy.wait_send()


def rms_scale(x):
    return lax.rsqrt(jnp.mean(x * x, axis=-1, keepdims=True) + EPS)


def forward_local(ins, outs, total):
    x_ref, keep_ref, gain_ref = ins
    new = x_ref[...] + keep_ref[:, 0:1] * total
    outs[0][...] = new
    return new * rms_scale(new) * gain_ref[...], None


def norm_back(ins, total):
    x_ref, keep_ref, gain_ref, grad_ref = ins[:4]
    x = x_ref[...]
    scale = rms_scale(x)
    weighted = gain_ref[...] * total
    middle = jnp.mean(weighted * x, axis=-1, keepdims=True)
    row = jnp.sum(total * x * scale, axis=0, keepdims=True)
    return grad_ref[...] + scale * weighted - x * (scale * scale * scale) * middle, row


def backward_local(ins, outs, total):
    new, row = norm_back(ins, total)
    outs[0][...] = new
    outs[1][...] = row
    return ins[1][:, 0:1] * new, None


def last_backward_local(ins, outs, total):
    return norm_back(ins, total)


def sum_local(ins, outs, total):
    return total, None


class Spread:
    def __init__(self, count, source, target, send_sem, recv_sem, own_sem):
        self.count, self.source, self.target = count, source, target
        self.send_sem, self.recv_sem = send_sem, recv_sem
        self.me = lax.axis_index("seq")
        self.own = pltpu.make_async_copy(source, target.at[self.me], own_sem)
        self.sent = []

    def start(self):
        for d in range(1, self.count):
            copy = remote(
                self.source, self.target.at[self.me], self.send_sem.at[d - 1],
                self.recv_sem.at[d - 1], "seq", lax.rem(self.me + d, self.count),
            )
            copy.start()
            self.sent.append(copy)
        self.own.start()

    def finish(self):
        for d in range(1, self.count):
            slot = self.target.at[lax.rem(self.me + self.count - d, self.count)]
            remote(
                slot, slot, self.send_sem.at[0], self.recv_sem.at[d - 1], "seq",
                lax.rem(self.me + d, self.count),
            ).wait_recv()
        self.own.wait()
        for copy in self.sent:
            copy.wait_send()


class PlaneScatter:
    def __init__(self, planes, part, target, got, send_sem, recv_sem):
        self.planes, self.part, self.target, self.got = planes, part, target, got
        self.send_sem, self.recv_sem = send_sem, recv_sem
        self.me = lax.axis_index("mp")
        self.sent = []

    def block(self, to):
        rows = self.part.shape[0] // self.planes
        return pl.ds(pl.multiple_of(to * rows, rows), rows)

    def start(self):
        for d in range(1, self.planes):
            to = lax.rem(self.me + d, self.planes)
            copy = remote(
                self.part.at[self.block(to)], self.got.at[d - 1], self.send_sem.at[d - 1],
                self.recv_sem.at[d - 1], "mp", to,
            )
            copy.start()
            self.sent.append(copy)

    def total(self):
        total = self.part[self.block(self.me), :].astype(jnp.float32)
        for d in range(1, self.planes):
            self.sent[d - 1].wait_recv()
            total = total + self.got[d - 1].astype(jnp.float32)
        return total

    def finish(self):
        self.target[...] = self.total()
        for copy in self.sent:
            copy.wait_send()


class PlaneCollect:
    def __init__(self, planes, source, target, send_sem, recv_sem):
        self.planes, self.source, self.target = planes, source, target
        self.send_sem, self.recv_sem = send_sem, recv_sem
        self.me = lax.axis_index("mp")
        rows = source.shape[0]
        self.own = target.at[pl.ds(pl.multiple_of(self.me * rows, rows), rows)]
        self.sent = []

    def start(self):
        for d in range(1, self.planes):
            copy = remote(
                self.source, self.own, self.send_sem.at[d - 1], self.recv_sem.at[d - 1],
                "mp", lax.rem(self.me + d, self.planes),
            )
            copy.start()
            self.sent.append(copy)
        self.own[...] = self.source[...]

    def finish(self):
        for copy in self.sent:
            copy.wait_recv()
        for copy in self.sent:
            copy.wait_send()


class LineSum:
    def __init__(self, part, got, stage, mine, full, sems):
        self.part, self.got, self.stage, self.mine, self.full = part, got, stage, mine, full
        self.sems = sems
        me = lax.axis_index("mp")
        self.me = me
        half = me // 2
        self.outer = (me == 0) | (me == 3)
        self.inner = (me == 1) | (me == 2)
        self.partner = 4 * half + 1 - me
        self.far_inner, self.far_outer = 2 - half, 3 - 3 * half

    def block(self, plane):
        rows = self.mine.shape[0]
        return pl.ds(pl.multiple_of(plane * rows, rows), rows)

    def toward(self, source, slot, sem, to):
        return remote(
            source, self.got.at[slot], self.sems[0].at[sem], self.sems[1].at[slot], "mp", to
        )

    def out(self, source, plane, sem, slot, to):
        return remote(
            source, self.full.at[self.block(plane)], self.sems[2].at[sem], self.sems[3].at[slot],
            "mp", to,
        )

    def start(self):
        part, partner = self.part, self.partner

        @pl.when(self.outer)
        def _():
            self.toward(part.at[self.block(self.far_outer)], 2, 0, partner).start()
            self.toward(part.at[self.block(self.far_inner)], 3, 1, partner).start()
            self.toward(part.at[self.block(partner)], 0, 2, partner).start()

        @pl.when(self.inner)
        def _():
            self.toward(part.at[self.block(partner)], 0, 2, partner).start()

    def relay(self):
        @pl.when(self.inner)
        def _():
            for slot, to in ((2, self.far_outer), (3, self.far_inner)):
                block = self.part.at[self.block(to)]
                self.toward(block, slot, slot - 2, self.partner).wait_recv()
                joined = block[...].astype(jnp.float32) + self.got[slot].astype(jnp.float32)
                self.stage[slot - 2] = joined.astype(self.stage.dtype)
                self.toward(self.stage.at[slot - 2], 1, slot - 2, to).start()

    def total(self):
        block = self.part.at[self.block(self.me)]
        total = block[...].astype(jnp.float32)
        for slot in (0, 1):
            self.toward(block, slot, 0, self.partner).wait_recv()
            total = total + self.got[slot].astype(jnp.float32)
        return total

    def collect(self):
        @pl.when(self.inner)
        def _():
            self.out(self.mine, self.me, 1, 1, self.far_inner).start()
            self.out(self.mine, self.me, 0, 0, self.partner).start()

        @pl.when(self.outer)
        def _():
            self.out(self.mine, self.me, 1, 2, self.far_inner).start()
            self.out(self.mine, self.me, 0, 0, self.partner).start()

        self.full[self.block(self.me), :] = self.mine[...]

    def arrive(self, plane, slot):
        block = self.full.at[self.block(plane)]
        self.out(block, plane, 0, slot, self.partner).wait_recv()
        return block

    def forward(self):
        @pl.when(self.inner)
        def _():
            block = self.arrive(self.far_inner, 1)
            self.out(block, self.far_inner, 2, 1, self.partner).start()
            block = self.arrive(self.far_outer, 2)
            self.out(block, self.far_outer, 3, 2, self.partner).start()

    def finish(self):
        self.arrive(self.partner, 0)

        @pl.when(self.outer)
        def _():
            self.arrive(self.far_inner, 1)
            self.arrive(self.far_outer, 2)

        block = self.part.at[self.block(self.me)]
        for sem in range(3):
            self.toward(block, 0, sem, self.partner).wait_send()
        for sem in range(2):
            self.out(self.mine, self.me, sem, 0, self.partner).wait_send()

        @pl.when(self.inner)
        def _():
            for sem in (2, 3):
                self.out(self.mine, self.me, sem, 0, self.partner).wait_send()


class DirectSum:
    def __init__(self, planes, part, got, mine, full, sems):
        self.scatter = PlaneScatter(planes, part, None, got, sems[0], sems[1])
        self.result = PlaneCollect(planes, mine, full, sems[2], sems[3])

    def start(self):
        self.scatter.start()

    def relay(self):
        pass

    def total(self):
        return self.scatter.total()

    def collect(self):
        self.result.start()

    def forward(self):
        pass

    def finish(self):
        self.result.finish()
        for copy in self.scatter.sent:
            copy.wait_send()


class SeqSum:
    def __init__(self, count, parts, out, low, got, mine, send_sem, recv_sem):
        self.count, self.parts, self.out = count, parts, out
        self.low, self.got, self.mine = low, got, mine
        self.send_sem, self.recv_sem = send_sem, recv_sem
        self.me = lax.axis_index("seq")
        self.rows = low.shape[0] // count
        self.first, self.second = [], []

    def block(self, device):
        return pl.ds(pl.multiple_of(device * self.rows, self.rows), self.rows)

    def start(self):
        at = 0
        for part in self.parts:
            size = part.shape[0]
            self.low[at : at + size, :] = part[...].astype(self.low.dtype)
            at += size
        if at < self.low.shape[0]:
            self.low[at:, :] = jnp.zeros((self.low.shape[0] - at, self.low.shape[1]), self.low.dtype)
        for d in range(1, self.count):
            to = lax.rem(self.me + d, self.count)
            copy = remote(
                self.low.at[self.block(to)], self.got.at[d - 1],
                self.send_sem.at[d - 1], self.recv_sem.at[d - 1], "seq", to,
            )
            copy.start()
            self.first.append(copy)

    def middle(self):
        own = self.block(self.me)
        total = self.low[own, :].astype(jnp.float32)
        for d in range(1, self.count):
            self.first[d - 1].wait_recv()
            total = total + self.got[d - 1].astype(jnp.float32)
        self.mine[...] = total.astype(self.mine.dtype)
        for d in range(1, self.count):
            copy = remote(
                self.mine, self.out.at[own], self.send_sem.at[self.count + d - 1],
                self.recv_sem.at[self.count + d - 1], "seq", lax.rem(self.me + d, self.count),
            )
            copy.start()
            self.second.append(copy)
        self.out[own, :] = self.mine[...]

    def finish(self):
        for d in range(1, self.count):
            slot = self.out.at[self.block(lax.rem(self.me + self.count - d, self.count))]
            remote(
                slot, slot, self.send_sem.at[self.count], self.recv_sem.at[self.count + d - 1],
                "seq", lax.rem(self.me + d, self.count),
            ).wait_recv()
        for copy in self.first + self.second:
            copy.wait_send()


class GainSum:
    def __init__(self, planes, count, rows, out, across, along, sems):
        self.planes, self.count, self.rows, self.out = planes, count, rows, out
        self.across, self.along, self.sems = across, along, sems
        self.me, self.plane = lax.axis_index("seq"), lax.axis_index("mp")
        self.first, self.second = [], []

    def start(self, row):
        held = self.rows.shape[0]
        self.out[...] = self.rows[...]
        self.out[held - 1 : held, :] = row
        for d in range(1, self.planes):
            copy = remote(
                self.out, self.across.at[d - 1], self.sems[0].at[d - 1], self.sems[1].at[d - 1],
                "mp", lax.rem(self.plane + d, self.planes),
            )
            copy.start()
            self.first.append(copy)

    def middle(self):
        total = self.out[...]
        for d in range(1, self.planes):
            self.first[d - 1].wait_recv()
            total = total + self.across[d - 1]
        for copy in self.first:
            copy.wait_send()
        self.out[...] = total
        for d in range(1, self.count):
            copy = remote(
                self.out, self.along.at[d - 1], self.sems[2].at[d - 1], self.sems[3].at[d - 1],
                "seq", lax.rem(self.me + d, self.count),
            )
            copy.start()
            self.second.append(copy)

    def finish(self):
        total = self.out[...]
        for d in range(1, self.count):
            self.second[d - 1].wait_recv()
            total = total + self.along[d - 1]
        for copy in self.second:
            copy.wait_send()
        self.out[...] = total


class Plan:
    def __init__(self, gathers=(), swaps=(), spreads=(), sums=()):
        self.count = lax.axis_size("seq")
        count = self.count
        vmem = pl.BlockSpec(memory_space=pltpu.VMEM)
        hbm = pl.BlockSpec(memory_space=pl.ANY)
        shape = jax.ShapeDtypeStruct
        self.sources, self.in_specs, self.shapes, self.out_specs, self.scratch = [], [], [], [], []
        self.kinds, self.after = [], []
        sems = [
            pltpu.SemaphoreType.DMA((2 * count,)), pltpu.SemaphoreType.DMA((2 * count,)),
            pltpu.SemaphoreType.DMA,
        ]
        for array, rows in gathers:
            height, width = array.shape
            by_rows = rows or width % LANES != 0
            self.add("rows" if by_rows else "columns", [array], hbm, hbm, sems, shape(
                (count * height, width) if by_rows else (height, count * width), array.dtype
            ))
            self.after[-1] = (height, width) if by_rows and not rows else None
        for array in swaps:
            height, width = array.shape[0], array.shape[1] // count
            if width % LANES:
                array = array.reshape(height, count, width).swapaxes(0, 1)
            self.add("swap", [array], hbm, hbm, sems, shape((count * height, width), array.dtype))
        for array in spreads:
            self.add("spread", [array], vmem, vmem, sems, shape((count,) + array.shape, array.dtype))
        for parts in sums:
            have, width = sum(part.shape[0] for part in parts), parts[0].shape[1]
            rows = -(-have // (16 * count)) * 16
            bf16 = jnp.bfloat16
            self.add("sum", list(parts), vmem, vmem, sems + [
                pltpu.VMEM((rows * count, width), bf16),
                pltpu.VMEM((count - 1, rows, width), bf16),
                pltpu.VMEM((rows, width), bf16),
            ], shape((rows * count, width), bf16))

    def add(self, kind, arrays, in_spec, out_spec, scratch, shape):
        self.kinds.append((kind, len(arrays), len(scratch)))
        self.sources += arrays
        self.in_specs += [in_spec] * len(arrays)
        self.shapes.append(shape)
        self.out_specs.append(out_spec)
        self.scratch += scratch
        self.after.append(None)

    def results(self, targets):
        return [
            t if cut is None
            else t.reshape((self.count,) + cut).swapaxes(0, 1).reshape(cut[0], self.count * cut[1])
            for t, cut in zip(targets, self.after)
        ]

    def bind(self, sources, targets, scratch):
        count = self.count
        self.ring = None
        self.items = []
        self.wide = False
        for (kind, many, held), target in zip(self.kinds, targets):
            mine, sources = sources[:many], sources[many:]
            sems, scratch = scratch[:held], scratch[held:]
            if kind in ("rows", "columns"):
                if self.ring is None:
                    self.ring = Ring(count)
                self.items.append(Gather(self.ring, mine[0], target, kind == "rows", *sems))
                continue
            self.wide = True
            if kind == "swap":
                self.items.append(Swap(count, mine[0], target, *sems))
            elif kind == "spread":
                self.items.append(Spread(count, mine[0], target, *sems))
            else:
                self.items.append(SeqSum(count, mine, target, *sems[3:], *sems[:2]))

    def greet(self, wide=False):
        if self.wide or wide:
            return greet("seq", others_of("seq", self.count))
        if self.ring is not None:
            near = [self.ring.long_next, self.ring.partner]
            if self.ring.short:
                near.append(self.ring.short_next)
            return greet("seq", near)
        return 0

    def start(self):
        for item in self.items:
            item.start()

    def hops(self):
        gathers = [item for item in self.items if isinstance(item, Gather)]
        if gathers:
            for i in range(1, self.ring.long + 1):
                for item in gathers:
                    item.hop(i)
        for item in self.items:
            if isinstance(item, SeqSum):
                item.middle()

    def finish(self):
        for item in self.items:
            item.finish()


def step_kernel(planes, plan, local, n_ins, n_outs, gain_at, work, *refs):
    part_ref, refs = refs[0], refs[1:]
    ins, refs = refs[:n_ins], refs[n_ins:]
    sources, refs = refs[: len(plan.sources)], refs[len(plan.sources) :]
    work_ins, refs = refs[:work], refs[work:]
    full_ref, refs = refs[0], refs[1:]
    outs, refs = refs[:n_outs], refs[n_outs:]
    targets, refs = refs[: len(plan.shapes)], refs[len(plan.shapes) :]
    work_outs, refs = refs[:work], refs[work:]
    got, mine, stage = refs[:3]
    sems, refs = refs[3:7], refs[7:]
    plan.bind(sources, targets, refs[: len(plan.scratch)])
    refs = refs[len(plan.scratch) :]
    turned, refs = refs[: work - 1 if work else 0], refs[work - 1 if work else 0 :]
    gains = None
    if gain_at is not None:
        gains = GainSum(planes, plan.count, ins[gain_at], outs[0], refs[0], refs[1], refs[2:])
    greeted = greet("mp", others_of("mp", planes)) + plan.greet(gains is not None)
    pl.semaphore_wait(pltpu.get_barrier_semaphore(), greeted)
    if planes == 4:
        line = LineSum(part_ref, got, stage, mine, full_ref, sems)
    else:
        line = DirectSum(planes, part_ref, got, mine, full_ref, sems)
    line.start()
    plan.start()
    line.relay()
    if work:
        ffn_grads_beside(work_ins, work_outs, turned)
    value, row = local(ins, outs, line.total())
    mine[...] = value.astype(mine.dtype)
    line.collect()
    if gains is not None:
        gains.start(row)
    line.forward()
    plan.hops()
    if gains is not None:
        gains.middle()
    line.finish()
    plan.finish()
    if gains is not None:
        gains.finish()


def remote_params(cid):
    return pltpu.CompilerParams(
        collective_id=cid, has_side_effects=True, vmem_limit_bytes=VMEM
    )


def z_step(name, cid, local, part, others, extra, out_dtype=jnp.bfloat16, gain_at=None, work=(), **carried):
    planes = lax.axis_size("mp")
    plan = Plan(**carried)
    rows, width = part.shape
    share = rows // planes
    f32 = jnp.float32
    shape = jax.ShapeDtypeStruct
    held = 0 if gain_at is None else others[gain_at].shape[0]
    kinds = {
        "share": shape((share, width), f32),
        "gain": shape((1, width), f32),
        "gains": shape((held, width), f32),
    }
    gain_scratch = [] if gain_at is None else [
        pltpu.VMEM((planes - 1, held, width), f32),
        pltpu.VMEM((plan.count - 1, held, width), f32),
        pltpu.SemaphoreType.DMA((planes,)),
        pltpu.SemaphoreType.DMA((planes,)),
        pltpu.SemaphoreType.DMA((plan.count,)),
        pltpu.SemaphoreType.DMA((plan.count,)),
    ]
    vmem = pl.BlockSpec(memory_space=pltpu.VMEM)
    hbm = pl.BlockSpec(memory_space=pl.ANY)
    work_shapes, turned = [], []
    if work:
        u, e, *side, acts, hidden = work
        low = jnp.bfloat16
        work_shapes = [shape((u.shape[1], hidden), low)] * 2 + [shape((hidden, e.shape[1]), low)]
        for o in side:
            work_shapes.append(shape((o.shape[1], acts.shape[1] - 3 * hidden), f32))
        turned = [pltpu.VMEM((u.shape[1], u.shape[0]), u.dtype)] * (2 + len(side))
    result = pl.pallas_call(
        functools.partial(
            step_kernel, planes, plan, local, len(others), len(extra), gain_at, len(work_shapes)
        ),
        out_shape=[shape((rows, width), out_dtype)] + [kinds[kind] for kind in extra]
        + plan.shapes + work_shapes,
        in_specs=[vmem] * (1 + len(others)) + plan.in_specs + ([vmem] * (len(work) - 2) + [hbm] if work else []),
        out_specs=[vmem] * (1 + len(extra)) + plan.out_specs + [hbm] * len(work_shapes),
        scratch_shapes=[
            pltpu.VMEM((max(planes, 4), share, width), part.dtype),
            pltpu.VMEM((share, width), out_dtype),
            pltpu.VMEM((2, share, width), part.dtype),
        ]
        + [pltpu.SemaphoreType.DMA((max(planes, 4),))] * 4
        + plan.scratch + turned + gain_scratch,
        compiler_params=remote_params(cid),
        name=name,
    )(part, *others, *plan.sources, *work[:-1])
    cut = 1 + len(extra)
    rest = cut + len(plan.shapes)
    return list(result[:cut]) + [plan.results(result[cut:rest])] + list(result[rest:])


def carry_kernel(planes, plan, scatters, collects, *refs):
    sources, refs = refs[: len(plan.sources)], refs[len(plan.sources) :]
    parts, refs = refs[:scatters], refs[scatters:]
    shares, refs = refs[:collects], refs[collects:]
    targets, refs = refs[: len(plan.shapes)], refs[len(plan.shapes) :]
    sums, refs = refs[:scatters], refs[scatters:]
    fulls, refs = refs[:collects], refs[collects:]
    plan.bind(sources, targets, refs[: len(plan.scratch)])
    refs = refs[len(plan.scratch) :]
    items = []
    for part, total in zip(parts, sums):
        items.append(PlaneScatter(planes, part, total, *refs[:3]))
        refs = refs[3:]
    for share, full in zip(shares, fulls):
        items.append(PlaneCollect(planes, share, full, *refs[:2]))
        refs = refs[2:]
    greeted = plan.greet()
    if items:
        greeted += greet("mp", others_of("mp", planes))
    pl.semaphore_wait(pltpu.get_barrier_semaphore(), greeted)
    plan.start()
    for item in items:
        item.start()
    plan.hops()
    plan.finish()
    for item in items:
        item.finish()


def carry(name, cid, scatters=(), collects=(), **carried):
    planes = lax.axis_size("mp")
    plan = Plan(**carried)
    vmem = pl.BlockSpec(memory_space=pltpu.VMEM)
    shape = jax.ShapeDtypeStruct
    sems = [pltpu.SemaphoreType.DMA((planes,))] * 2
    shapes, scratch = [], []
    for part in scatters:
        share = (part.shape[0] // planes, part.shape[1])
        shapes.append(shape(share, jnp.float32))
        scratch += [pltpu.VMEM((planes - 1,) + share, part.dtype)] + sems
    for part in collects:
        shapes.append(shape((part.shape[0] * planes, part.shape[1]), part.dtype))
        scratch += sems
    result = pl.pallas_call(
        functools.partial(carry_kernel, planes, plan, len(scatters), len(collects)),
        out_shape=plan.shapes + shapes,
        in_specs=plan.in_specs + [vmem] * (len(scatters) + len(collects)),
        out_specs=plan.out_specs + [vmem] * len(shapes),
        scratch_shapes=plan.scratch + scratch,
        compiler_params=remote_params(cid),
        name=name,
    )(*plan.sources, *scatters, *collects)
    cut = len(plan.shapes)
    return plan.results(result[:cut]) + list(result[cut:])


SCALE = 1.0 / math.sqrt(HEAD_DIM)


def nt(left, right):
    return lax.dot_general(
        left, right, (((1,), (1,)), ((), ())), preferred_element_type=jnp.float32
    )


def nn(left, right):
    return jnp.dot(left, right, preferred_element_type=jnp.float32)


def attend_kernel(q_ref, k_ref, v_ref, low_ref, high_ref, pos_ref, out_ref, lse_ref):
    scores = nt(q_ref[...], k_ref[...]) * SCALE
    pos = pos_ref[...]
    scores = jnp.where((pos >= low_ref[...]) & (pos <= high_ref[...]), scores, -1e30)
    top = jnp.max(scores, axis=-1, keepdims=True)
    expo = jnp.exp(scores - top)
    mass = jnp.sum(expo, axis=-1, keepdims=True)
    probs = (expo / mass).astype(jnp.bfloat16)
    out_ref[...] = nn(probs, v_ref[...]).astype(jnp.bfloat16)
    lse_ref[0] = top + jnp.log(mass)


def query_back_kernel(q_ref, k_ref, v_ref, g_ref, low_ref, high_ref, pos_ref, lse_ref, dq_ref, mid_ref):
    keys = k_ref[...]
    scores = nt(q_ref[...], keys) * SCALE
    pos = pos_ref[...]
    scores = jnp.where((pos >= low_ref[...]) & (pos <= high_ref[...]), scores, -1e30)
    probs = jnp.exp(scores - lse_ref[0])
    prob_grad = nt(g_ref[...], v_ref[...])
    middle = jnp.sum(probs * prob_grad, axis=-1, keepdims=True)
    score_grad = (probs * (prob_grad - middle)).astype(jnp.bfloat16)
    dq_ref[...] = (nn(score_grad, keys) * SCALE).astype(jnp.bfloat16)
    mid_ref[0] = middle


def key_back_kernel(k_ref, v_ref, q_ref, g_ref, pos_ref, low_ref, high_ref, lse_ref, mid_ref, dk_ref, dv_ref):
    queries, grads = q_ref[...], g_ref[...]
    scores = nt(k_ref[...], queries) * SCALE
    pos = pos_ref[...]
    scores = jnp.where((pos >= low_ref[...]) & (pos <= high_ref[...]), scores, -1e30)
    probs = jnp.exp(scores - lse_ref[0])
    prob_grad = nt(v_ref[...], grads)
    score_grad = (probs * (prob_grad - mid_ref[0])).astype(jnp.bfloat16)
    dk_ref[...] = (nn(score_grad, queries) * SCALE).astype(jnp.bfloat16)
    dv_ref[...] = nn(probs.astype(jnp.bfloat16), grads).astype(jnp.bfloat16)


def head_block(rows, first):
    return pl.BlockSpec((rows, HEAD_DIM), lambda h: (0, first + h))


def whole_block(*shape):
    return pl.BlockSpec(shape, lambda h: (0,) * len(shape))


def attend_params():
    return pltpu.CompilerParams(vmem_limit_bytes=VMEM, dimension_semantics=("arbitrary",))


def attend_call(q, pair, low, high, pos, heads):
    rows, keys = q.shape[0], pair.shape[0]
    return pl.pallas_call(
        attend_kernel,
        grid=(heads,),
        in_specs=[
            head_block(rows, 0), head_block(keys, 0), head_block(keys, heads),
            whole_block(rows, 1), whole_block(rows, 1), whole_block(1, keys),
        ],
        out_specs=[head_block(rows, 0), pl.BlockSpec((1, rows, 1), lambda h: (h, 0, 0))],
        out_shape=[
            jax.ShapeDtypeStruct(q.shape, jnp.bfloat16),
            jax.ShapeDtypeStruct((heads, rows, 1), jnp.float32),
        ],
        compiler_params=attend_params(),
        name="attend",
    )(q, pair, pair, low, high, pos)


def query_back_call(q, pair, grad, low, high, pos, lse, heads):
    rows, keys = q.shape[0], pair.shape[0]
    stat = pl.BlockSpec((1, rows, 1), lambda h: (h, 0, 0))
    return pl.pallas_call(
        query_back_kernel,
        grid=(heads,),
        in_specs=[
            head_block(rows, 0), head_block(keys, 0), head_block(keys, heads),
            head_block(rows, 0),
            whole_block(rows, 1), whole_block(rows, 1), whole_block(1, keys), stat,
        ],
        out_specs=[head_block(rows, 0), stat],
        out_shape=[
            jax.ShapeDtypeStruct(q.shape, jnp.bfloat16),
            jax.ShapeDtypeStruct((heads, rows, 1), jnp.float32),
        ],
        compiler_params=attend_params(),
        name="query_back",
    )(q, pair, pair, grad, low, high, pos, lse)


def key_back_call(pair, queries, grads, pos, low, high, lse, mid, heads):
    rows, many = pair.shape[0], queries.shape[0]
    stat = pl.BlockSpec((1, 1, many), lambda h: (h, 0, 0))
    shape = jax.ShapeDtypeStruct((rows, heads * HEAD_DIM), jnp.bfloat16)
    return pl.pallas_call(
        key_back_kernel,
        grid=(heads,),
        in_specs=[
            head_block(rows, 0), head_block(rows, heads), head_block(many, 0), head_block(many, 0),
            whole_block(rows, 1), whole_block(1, many), whole_block(1, many), stat, stat,
        ],
        out_specs=[head_block(rows, 0)] * 2,
        out_shape=[shape, shape],
        compiler_params=attend_params(),
        name="key_back",
    )(pair, pair, queries, grads, pos, low, high, lse, mid)


class Across:
    def __init__(self, count, send_sem, recv_sem, own_sem):
        self.chips = count // 2
        me = lax.axis_index("seq")
        self.me, self.chip, self.core = me, me // 2, me % 2
        self.partner = me + 1 - 2 * self.core
        self.send_sem, self.recv_sem, self.own_sem = send_sem, recv_sem, own_sem
        self.sent, self.kept = [], []

    def chip_at(self, hops):
        return lax.rem(self.chip + hops + self.chips, self.chips)

    def greet(self, with_partner):
        near = [self.chip_at(d) * 2 + self.core for d in range(1, self.chips)]
        return greet("seq", near + ([self.partner] if with_partner else []))

    def send(self, source, target, sem, to):
        copy = remote(
            source, target, self.send_sem.at[len(self.sent)], self.recv_sem.at[sem], "seq", to
        )
        copy.start()
        self.sent.append(copy)

    def keep(self, source, target):
        copy = pltpu.make_async_copy(source, target, self.own_sem.at[len(self.kept)])
        copy.start()
        self.kept.append(copy)

    def wait(self, target, sem):
        remote(
            target, target, self.send_sem.at[0], self.recv_sem.at[sem], "seq", self.partner
        ).wait_recv()

    def finish(self):
        for copy in self.kept:
            copy.wait()
        for copy in self.sent:
            copy.wait_send()


def cut(at, size):
    return pl.ds(pl.multiple_of(at * size, size), size)


def heads_in_kernel(count, qkv_ref, q_ref, kv_ref, *sems):
    ways = Across(count, *sems)
    pl.semaphore_wait(pltpu.get_barrier_semaphore(), ways.greet(True))
    rows, chips = qkv_ref.shape[0], ways.chips

    def places(chip):
        owner = 2 * chip + ways.core
        return (
            q_ref.at[cut(chip, rows)],
            kv_ref.at[cut(owner, rows), 0:HEAD_DIM],
            kv_ref.at[cut(owner, rows), HEAD_DIM : 2 * HEAD_DIM],
        )

    for d in list(range(1, chips)) + [0]:
        head = ways.chip_at(d)
        for kind, target in enumerate(places(ways.chip)):
            source = qkv_ref.at[:, cut(kind * chips + head, HEAD_DIM)]
            if d:
                ways.send(source, target, 3 * d + kind, 2 * head + ways.core)
            else:
                ways.keep(source, target)
    for copy in ways.kept:
        copy.wait()
    ways.kept = []
    for d in range(chips):
        chip = ways.chip_at(-d)
        if d:
            for kind, target in enumerate(places(chip)):
                ways.wait(target, 3 * d + kind)
        both = kv_ref.at[cut(2 * chip + ways.core, rows)]
        ways.send(both, both, 3 * chips + d, ways.partner)
    for d in range(chips):
        chip = ways.chip_at(-d)
        ways.wait(kv_ref.at[cut(2 * chip + 1 - ways.core, rows)], 3 * chips + d)
    ways.finish()


def blocks_to_columns_kernel(count, source_ref, target_ref, *sems):
    ways = Across(count, *sems)
    pl.semaphore_wait(pltpu.get_barrier_semaphore(), ways.greet(False))
    rows = target_ref.shape[0]
    mine = target_ref.at[:, cut(ways.chip, HEAD_DIM)]
    for d in range(1, ways.chips):
        chip = ways.chip_at(d)
        ways.send(source_ref.at[cut(chip, rows)], mine, d, 2 * chip + ways.core)
    ways.keep(source_ref.at[cut(ways.chip, rows)], mine)
    for d in range(1, ways.chips):
        ways.wait(target_ref.at[:, cut(ways.chip_at(-d), HEAD_DIM)], d)
    ways.finish()


def columns_to_blocks_kernel(count, source_ref, target_ref, *sems):
    ways = Across(count, *sems)
    pl.semaphore_wait(pltpu.get_barrier_semaphore(), ways.greet(False))
    rows = source_ref.shape[0]
    mine = target_ref.at[cut(ways.chip, rows)]
    for d in range(1, ways.chips):
        chip = ways.chip_at(d)
        ways.send(source_ref.at[:, cut(chip, HEAD_DIM)], mine, d, 2 * chip + ways.core)
    ways.keep(source_ref.at[:, cut(ways.chip, HEAD_DIM)], mine)
    for d in range(1, ways.chips):
        ways.wait(target_ref.at[cut(ways.chip_at(-d), rows)], d)
    ways.finish()


def heads_grads_kernel(
    count, planes, dq_ref, dk_ref, dv_ref, part_ref, out_ref, sum_ref,
    got_k, got_v, low_k, low_v, got_part, send_sem, recv_sem, own_sem, part_send, part_recv
):
    ways = Across(count, send_sem, recv_sem, own_sem)
    greeted = ways.greet(True) + greet("mp", others_of("mp", planes))
    pl.semaphore_wait(pltpu.get_barrier_semaphore(), greeted)
    rows, chips = out_ref.shape[0], ways.chips
    pairs = ((dk_ref, got_k, low_k), (dv_ref, got_v, low_v))
    for i in range(chips):
        for kind, (ref, got, _) in enumerate(pairs):
            block = ref.at[cut(2 * i + 1 - ways.core, rows)]
            ways.send(block, got.at[i], 3 * chips + 2 * i + kind, ways.partner)
    scatter = PlaneScatter(planes, part_ref, sum_ref, got_part, part_send, part_recv)
    scatter.start()

    def place(kind, chip):
        return out_ref.at[:, cut(kind * chips + chip, HEAD_DIM)]

    for d in range(1, chips):
        chip = ways.chip_at(d)
        ways.send(
            dq_ref.at[cut(chip, rows)], place(0, ways.chip), 3 * d, 2 * chip + ways.core
        )
    ways.keep(dq_ref.at[cut(ways.chip, rows)], place(0, ways.chip))
    for i in range(chips):
        for kind, (ref, got, low) in enumerate(pairs):
            ways.wait(got.at[i], 3 * chips + 2 * i + kind)
            total = ref[cut(2 * i + ways.core, rows), :] + got[i]
            low[i] = (total * (1.0, SCALE)[kind == 0]).astype(low.dtype)
    for d in range(1, chips):
        chip = ways.chip_at(d)
        for kind, (_, _, low) in enumerate(pairs):
            ways.send(
                low.at[chip], place(1 + kind, ways.chip), 3 * d + 1 + kind, 2 * chip + ways.core
            )
    for kind, (_, _, low) in enumerate(pairs):
        ways.keep(low.at[ways.chip], place(1 + kind, ways.chip))
    for d in range(1, chips):
        for kind in range(3):
            ways.wait(place(kind, ways.chip_at(-d)), 3 * d + kind)
    ways.finish()
    scatter.finish()


def across_sems(sends, receives, keeps):
    return [
        pltpu.SemaphoreType.DMA((sends,)), pltpu.SemaphoreType.DMA((receives,)),
        pltpu.SemaphoreType.DMA((keeps,)),
    ]


def across_call(kernel, name, cid, sources, shapes, sems):
    hbm = pl.BlockSpec(memory_space=pl.ANY)
    return pl.pallas_call(
        functools.partial(kernel, lax.axis_size("seq")),
        out_shape=shapes,
        in_specs=[hbm] * len(sources),
        out_specs=[hbm] * len(shapes),
        scratch_shapes=across_sems(*sems),
        compiler_params=remote_params(cid),
        name=name,
    )(*sources)


def heads_in(cid, qkv):
    count, rows = lax.axis_size("seq"), qkv.shape[0]
    chips = count // 2
    shape = jax.ShapeDtypeStruct
    return across_call(
        heads_in_kernel, "heads_in", cid, [qkv],
        [shape((chips * rows, HEAD_DIM), qkv.dtype), shape((count * rows, 2 * HEAD_DIM), qkv.dtype)],
        (4 * chips, 4 * chips, 3),
    )


def blocks_to_columns(name, cid, blocks):
    chips = lax.axis_size("seq") // 2
    shape = (blocks.shape[0] // chips, chips * HEAD_DIM)
    return across_call(
        blocks_to_columns_kernel, name, cid, [blocks],
        [jax.ShapeDtypeStruct(shape, blocks.dtype)], (chips, chips, 1),
    )[0]


def columns_to_blocks(name, cid, columns):
    chips = lax.axis_size("seq") // 2
    shape = (columns.shape[0] * chips, HEAD_DIM)
    return across_call(
        columns_to_blocks_kernel, name, cid, [columns],
        [jax.ShapeDtypeStruct(shape, columns.dtype)], (chips, chips, 1),
    )[0]


def heads_grads(cid, dq, dk, dv, part):
    count, planes = lax.axis_size("seq"), lax.axis_size("mp")
    chips = count // 2
    rows = dq.shape[0] // chips
    share = part.shape[0] // planes
    f32, bf16 = jnp.float32, jnp.bfloat16
    shape = jax.ShapeDtypeStruct
    vmem = pl.BlockSpec(memory_space=pltpu.VMEM)
    return pl.pallas_call(
        functools.partial(heads_grads_kernel, count, planes),
        out_shape=[shape((rows, 3 * chips * HEAD_DIM), bf16), shape((share, part.shape[1]), f32)],
        in_specs=[vmem] * 4,
        out_specs=[pl.BlockSpec(memory_space=pl.ANY), vmem],
        scratch_shapes=[pltpu.VMEM((chips, rows, HEAD_DIM), f32)] * 2
        + [pltpu.VMEM((chips, rows, HEAD_DIM), bf16)] * 2
        + [pltpu.VMEM((planes - 1, share, part.shape[1]), part.dtype)]
        + across_sems(2 * chips + 3 * (chips - 1), 5 * chips, 3)
        + [pltpu.SemaphoreType.DMA((planes,))] * 2,
        compiler_params=remote_params(cid),
        name="heads_grads",
    )(dq, dk, dv, part)


def tn(left, right):
    return lax.dot_general(
        left, right, (((0,), (0,)), ((), ())), preferred_element_type=jnp.float32
    )


def head_kernel(q_ref, k_ref, v_ref, low_ref, high_ref, pos_ref, out_ref, lse_ref):
    scores = nt(q_ref[...], k_ref[...]) * SCALE
    pos = pos_ref[...]
    scores = jnp.where((pos >= low_ref[...]) & (pos <= high_ref[...]), scores, -1e30)
    top = jnp.max(scores, axis=-1, keepdims=True)
    expo = jnp.exp(scores - top)
    mass = jnp.sum(expo, axis=-1, keepdims=True)
    probs = (expo / mass).astype(jnp.bfloat16)
    out_ref[...] = nn(probs, v_ref[...]).astype(jnp.bfloat16)
    lse_ref[...] = top + jnp.log(mass)


def head_back_kernel(q_ref, k_ref, v_ref, g_ref, low_ref, high_ref, pos_ref, lse_ref, dq_ref, dk_ref, dv_ref):
    queries, keys, grads = q_ref[...], k_ref[...], g_ref[...]
    scores = nt(queries, keys) * SCALE
    pos = pos_ref[...]
    scores = jnp.where((pos >= low_ref[...]) & (pos <= high_ref[...]), scores, -1e30)
    probs = jnp.exp(scores - lse_ref[...])
    prob_grad = nt(grads, v_ref[...])
    middle = jnp.sum(probs * prob_grad, axis=-1, keepdims=True)
    score_grad = (probs * (prob_grad - middle)).astype(jnp.bfloat16)
    dq_ref[...] = (nn(score_grad, keys) * SCALE).astype(jnp.bfloat16)
    dk = tn(score_grad, queries)
    dv = tn(probs.astype(jnp.bfloat16), grads)

    @pl.when(pl.program_id(0) == 0)
    def _():
        dk_ref[...] = dk
        dv_ref[...] = dv

    @pl.when(pl.program_id(0) > 0)
    def _():
        dk_ref[...] += dk
        dv_ref[...] += dv


def head_specs(rows, keys):
    block = pl.BlockSpec((rows, HEAD_DIM), lambda i: (i, 0))
    stat = pl.BlockSpec((rows, 1), lambda i: (i, 0))
    half = [pl.BlockSpec((keys, HEAD_DIM), lambda i, k=k: (0, k)) for k in range(2)]
    whole = pl.BlockSpec((keys, HEAD_DIM), lambda i: (0, 0))
    return block, stat, half, pl.BlockSpec((1, keys), lambda i: (0, 0)), whole


def head_call(q, kv, low, high, pos, rows):
    block, stat, half, line, _ = head_specs(rows, kv.shape[0])
    return pl.pallas_call(
        head_kernel,
        grid=(q.shape[0] // rows,),
        in_specs=[block, *half, stat, stat, line],
        out_specs=[block, stat],
        out_shape=[
            jax.ShapeDtypeStruct(q.shape, jnp.bfloat16),
            jax.ShapeDtypeStruct((q.shape[0], 1), jnp.float32),
        ],
        compiler_params=attend_params(),
        name="head",
    )(q, kv, kv, low, high, pos)


def head_back_call(q, kv, grad, low, high, pos, lse, rows):
    block, stat, half, line, whole = head_specs(rows, kv.shape[0])
    keys = jax.ShapeDtypeStruct((kv.shape[0], HEAD_DIM), jnp.float32)
    return pl.pallas_call(
        head_back_kernel,
        grid=(q.shape[0] // rows,),
        in_specs=[block, *half, block, stat, stat, line, stat],
        out_specs=[block, whole, whole],
        out_shape=[jax.ShapeDtypeStruct(q.shape, jnp.bfloat16), keys, keys],
        compiler_params=attend_params(),
        name="head_back",
    )(q, kv, kv, grad, low, high, pos, lse)


def shifted(value, axis, steps):
    count = lax.axis_size(axis)
    leading, last = (max(0, -steps), min(count, count - steps))
    return lax.ppermute(value, axis, [(source, source + steps) for source in range(leading, last)])


def matmul(left, right):
    return jnp.dot(left, right, preferred_element_type=jnp.float32)


def matmul_tn(left, right):
    return lax.dot_general(
        left, right, (((0,), (0,)), ((), ())), preferred_element_type=jnp.float32
    )


def matmul_nt(left, right):
    return lax.dot_general(
        left, right, (((1,), (1,)), ((), ())), preferred_element_type=jnp.float32
    )


def layout(lengths, positions, slot, total):
    starts = jnp.array([0, slot, 2 * slot, total - 2 * slot, total - slot], jnp.int32)
    seg = jnp.sum((positions[:, None] >= starts[None, :]).astype(jnp.int32), axis=1) - 1
    which = (seg[:, None] == jnp.arange(5, dtype=jnp.int32)[None, :]).astype(jnp.int32)
    start_of = jnp.sum(which * starts[None, :], axis=1)
    length_of = jnp.sum(which * lengths[None, :], axis=1)
    keep = (positions - start_of < length_of).astype(jnp.float32)
    first = (positions == start_of).astype(jnp.float32)
    return (start_of, keep, first)


def silu_slope(value):
    sigma = jax.nn.sigmoid(value)
    return sigma * (1.0 + value * (1.0 - sigma))


def gather_rows(array):
    return lax.all_gather(array, "seq", axis=0, tiled=True)


def gather_columns(array):
    return lax.all_gather(array, "seq", axis=1, tiled=True)


def after(value, *earlier):
    return lax.optimization_barrier((value,) + earlier)[0]


def by_chunk(value):
    rows = value.shape[0]
    return value.reshape((CHUNKS, rows // CHUNKS) + value.shape[1:]).swapaxes(0, 1)


def by_token(value):
    steps = value.shape[0]
    return value.swapaxes(0, 1).reshape((CHUNKS * steps,) + value.shape[2:])


def widened(gates, steps):
    gates = gates.reshape(STATE, steps, CHUNKS).swapaxes(0, 1)
    return jnp.broadcast_to(gates[..., None], (steps, STATE, CHUNKS, LANES))


def body(
    tokens,
    lengths,
    out_grad,
    mixer_gain,
    mixer_value,
    mixer_gate,
    conv_weight,
    conv_bias,
    select_proj,
    step_proj,
    step_bias,
    decay_log,
    skip_gain,
    mixer_out,
    first_gain,
    first_gate,
    first_lift,
    first_down,
    attend_gain,
    query_proj,
    key_proj,
    value_proj,
    attend_out,
    second_gain,
    second_gate,
    second_lift,
    second_down,
):
    f32, bf16 = jnp.float32, jnp.bfloat16
    length = tokens.shape[0]
    shards, planes = lax.axis_size("seq"), lax.axis_size("mp")
    me, plane = lax.axis_index("seq"), lax.axis_index("mp")
    total = length * shards
    slot = length // 4
    steps = length // CHUNKS
    share = length // planes
    positions = me * length + jnp.arange(length, dtype=jnp.int32)
    start_of, keep, first = layout(lengths, positions, slot, total)

    def mine(rows):
        return lax.dynamic_slice_in_dim(rows, plane * share, share)

    keep = keep[:, None]
    keep_share = jnp.broadcast_to(mine(keep), (share, LANES))
    x0 = tokens.astype(f32)
    x0_share = mine(x0)

    few = total <= tokens.shape[1]

    def collect(rows):
        return gather_rows(rows) if few else rows

    def hosted(*items):
        return list(items) if few else []

    def by_rows(result):
        if few:
            return result
        return lax.psum_scatter(
            result.astype(bf16), "seq", scatter_dimension=0, tiled=True
        ).astype(f32)

    def by_columns(result):
        if few:
            return result
        return lax.psum_scatter(
            result.astype(bf16), "seq", scatter_dimension=1, tiled=True
        ).astype(f32)

    def ffn_grads(u, e, acts):
        gate, lift, down = ffn_grads_call(u, e, acts, hidden)
        return by_rows(gate), by_rows(lift), by_columns(down)

    (value_w,) = carry("value_weights", 1, gathers=[(mixer_value, True)])
    gate_w = gather_rows(mixer_gate)
    hidden, head_width = first_gate.shape[1], query_proj.shape[1]
    first_both = gather_rows(
        after(
            jnp.concatenate([first_gate, first_lift], axis=1),
            value_w,
        )
    )

    u1 = by_chunk((x0 * rms_scale(x0) * mixer_gain).astype(bf16)).reshape(length, -1)
    inner = matmul(u1, value_w).reshape(steps, CHUNKS, -1)
    width = inner.shape[-1]
    zg = matmul(u1, gate_w)
    joined = 1.0 - first.reshape(CHUNKS, steps)[:, 0]
    prior = shifted(inner[steps - (CONV - 1) :, CHUNKS - 1], "seq", 1)
    halo = jnp.concatenate([prior[:, None], inner[steps - (CONV - 1) :, : CHUNKS - 1]], axis=1)
    padded = jnp.concatenate([halo * joined[None, :, None], inner], axis=0)
    conv = conv_bias[None, None, :]
    for tap in range(CONV):
        conv = conv + conv_weight[tap][None, None, :] * padded[tap : tap + steps]
    signal = jax.nn.silu(conv).astype(bf16)
    flat_signal = signal.reshape(length, width)
    select, (out_w,) = z_step(
        "select_sum", 2, sum_local, matmul_nt(select_proj, flat_signal), (), (), f32,
        gathers=[(mixer_out, False)],
    )
    step_low = select[:DT_RANK].astype(bf16)
    qkv_w = gather_rows(
        after(jnp.concatenate([query_proj, key_proj, value_proj], axis=1), select)
    )
    raised = (matmul_tn(step_low, step_proj) + step_bias[None, :]).reshape(steps, CHUNKS, width)
    dt = jax.nn.softplus(raised)
    signal_wide = signal.astype(f32)
    dx = dt * signal_wide
    rates = -jnp.exp(decay_log)
    rates2 = rates * LOG2E
    keep_chunk = jnp.broadcast_to(joined[:, None], (CHUNKS, LANES))
    ins = widened(select[DT_RANK : DT_RANK + STATE], steps)
    outs = widened(select[DT_RANK + STATE :], steps)
    order = jnp.arange(shards, dtype=jnp.int32)
    thr, off, summary = run_summary(dt, dx, ins, rates2, keep_chunk, False)
    (everyone,) = carry("state_spread", 3, spreads=[summary])
    states, enter = run_states(
        dt, dx, ins, outs, rates2, thr, off, everyone, (order < me).astype(jnp.int32)
    )
    ys = states + skip_gain[None, None, :] * signal_wide
    zg = zg.reshape(steps, CHUNKS, width)
    mix = by_token((ys * jax.nn.silu(zg)).astype(bf16))
    u2, x1_share, (first_w,) = z_step(
        "mixer_join", 4, forward_local, matmul(mix, out_w).astype(bf16),
        (x0_share, keep_share, first_gain[None]), ("share",), gathers=[(first_down, False)],
    )

    second_both = gather_rows(after(jnp.concatenate([second_gate, second_lift], axis=1), u2))

    gate1, lift1, part2 = ffn_forward_call(u2, first_both, first_w)
    u3, x2_share, (attend_w, *u1_all) = z_step(
        "first_join", 5, forward_local, part2,
        (x1_share, keep_share, attend_gain[None]), ("share",),
        gathers=[(attend_out, False)], swaps=hosted(u1),
    )

    qkv = matmul(u3, qkv_w).astype(bf16)
    heads = head_width // HEAD_DIM
    by_head = few and shards == 2 * heads
    if by_head:
        head_q, head_kv = heads_in(6, qkv)
        spot = jnp.arange(heads * length, dtype=jnp.int32)
        spot = (2 * (spot // length) + me % 2) * length + spot % length
        spot_start, _, _ = layout(lengths, spot, slot, total)
        low = jnp.maximum(spot_start, spot - (WINDOW - 1))[:, None]
        high = spot[:, None]
        key_pos = jnp.arange(total, dtype=jnp.int32)[None, :]
        head_att, lse = head_call(head_q, head_kv, low, high, key_pos, length)
        att = blocks_to_columns("heads_out", 12, head_att)
    else:
        query, pair = qkv[:, :head_width], qkv[:, head_width:]
        (pairs,) = carry("keys_values", 6, gathers=[(pair, True)])
        span = min(shards, WINDOW // length + 1) * length
        key_from = jnp.clip(positions[0] + length - span, 0, total - span)
        near_pairs = lax.dynamic_slice_in_dim(pairs, key_from, span)
        key_pos = (key_from + jnp.arange(span, dtype=jnp.int32))[None, :]
        low = jnp.maximum(start_of, positions - (WINDOW - 1))[:, None]
        high = positions[:, None]
        att, lse = attend_call(query, near_pairs, low, high, key_pos, heads)
    u4, x3_share, (second_w, *queries) = z_step(
        "attend_join", 7, forward_local, matmul(att, attend_w).astype(bf16),
        (x2_share, keep_share, second_gain[None]), ("share",),
        gathers=[(second_down, False)] + ([] if by_head else [(query, True)]),
    )
    early_all = collect(after(jnp.concatenate([mix, att], axis=1), u4))

    gate2, lift2, part4 = ffn_forward_call(u4, second_both, second_w)
    wide_grad = out_grad.astype(f32)
    e4 = (keep * wide_grad).astype(bf16)
    acts2, du4 = ffn_backward_call(e4, second_both, second_w, gate2, lift2)
    e3, g3_share, second_gain_part, ue4_all = z_step(
        "second_back", 8, backward_local, du4,
        (x3_share, keep_share, second_gain[None], mine(wide_grad)), ("share", "gain"),
        swaps=hosted(u4, e4),
    )
    acts2_all = collect(acts2)

    datt = matmul_nt(e3, attend_w).astype(bf16)
    if by_head:
        head_grad = columns_to_blocks("heads_grad_in", 9, datt)
        dq, dk, dv = head_back_call(head_q, head_kv, head_grad, low, high, key_pos, lse, length)
        dqkv, sum4 = heads_grads(16, dq, dk, dv, part4)
    else:
        dq, middle = query_back_call(query, near_pairs, datt, low, high, key_pos, lse, heads)
        stats = jnp.concatenate([lse, middle], axis=0).reshape(2 * heads, length)
        datts, all_stats, sum4 = carry(
            "query_grads", 9, gathers=[(datt, True), (stats, True)], scatters=[part4]
        )
        all_stats = all_stats.reshape(shards, 2 * heads, length).swapaxes(0, 1).reshape(2 * heads, total)
        query_from = jnp.clip(positions[0], 0, total - span)
        every_pos = query_from + jnp.arange(span, dtype=jnp.int32)
        every_start, _, _ = layout(lengths, every_pos, slot, total)
        every_low = jnp.maximum(every_start, every_pos - (WINDOW - 1))[None, :]
        near_stats = lax.dynamic_slice_in_dim(all_stats, query_from, span, axis=1)[:, None]
        dk, dv = key_back_call(
            pair,
            lax.dynamic_slice_in_dim(queries[0], query_from, span),
            lax.dynamic_slice_in_dim(datts, query_from, span),
            high, every_low, every_pos[None, :], near_stats[:heads], near_stats[heads:], heads,
        )
        dqkv = jnp.concatenate([dq, dk, dv], axis=1)
    du3 = matmul_nt(dqkv, qkv_w)
    e2, g2_share, attend_gain_part, ue3_all = z_step(
        "attend_back", 10, backward_local, after(du3.astype(bf16), early_all),
        (x2_share, keep_share, attend_gain[None], g3_share), ("share", "gain"),
        swaps=hosted(u3, e3),
    )

    acts1, du2 = ffn_backward_call(e2, first_both, first_w, gate1, lift1, dqkv)
    e1, g1_share, first_gain_part, ue2_all, *second_grads = z_step(
        "first_back", 11, backward_local, after(du2, acts2_all),
        (x1_share, keep_share, first_gain[None], g2_share), ("share", "gain"), swaps=hosted(u2, e2), work=(*ue4_all, acts2_all, hidden) if few else (),
    )
    acts1_all = collect(acts1)

    dmix = matmul_nt(by_chunk(e1).reshape(length, -1), out_w).reshape(steps, CHUNKS, width)
    dys = dmix * jax.nn.silu(zg)
    dzg = (dmix * ys * silu_slope(zg)).astype(bf16).reshape(length, width)
    skip_grad = jnp.sum(dys * signal_wide, axis=(0, 1))
    thr, off, summary = run_summary(dt, dys, outs, rates2, keep_chunk, True)
    everyone, mixed = carry(
        "grad_spread", 13, spreads=[summary],
        collects=[(x3_share + keep_share[:, 0:1] * sum4).astype(bf16)],
    )
    ddt, prod, gate_grads, log_wide = run_grads(
        dt, dx, dys, ins, outs, rates2, rates, enter, thr, off, everyone,
        (order > me).astype(jnp.int32),
    )
    dpre = (ddt + prod * signal_wide) * jax.nn.sigmoid(raised)
    step_bias_grad = jnp.sum(dpre, axis=(0, 1))
    dpr = dpre.astype(bf16).reshape(length, width)
    step_grad = matmul(step_low, dpr)
    dsel, e1_all = z_step(
        "select_back", 14, sum_local,
        jnp.concatenate([matmul_nt(step_proj, dpr), gate_grads]),
        (), (), f32, swaps=hosted(e1),
    )
    dsel = dsel.astype(bf16)
    select_grad = matmul(dsel, flat_signal)
    more = matmul_tn(dsel, select_proj).reshape(steps, CHUNKS, width)
    dconv, conv_sums = conv_back(prod, dys, dt, more, conv, padded, skip_gain)
    head = dconv[: CONV - 1] * joined[None, :, None]
    later = shifted(head[:, 0], "seq", -1)
    tail = jnp.concatenate([head[:, 1:], later[:, None]], axis=1)
    extended = jnp.concatenate([dconv, tail], axis=0)
    dxin = 0.0
    for tap in range(CONV):
        lag = CONV - 1 - tap
        dxin = dxin + conv_weight[tap][None, None, :] * extended[lag : lag + steps]
    dxin = dxin.astype(bf16).reshape(length, width)
    du1 = by_token(
        (matmul_nt(dxin, value_w) + matmul_nt(dzg, gate_w)).astype(bf16).reshape(steps, CHUNKS, -1)
    )
    few_rows = jnp.concatenate(
        [
            conv_sums[: CONV + 1],
            step_bias_grad[None],
            jnp.sum(log_wide, axis=1) * rates,
            skip_grad[None],
            jnp.zeros((1, width), f32),
        ]
    )
    tokens_grad, gain_sums, (*dxz_all, small), *first_grads = z_step(
        "mixer_back", 15, last_backward_local, after(du1, acts1_all),
        (
            x0_share, keep_share, mixer_gain[None], g1_share,
            jnp.concatenate(
                [first_gain_part, attend_gain_part, second_gain_part, jnp.zeros_like(first_gain_part)]
            ),
        ),
        ("gains",), gain_at=4,
        gathers=hosted((dxin, True), (dzg, True)), sums=[(select_grad, step_grad, few_rows)],
        work=(*ue2_all, ue3_all[0], acts1_all, hidden) if few else (),
    )

    if few:
        (u3_all, e3_all), (u1_all,), (dxin_all, dzg_all), (e1_all,) = ue3_all, u1_all, dxz_all, e1_all
    else:
        u1_all, u3_all, e3_all, e1_all, dxin_all, dzg_all = u1, u3, e3, e1, dxin, dzg
    *first_grads, qkv_grad = first_grads or [None]
    if not few:
        qkv_grad = by_rows(side_grads_call(u3_all, acts1_all, hidden, False))
    mixer_out_grad = by_columns(matmul_tn(early_all[:, :width], e1_all))
    attend_out_grad = by_columns(matmul_tn(early_all[:, width:], e3_all))
    cuts = []
    at = 0
    for size in (2 * STATE + DT_RANK, DT_RANK, CONV, 1, 1, STATE, 1):
        cuts.append(small[at : at + size].astype(f32))
        at += size
    select_sum, step_sum, conv_w_sum, conv_b_sum, step_b_sum, decay_sum, skip_sum = cuts
    return (
        mixed,
        tokens_grad.astype(f32),
        gain_sums[3],
        by_rows(matmul_tn(u1_all, dxin_all)),
        by_rows(matmul_tn(u1_all, dzg_all)),
        conv_w_sum,
        conv_b_sum[0],
        select_sum,
        step_sum,
        step_b_sum[0],
        decay_sum,
        skip_sum[0],
        mixer_out_grad,
        gain_sums[0],
        *([grad.astype(f32) for grad in first_grads] or ffn_grads(u2, e2, acts1)),
        gain_sums[1],
        qkv_grad[:, :head_width],
        qkv_grad[:, head_width : 2 * head_width],
        qkv_grad[:, 2 * head_width :],
        attend_out_grad,
        gain_sums[2],
        *([grad.astype(f32) for grad in second_grads] or ffn_grads(u4, e4, acts2)),
    )


def solution(mesh):
    return jax.shard_map(
        body,
        mesh=mesh,
        in_specs=(
            P("seq", None),
            P(),
            P("seq", None),
            P(),
            P("seq", "mp"),
            P("seq", "mp"),
            P(None, "mp"),
            P("mp"),
            P(None, "mp"),
            P(None, "mp"),
            P("mp"),
            P(None, "mp"),
            P("mp"),
            P("mp", "seq"),
            P(),
            P("seq", "mp"),
            P("seq", "mp"),
            P("mp", "seq"),
            P(),
            P("seq", "mp"),
            P("seq", "mp"),
            P("seq", "mp"),
            P("mp", "seq"),
            P(),
            P("seq", "mp"),
            P("seq", "mp"),
            P("mp", "seq"),
        ),
        out_specs=(
            P("seq", None),
            P("seq", None),
            P(),
            P("seq", "mp"),
            P("seq", "mp"),
            P(None, "mp"),
            P("mp"),
            P(None, "mp"),
            P(None, "mp"),
            P("mp"),
            P(None, "mp"),
            P("mp"),
            P("mp", "seq"),
            P(),
            P("seq", "mp"),
            P("seq", "mp"),
            P("mp", "seq"),
            P(),
            P("seq", "mp"),
            P("seq", "mp"),
            P("seq", "mp"),
            P("mp", "seq"),
            P(),
            P("seq", "mp"),
            P("seq", "mp"),
            P("mp", "seq"),
        ),
        check_vma=False,
    )
```

```python
import functools
import math

import jax
import jax.numpy as jnp
from jax import lax
from jax.experimental import pallas as pl
from jax.experimental.pallas import tpu as pltpu
from jax.sharding import PartitionSpec as P

STATE = 16
CONV = 4
DT_RANK = 128
HEAD_DIM = 128
WINDOW = 2048
EPS = 1e-05
CHUNKS = 8
LANES = 128
LOG2E = 1.4426950408889634

VMEM = 48 * 1024 * 1024
MESH = pl.DeviceIdType.MESH


def chunk_scan(p, q, reverse):
    rows = p.shape[0]
    at = lax.broadcasted_iota(jnp.int32, p.shape, 0)
    d = 1
    while d < rows:
        move = (rows - d) if reverse else d
        ok = (at < rows - d) if reverse else (at >= d)
        ps = jnp.where(ok, pltpu.roll(p, move, 0), 1.0)
        qs = jnp.where(ok, pltpu.roll(q, move, 0), 0.0)
        q = p * qs + q
        p = p * ps
        d *= 2
    move = (rows - 1) if reverse else 1
    ok = (at < rows - 1) if reverse else (at >= 1)
    return p, q, jnp.where(ok, pltpu.roll(p, move, 0), 1.0), jnp.where(ok, pltpu.roll(q, move, 0), 0.0)

def spread(row, like):
    return jnp.broadcast_to(row, like.shape)

def ssm_summary(dt_ref, dx_ref, in_ref, rate_ref, keep_ref, thr_ref, off_ref, sum_ref):
    steps = dt_ref.shape[0]
    zero = jnp.zeros(dt_ref.shape[1:], jnp.float32)
    rates = [spread(rate_ref[n:n + 1, :], zero) for n in range(STATE)]
    def step(t, carry):
        total, states = carry
        dt, dx = dt_ref[t], dx_ref[t]
        states = tuple(jnp.exp2(dt * rates[n]) * states[n] + in_ref[t, n] * dx for n in range(STATE))
        return total + dt, states
    total, states = lax.fori_loop(0, steps, step, (zero, (zero,) * STATE), unroll=4)
    keep = keep_ref[...]
    reach, thru = [], []
    for n in range(STATE):
        p, q, pe, qe = chunk_scan(jnp.exp2(total * rates[n]) * keep, states[n], False)
        thr_ref[n] = pe * keep
        off_ref[n] = qe * keep
        reach.append(q[q.shape[0] - 1:, :])
        thru.append(p[p.shape[0] - 1:, :])
    sum_ref[...] = jnp.concatenate(reach + thru, axis=0).astype(sum_ref.dtype)

def entering_state(all_ref, pick_ref, backwards):
    count = all_ref.shape[0]
    running = jnp.zeros((STATE, LANES), jnp.float32)
    for k in range(count):
        j = count - 1 - k if backwards else k
        both = all_ref[j].astype(jnp.float32)
        new = both[STATE:] * running + both[:STATE]
        running = jnp.where(pick_ref[j] > 0, new, running)
    return running

def ssm_states(dt_ref, dx_ref, in_ref, out_ref, rate_ref, thr_ref, off_ref, all_ref, pick_ref, y_ref, enter_ref):
    steps = dt_ref.shape[0]
    zero = jnp.zeros(dt_ref.shape[1:], jnp.float32)
    rates = [spread(rate_ref[n:n + 1, :], zero) for n in range(STATE)]
    running = entering_state(all_ref, pick_ref, False)
    start = []
    for n in range(STATE):
        e = thr_ref[n] * spread(running[n:n + 1, :], zero) + off_ref[n]
        enter_ref[n] = e
        start.append(e)
    def step(t, states):
        dt, dx = dt_ref[t], dx_ref[t]
        states = tuple(jnp.exp2(dt * rates[n]) * states[n] + in_ref[t, n] * dx for n in range(STATE))
        parts = [out_ref[t, n] * states[n] for n in range(STATE)]
        while len(parts) > 1:
            parts = [a + b for a, b in zip(parts[::2], parts[1::2])]
        y_ref[t] = parts[0]
        return states
    lax.fori_loop(0, steps, step, tuple(start), unroll=4)

def ssm_back_summary(dt_ref, dy_ref, out_ref, rate_ref, keep_ref, thr_ref, off_ref, sum_ref):
    steps = dt_ref.shape[0]
    zero = jnp.zeros(dt_ref.shape[1:], jnp.float32)
    rates = [spread(rate_ref[n:n + 1, :], zero) for n in range(STATE)]
    def step(k, carry):
        t = steps - 1 - k
        total, back = carry
        dt, dy = dt_ref[t], dy_ref[t]
        back = tuple(jnp.exp2(dt * rates[n]) * (back[n] + out_ref[t, n] * dy) for n in range(STATE))
        return total + dt, back
    total, back = lax.fori_loop(0, steps, step, (zero, (zero,) * STATE), unroll=4)
    keep = keep_ref[...]
    reach, thru = [], []
    for n in range(STATE):
        p, q, pe, qe = chunk_scan(jnp.exp2(total * rates[n]) * keep, back[n] * keep, True)
        thr_ref[n] = pe
        off_ref[n] = qe
        reach.append(q[0:1, :])
        thru.append(p[0:1, :])
    sum_ref[...] = jnp.concatenate(reach + thru, axis=0).astype(sum_ref.dtype)

def ssm_grads(dt_ref, dx_ref, dy_ref, in_ref, out_ref, rate_ref, true_ref, enter_ref, thr_ref, off_ref, all_ref, pick_ref,
              ddt_ref, prod_ref, gate_ref, log_ref, h_ref, a_ref, ing_ref, outg_ref):
    steps = dt_ref.shape[0]
    zero = jnp.zeros(dt_ref.shape[1:], jnp.float32)
    rates = [spread(rate_ref[n:n + 1, :], zero) for n in range(STATE)]
    @pl.when(pl.program_id(0) == 0)
    def _():
        ing_ref[...] = jnp.zeros_like(ing_ref)
        outg_ref[...] = jnp.zeros_like(outg_ref)
    def forward(t, states):
        dt, dx, dy = dt_ref[t], dx_ref[t], dy_ref[t]
        new = []
        for n in range(STATE):
            h_ref[t, n] = states[n]
            a = jnp.exp2(dt * rates[n])
            a_ref[t, n] = a
            h = a * states[n] + in_ref[t, n] * dx
            outg_ref[t, n] += dy * h
            new.append(h)
        return tuple(new)
    lax.fori_loop(0, steps, forward, tuple(enter_ref[n] for n in range(STATE)), unroll=2)
    running = entering_state(all_ref, pick_ref, True)
    start = tuple(thr_ref[n] * spread(running[n:n + 1, :], zero) + off_ref[n] for n in range(STATE))
    true = [spread(true_ref[n:n + 1, :], zero) for n in range(STATE)]
    log_ref[...] = jnp.zeros_like(log_ref)
    def backward(k, back):
        t = steps - 1 - k
        dt, dx, dy = dt_ref[t], dx_ref[t], dy_ref[t]
        new, ddt, prod = [], [], []
        for n in range(STATE):
            lam = back[n] + out_ref[t, n] * dy
            q = lam * a_ref[t, n]
            dea = q * h_ref[t, n]
            ddt.append(dea * true[n])
            log_ref[n] += dea * dt
            prod.append(lam * in_ref[t, n])
            ing_ref[t, n] += lam * dx
            new.append(q)
        while len(ddt) > 1:
            ddt = [a + b for a, b in zip(ddt[::2], ddt[1::2])]
            prod = [a + b for a, b in zip(prod[::2], prod[1::2])]
        ddt_ref[t] = ddt[0]
        prod_ref[t] = prod[0]
        return tuple(new)
    lax.fori_loop(0, steps, backward, start, unroll=2)
    @pl.when(pl.program_id(0) == pl.num_programs(0) - 1)
    def _():
        ones = jnp.ones((8, LANES), jnp.float32)
        rows = steps * zero.shape[0]
        for k, wide_ref in enumerate((ing_ref, outg_ref)):
            for n in range(STATE):
                sums = lax.dot_general(
                    ones, wide_ref[:, n].reshape(rows, LANES), (((1,), (1,)), ((), ())),
                    precision=lax.Precision.HIGHEST, preferred_element_type=jnp.float32,
                )
                gate_ref[k * STATE + n:k * STATE + n + 1, :] = sums[0:1, :]


def specs(steps, rows):
    chan = pl.BlockSpec((steps, rows, LANES), lambda i: (0, 0, i))
    wide = pl.BlockSpec((steps, STATE, rows, LANES), lambda i: (0, 0, 0, 0))
    rate = pl.BlockSpec((STATE, LANES), lambda i: (0, i))
    per = pl.BlockSpec((STATE, rows, LANES), lambda i: (0, 0, i))
    summ = pl.BlockSpec((2 * STATE, LANES), lambda i: (0, i))
    keep = pl.BlockSpec((rows, LANES), lambda i: (0, 0))
    return chan, wide, rate, per, summ, keep

def params():
    return pltpu.CompilerParams(vmem_limit_bytes=VMEM, dimension_semantics=("arbitrary",))

def run_summary(dt, src, gates, rate2, keep, backwards):
    steps, rows, width = dt.shape
    chan, wide, rate, per, summ, kp = specs(steps, rows)
    f = jnp.float32
    return pl.pallas_call(
        ssm_back_summary if backwards else ssm_summary,
        grid=(width // LANES,),
        in_specs=[chan, chan, wide, rate, kp],
        out_specs=[per, per, summ],
        out_shape=[jax.ShapeDtypeStruct((STATE, rows, width), f)] * 2 + [jax.ShapeDtypeStruct((2 * STATE, width), jnp.bfloat16)],
        compiler_params=params(), name="ssm_back_summary" if backwards else "ssm_summary",
    )(dt, src, gates, rate2, keep)

def run_states(dt, dx, ins, outs, rate2, thr, off, everyone, pick):
    steps, rows, width = dt.shape
    chan, wide, rate, per, summ, kp = specs(steps, rows)
    count = everyone.shape[0]
    alls = pl.BlockSpec((count, 2 * STATE, LANES), lambda i: (0, 0, i))
    f = jnp.float32
    return pl.pallas_call(
        ssm_states, grid=(width // LANES,),
        in_specs=[chan, chan, wide, wide, rate, per, per, alls, pl.BlockSpec(memory_space=pltpu.SMEM)],
        out_specs=[chan, per],
        out_shape=[jax.ShapeDtypeStruct((steps, rows, width), f), jax.ShapeDtypeStruct((STATE, rows, width), f)],
        compiler_params=params(), name="ssm_states",
    )(dt, dx, ins, outs, rate2, thr, off, everyone, pick)

def run_grads(dt, dx, dy, ins, outs, rate2, rates, enter, thr, off, everyone, pick):
    steps, rows, width = dt.shape
    chan, wide, rate, per, summ, kp = specs(steps, rows)
    count = everyone.shape[0]
    alls = pl.BlockSpec((count, 2 * STATE, LANES), lambda i: (0, 0, i))
    f = jnp.float32
    s = jax.ShapeDtypeStruct
    return pl.pallas_call(
        ssm_grads, grid=(width // LANES,),
        in_specs=[chan, chan, chan, wide, wide, rate, rate, per, per, per, alls, pl.BlockSpec(memory_space=pltpu.SMEM)],
        out_specs=[chan, chan, pl.BlockSpec((2 * STATE, steps * rows), lambda i: (0, 0)), per],
        out_shape=[s((steps, rows, width), f)] * 2 + [s((2 * STATE, steps * rows), f), s((STATE, rows, width), f)],
        scratch_shapes=[pltpu.VMEM((steps, STATE, rows, LANES), f)] * 4,
        compiler_params=params(), name="ssm_grads",
    )(dt, dx, dy, ins, outs, rate2, rates, enter, thr, off, everyone, pick)


def conv_back_kernel(prod_ref, dy_ref, dt_ref, more_ref, conv_ref, padded_ref, skip_ref, dconv_ref, sums_ref):
    steps = conv_ref.shape[0]
    zero = jnp.zeros(conv_ref.shape[1:], jnp.float32)
    skip = spread(skip_ref[...], zero)

    def step(t, sums):
        value = conv_ref[t]
        sigma = jax.nn.sigmoid(value)
        grad = prod_ref[t] * dt_ref[t] + dy_ref[t] * skip + more_ref[t]
        grad = grad * (sigma * (1.0 + value * (1.0 - sigma)))
        dconv_ref[t] = grad
        taps = tuple(sums[k] + grad * padded_ref[t + k] for k in range(CONV))
        return taps + (sums[CONV] + grad,)

    sums = lax.fori_loop(0, steps, step, (zero,) * (CONV + 1), unroll=2)
    sums_ref[...] = jnp.zeros_like(sums_ref)
    for k in range(CONV + 1):
        sums_ref[k : k + 1, :] = jnp.sum(sums[k], axis=0, keepdims=True)


def conv_back(prod, dys, dt, more, conv, padded, skip):
    steps, rows, width = conv.shape
    chan = pl.BlockSpec((steps, rows, LANES), lambda i: (0, 0, i))
    longer = pl.BlockSpec((padded.shape[0], rows, LANES), lambda i: (0, 0, i))
    f32 = jnp.float32
    return pl.pallas_call(
        conv_back_kernel,
        grid=(width // LANES,),
        in_specs=[chan] * 5 + [longer, pl.BlockSpec((1, LANES), lambda i: (0, i))],
        out_specs=[chan, pl.BlockSpec((8, LANES), lambda i: (0, i))],
        out_shape=[
            jax.ShapeDtypeStruct((steps, rows, width), f32), jax.ShapeDtypeStruct((8, width), f32)
        ],
        compiler_params=params(),
        name="conv_back",
    )(prod, dys, dt, more, conv, padded, skip[None])


FFN_TILE = 512


def mm(left, right):
    return jnp.dot(left, right, preferred_element_type=jnp.float32)


def mm_nt(left, right):
    return lax.dot_general(
        left, right, (((1,), (1,)), ((), ())), preferred_element_type=jnp.float32
    )


def ffn_forward_kernel(u_ref, gate_w_ref, lift_w_ref, down_ref, gate_ref, lift_ref, part_ref, total):
    at = pl.program_id(0)
    u = u_ref[...]
    gate = mm(u, gate_w_ref[...])
    lift = mm(u, lift_w_ref[...])
    gate_ref[...] = gate
    lift_ref[...] = lift
    hidden = (gate * jax.nn.sigmoid(gate) * lift).astype(jnp.bfloat16)
    piece = mm(hidden, down_ref[...])

    @pl.when(at == 0)
    def _():
        total[...] = piece

    @pl.when(at > 0)
    def _():
        total[...] += piece

    @pl.when(at == pl.num_programs(0) - 1)
    def _():
        part_ref[...] = total[...].astype(part_ref.dtype)


def ffn_forward_call(u, both_w, down_w):
    rows, feat = u.shape
    hidden = down_w.shape[0]
    tile = min(FFN_TILE, hidden)
    count = hidden // tile
    f32, bf16 = jnp.float32, jnp.bfloat16
    shape = jax.ShapeDtypeStruct
    whole = pl.BlockSpec((rows, feat), lambda i: (0, 0))
    act = pl.BlockSpec((rows, tile), lambda i: (0, i))
    return pl.pallas_call(
        ffn_forward_kernel,
        grid=(count,),
        in_specs=[
            whole,
            pl.BlockSpec((feat, tile), lambda i: (0, i)),
            pl.BlockSpec((feat, tile), lambda i: (0, count + i)),
            pl.BlockSpec((tile, feat), lambda i: (i, 0)),
        ],
        out_specs=[act, act, whole],
        out_shape=[shape((rows, hidden), f32), shape((rows, hidden), f32), shape((rows, feat), bf16)],
        scratch_shapes=[pltpu.VMEM((rows, feat), f32)],
        compiler_params=params(),
        name="ffn_forward",
    )(u, both_w, both_w, down_w)


def ffn_backward_kernel(e_ref, gate_w_ref, lift_w_ref, down_ref, gate_ref, lift_ref, *rest):
    *side_ref, acts_ref, part_ref, total = rest
    at = pl.program_id(0)
    tile = gate_ref.shape[1]
    grad = mm_nt(e_ref[...], down_ref[...])
    gate, lift = gate_ref[...], lift_ref[...]
    sigma = jax.nn.sigmoid(gate)
    silu = gate * sigma
    gate_low = (grad * lift * (sigma * (1.0 + gate * (1.0 - sigma)))).astype(jnp.bfloat16)
    lift_low = (grad * silu).astype(jnp.bfloat16)
    acts_ref[:, 0:tile] = (silu * lift).astype(jnp.bfloat16)
    acts_ref[:, tile : 2 * tile] = gate_low
    acts_ref[:, 2 * tile : 3 * tile] = lift_low
    if side_ref:
        acts_ref[:, 3 * tile :] = side_ref[0][...]
    piece = mm_nt(gate_low, gate_w_ref[...]) + mm_nt(lift_low, lift_w_ref[...])

    @pl.when(at == 0)
    def _():
        total[...] = piece

    @pl.when(at > 0)
    def _():
        total[...] += piece

    @pl.when(at == pl.num_programs(0) - 1)
    def _():
        part_ref[...] = total[...].astype(part_ref.dtype)


def ffn_backward_call(e, both_w, down_w, gate, lift, *side):
    more = side[0].shape[1] if side else 0
    rows, feat = e.shape
    hidden = down_w.shape[0]
    tile = min(FFN_TILE, hidden)
    count = hidden // tile
    f32, bf16 = jnp.float32, jnp.bfloat16
    shape = jax.ShapeDtypeStruct
    whole = pl.BlockSpec((rows, feat), lambda i: (0, 0))
    act = pl.BlockSpec((rows, tile), lambda i: (0, i))
    return pl.pallas_call(
        ffn_backward_kernel,
        grid=(count,),
        in_specs=[
            whole,
            pl.BlockSpec((feat, tile), lambda i: (0, i)),
            pl.BlockSpec((feat, tile), lambda i: (0, count + i)),
            pl.BlockSpec((tile, feat), lambda i: (i, 0)),
            act, act,
        ]
        + [pl.BlockSpec((rows, more // count), lambda i: (0, i)) for _ in side],
        out_specs=[pl.BlockSpec((rows, 3 * tile + more // count), lambda i: (0, i)), whole],
        out_shape=[shape((rows, 3 * hidden + more), bf16), shape((rows, feat), bf16)],
        scratch_shapes=[pltpu.VMEM((rows, feat), f32)],
        compiler_params=params(),
        name="ffn_backward",
    )(e, both_w, both_w, down_w, gate, lift, *side)


def ffn_grads_tile(u_t, e_t, acts_ref, gate_ref, lift_ref, down_ref):
    tile = gate_ref.shape[1]
    down_ref[...] = mm(e_t[...], acts_ref[:, 0:tile]).T.astype(down_ref.dtype)
    gate_ref[...] = mm(u_t[...], acts_ref[:, tile : 2 * tile]).astype(gate_ref.dtype)
    lift_ref[...] = mm(u_t[...], acts_ref[:, 2 * tile : 3 * tile]).astype(lift_ref.dtype)


def ffn_grads_specs(rows, feat, hidden, wide):
    tile = min(FFN_TILE, hidden)
    count = hidden // tile
    out = pl.BlockSpec((feat, tile), lambda i: (0, i))
    return (
        (count,), pl.BlockSpec((rows, wide // count), lambda i: (0, i)),
        [out, out, pl.BlockSpec((tile, feat), lambda i: (i, 0))],
    )


def ffn_grads_kernel(u_ref, e_ref, acts_ref, gate_ref, lift_ref, down_ref, u_t, e_t):
    @pl.when(pl.program_id(0) == 0)
    def _():
        u_t[...] = u_ref[...].T
        e_t[...] = e_ref[...].T

    ffn_grads_tile(u_t, e_t, acts_ref, gate_ref, lift_ref, down_ref)


def ffn_grads_call(u, e, acts, hidden):
    rows, feat = u.shape
    grid, block, outs = ffn_grads_specs(rows, feat, hidden, acts.shape[1])
    shape = jax.ShapeDtypeStruct
    whole = pl.BlockSpec((rows, feat), lambda i: (0, 0))
    return pl.pallas_call(
        ffn_grads_kernel,
        grid=grid,
        in_specs=[whole, whole, block],
        out_specs=outs,
        out_shape=[shape((feat, hidden), jnp.float32)] * 2 + [shape((hidden, feat), jnp.float32)],
        scratch_shapes=[pltpu.VMEM((feat, rows), u.dtype)] * 2,
        compiler_params=params(),
        name="ffn_grads",
    )(u, e, acts)


def ffn_grads_beside(sources, outs, turned):
    *sources, acts_ref = sources
    for source, target in zip(sources, turned):
        target[...] = source[...].T
    rows, feat = sources[0].shape
    grid, block, specs = ffn_grads_specs(rows, feat, outs[0].shape[1], acts_ref.shape[1])

    def tiles(acts, gate, lift, down, *side):
        ffn_grads_tile(turned[0], turned[1], acts, gate, lift, down)
        for o_t, out in zip(turned[2:], side):
            out[...] = mm(o_t[...], acts[:, acts.shape[1] - out.shape[1] :])

    specs = specs + [
        pl.BlockSpec((feat, out.shape[1] // grid[0]), lambda i: (0, i)) for out in outs[3:]
    ]
    pltpu.emit_pipeline(tiles, grid=grid, in_specs=[block], out_specs=specs)(acts_ref, *outs)


def columns_grad_beside(o_ref, source_ref, out_ref, o_t, first):
    o_t[...] = o_ref[...].T
    rows, feat = o_ref.shape
    tile = min(FFN_TILE, out_ref.shape[0])

    def tiles(source, out):
        out[...] = mm(o_t[...], source[...]).T

    pltpu.emit_pipeline(
        tiles,
        grid=(out_ref.shape[0] // tile,),
        in_specs=[pl.BlockSpec((rows, tile), lambda i: (0, first // tile + i))],
        out_specs=[pl.BlockSpec((tile, feat), lambda i: (i, 0))],
    )(source_ref, out_ref)


def side_grads_kernel(turned, o_ref, side_ref, out_ref, o_t):
    @pl.when(pl.program_id(0) == 0)
    def _():
        o_t[...] = o_ref[...].T

    result = mm(o_t[...], side_ref[...])
    out_ref[...] = result.T if turned else result


def side_grads_call(o, acts, hidden, turned):
    rows, feat = o.shape
    count = hidden // min(FFN_TILE, hidden)
    side = (acts.shape[1] - 3 * hidden) // count
    step = acts.shape[1] // count // side
    out = (count * side, feat) if turned else (feat, count * side)
    return pl.pallas_call(
        functools.partial(side_grads_kernel, turned),
        grid=(count,),
        in_specs=[
            pl.BlockSpec((rows, feat), lambda i: (0, 0)),
            pl.BlockSpec((rows, side), lambda i: (0, step * i + step - 1)),
        ],
        out_specs=pl.BlockSpec((side, feat), lambda i: (i, 0)) if turned
        else pl.BlockSpec((feat, side), lambda i: (0, i)),
        out_shape=jax.ShapeDtypeStruct(out, jnp.float32),
        scratch_shapes=[pltpu.VMEM((feat, rows), o.dtype)],
        compiler_params=params(),
        name="side_grads",
    )(o, acts)


class Ring:
    def __init__(self, count):
        self.count = count
        self.chips = count // 2
        self.side = math.isqrt(self.chips)
        self.long = self.chips // 2
        self.short = self.chips - 1 - self.long
        self.me = lax.axis_index("seq")
        self.core = self.me % 2
        self.way = 1 - 2 * self.core
        self.at = self.flip(self.me // 2)
        self.partner = self.me + self.way
        self.long_next = self.device(1, self.core)
        self.short_next = self.device(-1, self.core)

    def flip(self, chip):
        row, column = chip // self.side, chip % self.side
        return row * self.side + column + (row % 2) * (self.side - 1 - 2 * column)

    def device(self, hops, core):
        place = (self.at + hops * self.way + 2 * self.chips) % self.chips
        return self.flip(place) * 2 + core


def remote(source, target, send_sem, recv_sem, axis, to):
    return pltpu.make_async_remote_copy(
        src_ref=source,
        dst_ref=target,
        send_sem=send_sem,
        recv_sem=recv_sem,
        device_id={axis: to},
        device_id_type=MESH,
    )


def greet(axis, devices):
    barrier = pltpu.get_barrier_semaphore()
    for to in devices:
        pl.semaphore_signal(barrier, inc=1, device_id={axis: to}, device_id_type=MESH)
    return len(devices)


def others_of(axis, count):
    me = lax.axis_index(axis)
    return [lax.rem(me + d, count) for d in range(1, count)]


class Gather:
    def __init__(self, ring, shard, full, by_rows, send_sem, recv_sem, own_sem):
        self.ring, self.shard, self.full, self.by_rows = ring, shard, full, by_rows
        self.send_sem, self.recv_sem = send_sem, recv_sem
        self.size = shard.shape[0 if by_rows else 1]
        self.own = pltpu.make_async_copy(shard, self.slot(ring.me), own_sem)
        self.sent = []

    def slot(self, device):
        part = pl.ds(pl.multiple_of(device * self.size, self.size), self.size)
        return self.full.at[part] if self.by_rows else self.full.at[:, part]

    def send(self, source, device, sem, to):
        copy = remote(
            source, self.slot(device), self.send_sem.at[len(self.sent)], self.recv_sem.at[sem],
            "seq", to,
        )
        copy.start()
        self.sent.append(copy)

    def wait(self, device, sem):
        slot = self.slot(device)
        remote(
            slot, slot, self.send_sem.at[0], self.recv_sem.at[sem], "seq", self.ring.partner
        ).wait_recv()

    def start(self):
        ring = self.ring
        self.send(self.shard, ring.me, 0, ring.long_next)
        if ring.short:
            self.send(self.shard, ring.me, ring.long, ring.short_next)
        self.send(self.shard, ring.me, ring.long + ring.short, ring.partner)
        self.own.start()

    def hop(self, i):
        ring = self.ring
        base = ring.long + ring.short + 1
        if i <= ring.long:
            device = ring.device(-i, ring.core)
            self.wait(device, i - 1)
            if i < ring.long:
                self.send(self.slot(device), device, i, ring.long_next)
            self.send(self.slot(device), device, base + i - 1, ring.partner)
        if i <= ring.short:
            device = ring.device(i, ring.core)
            self.wait(device, ring.long + i - 1)
            if i < ring.short:
                self.send(self.slot(device), device, ring.long + i, ring.short_next)
            self.send(self.slot(device), device, base + ring.long + i - 1, ring.partner)

    def finish(self):
        ring = self.ring
        base = ring.long + ring.short + 1
        other = 1 - ring.core
        self.wait(ring.partner, base - 1)
        for i in range(1, ring.long + 1):
            self.wait(ring.device(i, other), base + i - 1)
        for i in range(1, ring.short + 1):
            self.wait(ring.device(-i, other), base + ring.long + i - 1)
        self.own.wait()
        for copy in self.sent:
            copy.wait_send()


class Swap:
    def __init__(self, count, source, target, send_sem, recv_sem, own_sem):
        self.count, self.source, self.target = count, source, target
        self.send_sem, self.recv_sem = send_sem, recv_sem
        self.me = lax.axis_index("seq")
        self.rows = target.shape[0] // count
        self.width = target.shape[1]
        self.own = pltpu.make_async_copy(self.block(self.me), self.slot(self.me), own_sem)
        self.sent = []

    def block(self, to):
        if len(self.source.shape) == 3:
            return self.source.at[to]
        return self.source.at[:, pl.ds(pl.multiple_of(to * self.width, self.width), self.width)]

    def slot(self, device):
        return self.target.at[pl.ds(pl.multiple_of(device * self.rows, self.rows), self.rows)]

    def start(self):
        for d in range(1, self.count):
            to = lax.rem(self.me + d, self.count)
            copy = remote(
                self.block(to), self.slot(self.me), self.send_sem.at[d - 1],
                self.recv_sem.at[d - 1], "seq", to,
            )
            copy.start()
            self.sent.append(copy)
        self.own.start()

    def finish(self):
        for d in range(1, self.count):
            slot = self.slot(lax.rem(self.me + self.count - d, self.count))
            remote(
                slot, slot, self.send_sem.at[0], self.recv_sem.at[d - 1], "seq",
                lax.rem(self.me + d, self.count),
            ).wait_recv()
        self.own.wait()
        for copy in self.sent:
            copy.wait_send()


def rms_scale(x):
    return lax.rsqrt(jnp.mean(x * x, axis=-1, keepdims=True) + EPS)


def forward_local(ins, outs, total):
    x_ref, keep_ref, gain_ref = ins
    new = x_ref[...] + keep_ref[:, 0:1] * total
    outs[0][...] = new
    return new * rms_scale(new) * gain_ref[...], None


def norm_back(ins, total):
    x_ref, keep_ref, gain_ref, grad_ref = ins[:4]
    x = x_ref[...]
    scale = rms_scale(x)
    weighted = gain_ref[...] * total
    middle = jnp.mean(weighted * x, axis=-1, keepdims=True)
    row = jnp.sum(total * x * scale, axis=0, keepdims=True)
    return grad_ref[...] + scale * weighted - x * (scale * scale * scale) * middle, row


def backward_local(ins, outs, total):
    new, row = norm_back(ins, total)
    outs[0][...] = new
    outs[1][...] = row
    return ins[1][:, 0:1] * new, None


def last_backward_local(ins, outs, total):
    return norm_back(ins, total)


def sum_local(ins, outs, total):
    return total, None


class Quarter(Swap):
    def __init__(self, count, planes, source, target, send_sem, recv_sem, own_sem):
        self.count, self.source, self.target = count, source, target
        self.send_sem, self.recv_sem = send_sem, recv_sem
        self.me = lax.axis_index("seq")
        self.rows, self.width = target.shape[1:]
        self.share = pl.ds(
            pl.multiple_of(lax.axis_index("mp") * self.rows, self.rows), self.rows
        )
        self.own = pltpu.make_async_copy(self.block(self.me), self.slot(self.me), own_sem)
        self.sent = []

    def block(self, to):
        columns = pl.ds(pl.multiple_of(to * self.width, self.width), self.width)
        return self.source.at[self.share, columns]

    def slot(self, device):
        return self.target.at[device]


class PlaneSpread:
    def __init__(self, planes, source, target, send_sem, recv_sem, own_sem):
        self.planes, self.source, self.target = planes, source, target
        self.send_sem, self.recv_sem = send_sem, recv_sem
        self.me = lax.axis_index("mp")
        self.own = pltpu.make_async_copy(source, target.at[:, self.me], own_sem)
        self.sent = []

    def start(self):
        for d in range(1, self.planes):
            copy = remote(
                self.source, self.target.at[:, self.me], self.send_sem.at[d - 1],
                self.recv_sem.at[d - 1], "mp", lax.rem(self.me + d, self.planes),
            )
            copy.start()
            self.sent.append(copy)
        self.own.start()

    def finish(self):
        for d in range(1, self.planes):
            slot = self.target.at[:, lax.rem(self.me + self.planes - d, self.planes)]
            remote(
                slot, slot, self.send_sem.at[0], self.recv_sem.at[d - 1], "mp",
                lax.rem(self.me + d, self.planes),
            ).wait_recv()
        self.own.wait()
        for copy in self.sent:
            copy.wait_send()


class Spread:
    def __init__(self, count, source, target, send_sem, recv_sem, own_sem):
        self.count, self.source, self.target = count, source, target
        self.send_sem, self.recv_sem = send_sem, recv_sem
        self.me = lax.axis_index("seq")
        self.own = pltpu.make_async_copy(source, target.at[self.me], own_sem)
        self.sent = []

    def start(self):
        for d in range(1, self.count):
            copy = remote(
                self.source, self.target.at[self.me], self.send_sem.at[d - 1],
                self.recv_sem.at[d - 1], "seq", lax.rem(self.me + d, self.count),
            )
            copy.start()
            self.sent.append(copy)
        self.own.start()

    def finish(self):
        for d in range(1, self.count):
            slot = self.target.at[lax.rem(self.me + self.count - d, self.count)]
            remote(
                slot, slot, self.send_sem.at[0], self.recv_sem.at[d - 1], "seq",
                lax.rem(self.me + d, self.count),
            ).wait_recv()
        self.own.wait()
        for copy in self.sent:
            copy.wait_send()


class PlaneScatter:
    def __init__(self, planes, part, target, got, send_sem, recv_sem):
        self.planes, self.part, self.target, self.got = planes, part, target, got
        self.send_sem, self.recv_sem = send_sem, recv_sem
        self.me = lax.axis_index("mp")
        self.sent = []

    def block(self, to):
        rows = self.part.shape[0] // self.planes
        return pl.ds(pl.multiple_of(to * rows, rows), rows)

    def start(self):
        for d in range(1, self.planes):
            to = lax.rem(self.me + d, self.planes)
            copy = remote(
                self.part.at[self.block(to)], self.got.at[d - 1], self.send_sem.at[d - 1],
                self.recv_sem.at[d - 1], "mp", to,
            )
            copy.start()
            self.sent.append(copy)

    def total(self):
        total = self.part[self.block(self.me), :].astype(jnp.float32)
        for d in range(1, self.planes):
            self.sent[d - 1].wait_recv()
            total = total + self.got[d - 1].astype(jnp.float32)
        return total

    def finish(self):
        self.target[...] = self.total()
        for copy in self.sent:
            copy.wait_send()


class PlaneCollect:
    def __init__(self, planes, source, target, send_sem, recv_sem):
        self.planes, self.source, self.target = planes, source, target
        self.send_sem, self.recv_sem = send_sem, recv_sem
        self.me = lax.axis_index("mp")
        rows = source.shape[0]
        self.own = target.at[pl.ds(pl.multiple_of(self.me * rows, rows), rows)]
        self.sent = []

    def start(self):
        for d in range(1, self.planes):
            copy = remote(
                self.source, self.own, self.send_sem.at[d - 1], self.recv_sem.at[d - 1],
                "mp", lax.rem(self.me + d, self.planes),
            )
            copy.start()
            self.sent.append(copy)
        self.own[...] = self.source[...]

    def finish(self):
        for copy in self.sent:
            copy.wait_recv()
        for copy in self.sent:
            copy.wait_send()


class LineSum:
    def __init__(self, part, got, stage, mine, full, sems):
        self.part, self.got, self.stage, self.mine, self.full = part, got, stage, mine, full
        self.sems = sems
        me = lax.axis_index("mp")
        self.me = me
        half = me // 2
        self.outer = (me == 0) | (me == 3)
        self.inner = (me == 1) | (me == 2)
        self.partner = 4 * half + 1 - me
        self.far_inner, self.far_outer = 2 - half, 3 - 3 * half

    def block(self, plane):
        rows = self.mine.shape[0]
        return pl.ds(pl.multiple_of(plane * rows, rows), rows)

    def toward(self, source, slot, sem, to):
        return remote(
            source, self.got.at[slot], self.sems[0].at[sem], self.sems[1].at[slot], "mp", to
        )

    def out(self, source, plane, sem, slot, to):
        return remote(
            source, self.full.at[self.block(plane)], self.sems[2].at[sem], self.sems[3].at[slot],
            "mp", to,
        )

    def start(self):
        part, partner = self.part, self.partner

        @pl.when(self.outer)
        def _():
            self.toward(part.at[self.block(self.far_outer)], 2, 0, partner).start()
            self.toward(part.at[self.block(self.far_inner)], 3, 1, partner).start()
            self.toward(part.at[self.block(partner)], 0, 2, partner).start()

        @pl.when(self.inner)
        def _():
            self.toward(part.at[self.block(partner)], 0, 2, partner).start()

    def relay(self):
        @pl.when(self.inner)
        def _():
            for slot, to in ((2, self.far_outer), (3, self.far_inner)):
                block = self.part.at[self.block(to)]
                self.toward(block, slot, slot - 2, self.partner).wait_recv()
                joined = block[...].astype(jnp.float32) + self.got[slot].astype(jnp.float32)
                self.stage[slot - 2] = joined.astype(self.stage.dtype)
                self.toward(self.stage.at[slot - 2], 1, slot - 2, to).start()

    def total(self):
        block = self.part.at[self.block(self.me)]
        total = block[...].astype(jnp.float32)
        for slot in (0, 1):
            self.toward(block, slot, 0, self.partner).wait_recv()
            total = total + self.got[slot].astype(jnp.float32)
        return total

    def collect(self):
        @pl.when(self.inner)
        def _():
            self.out(self.mine, self.me, 1, 1, self.far_inner).start()
            self.out(self.mine, self.me, 0, 0, self.partner).start()

        @pl.when(self.outer)
        def _():
            self.out(self.mine, self.me, 1, 2, self.far_inner).start()
            self.out(self.mine, self.me, 0, 0, self.partner).start()

        self.full[self.block(self.me), :] = self.mine[...]

    def arrive(self, plane, slot):
        block = self.full.at[self.block(plane)]
        self.out(block, plane, 0, slot, self.partner).wait_recv()
        return block

    def forward(self):
        @pl.when(self.inner)
        def _():
            block = self.arrive(self.far_inner, 1)
            self.out(block, self.far_inner, 2, 1, self.partner).start()
            block = self.arrive(self.far_outer, 2)
            self.out(block, self.far_outer, 3, 2, self.partner).start()

    def finish(self):
        self.arrive(self.partner, 0)

        @pl.when(self.outer)
        def _():
            self.arrive(self.far_inner, 1)
            self.arrive(self.far_outer, 2)

        block = self.part.at[self.block(self.me)]
        for sem in range(3):
            self.toward(block, 0, sem, self.partner).wait_send()
        for sem in range(2):
            self.out(self.mine, self.me, sem, 0, self.partner).wait_send()

        @pl.when(self.inner)
        def _():
            for sem in (2, 3):
                self.out(self.mine, self.me, sem, 0, self.partner).wait_send()


class DirectSum:
    def __init__(self, planes, part, got, mine, full, sems):
        self.scatter = PlaneScatter(planes, part, None, got, sems[0], sems[1])
        self.result = PlaneCollect(planes, mine, full, sems[2], sems[3])

    def start(self):
        self.scatter.start()

    def relay(self):
        pass

    def total(self):
        return self.scatter.total()

    def collect(self):
        self.result.start()

    def forward(self):
        pass

    def finish(self):
        self.result.finish()
        for copy in self.scatter.sent:
            copy.wait_send()


class SeqSum:
    def __init__(self, count, parts, out, low, got, mine, send_sem, recv_sem):
        self.count, self.parts, self.out = count, parts, out
        self.low, self.got, self.mine = low, got, mine
        self.send_sem, self.recv_sem = send_sem, recv_sem
        self.me = lax.axis_index("seq")
        self.rows = low.shape[0] // count
        self.first, self.second = [], []

    def block(self, device):
        return pl.ds(pl.multiple_of(device * self.rows, self.rows), self.rows)

    def start(self):
        at = 0
        for part in self.parts:
            size = part.shape[0]
            self.low[at : at + size, :] = part[...].astype(self.low.dtype)
            at += size
        if at < self.low.shape[0]:
            self.low[at:, :] = jnp.zeros((self.low.shape[0] - at, self.low.shape[1]), self.low.dtype)
        for d in range(1, self.count):
            to = lax.rem(self.me + d, self.count)
            copy = remote(
                self.low.at[self.block(to)], self.got.at[d - 1],
                self.send_sem.at[d - 1], self.recv_sem.at[d - 1], "seq", to,
            )
            copy.start()
            self.first.append(copy)

    def middle(self):
        own = self.block(self.me)
        total = self.low[own, :].astype(jnp.float32)
        for d in range(1, self.count):
            self.first[d - 1].wait_recv()
            total = total + self.got[d - 1].astype(jnp.float32)
        self.mine[...] = total.astype(self.mine.dtype)
        for d in range(1, self.count):
            copy = remote(
                self.mine, self.out.at[own], self.send_sem.at[self.count + d - 1],
                self.recv_sem.at[self.count + d - 1], "seq", lax.rem(self.me + d, self.count),
            )
            copy.start()
            self.second.append(copy)
        self.out[own, :] = self.mine[...]

    def finish(self):
        for d in range(1, self.count):
            slot = self.out.at[self.block(lax.rem(self.me + self.count - d, self.count))]
            remote(
                slot, slot, self.send_sem.at[self.count], self.recv_sem.at[self.count + d - 1],
                "seq", lax.rem(self.me + d, self.count),
            ).wait_recv()
        for copy in self.first + self.second:
            copy.wait_send()


class GainSum:
    def __init__(self, planes, count, rows, out, across, along, sems):
        self.planes, self.count, self.rows, self.out = planes, count, rows, out
        self.across, self.along, self.sems = across, along, sems
        self.me, self.plane = lax.axis_index("seq"), lax.axis_index("mp")
        self.first, self.second = [], []

    def start(self, row):
        held = self.rows.shape[0]
        self.out[...] = self.rows[...]
        self.out[held - 1 : held, :] = row
        for d in range(1, self.planes):
            copy = remote(
                self.out, self.across.at[d - 1], self.sems[0].at[d - 1], self.sems[1].at[d - 1],
                "mp", lax.rem(self.plane + d, self.planes),
            )
            copy.start()
            self.first.append(copy)

    def middle(self):
        total = self.out[...]
        for d in range(1, self.planes):
            self.first[d - 1].wait_recv()
            total = total + self.across[d - 1]
        for copy in self.first:
            copy.wait_send()
        self.out[...] = total
        for d in range(1, self.count):
            copy = remote(
                self.out, self.along.at[d - 1], self.sems[2].at[d - 1], self.sems[3].at[d - 1],
                "seq", lax.rem(self.me + d, self.count),
            )
            copy.start()
            self.second.append(copy)

    def finish(self):
        total = self.out[...]
        for d in range(1, self.count):
            self.second[d - 1].wait_recv()
            total = total + self.along[d - 1]
        for copy in self.second:
            copy.wait_send()
        self.out[...] = total


class Plan:
    def __init__(self, gathers=(), swaps=(), spreads=(), sums=(), quarters=(), planes=(), collects=()):
        self.count = lax.axis_size("seq")
        self.planes = lax.axis_size("mp")
        self.upright = bool(planes or collects)
        count = self.count
        vmem = pl.BlockSpec(memory_space=pltpu.VMEM)
        hbm = pl.BlockSpec(memory_space=pl.ANY)
        shape = jax.ShapeDtypeStruct
        self.sources, self.in_specs, self.shapes, self.out_specs, self.scratch = [], [], [], [], []
        self.kinds, self.after = [], []
        sems = [
            pltpu.SemaphoreType.DMA((2 * count,)), pltpu.SemaphoreType.DMA((2 * count,)),
            pltpu.SemaphoreType.DMA,
        ]
        for array, rows in gathers:
            height, width = array.shape
            by_rows = rows or width % LANES != 0
            self.add("rows" if by_rows else "columns", [array], hbm, hbm, sems, shape(
                (count * height, width) if by_rows else (height, count * width), array.dtype
            ))
            self.after[-1] = (height, width) if by_rows and not rows else None
        for array in swaps:
            height, width = array.shape[0], array.shape[1] // count
            if width % LANES:
                array = array.reshape(height, count, width).swapaxes(0, 1)
            self.add("swap", [array], hbm, hbm, sems, shape((count * height, width), array.dtype))
        for array in spreads:
            self.add("spread", [array], vmem, vmem, sems, shape((count,) + array.shape, array.dtype))
        for parts in sums:
            have, width = sum(part.shape[0] for part in parts), parts[0].shape[1]
            rows = -(-have // (16 * count)) * 16
            bf16 = jnp.bfloat16
            self.add("sum", list(parts), vmem, vmem, sems + [
                pltpu.VMEM((rows * count, width), bf16),
                pltpu.VMEM((count - 1, rows, width), bf16),
                pltpu.VMEM((rows, width), bf16),
            ], shape((rows * count, width), bf16))

        for array in quarters:
            rows, width = array.shape
            self.add("quarter", [array], hbm, hbm, sems, shape(
                (count, rows // self.planes, width // count), array.dtype
            ))
        for array in planes:
            self.add("plane", [array], hbm, hbm, sems, shape(
                (array.shape[0], self.planes) + array.shape[1:], array.dtype
            ))
        for array in collects:
            self.add("collect", [array], vmem, vmem, sems[:2], shape(
                (self.planes * array.shape[0], array.shape[1]), array.dtype
            ))

    def add(self, kind, arrays, in_spec, out_spec, scratch, shape):
        self.kinds.append((kind, len(arrays), len(scratch)))
        self.sources += arrays
        self.in_specs += [in_spec] * len(arrays)
        self.shapes.append(shape)
        self.out_specs.append(out_spec)
        self.scratch += scratch
        self.after.append(None)

    def results(self, targets):
        return [
            t if cut is None
            else t.reshape((self.count,) + cut).swapaxes(0, 1).reshape(cut[0], self.count * cut[1])
            for t, cut in zip(targets, self.after)
        ]

    def bind(self, sources, targets, scratch):
        count = self.count
        self.ring = None
        self.items = []
        self.wide = False
        for (kind, many, held), target in zip(self.kinds, targets):
            mine, sources = sources[:many], sources[many:]
            sems, scratch = scratch[:held], scratch[held:]
            if kind in ("rows", "columns"):
                if self.ring is None:
                    self.ring = Ring(count)
                self.items.append(Gather(self.ring, mine[0], target, kind == "rows", *sems))
                continue
            if kind == "plane":
                self.items.append(PlaneSpread(self.planes, mine[0], target, *sems))
                continue
            if kind == "collect":
                self.items.append(PlaneCollect(self.planes, mine[0], target, *sems))
                continue
            self.wide = True
            if kind == "quarter":
                self.items.append(Quarter(count, self.planes, mine[0], target, *sems))
            elif kind == "swap":
                self.items.append(Swap(count, mine[0], target, *sems))
            elif kind == "spread":
                self.items.append(Spread(count, mine[0], target, *sems))
            else:
                self.items.append(SeqSum(count, mine, target, *sems[3:], *sems[:2]))

    def greet(self, wide=False):
        if self.wide or wide:
            return greet("seq", others_of("seq", self.count))
        if self.ring is not None:
            near = [self.ring.long_next, self.ring.partner]
            if self.ring.short:
                near.append(self.ring.short_next)
            return greet("seq", near)
        return 0

    def start(self):
        for item in self.items:
            item.start()

    def hops(self):
        gathers = [item for item in self.items if isinstance(item, Gather)]
        if gathers:
            for i in range(1, self.ring.long + 1):
                for item in gathers:
                    item.hop(i)
        for item in self.items:
            if isinstance(item, SeqSum):
                item.middle()

    def finish(self):
        for item in self.items:
            item.finish()


def step_kernel(planes, plan, local, n_ins, n_outs, gain_at, work, pieces, *refs):
    part_ref, refs = refs[0], refs[1:]
    ins, refs = refs[:n_ins], refs[n_ins:]
    sources, refs = refs[: len(plan.sources)], refs[len(plan.sources) :]
    work_ins, refs = refs[:work], refs[work:]
    piece_ins, refs = refs[: 2 * len(pieces)], refs[2 * len(pieces) :]
    full_ref, refs = refs[0], refs[1:]
    outs, refs = refs[:n_outs], refs[n_outs:]
    targets, refs = refs[: len(plan.shapes)], refs[len(plan.shapes) :]
    work_outs, refs = refs[:work], refs[work:]
    piece_outs, refs = refs[: len(pieces)], refs[len(pieces) :]
    got, mine, stage = refs[:3]
    sems, refs = refs[3:7], refs[7:]
    plan.bind(sources, targets, refs[: len(plan.scratch)])
    refs = refs[len(plan.scratch) :]
    turned, refs = refs[: work - 1 if work else 0], refs[work - 1 if work else 0 :]
    piece_turned, refs = refs[: len(pieces)], refs[len(pieces) :]
    gains = None
    if gain_at is not None:
        gains = GainSum(planes, plan.count, ins[gain_at], outs[0], refs[0], refs[1], refs[2:])
    greeted = greet("mp", others_of("mp", planes)) + plan.greet(gains is not None)
    pl.semaphore_wait(pltpu.get_barrier_semaphore(), greeted)
    if planes == 4:
        line = LineSum(part_ref, got, stage, mine, full_ref, sems)
    else:
        line = DirectSum(planes, part_ref, got, mine, full_ref, sems)
    line.start()
    plan.start()
    line.relay()
    if work:
        ffn_grads_beside(work_ins, work_outs, turned)
    for i, first in enumerate(pieces):
        columns_grad_beside(*piece_ins[2 * i : 2 * i + 2], piece_outs[i], piece_turned[i], first)
    value, row = local(ins, outs, line.total())
    mine[...] = value.astype(mine.dtype)
    line.collect()
    if gains is not None:
        gains.start(row)
    line.forward()
    plan.hops()
    if gains is not None:
        gains.middle()
    line.finish()
    plan.finish()
    if gains is not None:
        gains.finish()


def remote_params(cid):
    return pltpu.CompilerParams(
        collective_id=cid, has_side_effects=True, vmem_limit_bytes=VMEM
    )


def z_step(name, cid, local, part, others, extra, out_dtype=jnp.bfloat16, gain_at=None, work=(), pieces=(), **carried):
    planes = lax.axis_size("mp")
    plan = Plan(**carried)
    rows, width = part.shape
    share = rows // planes
    f32 = jnp.float32
    shape = jax.ShapeDtypeStruct
    held = 0 if gain_at is None else others[gain_at].shape[0]
    kinds = {
        "share": shape((share, width), f32),
        "gain": shape((1, width), f32),
        "gains": shape((held, width), f32),
    }
    gain_scratch = [] if gain_at is None else [
        pltpu.VMEM((planes - 1, held, width), f32),
        pltpu.VMEM((plan.count - 1, held, width), f32),
        pltpu.SemaphoreType.DMA((planes,)),
        pltpu.SemaphoreType.DMA((planes,)),
        pltpu.SemaphoreType.DMA((plan.count,)),
        pltpu.SemaphoreType.DMA((plan.count,)),
    ]
    vmem = pl.BlockSpec(memory_space=pltpu.VMEM)
    hbm = pl.BlockSpec(memory_space=pl.ANY)
    work_shapes, turned = [], []
    if work:
        u, e, *side, acts, hidden = work
        low = jnp.bfloat16
        work_shapes = [shape((u.shape[1], hidden), low)] * 2 + [shape((hidden, e.shape[1]), low)]
        for o in side:
            work_shapes.append(shape((o.shape[1], acts.shape[1] - 3 * hidden), f32))
        turned = [pltpu.VMEM((u.shape[1], u.shape[0]), u.dtype)] * (2 + len(side))
    piece_ins, piece_shapes, piece_turned = [], [], []
    for o, source, _, size in pieces:
        piece_ins += [o, source]
        piece_shapes.append(shape((size, o.shape[1]), f32))
        piece_turned.append(pltpu.VMEM((o.shape[1], o.shape[0]), o.dtype))
    result = pl.pallas_call(
        functools.partial(
            step_kernel, planes, plan, local, len(others), len(extra), gain_at, len(work_shapes),
            tuple(first for _, _, first, _ in pieces),
        ),
        out_shape=[shape((rows, width), out_dtype)] + [kinds[kind] for kind in extra]
        + plan.shapes + work_shapes + piece_shapes,
        in_specs=[vmem] * (1 + len(others)) + plan.in_specs + ([vmem] * (len(work) - 2) + [hbm] if work else [])
        + [vmem, hbm] * len(pieces),
        out_specs=[vmem] * (1 + len(extra)) + plan.out_specs + [hbm] * len(work_shapes + piece_shapes),
        scratch_shapes=[
            pltpu.VMEM((max(planes, 4), share, width), part.dtype),
            pltpu.VMEM((share, width), out_dtype),
            pltpu.VMEM((2, share, width), part.dtype),
        ]
        + [pltpu.SemaphoreType.DMA((max(planes, 4),))] * 4
        + plan.scratch + turned + piece_turned + gain_scratch,
        compiler_params=remote_params(cid),
        name=name,
    )(part, *others, *plan.sources, *work[:-1], *piece_ins)
    cut = 1 + len(extra)
    rest = cut + len(plan.shapes)
    return list(result[:cut]) + [plan.results(result[cut:rest])] + list(result[rest:])


def carry_kernel(planes, plan, scatters, *refs):
    sources, refs = refs[: len(plan.sources)], refs[len(plan.sources) :]
    parts, refs = refs[:scatters], refs[scatters:]
    targets, refs = refs[: len(plan.shapes)], refs[len(plan.shapes) :]
    sums, refs = refs[:scatters], refs[scatters:]
    plan.bind(sources, targets, refs[: len(plan.scratch)])
    refs = refs[len(plan.scratch) :]
    items = []
    for part, total in zip(parts, sums):
        items.append(PlaneScatter(planes, part, total, *refs[:3]))
        refs = refs[3:]
    greeted = plan.greet()
    if items or plan.upright:
        greeted += greet("mp", others_of("mp", planes))
    pl.semaphore_wait(pltpu.get_barrier_semaphore(), greeted)
    plan.start()
    for item in items:
        item.start()
    plan.hops()
    plan.finish()
    for item in items:
        item.finish()


def carry(name, cid, scatters=(), **carried):
    planes = lax.axis_size("mp")
    plan = Plan(**carried)
    vmem = pl.BlockSpec(memory_space=pltpu.VMEM)
    shape = jax.ShapeDtypeStruct
    sems = [pltpu.SemaphoreType.DMA((planes,))] * 2
    shapes, scratch = [], []
    for part in scatters:
        share = (part.shape[0] // planes, part.shape[1])
        shapes.append(shape(share, jnp.float32))
        scratch += [pltpu.VMEM((planes - 1,) + share, part.dtype)] + sems
    result = pl.pallas_call(
        functools.partial(carry_kernel, planes, plan, len(scatters)),
        out_shape=plan.shapes + shapes,
        in_specs=plan.in_specs + [vmem] * len(scatters),
        out_specs=plan.out_specs + [vmem] * len(shapes),
        scratch_shapes=plan.scratch + scratch,
        compiler_params=remote_params(cid),
        name=name,
    )(*plan.sources, *scatters)
    cut = len(plan.shapes)
    return plan.results(result[:cut]) + list(result[cut:])


SCALE = 1.0 / math.sqrt(HEAD_DIM)


def nt(left, right):
    return lax.dot_general(
        left, right, (((1,), (1,)), ((), ())), preferred_element_type=jnp.float32
    )


def nn(left, right):
    return jnp.dot(left, right, preferred_element_type=jnp.float32)


def attend_kernel(q_ref, k_ref, v_ref, low_ref, high_ref, pos_ref, out_ref, lse_ref):
    scores = nt(q_ref[...], k_ref[...]) * SCALE
    pos = pos_ref[...]
    scores = jnp.where((pos >= low_ref[...]) & (pos <= high_ref[...]), scores, -1e30)
    top = jnp.max(scores, axis=-1, keepdims=True)
    expo = jnp.exp(scores - top)
    mass = jnp.sum(expo, axis=-1, keepdims=True)
    probs = (expo / mass).astype(jnp.bfloat16)
    out_ref[...] = nn(probs, v_ref[...]).astype(jnp.bfloat16)
    lse_ref[0] = top + jnp.log(mass)


def query_back_kernel(q_ref, k_ref, v_ref, g_ref, low_ref, high_ref, pos_ref, lse_ref, dq_ref, mid_ref):
    keys = k_ref[...]
    scores = nt(q_ref[...], keys) * SCALE
    pos = pos_ref[...]
    scores = jnp.where((pos >= low_ref[...]) & (pos <= high_ref[...]), scores, -1e30)
    probs = jnp.exp(scores - lse_ref[0])
    prob_grad = nt(g_ref[...], v_ref[...])
    middle = jnp.sum(probs * prob_grad, axis=-1, keepdims=True)
    score_grad = (probs * (prob_grad - middle)).astype(jnp.bfloat16)
    dq_ref[...] = (nn(score_grad, keys) * SCALE).astype(jnp.bfloat16)
    mid_ref[0] = middle


def key_back_kernel(k_ref, v_ref, q_ref, g_ref, pos_ref, low_ref, high_ref, lse_ref, mid_ref, dk_ref, dv_ref):
    queries, grads = q_ref[...], g_ref[...]
    scores = nt(k_ref[...], queries) * SCALE
    pos = pos_ref[...]
    scores = jnp.where((pos >= low_ref[...]) & (pos <= high_ref[...]), scores, -1e30)
    probs = jnp.exp(scores - lse_ref[0])
    prob_grad = nt(v_ref[...], grads)
    score_grad = (probs * (prob_grad - mid_ref[0])).astype(jnp.bfloat16)
    dk_ref[...] = (nn(score_grad, queries) * SCALE).astype(jnp.bfloat16)
    dv_ref[...] = nn(probs.astype(jnp.bfloat16), grads).astype(jnp.bfloat16)


def head_block(rows, first):
    return pl.BlockSpec((rows, HEAD_DIM), lambda h: (0, first + h))


def whole_block(*shape):
    return pl.BlockSpec(shape, lambda h: (0,) * len(shape))


def attend_params():
    return pltpu.CompilerParams(vmem_limit_bytes=VMEM, dimension_semantics=("arbitrary",))


def attend_call(q, pair, low, high, pos, heads):
    rows, keys = q.shape[0], pair.shape[0]
    return pl.pallas_call(
        attend_kernel,
        grid=(heads,),
        in_specs=[
            head_block(rows, 0), head_block(keys, 0), head_block(keys, heads),
            whole_block(rows, 1), whole_block(rows, 1), whole_block(1, keys),
        ],
        out_specs=[head_block(rows, 0), pl.BlockSpec((1, rows, 1), lambda h: (h, 0, 0))],
        out_shape=[
            jax.ShapeDtypeStruct(q.shape, jnp.bfloat16),
            jax.ShapeDtypeStruct((heads, rows, 1), jnp.float32),
        ],
        compiler_params=attend_params(),
        name="attend",
    )(q, pair, pair, low, high, pos)


def query_back_call(q, pair, grad, low, high, pos, lse, heads):
    rows, keys = q.shape[0], pair.shape[0]
    stat = pl.BlockSpec((1, rows, 1), lambda h: (h, 0, 0))
    return pl.pallas_call(
        query_back_kernel,
        grid=(heads,),
        in_specs=[
            head_block(rows, 0), head_block(keys, 0), head_block(keys, heads),
            head_block(rows, 0),
            whole_block(rows, 1), whole_block(rows, 1), whole_block(1, keys), stat,
        ],
        out_specs=[head_block(rows, 0), stat],
        out_shape=[
            jax.ShapeDtypeStruct(q.shape, jnp.bfloat16),
            jax.ShapeDtypeStruct((heads, rows, 1), jnp.float32),
        ],
        compiler_params=attend_params(),
        name="query_back",
    )(q, pair, pair, grad, low, high, pos, lse)


def key_back_call(pair, queries, grads, pos, low, high, lse, mid, heads):
    rows, many = pair.shape[0], queries.shape[0]
    stat = pl.BlockSpec((1, 1, many), lambda h: (h, 0, 0))
    shape = jax.ShapeDtypeStruct((rows, heads * HEAD_DIM), jnp.bfloat16)
    return pl.pallas_call(
        key_back_kernel,
        grid=(heads,),
        in_specs=[
            head_block(rows, 0), head_block(rows, heads), head_block(many, 0), head_block(many, 0),
            whole_block(rows, 1), whole_block(1, many), whole_block(1, many), stat, stat,
        ],
        out_specs=[head_block(rows, 0)] * 2,
        out_shape=[shape, shape],
        compiler_params=attend_params(),
        name="key_back",
    )(pair, pair, queries, grads, pos, low, high, lse, mid)


class Across:
    def __init__(self, count, send_sem, recv_sem, own_sem):
        self.chips = count // 2
        me = lax.axis_index("seq")
        self.me, self.chip, self.core = me, me // 2, me % 2
        self.partner = me + 1 - 2 * self.core
        self.send_sem, self.recv_sem, self.own_sem = send_sem, recv_sem, own_sem
        self.sent, self.kept = [], []

    def chip_at(self, hops):
        return lax.rem(self.chip + hops + self.chips, self.chips)

    def greet(self, with_partner):
        near = [self.chip_at(d) * 2 + self.core for d in range(1, self.chips)]
        return greet("seq", near + ([self.partner] if with_partner else []))

    def send(self, source, target, sem, to):
        copy = remote(
            source, target, self.send_sem.at[len(self.sent)], self.recv_sem.at[sem], "seq", to
        )
        copy.start()
        self.sent.append(copy)

    def keep(self, source, target):
        copy = pltpu.make_async_copy(source, target, self.own_sem.at[len(self.kept)])
        copy.start()
        self.kept.append(copy)

    def wait(self, target, sem):
        remote(
            target, target, self.send_sem.at[0], self.recv_sem.at[sem], "seq", self.partner
        ).wait_recv()

    def finish(self):
        for copy in self.kept:
            copy.wait()
        for copy in self.sent:
            copy.wait_send()


def cut(at, size):
    return pl.ds(pl.multiple_of(at * size, size), size)


def heads_in_kernel(count, planes, qkv_ref, side_ref, q_ref, kv_ref, side_out, *sems):
    ways = Across(count, *sems[:3])
    greeted = ways.greet(True) + greet("mp", others_of("mp", planes))
    pl.semaphore_wait(pltpu.get_barrier_semaphore(), greeted)
    side = PlaneSpread(planes, side_ref, side_out, *sems[3:])
    side.start()
    rows, chips = qkv_ref.shape[0], ways.chips

    def places(chip):
        owner = 2 * chip + ways.core
        return (
            q_ref.at[cut(chip, rows)],
            kv_ref.at[cut(owner, rows), 0:HEAD_DIM],
            kv_ref.at[cut(owner, rows), HEAD_DIM : 2 * HEAD_DIM],
        )

    for d in list(range(1, chips)) + [0]:
        head = ways.chip_at(d)
        for kind, target in enumerate(places(ways.chip)):
            source = qkv_ref.at[:, cut(kind * chips + head, HEAD_DIM)]
            if d:
                ways.send(source, target, 3 * d + kind, 2 * head + ways.core)
            else:
                ways.keep(source, target)
    for copy in ways.kept:
        copy.wait()
    ways.kept = []
    for d in range(chips):
        chip = ways.chip_at(-d)
        if d:
            for kind, target in enumerate(places(chip)):
                ways.wait(target, 3 * d + kind)
        both = kv_ref.at[cut(2 * chip + ways.core, rows)]
        ways.send(both, both, 3 * chips + d, ways.partner)
    for d in range(chips):
        chip = ways.chip_at(-d)
        ways.wait(kv_ref.at[cut(2 * chip + 1 - ways.core, rows)], 3 * chips + d)
    ways.finish()
    side.finish()


def blocks_to_columns_kernel(count, source_ref, target_ref, *sems):
    ways = Across(count, *sems)
    pl.semaphore_wait(pltpu.get_barrier_semaphore(), ways.greet(False))
    rows = target_ref.shape[0]
    mine = target_ref.at[:, cut(ways.chip, HEAD_DIM)]
    for d in range(1, ways.chips):
        chip = ways.chip_at(d)
        ways.send(source_ref.at[cut(chip, rows)], mine, d, 2 * chip + ways.core)
    ways.keep(source_ref.at[cut(ways.chip, rows)], mine)
    for d in range(1, ways.chips):
        ways.wait(target_ref.at[:, cut(ways.chip_at(-d), HEAD_DIM)], d)
    ways.finish()


def columns_to_blocks_kernel(count, source_ref, target_ref, *sems):
    ways = Across(count, *sems)
    pl.semaphore_wait(pltpu.get_barrier_semaphore(), ways.greet(False))
    rows = source_ref.shape[0]
    mine = target_ref.at[cut(ways.chip, rows)]
    for d in range(1, ways.chips):
        chip = ways.chip_at(d)
        ways.send(source_ref.at[:, cut(chip, HEAD_DIM)], mine, d, 2 * chip + ways.core)
    ways.keep(source_ref.at[:, cut(ways.chip, HEAD_DIM)], mine)
    for d in range(1, ways.chips):
        ways.wait(target_ref.at[cut(ways.chip_at(-d), rows)], d)
    ways.finish()


def heads_grads_kernel(
    count, dq_ref, dk_ref, dv_ref, out_ref, got_k, got_v, low_k, low_v, send_sem, recv_sem, own_sem
):
    ways = Across(count, send_sem, recv_sem, own_sem)
    pl.semaphore_wait(pltpu.get_barrier_semaphore(), ways.greet(True))
    rows, chips = out_ref.shape[0], ways.chips
    pairs = ((dk_ref, got_k, low_k), (dv_ref, got_v, low_v))
    for i in range(chips):
        for kind, (ref, got, _) in enumerate(pairs):
            block = ref.at[cut(2 * i + 1 - ways.core, rows)]
            ways.send(block, got.at[i], 3 * chips + 2 * i + kind, ways.partner)

    def place(kind, chip):
        return out_ref.at[:, cut(kind * chips + chip, HEAD_DIM)]

    for d in range(1, chips):
        chip = ways.chip_at(d)
        ways.send(
            dq_ref.at[cut(chip, rows)], place(0, ways.chip), 3 * d, 2 * chip + ways.core
        )
    ways.keep(dq_ref.at[cut(ways.chip, rows)], place(0, ways.chip))
    for i in range(chips):
        for kind, (ref, got, low) in enumerate(pairs):
            ways.wait(got.at[i], 3 * chips + 2 * i + kind)
            total = ref[cut(2 * i + ways.core, rows), :] + got[i]
            low[i] = (total * (1.0, SCALE)[kind == 0]).astype(low.dtype)
    for d in range(1, chips):
        chip = ways.chip_at(d)
        for kind, (_, _, low) in enumerate(pairs):
            ways.send(
                low.at[chip], place(1 + kind, ways.chip), 3 * d + 1 + kind, 2 * chip + ways.core
            )
    for kind, (_, _, low) in enumerate(pairs):
        ways.keep(low.at[ways.chip], place(1 + kind, ways.chip))
    for d in range(1, chips):
        for kind in range(3):
            ways.wait(place(kind, ways.chip_at(-d)), 3 * d + kind)
    ways.finish()


def across_sems(sends, receives, keeps):
    return [
        pltpu.SemaphoreType.DMA((sends,)), pltpu.SemaphoreType.DMA((receives,)),
        pltpu.SemaphoreType.DMA((keeps,)),
    ]


def across_call(kernel, name, cid, sources, shapes, sems):
    hbm = pl.BlockSpec(memory_space=pl.ANY)
    return pl.pallas_call(
        functools.partial(kernel, lax.axis_size("seq")),
        out_shape=shapes,
        in_specs=[hbm] * len(sources),
        out_specs=[hbm] * len(shapes),
        scratch_shapes=across_sems(*sems),
        compiler_params=remote_params(cid),
        name=name,
    )(*sources)


def heads_in(cid, qkv, side):
    count, planes, rows = lax.axis_size("seq"), lax.axis_size("mp"), qkv.shape[0]
    chips = count // 2
    shape = jax.ShapeDtypeStruct
    hbm = pl.BlockSpec(memory_space=pl.ANY)
    return pl.pallas_call(
        functools.partial(heads_in_kernel, count, planes),
        out_shape=[
            shape((chips * rows, HEAD_DIM), qkv.dtype),
            shape((count * rows, 2 * HEAD_DIM), qkv.dtype),
            shape((count, planes) + side.shape[1:], side.dtype),
        ],
        in_specs=[hbm] * 2,
        out_specs=[hbm] * 3,
        scratch_shapes=across_sems(4 * chips, 4 * chips, 3)
        + [pltpu.SemaphoreType.DMA((planes,))] * 2 + [pltpu.SemaphoreType.DMA],
        compiler_params=remote_params(cid),
        name="heads_in",
    )(qkv, side)


def blocks_to_columns(name, cid, blocks):
    chips = lax.axis_size("seq") // 2
    shape = (blocks.shape[0] // chips, chips * HEAD_DIM)
    return across_call(
        blocks_to_columns_kernel, name, cid, [blocks],
        [jax.ShapeDtypeStruct(shape, blocks.dtype)], (chips, chips, 1),
    )[0]


def columns_to_blocks(name, cid, columns):
    chips = lax.axis_size("seq") // 2
    shape = (columns.shape[0] * chips, HEAD_DIM)
    return across_call(
        columns_to_blocks_kernel, name, cid, [columns],
        [jax.ShapeDtypeStruct(shape, columns.dtype)], (chips, chips, 1),
    )[0]


def heads_grads(cid, dq, dk, dv):
    count = lax.axis_size("seq")
    chips = count // 2
    rows = dq.shape[0] // chips
    f32, bf16 = jnp.float32, jnp.bfloat16
    vmem = pl.BlockSpec(memory_space=pltpu.VMEM)
    return pl.pallas_call(
        functools.partial(heads_grads_kernel, count),
        out_shape=jax.ShapeDtypeStruct((rows, 3 * chips * HEAD_DIM), bf16),
        in_specs=[vmem] * 3,
        out_specs=pl.BlockSpec(memory_space=pl.ANY),
        scratch_shapes=[pltpu.VMEM((chips, rows, HEAD_DIM), f32)] * 2
        + [pltpu.VMEM((chips, rows, HEAD_DIM), bf16)] * 2
        + across_sems(2 * chips + 3 * (chips - 1), 5 * chips, 3),
        compiler_params=remote_params(cid),
        name="heads_grads",
    )(dq, dk, dv)


def tn(left, right):
    return lax.dot_general(
        left, right, (((0,), (0,)), ((), ())), preferred_element_type=jnp.float32
    )


def head_kernel(q_ref, k_ref, v_ref, low_ref, high_ref, pos_ref, out_ref, lse_ref):
    scores = nt(q_ref[...], k_ref[...]) * SCALE
    pos = pos_ref[...]
    scores = jnp.where((pos >= low_ref[...]) & (pos <= high_ref[...]), scores, -1e30)
    top = jnp.max(scores, axis=-1, keepdims=True)
    expo = jnp.exp(scores - top)
    mass = jnp.sum(expo, axis=-1, keepdims=True)
    probs = (expo / mass).astype(jnp.bfloat16)
    out_ref[...] = nn(probs, v_ref[...]).astype(jnp.bfloat16)
    lse_ref[...] = top + jnp.log(mass)


def head_back_kernel(q_ref, k_ref, v_ref, g_ref, low_ref, high_ref, pos_ref, lse_ref, dq_ref, dk_ref, dv_ref):
    queries, keys, grads = q_ref[...], k_ref[...], g_ref[...]
    scores = nt(queries, keys) * SCALE
    pos = pos_ref[...]
    scores = jnp.where((pos >= low_ref[...]) & (pos <= high_ref[...]), scores, -1e30)
    probs = jnp.exp(scores - lse_ref[...])
    prob_grad = nt(grads, v_ref[...])
    middle = jnp.sum(probs * prob_grad, axis=-1, keepdims=True)
    score_grad = (probs * (prob_grad - middle)).astype(jnp.bfloat16)
    dq_ref[...] = (nn(score_grad, keys) * SCALE).astype(jnp.bfloat16)
    dk = tn(score_grad, queries)
    dv = tn(probs.astype(jnp.bfloat16), grads)

    @pl.when(pl.program_id(0) == 0)
    def _():
        dk_ref[...] = dk
        dv_ref[...] = dv

    @pl.when(pl.program_id(0) > 0)
    def _():
        dk_ref[...] += dk
        dv_ref[...] += dv


def head_specs(rows, keys):
    block = pl.BlockSpec((rows, HEAD_DIM), lambda i: (i, 0))
    stat = pl.BlockSpec((rows, 1), lambda i: (i, 0))
    half = [pl.BlockSpec((keys, HEAD_DIM), lambda i, k=k: (0, k)) for k in range(2)]
    whole = pl.BlockSpec((keys, HEAD_DIM), lambda i: (0, 0))
    return block, stat, half, pl.BlockSpec((1, keys), lambda i: (0, 0)), whole


def head_call(q, kv, low, high, pos, rows):
    block, stat, half, line, _ = head_specs(rows, kv.shape[0])
    return pl.pallas_call(
        head_kernel,
        grid=(q.shape[0] // rows,),
        in_specs=[block, *half, stat, stat, line],
        out_specs=[block, stat],
        out_shape=[
            jax.ShapeDtypeStruct(q.shape, jnp.bfloat16),
            jax.ShapeDtypeStruct((q.shape[0], 1), jnp.float32),
        ],
        compiler_params=attend_params(),
        name="head",
    )(q, kv, kv, low, high, pos)


def head_back_call(q, kv, grad, low, high, pos, lse, rows):
    block, stat, half, line, whole = head_specs(rows, kv.shape[0])
    keys = jax.ShapeDtypeStruct((kv.shape[0], HEAD_DIM), jnp.float32)
    return pl.pallas_call(
        head_back_kernel,
        grid=(q.shape[0] // rows,),
        in_specs=[block, *half, block, stat, stat, line, stat],
        out_specs=[block, whole, whole],
        out_shape=[jax.ShapeDtypeStruct(q.shape, jnp.bfloat16), keys, keys],
        compiler_params=attend_params(),
        name="head_back",
    )(q, kv, kv, grad, low, high, pos, lse)


def shifted(value, axis, steps):
    count = lax.axis_size(axis)
    leading, last = (max(0, -steps), min(count, count - steps))
    return lax.ppermute(value, axis, [(source, source + steps) for source in range(leading, last)])


def matmul(left, right):
    return jnp.dot(left, right, preferred_element_type=jnp.float32)


def matmul_tn(left, right):
    return lax.dot_general(
        left, right, (((0,), (0,)), ((), ())), preferred_element_type=jnp.float32
    )


def matmul_nt(left, right):
    return lax.dot_general(
        left, right, (((1,), (1,)), ((), ())), preferred_element_type=jnp.float32
    )


def layout(lengths, positions, slot, total):
    starts = jnp.array([0, slot, 2 * slot, total - 2 * slot, total - slot], jnp.int32)
    seg = jnp.sum((positions[:, None] >= starts[None, :]).astype(jnp.int32), axis=1) - 1
    which = (seg[:, None] == jnp.arange(5, dtype=jnp.int32)[None, :]).astype(jnp.int32)
    start_of = jnp.sum(which * starts[None, :], axis=1)
    length_of = jnp.sum(which * lengths[None, :], axis=1)
    keep = (positions - start_of < length_of).astype(jnp.float32)
    first = (positions == start_of).astype(jnp.float32)
    return (start_of, keep, first)


def silu_slope(value):
    sigma = jax.nn.sigmoid(value)
    return sigma * (1.0 + value * (1.0 - sigma))


def gather_rows(array):
    return lax.all_gather(array, "seq", axis=0, tiled=True)


def gather_columns(array):
    return lax.all_gather(array, "seq", axis=1, tiled=True)


def after(value, *earlier):
    return lax.optimization_barrier((value,) + earlier)[0]


def by_chunk(value):
    rows = value.shape[0]
    return value.reshape((CHUNKS, rows // CHUNKS) + value.shape[1:]).swapaxes(0, 1)


def by_token(value):
    steps = value.shape[0]
    return value.swapaxes(0, 1).reshape((CHUNKS * steps,) + value.shape[2:])


def widened(gates, steps):
    gates = gates.reshape(STATE, steps, CHUNKS).swapaxes(0, 1)
    return jnp.broadcast_to(gates[..., None], (steps, STATE, CHUNKS, LANES))


def body(
    tokens,
    lengths,
    out_grad,
    mixer_gain,
    mixer_value,
    mixer_gate,
    conv_weight,
    conv_bias,
    select_proj,
    step_proj,
    step_bias,
    decay_log,
    skip_gain,
    mixer_out,
    first_gain,
    first_gate,
    first_lift,
    first_down,
    attend_gain,
    query_proj,
    key_proj,
    value_proj,
    attend_out,
    second_gain,
    second_gate,
    second_lift,
    second_down,
):
    f32, bf16 = jnp.float32, jnp.bfloat16
    length = tokens.shape[0]
    shards, planes = lax.axis_size("seq"), lax.axis_size("mp")
    me, plane = lax.axis_index("seq"), lax.axis_index("mp")
    total = length * shards
    slot = length // 4
    steps = length // CHUNKS
    share = length // planes
    positions = me * length + jnp.arange(length, dtype=jnp.int32)
    start_of, keep, first = layout(lengths, positions, slot, total)

    def mine(rows):
        return lax.dynamic_slice_in_dim(rows, plane * share, share)

    keep = keep[:, None]
    keep_share = jnp.broadcast_to(mine(keep), (share, LANES))
    x0 = tokens.astype(f32)
    x0_share = mine(x0)

    few = total <= tokens.shape[1]

    def collect(rows):
        return gather_rows(rows) if few else rows

    def hosted(*items):
        return list(items) if few else []

    def by_rows(result):
        if few:
            return result
        return lax.psum_scatter(
            result.astype(bf16), "seq", scatter_dimension=0, tiled=True
        ).astype(f32)

    def by_columns(result):
        if few:
            return result
        return lax.psum_scatter(
            result.astype(bf16), "seq", scatter_dimension=1, tiled=True
        ).astype(f32)

    def ffn_grads(u, e, acts):
        gate, lift, down = ffn_grads_call(u, e, acts, hidden)
        return by_rows(gate), by_rows(lift), by_columns(down)

    (value_w,) = carry("value_weights", 1, gathers=[(mixer_value, True)])
    gate_w = gather_rows(mixer_gate)
    hidden, head_width = first_gate.shape[1], query_proj.shape[1]
    first_both = gather_rows(
        after(
            jnp.concatenate([first_gate, first_lift], axis=1),
            value_w,
        )
    )

    u1 = by_chunk((x0 * rms_scale(x0) * mixer_gain).astype(bf16)).reshape(length, -1)
    inner = matmul(u1, value_w).reshape(steps, CHUNKS, -1)
    width = inner.shape[-1]
    zg = matmul(u1, gate_w)
    joined = 1.0 - first.reshape(CHUNKS, steps)[:, 0]
    prior = shifted(inner[steps - (CONV - 1) :, CHUNKS - 1], "seq", 1)
    halo = jnp.concatenate([prior[:, None], inner[steps - (CONV - 1) :, : CHUNKS - 1]], axis=1)
    padded = jnp.concatenate([halo * joined[None, :, None], inner], axis=0)
    conv = conv_bias[None, None, :]
    for tap in range(CONV):
        conv = conv + conv_weight[tap][None, None, :] * padded[tap : tap + steps]
    signal = jax.nn.silu(conv).astype(bf16)
    flat_signal = signal.reshape(length, width)
    select, (out_w,) = z_step(
        "select_sum", 2, sum_local, matmul_nt(select_proj, flat_signal), (), (), f32,
        gathers=[(mixer_out, False)],
    )
    step_low = select[:DT_RANK].astype(bf16)
    qkv_w = gather_rows(
        after(jnp.concatenate([query_proj, key_proj, value_proj], axis=1), select)
    )
    raised = (matmul_tn(step_low, step_proj) + step_bias[None, :]).reshape(steps, CHUNKS, width)
    dt = jax.nn.softplus(raised)
    signal_wide = signal.astype(f32)
    dx = dt * signal_wide
    rates = -jnp.exp(decay_log)
    rates2 = rates * LOG2E
    keep_chunk = jnp.broadcast_to(joined[:, None], (CHUNKS, LANES))
    ins = widened(select[DT_RANK : DT_RANK + STATE], steps)
    outs = widened(select[DT_RANK + STATE :], steps)
    order = jnp.arange(shards, dtype=jnp.int32)
    thr, off, summary = run_summary(dt, dx, ins, rates2, keep_chunk, False)
    (everyone,) = carry("state_spread", 3, spreads=[summary])
    states, enter = run_states(
        dt, dx, ins, outs, rates2, thr, off, everyone, (order < me).astype(jnp.int32)
    )
    ys = states + skip_gain[None, None, :] * signal_wide
    zg = zg.reshape(steps, CHUNKS, width)
    mix = by_token((ys * jax.nn.silu(zg)).astype(bf16))
    u2, x1_share, (first_w,) = z_step(
        "mixer_join", 4, forward_local, matmul(mix, out_w).astype(bf16),
        (x0_share, keep_share, first_gain[None]), ("share",), gathers=[(first_down, False)],
    )

    second_both = gather_rows(after(jnp.concatenate([second_gate, second_lift], axis=1), u2))

    gate1, lift1, part2 = ffn_forward_call(u2, first_both, first_w)
    heads = query_proj.shape[1] // HEAD_DIM
    by_head = few and shards == 2 * heads
    u3, x2_share, (attend_w, *u2_part) = z_step(
        "first_join", 5, forward_local, part2,
        (x1_share, keep_share, attend_gain[None]), ("share",),
        gathers=[(attend_out, False)], quarters=[u2] if by_head else [],
    )

    qkv = matmul(u3, qkv_w).astype(bf16)
    if by_head:
        head_q, head_kv, u2_all = heads_in(6, qkv, u2_part[0])
        u2_all = [u2_all.reshape(total, -1)]
        spot = jnp.arange(heads * length, dtype=jnp.int32)
        spot = (2 * (spot // length) + me % 2) * length + spot % length
        spot_start, _, _ = layout(lengths, spot, slot, total)
        low = jnp.maximum(spot_start, spot - (WINDOW - 1))[:, None]
        high = spot[:, None]
        key_pos = jnp.arange(total, dtype=jnp.int32)[None, :]
        head_att, lse = head_call(head_q, head_kv, low, high, key_pos, length)
        att = blocks_to_columns("heads_out", 12, head_att)
    else:
        query, pair = qkv[:, :head_width], qkv[:, head_width:]
        (pairs,) = carry("keys_values", 6, gathers=[(pair, True)])
        span = min(shards, WINDOW // length + 1) * length
        key_from = jnp.clip(positions[0] + length - span, 0, total - span)
        near_pairs = lax.dynamic_slice_in_dim(pairs, key_from, span)
        key_pos = (key_from + jnp.arange(span, dtype=jnp.int32))[None, :]
        low = jnp.maximum(start_of, positions - (WINDOW - 1))[:, None]
        high = positions[:, None]
        att, lse = attend_call(query, near_pairs, low, high, key_pos, heads)
    u4, x3_share, (second_w, *queries) = z_step(
        "attend_join", 7, forward_local, matmul(att, attend_w).astype(bf16),
        (x2_share, keep_share, second_gain[None]), ("share",),
        gathers=[(second_down, False)] + ([] if by_head else [(query, True)]),
        swaps=hosted(u1),
    )
    queries, u1_all = (queries[:-1], queries[-1:]) if few else (queries, [])
    early_all = collect(after(jnp.concatenate([mix, att], axis=1), u4))

    gate2, lift2, part4 = ffn_forward_call(u4, second_both, second_w)
    wide_grad = out_grad.astype(f32)
    e4 = (keep * wide_grad).astype(bf16)
    acts2, du4 = ffn_backward_call(e4, second_both, second_w, gate2, lift2)
    e3, g3_share, second_gain_part, ue4_all = z_step(
        "second_back", 8, backward_local, du4,
        (x3_share, keep_share, second_gain[None], mine(wide_grad)), ("share", "gain"),
        swaps=hosted(u4, e4),
    )
    acts2_all = collect(acts2)

    datt = matmul_nt(e3, attend_w).astype(bf16)
    if by_head:
        head_grad = columns_to_blocks("heads_grad_in", 9, datt)
        dq, dk, dv = head_back_call(head_q, head_kv, head_grad, low, high, key_pos, lse, length)
        dqkv = heads_grads(16, dq, dk, dv)
    else:
        dq, middle = query_back_call(query, near_pairs, datt, low, high, key_pos, lse, heads)
        stats = jnp.concatenate([lse, middle], axis=0).reshape(2 * heads, length)
        datts, all_stats = carry("query_grads", 9, gathers=[(datt, True), (stats, True)])
        all_stats = all_stats.reshape(shards, 2 * heads, length).swapaxes(0, 1).reshape(2 * heads, total)
        query_from = jnp.clip(positions[0], 0, total - span)
        every_pos = query_from + jnp.arange(span, dtype=jnp.int32)
        every_start, _, _ = layout(lengths, every_pos, slot, total)
        every_low = jnp.maximum(every_start, every_pos - (WINDOW - 1))[None, :]
        near_stats = lax.dynamic_slice_in_dim(all_stats, query_from, span, axis=1)[:, None]
        dk, dv = key_back_call(
            pair,
            lax.dynamic_slice_in_dim(queries[0], query_from, span),
            lax.dynamic_slice_in_dim(datts, query_from, span),
            high, every_low, every_pos[None, :], near_stats[:heads], near_stats[heads:], heads,
        )
        dqkv = jnp.concatenate([dq, dk, dv], axis=1)
    du3 = matmul_nt(dqkv, qkv_w)
    e2, g2_share, attend_gain_part, u3_all = z_step(
        "attend_back", 10, backward_local, after(du3.astype(bf16), early_all),
        (x2_share, keep_share, attend_gain[None], g3_share), ("share", "gain"),
        swaps=hosted(u3),
    )

    acts1, du2 = ffn_backward_call(e2, first_both, first_w, gate1, lift1, dqkv)
    e1, g1_share, first_gain_part, e2_all, *second_grads = z_step(
        "first_back", 11, backward_local, after(du2, acts2_all),
        (x1_share, keep_share, first_gain[None], g2_share), ("share", "gain"), swaps=hosted(e2) if by_head else hosted(u2, e2), work=(*ue4_all, acts2_all, hidden) if few else (),
    )
    acts1_all = collect(acts1)

    if few and not by_head:
        *u2_all, last = e2_all
        e2_all = [last]

    dmix = matmul_nt(by_chunk(e1).reshape(length, -1), out_w).reshape(steps, CHUNKS, width)
    dys = dmix * jax.nn.silu(zg)
    dzg = (dmix * ys * silu_slope(zg)).astype(bf16).reshape(length, width)
    skip_grad = jnp.sum(dys * signal_wide, axis=(0, 1))
    thr, off, summary = run_summary(dt, dys, outs, rates2, keep_chunk, True)
    everyone, *e1_part, sum4 = carry(
        "grad_spread", 13, spreads=[summary], quarters=[e1] if by_head else [], scatters=[part4],
    )
    ddt, prod, gate_grads, log_wide = run_grads(
        dt, dx, dys, ins, outs, rates2, rates, enter, thr, off, everyone,
        (order > me).astype(jnp.int32),
    )
    dpre = (ddt + prod * signal_wide) * jax.nn.sigmoid(raised)
    step_bias_grad = jnp.sum(dpre, axis=(0, 1))
    dpr = dpre.astype(bf16).reshape(length, width)
    step_grad = matmul(step_low, dpr)
    dsel, e31_all = z_step(
        "select_back", 14, sum_local,
        jnp.concatenate([matmul_nt(step_proj, dpr), gate_grads]),
        (), (), f32, swaps=hosted(e3) if by_head else hosted(e3, e1), planes=e1_part,
    )
    dsel = dsel.astype(bf16)
    select_grad = matmul(dsel, flat_signal)
    more = matmul_tn(dsel, select_proj).reshape(steps, CHUNKS, width)
    dconv, conv_sums = conv_back(prod, dys, dt, more, conv, padded, skip_gain)
    head = dconv[: CONV - 1] * joined[None, :, None]
    later = shifted(head[:, 0], "seq", -1)
    tail = jnp.concatenate([head[:, 1:], later[:, None]], axis=1)
    extended = jnp.concatenate([dconv, tail], axis=0)
    dxin = 0.0
    for tap in range(CONV):
        lag = CONV - 1 - tap
        dxin = dxin + conv_weight[tap][None, None, :] * extended[lag : lag + steps]
    dxin = dxin.astype(bf16).reshape(length, width)
    du1 = by_token(
        (matmul_nt(dxin, value_w) + matmul_nt(dzg, gate_w)).astype(bf16).reshape(steps, CHUNKS, -1)
    )
    few_rows = jnp.concatenate(
        [
            conv_sums[: CONV + 1],
            step_bias_grad[None],
            jnp.sum(log_wide, axis=1) * rates,
            skip_grad[None],
            jnp.zeros((1, width), f32),
        ]
    )
    pieces = []
    if few:
        e3_all, e1_all = e31_all
        e1_all = e1_all.reshape(total, -1)
        pieces = [
            (e1_all, early_all, 0, width), (e3_all, early_all, width, early_all.shape[1] - width)
        ]
    tokens_grad, gain_sums, (*dxz_all, small, mixed), *first_grads = z_step(
        "mixer_back", 15, last_backward_local, after(du1, acts1_all),
        (
            x0_share, keep_share, mixer_gain[None], g1_share,
            jnp.concatenate(
                [first_gain_part, attend_gain_part, second_gain_part, jnp.zeros_like(first_gain_part)]
            ),
        ),
        ("gains",), gain_at=4,
        gathers=hosted((dxin, True), (dzg, True)), sums=[(select_grad, step_grad, few_rows)],
        collects=[(x3_share + keep_share[:, 0:1] * sum4).astype(bf16)],
        work=(*u2_all, *e2_all, *u3_all, acts1_all, hidden) if few else (), pieces=pieces,
    )

    if few:
        (u1_all,), (dxin_all, dzg_all) = u1_all, dxz_all
        *first_grads, qkv_grad, mixer_out_grad, attend_out_grad = first_grads
    else:
        u1_all, dxin_all, dzg_all = u1, dxin, dzg
        qkv_grad = by_rows(side_grads_call(u3, acts1_all, hidden, False))
        mixer_out_grad = by_columns(matmul_tn(early_all[:, :width], e1))
        attend_out_grad = by_columns(matmul_tn(early_all[:, width:], e3))
    cuts = []
    at = 0
    for size in (2 * STATE + DT_RANK, DT_RANK, CONV, 1, 1, STATE, 1):
        cuts.append(small[at : at + size].astype(f32))
        at += size
    select_sum, step_sum, conv_w_sum, conv_b_sum, step_b_sum, decay_sum, skip_sum = cuts
    return (
        mixed,
        tokens_grad.astype(f32),
        gain_sums[3],
        by_rows(matmul_tn(u1_all, dxin_all)),
        by_rows(matmul_tn(u1_all, dzg_all)),
        conv_w_sum,
        conv_b_sum[0],
        select_sum,
        step_sum,
        step_b_sum[0],
        decay_sum,
        skip_sum[0],
        mixer_out_grad,
        gain_sums[0],
        *([grad.astype(f32) for grad in first_grads] or ffn_grads(u2, e2, acts1)),
        gain_sums[1],
        qkv_grad[:, :head_width],
        qkv_grad[:, head_width : 2 * head_width],
        qkv_grad[:, 2 * head_width :],
        attend_out_grad,
        gain_sums[2],
        *([grad.astype(f32) for grad in second_grads] or ffn_grads(u4, e4, acts2)),
    )


def solution(mesh):
    return jax.shard_map(
        body,
        mesh=mesh,
        in_specs=(
            P("seq", None),
            P(),
            P("seq", None),
            P(),
            P("seq", "mp"),
            P("seq", "mp"),
            P(None, "mp"),
            P("mp"),
            P(None, "mp"),
            P(None, "mp"),
            P("mp"),
            P(None, "mp"),
            P("mp"),
            P("mp", "seq"),
            P(),
            P("seq", "mp"),
            P("seq", "mp"),
            P("mp", "seq"),
            P(),
            P("seq", "mp"),
            P("seq", "mp"),
            P("seq", "mp"),
            P("mp", "seq"),
            P(),
            P("seq", "mp"),
            P("seq", "mp"),
            P("mp", "seq"),
        ),
        out_specs=(
            P("seq", None),
            P("seq", None),
            P(),
            P("seq", "mp"),
            P("seq", "mp"),
            P(None, "mp"),
            P("mp"),
            P(None, "mp"),
            P(None, "mp"),
            P("mp"),
            P(None, "mp"),
            P("mp"),
            P("mp", "seq"),
            P(),
            P("seq", "mp"),
            P("seq", "mp"),
            P("mp", "seq"),
            P(),
            P("seq", "mp"),
            P("seq", "mp"),
            P("seq", "mp"),
            P("mp", "seq"),
            P(),
            P("seq", "mp"),
            P("seq", "mp"),
            P("mp", "seq"),
        ),
        check_vma=False,
    )
```

```python
import functools
import math

import jax
import jax.numpy as jnp
from jax import lax
from jax.experimental import pallas as pl
from jax.experimental.pallas import tpu as pltpu
from jax.sharding import PartitionSpec as P

STATE = 16
CONV = 4
DT_RANK = 128
HEAD_DIM = 128
WINDOW = 2048
EPS = 1e-05
CHUNKS = 8
LANES = 128
LOG2E = 1.4426950408889634

VMEM = 48 * 1024 * 1024
MESH = pl.DeviceIdType.MESH


def chunk_scan(p, q, reverse):
    rows = p.shape[0]
    at = lax.broadcasted_iota(jnp.int32, p.shape, 0)
    d = 1
    while d < rows:
        move = (rows - d) if reverse else d
        ok = (at < rows - d) if reverse else (at >= d)
        ps = jnp.where(ok, pltpu.roll(p, move, 0), 1.0)
        qs = jnp.where(ok, pltpu.roll(q, move, 0), 0.0)
        q = p * qs + q
        p = p * ps
        d *= 2
    move = (rows - 1) if reverse else 1
    ok = (at < rows - 1) if reverse else (at >= 1)
    return p, q, jnp.where(ok, pltpu.roll(p, move, 0), 1.0), jnp.where(ok, pltpu.roll(q, move, 0), 0.0)

def spread(row, like):
    return jnp.broadcast_to(row, like.shape)

def ssm_summary(dt_ref, dx_ref, in_ref, rate_ref, keep_ref, thr_ref, off_ref, sum_ref):
    steps = dt_ref.shape[0]
    zero = jnp.zeros(dt_ref.shape[1:], jnp.float32)
    rates = [spread(rate_ref[n:n + 1, :], zero) for n in range(STATE)]
    def step(t, carry):
        total, states = carry
        dt, dx = dt_ref[t], dx_ref[t]
        states = tuple(jnp.exp2(dt * rates[n]) * states[n] + in_ref[t, n] * dx for n in range(STATE))
        return total + dt, states
    total, states = lax.fori_loop(0, steps, step, (zero, (zero,) * STATE), unroll=4)
    keep = keep_ref[...]
    reach, thru = [], []
    for n in range(STATE):
        p, q, pe, qe = chunk_scan(jnp.exp2(total * rates[n]) * keep, states[n], False)
        thr_ref[n] = pe * keep
        off_ref[n] = qe * keep
        reach.append(q[q.shape[0] - 1:, :])
        thru.append(p[p.shape[0] - 1:, :])
    sum_ref[...] = jnp.concatenate(reach + thru, axis=0).astype(sum_ref.dtype)

def entering_state(all_ref, pick_ref, backwards):
    count = all_ref.shape[0]
    running = jnp.zeros((STATE, LANES), jnp.float32)
    for k in range(count):
        j = count - 1 - k if backwards else k
        both = all_ref[j].astype(jnp.float32)
        new = both[STATE:] * running + both[:STATE]
        running = jnp.where(pick_ref[j] > 0, new, running)
    return running

def ssm_states(dt_ref, dx_ref, in_ref, out_ref, rate_ref, thr_ref, off_ref, all_ref, pick_ref, y_ref, enter_ref):
    steps = dt_ref.shape[0]
    zero = jnp.zeros(dt_ref.shape[1:], jnp.float32)
    rates = [spread(rate_ref[n:n + 1, :], zero) for n in range(STATE)]
    running = entering_state(all_ref, pick_ref, False)
    start = []
    for n in range(STATE):
        e = thr_ref[n] * spread(running[n:n + 1, :], zero) + off_ref[n]
        enter_ref[n] = e
        start.append(e)
    def step(t, states):
        dt, dx = dt_ref[t], dx_ref[t]
        states = tuple(jnp.exp2(dt * rates[n]) * states[n] + in_ref[t, n] * dx for n in range(STATE))
        parts = [out_ref[t, n] * states[n] for n in range(STATE)]
        while len(parts) > 1:
            parts = [a + b for a, b in zip(parts[::2], parts[1::2])]
        y_ref[t] = parts[0]
        return states
    lax.fori_loop(0, steps, step, tuple(start), unroll=4)

def ssm_back_summary(dt_ref, dy_ref, out_ref, rate_ref, keep_ref, thr_ref, off_ref, sum_ref):
    steps = dt_ref.shape[0]
    zero = jnp.zeros(dt_ref.shape[1:], jnp.float32)
    rates = [spread(rate_ref[n:n + 1, :], zero) for n in range(STATE)]
    def step(k, carry):
        t = steps - 1 - k
        total, back = carry
        dt, dy = dt_ref[t], dy_ref[t]
        back = tuple(jnp.exp2(dt * rates[n]) * (back[n] + out_ref[t, n] * dy) for n in range(STATE))
        return total + dt, back
    total, back = lax.fori_loop(0, steps, step, (zero, (zero,) * STATE), unroll=4)
    keep = keep_ref[...]
    reach, thru = [], []
    for n in range(STATE):
        p, q, pe, qe = chunk_scan(jnp.exp2(total * rates[n]) * keep, back[n] * keep, True)
        thr_ref[n] = pe
        off_ref[n] = qe
        reach.append(q[0:1, :])
        thru.append(p[0:1, :])
    sum_ref[...] = jnp.concatenate(reach + thru, axis=0).astype(sum_ref.dtype)

def ssm_grads(dt_ref, dx_ref, dy_ref, in_ref, out_ref, rate_ref, true_ref, enter_ref, thr_ref, off_ref, all_ref, pick_ref,
              ddt_ref, prod_ref, gate_ref, log_ref, h_ref, a_ref, ing_ref, outg_ref):
    steps = dt_ref.shape[0]
    zero = jnp.zeros(dt_ref.shape[1:], jnp.float32)
    rates = [spread(rate_ref[n:n + 1, :], zero) for n in range(STATE)]
    @pl.when(pl.program_id(0) == 0)
    def _():
        ing_ref[...] = jnp.zeros_like(ing_ref)
        outg_ref[...] = jnp.zeros_like(outg_ref)
    def forward(t, states):
        dt, dx, dy = dt_ref[t], dx_ref[t], dy_ref[t]
        new = []
        for n in range(STATE):
            h_ref[t, n] = states[n]
            a = jnp.exp2(dt * rates[n])
            a_ref[t, n] = a
            h = a * states[n] + in_ref[t, n] * dx
            outg_ref[t, n] += dy * h
            new.append(h)
        return tuple(new)
    lax.fori_loop(0, steps, forward, tuple(enter_ref[n] for n in range(STATE)), unroll=2)
    running = entering_state(all_ref, pick_ref, True)
    start = tuple(thr_ref[n] * spread(running[n:n + 1, :], zero) + off_ref[n] for n in range(STATE))
    true = [spread(true_ref[n:n + 1, :], zero) for n in range(STATE)]
    log_ref[...] = jnp.zeros_like(log_ref)
    def backward(k, back):
        t = steps - 1 - k
        dt, dx, dy = dt_ref[t], dx_ref[t], dy_ref[t]
        new, ddt, prod = [], [], []
        for n in range(STATE):
            lam = back[n] + out_ref[t, n] * dy
            q = lam * a_ref[t, n]
            dea = q * h_ref[t, n]
            ddt.append(dea * true[n])
            log_ref[n] += dea * dt
            prod.append(lam * in_ref[t, n])
            ing_ref[t, n] += lam * dx
            new.append(q)
        while len(ddt) > 1:
            ddt = [a + b for a, b in zip(ddt[::2], ddt[1::2])]
            prod = [a + b for a, b in zip(prod[::2], prod[1::2])]
        ddt_ref[t] = ddt[0]
        prod_ref[t] = prod[0]
        return tuple(new)
    lax.fori_loop(0, steps, backward, start, unroll=2)
    @pl.when(pl.program_id(0) == pl.num_programs(0) - 1)
    def _():
        ones = jnp.ones((8, LANES), jnp.float32)
        rows = steps * zero.shape[0]
        for k, wide_ref in enumerate((ing_ref, outg_ref)):
            for n in range(STATE):
                sums = lax.dot_general(
                    ones, wide_ref[:, n].reshape(rows, LANES), (((1,), (1,)), ((), ())),
                    precision=lax.Precision.HIGHEST, preferred_element_type=jnp.float32,
                )
                gate_ref[k * STATE + n:k * STATE + n + 1, :] = sums[0:1, :]


def specs(steps, rows):
    chan = pl.BlockSpec((steps, rows, LANES), lambda i: (0, 0, i))
    wide = pl.BlockSpec((steps, STATE, rows, LANES), lambda i: (0, 0, 0, 0))
    rate = pl.BlockSpec((STATE, LANES), lambda i: (0, i))
    per = pl.BlockSpec((STATE, rows, LANES), lambda i: (0, 0, i))
    summ = pl.BlockSpec((2 * STATE, LANES), lambda i: (0, i))
    keep = pl.BlockSpec((rows, LANES), lambda i: (0, 0))
    return chan, wide, rate, per, summ, keep

def params():
    return pltpu.CompilerParams(vmem_limit_bytes=VMEM, dimension_semantics=("arbitrary",))

def run_summary(dt, src, gates, rate2, keep, backwards):
    steps, rows, width = dt.shape
    chan, wide, rate, per, summ, kp = specs(steps, rows)
    f = jnp.float32
    return pl.pallas_call(
        ssm_back_summary if backwards else ssm_summary,
        grid=(width // LANES,),
        in_specs=[chan, chan, wide, rate, kp],
        out_specs=[per, per, summ],
        out_shape=[jax.ShapeDtypeStruct((STATE, rows, width), f)] * 2 + [jax.ShapeDtypeStruct((2 * STATE, width), jnp.bfloat16)],
        compiler_params=params(), name="ssm_back_summary" if backwards else "ssm_summary",
    )(dt, src, gates, rate2, keep)

def run_states(dt, dx, ins, outs, rate2, thr, off, everyone, pick):
    steps, rows, width = dt.shape
    chan, wide, rate, per, summ, kp = specs(steps, rows)
    count = everyone.shape[0]
    alls = pl.BlockSpec((count, 2 * STATE, LANES), lambda i: (0, 0, i))
    f = jnp.float32
    return pl.pallas_call(
        ssm_states, grid=(width // LANES,),
        in_specs=[chan, chan, wide, wide, rate, per, per, alls, pl.BlockSpec(memory_space=pltpu.SMEM)],
        out_specs=[chan, per],
        out_shape=[jax.ShapeDtypeStruct((steps, rows, width), f), jax.ShapeDtypeStruct((STATE, rows, width), f)],
        compiler_params=params(), name="ssm_states",
    )(dt, dx, ins, outs, rate2, thr, off, everyone, pick)

def run_grads(dt, dx, dy, ins, outs, rate2, rates, enter, thr, off, everyone, pick):
    steps, rows, width = dt.shape
    chan, wide, rate, per, summ, kp = specs(steps, rows)
    count = everyone.shape[0]
    alls = pl.BlockSpec((count, 2 * STATE, LANES), lambda i: (0, 0, i))
    f = jnp.float32
    s = jax.ShapeDtypeStruct
    return pl.pallas_call(
        ssm_grads, grid=(width // LANES,),
        in_specs=[chan, chan, chan, wide, wide, rate, rate, per, per, per, alls, pl.BlockSpec(memory_space=pltpu.SMEM)],
        out_specs=[chan, chan, pl.BlockSpec((2 * STATE, steps * rows), lambda i: (0, 0)), per],
        out_shape=[s((steps, rows, width), f)] * 2 + [s((2 * STATE, steps * rows), f), s((STATE, rows, width), f)],
        scratch_shapes=[pltpu.VMEM((steps, STATE, rows, LANES), f)] * 4,
        compiler_params=params(), name="ssm_grads",
    )(dt, dx, dy, ins, outs, rate2, rates, enter, thr, off, everyone, pick)


def conv_back_kernel(prod_ref, dy_ref, dt_ref, more_ref, conv_ref, padded_ref, skip_ref, dconv_ref, sums_ref):
    steps = conv_ref.shape[0]
    zero = jnp.zeros(conv_ref.shape[1:], jnp.float32)
    skip = spread(skip_ref[...], zero)

    def step(t, sums):
        value = conv_ref[t]
        sigma = jax.nn.sigmoid(value)
        grad = prod_ref[t] * dt_ref[t] + dy_ref[t] * skip + more_ref[t]
        grad = grad * (sigma * (1.0 + value * (1.0 - sigma)))
        dconv_ref[t] = grad
        taps = tuple(sums[k] + grad * padded_ref[t + k] for k in range(CONV))
        return taps + (sums[CONV] + grad,)

    sums = lax.fori_loop(0, steps, step, (zero,) * (CONV + 1), unroll=2)
    sums_ref[...] = jnp.zeros_like(sums_ref)
    for k in range(CONV + 1):
        sums_ref[k : k + 1, :] = jnp.sum(sums[k], axis=0, keepdims=True)


def conv_back(prod, dys, dt, more, conv, padded, skip):
    steps, rows, width = conv.shape
    chan = pl.BlockSpec((steps, rows, LANES), lambda i: (0, 0, i))
    longer = pl.BlockSpec((padded.shape[0], rows, LANES), lambda i: (0, 0, i))
    f32 = jnp.float32
    return pl.pallas_call(
        conv_back_kernel,
        grid=(width // LANES,),
        in_specs=[chan] * 5 + [longer, pl.BlockSpec((1, LANES), lambda i: (0, i))],
        out_specs=[chan, pl.BlockSpec((8, LANES), lambda i: (0, i))],
        out_shape=[
            jax.ShapeDtypeStruct((steps, rows, width), f32), jax.ShapeDtypeStruct((8, width), f32)
        ],
        compiler_params=params(),
        name="conv_back",
    )(prod, dys, dt, more, conv, padded, skip[None])


FFN_TILE = 512


def mm(left, right):
    return jnp.dot(left, right, preferred_element_type=jnp.float32)


def mm_nt(left, right):
    return lax.dot_general(
        left, right, (((1,), (1,)), ((), ())), preferred_element_type=jnp.float32
    )


def ffn_forward_kernel(u_ref, gate_w_ref, lift_w_ref, down_ref, gate_ref, lift_ref, part_ref, total):
    at = pl.program_id(0)
    u = u_ref[...]
    gate = mm(u, gate_w_ref[...])
    lift = mm(u, lift_w_ref[...])
    gate_ref[...] = gate
    lift_ref[...] = lift
    hidden = (gate * jax.nn.sigmoid(gate) * lift).astype(jnp.bfloat16)
    piece = mm(hidden, down_ref[...])

    @pl.when(at == 0)
    def _():
        total[...] = piece

    @pl.when(at > 0)
    def _():
        total[...] += piece

    @pl.when(at == pl.num_programs(0) - 1)
    def _():
        part_ref[...] = total[...].astype(part_ref.dtype)


def ffn_forward_call(u, both_w, down_w):
    rows, feat = u.shape
    hidden = down_w.shape[0]
    tile = min(FFN_TILE, hidden)
    count = hidden // tile
    f32, bf16 = jnp.float32, jnp.bfloat16
    shape = jax.ShapeDtypeStruct
    whole = pl.BlockSpec((rows, feat), lambda i: (0, 0))
    act = pl.BlockSpec((rows, tile), lambda i: (0, i))
    return pl.pallas_call(
        ffn_forward_kernel,
        grid=(count,),
        in_specs=[
            whole,
            pl.BlockSpec((feat, tile), lambda i: (0, i)),
            pl.BlockSpec((feat, tile), lambda i: (0, count + i)),
            pl.BlockSpec((tile, feat), lambda i: (i, 0)),
        ],
        out_specs=[act, act, whole],
        out_shape=[shape((rows, hidden), f32), shape((rows, hidden), f32), shape((rows, feat), bf16)],
        scratch_shapes=[pltpu.VMEM((rows, feat), f32)],
        compiler_params=params(),
        name="ffn_forward",
    )(u, both_w, both_w, down_w)


def ffn_backward_kernel(e_ref, gate_w_ref, lift_w_ref, down_ref, gate_ref, lift_ref, *rest):
    *side_ref, acts_ref, part_ref, total = rest
    at = pl.program_id(0)
    tile = gate_ref.shape[1]
    grad = mm_nt(e_ref[...], down_ref[...])
    gate, lift = gate_ref[...], lift_ref[...]
    sigma = jax.nn.sigmoid(gate)
    silu = gate * sigma
    gate_low = (grad * lift * (sigma * (1.0 + gate * (1.0 - sigma)))).astype(jnp.bfloat16)
    lift_low = (grad * silu).astype(jnp.bfloat16)
    acts_ref[:, 0:tile] = (silu * lift).astype(jnp.bfloat16)
    acts_ref[:, tile : 2 * tile] = gate_low
    acts_ref[:, 2 * tile : 3 * tile] = lift_low
    if side_ref:
        acts_ref[:, 3 * tile :] = side_ref[0][...]
    piece = mm_nt(gate_low, gate_w_ref[...]) + mm_nt(lift_low, lift_w_ref[...])

    @pl.when(at == 0)
    def _():
        total[...] = piece

    @pl.when(at > 0)
    def _():
        total[...] += piece

    @pl.when(at == pl.num_programs(0) - 1)
    def _():
        part_ref[...] = total[...].astype(part_ref.dtype)


def ffn_backward_call(e, both_w, down_w, gate, lift, *side):
    more = side[0].shape[1] if side else 0
    rows, feat = e.shape
    hidden = down_w.shape[0]
    tile = min(FFN_TILE, hidden)
    count = hidden // tile
    f32, bf16 = jnp.float32, jnp.bfloat16
    shape = jax.ShapeDtypeStruct
    whole = pl.BlockSpec((rows, feat), lambda i: (0, 0))
    act = pl.BlockSpec((rows, tile), lambda i: (0, i))
    return pl.pallas_call(
        ffn_backward_kernel,
        grid=(count,),
        in_specs=[
            whole,
            pl.BlockSpec((feat, tile), lambda i: (0, i)),
            pl.BlockSpec((feat, tile), lambda i: (0, count + i)),
            pl.BlockSpec((tile, feat), lambda i: (i, 0)),
            act, act,
        ]
        + [pl.BlockSpec((rows, more // count), lambda i: (0, i)) for _ in side],
        out_specs=[pl.BlockSpec((rows, 3 * tile + more // count), lambda i: (0, i)), whole],
        out_shape=[shape((rows, 3 * hidden + more), bf16), shape((rows, feat), bf16)],
        scratch_shapes=[pltpu.VMEM((rows, feat), f32)],
        compiler_params=params(),
        name="ffn_backward",
    )(e, both_w, both_w, down_w, gate, lift, *side)


def ffn_grads_tile(u_t, e_t, acts_ref, gate_ref, lift_ref, down_ref):
    tile = gate_ref.shape[1]
    down_ref[...] = mm(e_t[...], acts_ref[:, 0:tile]).T.astype(down_ref.dtype)
    gate_ref[...] = mm(u_t[...], acts_ref[:, tile : 2 * tile]).astype(gate_ref.dtype)
    lift_ref[...] = mm(u_t[...], acts_ref[:, 2 * tile : 3 * tile]).astype(lift_ref.dtype)


def ffn_grads_specs(rows, feat, hidden, wide):
    tile = min(FFN_TILE, hidden)
    count = hidden // tile
    out = pl.BlockSpec((feat, tile), lambda i: (0, i))
    return (
        (count,), pl.BlockSpec((rows, wide // count), lambda i: (0, i)),
        [out, out, pl.BlockSpec((tile, feat), lambda i: (i, 0))],
    )


def ffn_grads_kernel(u_ref, e_ref, acts_ref, gate_ref, lift_ref, down_ref, u_t, e_t):
    @pl.when(pl.program_id(0) == 0)
    def _():
        u_t[...] = u_ref[...].T
        e_t[...] = e_ref[...].T

    ffn_grads_tile(u_t, e_t, acts_ref, gate_ref, lift_ref, down_ref)


def ffn_grads_call(u, e, acts, hidden):
    rows, feat = u.shape
    grid, block, outs = ffn_grads_specs(rows, feat, hidden, acts.shape[1])
    shape = jax.ShapeDtypeStruct
    whole = pl.BlockSpec((rows, feat), lambda i: (0, 0))
    return pl.pallas_call(
        ffn_grads_kernel,
        grid=grid,
        in_specs=[whole, whole, block],
        out_specs=outs,
        out_shape=[shape((feat, hidden), jnp.float32)] * 2 + [shape((hidden, feat), jnp.float32)],
        scratch_shapes=[pltpu.VMEM((feat, rows), u.dtype)] * 2,
        compiler_params=params(),
        name="ffn_grads",
    )(u, e, acts)


def ffn_grads_beside(sources, outs, turned):
    *sources, acts_ref = sources
    for source, target in zip(sources, turned):
        target[...] = source[...].T
    rows, feat = sources[0].shape
    grid, block, specs = ffn_grads_specs(rows, feat, outs[0].shape[1], acts_ref.shape[1])

    def tiles(acts, gate, lift, down, *side):
        ffn_grads_tile(turned[0], turned[1], acts, gate, lift, down)
        for o_t, out in zip(turned[2:], side):
            out[...] = mm(o_t[...], acts[:, acts.shape[1] - out.shape[1] :])

    specs = specs + [
        pl.BlockSpec((feat, out.shape[1] // grid[0]), lambda i: (0, i)) for out in outs[3:]
    ]
    pltpu.emit_pipeline(tiles, grid=grid, in_specs=[block], out_specs=specs)(acts_ref, *outs)


def columns_grad_beside(o_ref, source_ref, out_ref, o_t, first):
    o_t[...] = o_ref[...].T
    rows, feat = o_ref.shape
    tile = min(FFN_TILE, out_ref.shape[0])

    def tiles(source, out):
        out[...] = mm(o_t[...], source[...]).T

    pltpu.emit_pipeline(
        tiles,
        grid=(out_ref.shape[0] // tile,),
        in_specs=[pl.BlockSpec((rows, tile), lambda i: (0, first // tile + i))],
        out_specs=[pl.BlockSpec((tile, feat), lambda i: (i, 0))],
    )(source_ref, out_ref)


def side_grads_kernel(turned, o_ref, side_ref, out_ref, o_t):
    @pl.when(pl.program_id(0) == 0)
    def _():
        o_t[...] = o_ref[...].T

    result = mm(o_t[...], side_ref[...])
    out_ref[...] = result.T if turned else result


def side_grads_call(o, acts, hidden, turned):
    rows, feat = o.shape
    count = hidden // min(FFN_TILE, hidden)
    side = (acts.shape[1] - 3 * hidden) // count
    step = acts.shape[1] // count // side
    out = (count * side, feat) if turned else (feat, count * side)
    return pl.pallas_call(
        functools.partial(side_grads_kernel, turned),
        grid=(count,),
        in_specs=[
            pl.BlockSpec((rows, feat), lambda i: (0, 0)),
            pl.BlockSpec((rows, side), lambda i: (0, step * i + step - 1)),
        ],
        out_specs=pl.BlockSpec((side, feat), lambda i: (i, 0)) if turned
        else pl.BlockSpec((feat, side), lambda i: (0, i)),
        out_shape=jax.ShapeDtypeStruct(out, jnp.float32),
        scratch_shapes=[pltpu.VMEM((feat, rows), o.dtype)],
        compiler_params=params(),
        name="side_grads",
    )(o, acts)


class Ring:
    def __init__(self, count):
        self.count = count
        self.chips = count // 2
        self.side = math.isqrt(self.chips)
        self.long = self.chips // 2
        self.short = self.chips - 1 - self.long
        self.me = lax.axis_index("seq")
        self.core = self.me % 2
        self.way = 1 - 2 * self.core
        self.at = self.flip(self.me // 2)
        self.partner = self.me + self.way
        self.long_next = self.device(1, self.core)
        self.short_next = self.device(-1, self.core)

    def flip(self, chip):
        row, column = chip // self.side, chip % self.side
        return row * self.side + column + (row % 2) * (self.side - 1 - 2 * column)

    def device(self, hops, core):
        place = (self.at + hops * self.way + 2 * self.chips) % self.chips
        return self.flip(place) * 2 + core


def remote(source, target, send_sem, recv_sem, axis, to):
    return pltpu.make_async_remote_copy(
        src_ref=source,
        dst_ref=target,
        send_sem=send_sem,
        recv_sem=recv_sem,
        device_id={axis: to},
        device_id_type=MESH,
    )


def greet(axis, devices):
    barrier = pltpu.get_barrier_semaphore()
    for to in devices:
        pl.semaphore_signal(barrier, inc=1, device_id={axis: to}, device_id_type=MESH)
    return len(devices)


def others_of(axis, count):
    me = lax.axis_index(axis)
    return [lax.rem(me + d, count) for d in range(1, count)]


class Gather:
    def __init__(self, ring, shard, full, by_rows, send_sem, recv_sem, own_sem):
        self.ring, self.shard, self.full, self.by_rows = ring, shard, full, by_rows
        self.send_sem, self.recv_sem = send_sem, recv_sem
        self.size = shard.shape[0 if by_rows else 1]
        self.own = pltpu.make_async_copy(shard, self.slot(ring.me), own_sem)
        self.sent = []

    def slot(self, device):
        part = pl.ds(pl.multiple_of(device * self.size, self.size), self.size)
        return self.full.at[part] if self.by_rows else self.full.at[:, part]

    def send(self, source, device, sem, to):
        copy = remote(
            source, self.slot(device), self.send_sem.at[len(self.sent)], self.recv_sem.at[sem],
            "seq", to,
        )
        copy.start()
        self.sent.append(copy)

    def wait(self, device, sem):
        slot = self.slot(device)
        remote(
            slot, slot, self.send_sem.at[0], self.recv_sem.at[sem], "seq", self.ring.partner
        ).wait_recv()

    def start(self):
        ring = self.ring
        self.send(self.shard, ring.me, 0, ring.long_next)
        if ring.short:
            self.send(self.shard, ring.me, ring.long, ring.short_next)
        self.send(self.shard, ring.me, ring.long + ring.short, ring.partner)
        self.own.start()

    def hop(self, i):
        ring = self.ring
        base = ring.long + ring.short + 1
        if i <= ring.long:
            device = ring.device(-i, ring.core)
            self.wait(device, i - 1)
            if i < ring.long:
                self.send(self.slot(device), device, i, ring.long_next)
            self.send(self.slot(device), device, base + i - 1, ring.partner)
        if i <= ring.short:
            device = ring.device(i, ring.core)
            self.wait(device, ring.long + i - 1)
            if i < ring.short:
                self.send(self.slot(device), device, ring.long + i, ring.short_next)
            self.send(self.slot(device), device, base + ring.long + i - 1, ring.partner)

    def finish(self):
        ring = self.ring
        base = ring.long + ring.short + 1
        other = 1 - ring.core
        self.wait(ring.partner, base - 1)
        for i in range(1, ring.long + 1):
            self.wait(ring.device(i, other), base + i - 1)
        for i in range(1, ring.short + 1):
            self.wait(ring.device(-i, other), base + ring.long + i - 1)
        self.own.wait()
        for copy in self.sent:
            copy.wait_send()


class Swap:
    def __init__(self, count, source, target, send_sem, recv_sem, own_sem):
        self.count, self.source, self.target = count, source, target
        self.send_sem, self.recv_sem = send_sem, recv_sem
        self.me = lax.axis_index("seq")
        self.rows = target.shape[0] // count
        self.width = target.shape[1]
        self.own = pltpu.make_async_copy(self.block(self.me), self.slot(self.me), own_sem)
        self.sent = []

    def block(self, to):
        if len(self.source.shape) == 3:
            return self.source.at[to]
        return self.source.at[:, pl.ds(pl.multiple_of(to * self.width, self.width), self.width)]

    def slot(self, device):
        return self.target.at[pl.ds(pl.multiple_of(device * self.rows, self.rows), self.rows)]

    def start(self):
        for d in range(1, self.count):
            to = lax.rem(self.me + d, self.count)
            copy = remote(
                self.block(to), self.slot(self.me), self.send_sem.at[d - 1],
                self.recv_sem.at[d - 1], "seq", to,
            )
            copy.start()
            self.sent.append(copy)
        self.own.start()

    def finish(self):
        for d in range(1, self.count):
            slot = self.slot(lax.rem(self.me + self.count - d, self.count))
            remote(
                slot, slot, self.send_sem.at[0], self.recv_sem.at[d - 1], "seq",
                lax.rem(self.me + d, self.count),
            ).wait_recv()
        self.own.wait()
        for copy in self.sent:
            copy.wait_send()


def rms_scale(x):
    return lax.rsqrt(jnp.mean(x * x, axis=-1, keepdims=True) + EPS)


def forward_local(ins, outs, total):
    x_ref, keep_ref, gain_ref = ins
    new = x_ref[...] + keep_ref[:, 0:1] * total
    outs[0][...] = new
    return new * rms_scale(new) * gain_ref[...], None


def norm_back(ins, total):
    x_ref, keep_ref, gain_ref, grad_ref = ins[:4]
    x = x_ref[...]
    scale = rms_scale(x)
    weighted = gain_ref[...] * total
    middle = jnp.mean(weighted * x, axis=-1, keepdims=True)
    row = jnp.sum(total * x * scale, axis=0, keepdims=True)
    return grad_ref[...] + scale * weighted - x * (scale * scale * scale) * middle, row


def backward_local(ins, outs, total):
    new, row = norm_back(ins, total)
    outs[0][...] = new
    outs[1][...] = row
    return ins[1][:, 0:1] * new, None


def last_backward_local(ins, outs, total):
    return norm_back(ins, total)


def sum_local(ins, outs, total):
    return total, None


class Quarter(Swap):
    def __init__(self, count, planes, source, target, send_sem, recv_sem, own_sem):
        self.count, self.source, self.target = count, source, target
        self.send_sem, self.recv_sem = send_sem, recv_sem
        self.me = lax.axis_index("seq")
        self.rows, self.width = target.shape[1:]
        self.share = pl.ds(
            pl.multiple_of(lax.axis_index("mp") * self.rows, self.rows), self.rows
        )
        self.own = pltpu.make_async_copy(self.block(self.me), self.slot(self.me), own_sem)
        self.sent = []

    def block(self, to):
        columns = pl.ds(pl.multiple_of(to * self.width, self.width), self.width)
        return self.source.at[self.share, columns]

    def slot(self, device):
        return self.target.at[device]


class PlaneSpread:
    def __init__(self, planes, source, target, send_sem, recv_sem, own_sem):
        self.planes, self.source, self.target = planes, source, target
        self.send_sem, self.recv_sem = send_sem, recv_sem
        self.me = lax.axis_index("mp")
        self.own = pltpu.make_async_copy(source, target.at[:, self.me], own_sem)
        self.sent = []

    def start(self):
        for d in range(1, self.planes):
            copy = remote(
                self.source, self.target.at[:, self.me], self.send_sem.at[d - 1],
                self.recv_sem.at[d - 1], "mp", lax.rem(self.me + d, self.planes),
            )
            copy.start()
            self.sent.append(copy)
        self.own.start()

    def finish(self):
        for d in range(1, self.planes):
            slot = self.target.at[:, lax.rem(self.me + self.planes - d, self.planes)]
            remote(
                slot, slot, self.send_sem.at[0], self.recv_sem.at[d - 1], "mp",
                lax.rem(self.me + d, self.planes),
            ).wait_recv()
        self.own.wait()
        for copy in self.sent:
            copy.wait_send()


class Spread:
    def __init__(self, count, source, target, send_sem, recv_sem, own_sem):
        self.count, self.source, self.target = count, source, target
        self.send_sem, self.recv_sem = send_sem, recv_sem
        self.me = lax.axis_index("seq")
        self.own = pltpu.make_async_copy(source, target.at[self.me], own_sem)
        self.sent = []

    def start(self):
        for d in range(1, self.count):
            copy = remote(
                self.source, self.target.at[self.me], self.send_sem.at[d - 1],
                self.recv_sem.at[d - 1], "seq", lax.rem(self.me + d, self.count),
            )
            copy.start()
            self.sent.append(copy)
        self.own.start()

    def finish(self):
        for d in range(1, self.count):
            slot = self.target.at[lax.rem(self.me + self.count - d, self.count)]
            remote(
                slot, slot, self.send_sem.at[0], self.recv_sem.at[d - 1], "seq",
                lax.rem(self.me + d, self.count),
            ).wait_recv()
        self.own.wait()
        for copy in self.sent:
            copy.wait_send()


class PlaneScatter:
    def __init__(self, planes, part, target, got, send_sem, recv_sem):
        self.planes, self.part, self.target, self.got = planes, part, target, got
        self.send_sem, self.recv_sem = send_sem, recv_sem
        self.me = lax.axis_index("mp")
        self.sent = []

    def block(self, to):
        rows = self.part.shape[0] // self.planes
        return pl.ds(pl.multiple_of(to * rows, rows), rows)

    def start(self):
        for d in range(1, self.planes):
            to = lax.rem(self.me + d, self.planes)
            copy = remote(
                self.part.at[self.block(to)], self.got.at[d - 1], self.send_sem.at[d - 1],
                self.recv_sem.at[d - 1], "mp", to,
            )
            copy.start()
            self.sent.append(copy)

    def total(self):
        total = self.part[self.block(self.me), :].astype(jnp.float32)
        for d in range(1, self.planes):
            self.sent[d - 1].wait_recv()
            total = total + self.got[d - 1].astype(jnp.float32)
        return total

    def finish(self):
        self.target[...] = self.total()
        for copy in self.sent:
            copy.wait_send()


class PlaneCollect:
    def __init__(self, planes, source, target, send_sem, recv_sem):
        self.planes, self.source, self.target = planes, source, target
        self.send_sem, self.recv_sem = send_sem, recv_sem
        self.me = lax.axis_index("mp")
        rows = source.shape[0]
        self.own = target.at[pl.ds(pl.multiple_of(self.me * rows, rows), rows)]
        self.sent = []

    def start(self):
        for d in range(1, self.planes):
            copy = remote(
                self.source, self.own, self.send_sem.at[d - 1], self.recv_sem.at[d - 1],
                "mp", lax.rem(self.me + d, self.planes),
            )
            copy.start()
            self.sent.append(copy)
        self.own[...] = self.source[...]

    def finish(self):
        for copy in self.sent:
            copy.wait_recv()
        for copy in self.sent:
            copy.wait_send()


class LineSum:
    def __init__(self, part, got, stage, mine, full, sems):
        self.part, self.got, self.stage, self.mine, self.full = part, got, stage, mine, full
        self.sems = sems
        me = lax.axis_index("mp")
        self.me = me
        half = me // 2
        self.outer = (me == 0) | (me == 3)
        self.inner = (me == 1) | (me == 2)
        self.partner = 4 * half + 1 - me
        self.far_inner, self.far_outer = 2 - half, 3 - 3 * half

    def block(self, plane):
        rows = self.mine.shape[0]
        return pl.ds(pl.multiple_of(plane * rows, rows), rows)

    def toward(self, source, slot, sem, to):
        return remote(
            source, self.got.at[slot], self.sems[0].at[sem], self.sems[1].at[slot], "mp", to
        )

    def out(self, source, plane, sem, slot, to):
        return remote(
            source, self.full.at[self.block(plane)], self.sems[2].at[sem], self.sems[3].at[slot],
            "mp", to,
        )

    def start(self):
        part, partner = self.part, self.partner

        @pl.when(self.outer)
        def _():
            self.toward(part.at[self.block(self.far_outer)], 2, 0, partner).start()
            self.toward(part.at[self.block(self.far_inner)], 3, 1, partner).start()
            self.toward(part.at[self.block(partner)], 0, 2, partner).start()

        @pl.when(self.inner)
        def _():
            self.toward(part.at[self.block(partner)], 0, 2, partner).start()

    def relay(self):
        @pl.when(self.inner)
        def _():
            for slot, to in ((2, self.far_outer), (3, self.far_inner)):
                block = self.part.at[self.block(to)]
                self.toward(block, slot, slot - 2, self.partner).wait_recv()
                joined = block[...].astype(jnp.float32) + self.got[slot].astype(jnp.float32)
                self.stage[slot - 2] = joined.astype(self.stage.dtype)
                self.toward(self.stage.at[slot - 2], 1, slot - 2, to).start()

    def total(self):
        block = self.part.at[self.block(self.me)]
        total = block[...].astype(jnp.float32)
        for slot in (0, 1):
            self.toward(block, slot, 0, self.partner).wait_recv()
            total = total + self.got[slot].astype(jnp.float32)
        return total

    def collect(self):
        @pl.when(self.inner)
        def _():
            self.out(self.mine, self.me, 1, 1, self.far_inner).start()
            self.out(self.mine, self.me, 0, 0, self.partner).start()

        @pl.when(self.outer)
        def _():
            self.out(self.mine, self.me, 1, 2, self.far_inner).start()
            self.out(self.mine, self.me, 0, 0, self.partner).start()

        self.full[self.block(self.me), :] = self.mine[...]

    def arrive(self, plane, slot):
        block = self.full.at[self.block(plane)]
        self.out(block, plane, 0, slot, self.partner).wait_recv()
        return block

    def forward(self):
        @pl.when(self.inner)
        def _():
            block = self.arrive(self.far_inner, 1)
            self.out(block, self.far_inner, 2, 1, self.partner).start()
            block = self.arrive(self.far_outer, 2)
            self.out(block, self.far_outer, 3, 2, self.partner).start()

    def finish(self):
        self.arrive(self.partner, 0)

        @pl.when(self.outer)
        def _():
            self.arrive(self.far_inner, 1)
            self.arrive(self.far_outer, 2)

        block = self.part.at[self.block(self.me)]
        for sem in range(3):
            self.toward(block, 0, sem, self.partner).wait_send()
        for sem in range(2):
            self.out(self.mine, self.me, sem, 0, self.partner).wait_send()

        @pl.when(self.inner)
        def _():
            for sem in (2, 3):
                self.out(self.mine, self.me, sem, 0, self.partner).wait_send()


class DirectSum:
    def __init__(self, planes, part, got, mine, full, sems):
        self.scatter = PlaneScatter(planes, part, None, got, sems[0], sems[1])
        self.result = PlaneCollect(planes, mine, full, sems[2], sems[3])

    def start(self):
        self.scatter.start()

    def relay(self):
        pass

    def total(self):
        return self.scatter.total()

    def collect(self):
        self.result.start()

    def forward(self):
        pass

    def finish(self):
        self.result.finish()
        for copy in self.scatter.sent:
            copy.wait_send()


class SeqSum:
    def __init__(self, count, parts, out, low, got, mine, send_sem, recv_sem):
        self.count, self.parts, self.out = count, parts, out
        self.low, self.got, self.mine = low, got, mine
        self.send_sem, self.recv_sem = send_sem, recv_sem
        self.me = lax.axis_index("seq")
        self.rows = low.shape[0] // count
        self.first, self.second = [], []

    def block(self, device):
        return pl.ds(pl.multiple_of(device * self.rows, self.rows), self.rows)

    def start(self):
        at = 0
        for part in self.parts:
            size = part.shape[0]
            self.low[at : at + size, :] = part[...].astype(self.low.dtype)
            at += size
        if at < self.low.shape[0]:
            self.low[at:, :] = jnp.zeros((self.low.shape[0] - at, self.low.shape[1]), self.low.dtype)
        for d in range(1, self.count):
            to = lax.rem(self.me + d, self.count)
            copy = remote(
                self.low.at[self.block(to)], self.got.at[d - 1],
                self.send_sem.at[d - 1], self.recv_sem.at[d - 1], "seq", to,
            )
            copy.start()
            self.first.append(copy)

    def middle(self):
        own = self.block(self.me)
        total = self.low[own, :].astype(jnp.float32)
        for d in range(1, self.count):
            self.first[d - 1].wait_recv()
            total = total + self.got[d - 1].astype(jnp.float32)
        self.mine[...] = total.astype(self.mine.dtype)
        for d in range(1, self.count):
            copy = remote(
                self.mine, self.out.at[own], self.send_sem.at[self.count + d - 1],
                self.recv_sem.at[self.count + d - 1], "seq", lax.rem(self.me + d, self.count),
            )
            copy.start()
            self.second.append(copy)
        self.out[own, :] = self.mine[...]

    def finish(self):
        for d in range(1, self.count):
            slot = self.out.at[self.block(lax.rem(self.me + self.count - d, self.count))]
            remote(
                slot, slot, self.send_sem.at[self.count], self.recv_sem.at[self.count + d - 1],
                "seq", lax.rem(self.me + d, self.count),
            ).wait_recv()
        for copy in self.first + self.second:
            copy.wait_send()


class GainSum:
    def __init__(self, planes, count, rows, out, across, along, sems):
        self.planes, self.count, self.rows, self.out = planes, count, rows, out
        self.across, self.along, self.sems = across, along, sems
        self.me, self.plane = lax.axis_index("seq"), lax.axis_index("mp")
        self.first, self.second = [], []

    def start(self, row):
        held = self.rows.shape[0]
        self.out[...] = self.rows[...]
        self.out[held - 1 : held, :] = row
        for d in range(1, self.planes):
            copy = remote(
                self.out, self.across.at[d - 1], self.sems[0].at[d - 1], self.sems[1].at[d - 1],
                "mp", lax.rem(self.plane + d, self.planes),
            )
            copy.start()
            self.first.append(copy)

    def middle(self):
        total = self.out[...]
        for d in range(1, self.planes):
            self.first[d - 1].wait_recv()
            total = total + self.across[d - 1]
        for copy in self.first:
            copy.wait_send()
        self.out[...] = total
        for d in range(1, self.count):
            copy = remote(
                self.out, self.along.at[d - 1], self.sems[2].at[d - 1], self.sems[3].at[d - 1],
                "seq", lax.rem(self.me + d, self.count),
            )
            copy.start()
            self.second.append(copy)

    def finish(self):
        total = self.out[...]
        for d in range(1, self.count):
            self.second[d - 1].wait_recv()
            total = total + self.along[d - 1]
        for copy in self.second:
            copy.wait_send()
        self.out[...] = total


class Plan:
    def __init__(self, gathers=(), swaps=(), spreads=(), sums=(), quarters=(), planes=(), collects=()):
        self.count = lax.axis_size("seq")
        self.planes = lax.axis_size("mp")
        self.upright = bool(planes or collects)
        count = self.count
        vmem = pl.BlockSpec(memory_space=pltpu.VMEM)
        hbm = pl.BlockSpec(memory_space=pl.ANY)
        shape = jax.ShapeDtypeStruct
        self.sources, self.in_specs, self.shapes, self.out_specs, self.scratch = [], [], [], [], []
        self.kinds, self.after = [], []
        sems = [
            pltpu.SemaphoreType.DMA((2 * count,)), pltpu.SemaphoreType.DMA((2 * count,)),
            pltpu.SemaphoreType.DMA,
        ]
        for array, rows in gathers:
            height, width = array.shape
            by_rows = rows or width % LANES != 0
            self.add("rows" if by_rows else "columns", [array], hbm, hbm, sems, shape(
                (count * height, width) if by_rows else (height, count * width), array.dtype
            ))
            self.after[-1] = (height, width) if by_rows and not rows else None
        for array in swaps:
            height, width = array.shape[0], array.shape[1] // count
            if width % LANES:
                array = array.reshape(height, count, width).swapaxes(0, 1)
            self.add("swap", [array], hbm, hbm, sems, shape((count * height, width), array.dtype))
        for array in spreads:
            self.add("spread", [array], vmem, vmem, sems, shape((count,) + array.shape, array.dtype))
        for parts in sums:
            have, width = sum(part.shape[0] for part in parts), parts[0].shape[1]
            rows = -(-have // (16 * count)) * 16
            bf16 = jnp.bfloat16
            self.add("sum", list(parts), vmem, vmem, sems + [
                pltpu.VMEM((rows * count, width), bf16),
                pltpu.VMEM((count - 1, rows, width), bf16),
                pltpu.VMEM((rows, width), bf16),
            ], shape((rows * count, width), bf16))

        for array in quarters:
            rows, width = array.shape
            self.add("quarter", [array], hbm, hbm, sems, shape(
                (count, rows // self.planes, width // count), array.dtype
            ))
        for array in planes:
            self.add("plane", [array], hbm, hbm, sems, shape(
                (array.shape[0], self.planes) + array.shape[1:], array.dtype
            ))
        for array in collects:
            self.add("collect", [array], vmem, vmem, sems[:2], shape(
                (self.planes * array.shape[0], array.shape[1]), array.dtype
            ))

    def add(self, kind, arrays, in_spec, out_spec, scratch, shape):
        self.kinds.append((kind, len(arrays), len(scratch)))
        self.sources += arrays
        self.in_specs += [in_spec] * len(arrays)
        self.shapes.append(shape)
        self.out_specs.append(out_spec)
        self.scratch += scratch
        self.after.append(None)

    def results(self, targets):
        return [
            t if cut is None
            else t.reshape((self.count,) + cut).swapaxes(0, 1).reshape(cut[0], self.count * cut[1])
            for t, cut in zip(targets, self.after)
        ]

    def bind(self, sources, targets, scratch):
        count = self.count
        self.ring = None
        self.items = []
        self.wide = False
        for (kind, many, held), target in zip(self.kinds, targets):
            mine, sources = sources[:many], sources[many:]
            sems, scratch = scratch[:held], scratch[held:]
            if kind in ("rows", "columns"):
                if self.ring is None:
                    self.ring = Ring(count)
                self.items.append(Gather(self.ring, mine[0], target, kind == "rows", *sems))
                continue
            if kind == "plane":
                self.items.append(PlaneSpread(self.planes, mine[0], target, *sems))
                continue
            if kind == "collect":
                self.items.append(PlaneCollect(self.planes, mine[0], target, *sems))
                continue
            self.wide = True
            if kind == "quarter":
                self.items.append(Quarter(count, self.planes, mine[0], target, *sems))
            elif kind == "swap":
                self.items.append(Swap(count, mine[0], target, *sems))
            elif kind == "spread":
                self.items.append(Spread(count, mine[0], target, *sems))
            else:
                self.items.append(SeqSum(count, mine, target, *sems[3:], *sems[:2]))

    def greet(self, wide=False):
        if self.wide or wide:
            return greet("seq", others_of("seq", self.count))
        if self.ring is not None:
            near = [self.ring.long_next, self.ring.partner]
            if self.ring.short:
                near.append(self.ring.short_next)
            return greet("seq", near)
        return 0

    def start(self):
        for item in self.items:
            item.start()

    def hops(self):
        gathers = [item for item in self.items if isinstance(item, Gather)]
        if gathers:
            for i in range(1, self.ring.long + 1):
                for item in gathers:
                    item.hop(i)
        for item in self.items:
            if isinstance(item, SeqSum):
                item.middle()

    def finish(self):
        for item in self.items:
            item.finish()


def step_kernel(planes, plan, local, n_ins, n_outs, gain_at, work, pieces, *refs):
    part_ref, refs = refs[0], refs[1:]
    ins, refs = refs[:n_ins], refs[n_ins:]
    sources, refs = refs[: len(plan.sources)], refs[len(plan.sources) :]
    work_ins, refs = refs[:work], refs[work:]
    piece_ins, refs = refs[: 2 * len(pieces)], refs[2 * len(pieces) :]
    full_ref, refs = refs[0], refs[1:]
    outs, refs = refs[:n_outs], refs[n_outs:]
    targets, refs = refs[: len(plan.shapes)], refs[len(plan.shapes) :]
    work_outs, refs = refs[:work], refs[work:]
    piece_outs, refs = refs[: len(pieces)], refs[len(pieces) :]
    got, mine, stage = refs[:3]
    sems, refs = refs[3:7], refs[7:]
    plan.bind(sources, targets, refs[: len(plan.scratch)])
    refs = refs[len(plan.scratch) :]
    turned, refs = refs[: work - 1 if work else 0], refs[work - 1 if work else 0 :]
    piece_turned, refs = refs[: len(pieces)], refs[len(pieces) :]
    gains = None
    if gain_at is not None:
        gains = GainSum(planes, plan.count, ins[gain_at], outs[0], refs[0], refs[1], refs[2:])
    greeted = greet("mp", others_of("mp", planes)) + plan.greet(gains is not None)
    pl.semaphore_wait(pltpu.get_barrier_semaphore(), greeted)
    if planes == 4:
        line = LineSum(part_ref, got, stage, mine, full_ref, sems)
    else:
        line = DirectSum(planes, part_ref, got, mine, full_ref, sems)
    line.start()
    plan.start()
    line.relay()
    if work:
        ffn_grads_beside(work_ins, work_outs, turned)
    for i, first in enumerate(pieces):
        columns_grad_beside(*piece_ins[2 * i : 2 * i + 2], piece_outs[i], piece_turned[i], first)
    value, row = local(ins, outs, line.total())
    mine[...] = value.astype(mine.dtype)
    line.collect()
    if gains is not None:
        gains.start(row)
    line.forward()
    plan.hops()
    if gains is not None:
        gains.middle()
    line.finish()
    plan.finish()
    if gains is not None:
        gains.finish()


def remote_params(cid):
    return pltpu.CompilerParams(
        collective_id=cid, has_side_effects=True, vmem_limit_bytes=VMEM
    )


def z_step(name, cid, local, part, others, extra, out_dtype=jnp.bfloat16, gain_at=None, work=(), pieces=(), **carried):
    planes = lax.axis_size("mp")
    plan = Plan(**carried)
    rows, width = part.shape
    share = rows // planes
    f32 = jnp.float32
    shape = jax.ShapeDtypeStruct
    held = 0 if gain_at is None else others[gain_at].shape[0]
    kinds = {
        "share": shape((share, width), f32),
        "gain": shape((1, width), f32),
        "gains": shape((held, width), f32),
    }
    gain_scratch = [] if gain_at is None else [
        pltpu.VMEM((planes - 1, held, width), f32),
        pltpu.VMEM((plan.count - 1, held, width), f32),
        pltpu.SemaphoreType.DMA((planes,)),
        pltpu.SemaphoreType.DMA((planes,)),
        pltpu.SemaphoreType.DMA((plan.count,)),
        pltpu.SemaphoreType.DMA((plan.count,)),
    ]
    vmem = pl.BlockSpec(memory_space=pltpu.VMEM)
    hbm = pl.BlockSpec(memory_space=pl.ANY)
    work_shapes, turned = [], []
    if work:
        u, e, *side, acts, hidden = work
        low = jnp.bfloat16
        work_shapes = [shape((u.shape[1], hidden), low)] * 2 + [shape((hidden, e.shape[1]), low)]
        for o in side:
            work_shapes.append(shape((o.shape[1], acts.shape[1] - 3 * hidden), f32))
        turned = [pltpu.VMEM((u.shape[1], u.shape[0]), u.dtype)] * (2 + len(side))
    piece_ins, piece_shapes, piece_turned = [], [], []
    for o, source, _, size in pieces:
        piece_ins += [o, source]
        piece_shapes.append(shape((size, o.shape[1]), f32))
        piece_turned.append(pltpu.VMEM((o.shape[1], o.shape[0]), o.dtype))
    result = pl.pallas_call(
        functools.partial(
            step_kernel, planes, plan, local, len(others), len(extra), gain_at, len(work_shapes),
            tuple(first for _, _, first, _ in pieces),
        ),
        out_shape=[shape((rows, width), out_dtype)] + [kinds[kind] for kind in extra]
        + plan.shapes + work_shapes + piece_shapes,
        in_specs=[vmem] * (1 + len(others)) + plan.in_specs + ([vmem] * (len(work) - 2) + [hbm] if work else [])
        + [vmem, hbm] * len(pieces),
        out_specs=[vmem] * (1 + len(extra)) + plan.out_specs + [hbm] * len(work_shapes + piece_shapes),
        scratch_shapes=[
            pltpu.VMEM((max(planes, 4), share, width), part.dtype),
            pltpu.VMEM((share, width), out_dtype),
            pltpu.VMEM((2, share, width), part.dtype),
        ]
        + [pltpu.SemaphoreType.DMA((max(planes, 4),))] * 4
        + plan.scratch + turned + piece_turned + gain_scratch,
        compiler_params=remote_params(cid),
        name=name,
    )(part, *others, *plan.sources, *work[:-1], *piece_ins)
    cut = 1 + len(extra)
    rest = cut + len(plan.shapes)
    return list(result[:cut]) + [plan.results(result[cut:rest])] + list(result[rest:])


def carry_kernel(planes, plan, scatters, *refs):
    sources, refs = refs[: len(plan.sources)], refs[len(plan.sources) :]
    parts, refs = refs[:scatters], refs[scatters:]
    targets, refs = refs[: len(plan.shapes)], refs[len(plan.shapes) :]
    sums, refs = refs[:scatters], refs[scatters:]
    plan.bind(sources, targets, refs[: len(plan.scratch)])
    refs = refs[len(plan.scratch) :]
    items = []
    for part, total in zip(parts, sums):
        items.append(PlaneScatter(planes, part, total, *refs[:3]))
        refs = refs[3:]
    greeted = plan.greet()
    if items or plan.upright:
        greeted += greet("mp", others_of("mp", planes))
    pl.semaphore_wait(pltpu.get_barrier_semaphore(), greeted)
    plan.start()
    for item in items:
        item.start()
    plan.hops()
    plan.finish()
    for item in items:
        item.finish()


def carry(name, cid, scatters=(), **carried):
    planes = lax.axis_size("mp")
    plan = Plan(**carried)
    vmem = pl.BlockSpec(memory_space=pltpu.VMEM)
    shape = jax.ShapeDtypeStruct
    sems = [pltpu.SemaphoreType.DMA((planes,))] * 2
    shapes, scratch = [], []
    for part in scatters:
        share = (part.shape[0] // planes, part.shape[1])
        shapes.append(shape(share, jnp.float32))
        scratch += [pltpu.VMEM((planes - 1,) + share, part.dtype)] + sems
    result = pl.pallas_call(
        functools.partial(carry_kernel, planes, plan, len(scatters)),
        out_shape=plan.shapes + shapes,
        in_specs=plan.in_specs + [vmem] * len(scatters),
        out_specs=plan.out_specs + [vmem] * len(shapes),
        scratch_shapes=plan.scratch + scratch,
        compiler_params=remote_params(cid),
        name=name,
    )(*plan.sources, *scatters)
    cut = len(plan.shapes)
    return plan.results(result[:cut]) + list(result[cut:])


SCALE = 1.0 / math.sqrt(HEAD_DIM)


def nt(left, right):
    return lax.dot_general(
        left, right, (((1,), (1,)), ((), ())), preferred_element_type=jnp.float32
    )


def nn(left, right):
    return jnp.dot(left, right, preferred_element_type=jnp.float32)


def attend_kernel(q_ref, k_ref, v_ref, low_ref, high_ref, pos_ref, out_ref, lse_ref):
    scores = nt(q_ref[...], k_ref[...]) * SCALE
    pos = pos_ref[...]
    scores = jnp.where((pos >= low_ref[...]) & (pos <= high_ref[...]), scores, -1e30)
    top = jnp.max(scores, axis=-1, keepdims=True)
    expo = jnp.exp(scores - top)
    mass = jnp.sum(expo, axis=-1, keepdims=True)
    probs = (expo / mass).astype(jnp.bfloat16)
    out_ref[...] = nn(probs, v_ref[...]).astype(jnp.bfloat16)
    lse_ref[0] = top + jnp.log(mass)


def query_back_kernel(q_ref, k_ref, v_ref, g_ref, low_ref, high_ref, pos_ref, lse_ref, dq_ref, mid_ref):
    keys = k_ref[...]
    scores = nt(q_ref[...], keys) * SCALE
    pos = pos_ref[...]
    scores = jnp.where((pos >= low_ref[...]) & (pos <= high_ref[...]), scores, -1e30)
    probs = jnp.exp(scores - lse_ref[0])
    prob_grad = nt(g_ref[...], v_ref[...])
    middle = jnp.sum(probs * prob_grad, axis=-1, keepdims=True)
    score_grad = (probs * (prob_grad - middle)).astype(jnp.bfloat16)
    dq_ref[...] = (nn(score_grad, keys) * SCALE).astype(jnp.bfloat16)
    mid_ref[0] = middle


def key_back_kernel(k_ref, v_ref, q_ref, g_ref, pos_ref, low_ref, high_ref, lse_ref, mid_ref, dk_ref, dv_ref):
    queries, grads = q_ref[...], g_ref[...]
    scores = nt(k_ref[...], queries) * SCALE
    pos = pos_ref[...]
    scores = jnp.where((pos >= low_ref[...]) & (pos <= high_ref[...]), scores, -1e30)
    probs = jnp.exp(scores - lse_ref[0])
    prob_grad = nt(v_ref[...], grads)
    score_grad = (probs * (prob_grad - mid_ref[0])).astype(jnp.bfloat16)
    dk_ref[...] = (nn(score_grad, queries) * SCALE).astype(jnp.bfloat16)
    dv_ref[...] = nn(probs.astype(jnp.bfloat16), grads).astype(jnp.bfloat16)


def head_block(rows, first):
    return pl.BlockSpec((rows, HEAD_DIM), lambda h: (0, first + h))


def whole_block(*shape):
    return pl.BlockSpec(shape, lambda h: (0,) * len(shape))


def attend_params():
    return pltpu.CompilerParams(vmem_limit_bytes=VMEM, dimension_semantics=("arbitrary",))


def attend_call(q, pair, low, high, pos, heads):
    rows, keys = q.shape[0], pair.shape[0]
    return pl.pallas_call(
        attend_kernel,
        grid=(heads,),
        in_specs=[
            head_block(rows, 0), head_block(keys, 0), head_block(keys, heads),
            whole_block(rows, 1), whole_block(rows, 1), whole_block(1, keys),
        ],
        out_specs=[head_block(rows, 0), pl.BlockSpec((1, rows, 1), lambda h: (h, 0, 0))],
        out_shape=[
            jax.ShapeDtypeStruct(q.shape, jnp.bfloat16),
            jax.ShapeDtypeStruct((heads, rows, 1), jnp.float32),
        ],
        compiler_params=attend_params(),
        name="attend",
    )(q, pair, pair, low, high, pos)


def query_back_call(q, pair, grad, low, high, pos, lse, heads):
    rows, keys = q.shape[0], pair.shape[0]
    stat = pl.BlockSpec((1, rows, 1), lambda h: (h, 0, 0))
    return pl.pallas_call(
        query_back_kernel,
        grid=(heads,),
        in_specs=[
            head_block(rows, 0), head_block(keys, 0), head_block(keys, heads),
            head_block(rows, 0),
            whole_block(rows, 1), whole_block(rows, 1), whole_block(1, keys), stat,
        ],
        out_specs=[head_block(rows, 0), stat],
        out_shape=[
            jax.ShapeDtypeStruct(q.shape, jnp.bfloat16),
            jax.ShapeDtypeStruct((heads, rows, 1), jnp.float32),
        ],
        compiler_params=attend_params(),
        name="query_back",
    )(q, pair, pair, grad, low, high, pos, lse)


def key_back_call(pair, queries, grads, pos, low, high, lse, mid, heads):
    rows, many = pair.shape[0], queries.shape[0]
    stat = pl.BlockSpec((1, 1, many), lambda h: (h, 0, 0))
    shape = jax.ShapeDtypeStruct((rows, heads * HEAD_DIM), jnp.bfloat16)
    return pl.pallas_call(
        key_back_kernel,
        grid=(heads,),
        in_specs=[
            head_block(rows, 0), head_block(rows, heads), head_block(many, 0), head_block(many, 0),
            whole_block(rows, 1), whole_block(1, many), whole_block(1, many), stat, stat,
        ],
        out_specs=[head_block(rows, 0)] * 2,
        out_shape=[shape, shape],
        compiler_params=attend_params(),
        name="key_back",
    )(pair, pair, queries, grads, pos, low, high, lse, mid)


class Across:
    def __init__(self, count, send_sem, recv_sem, own_sem):
        self.chips = count // 2
        me = lax.axis_index("seq")
        self.me, self.chip, self.core = me, me // 2, me % 2
        self.partner = me + 1 - 2 * self.core
        self.send_sem, self.recv_sem, self.own_sem = send_sem, recv_sem, own_sem
        self.sent, self.kept = [], []

    def chip_at(self, hops):
        return lax.rem(self.chip + hops + self.chips, self.chips)

    def greet(self, with_partner):
        near = [self.chip_at(d) * 2 + self.core for d in range(1, self.chips)]
        return greet("seq", near + ([self.partner] if with_partner else []))

    def send(self, source, target, sem, to):
        copy = remote(
            source, target, self.send_sem.at[len(self.sent)], self.recv_sem.at[sem], "seq", to
        )
        copy.start()
        self.sent.append(copy)

    def keep(self, source, target):
        copy = pltpu.make_async_copy(source, target, self.own_sem.at[len(self.kept)])
        copy.start()
        self.kept.append(copy)

    def wait(self, target, sem):
        remote(
            target, target, self.send_sem.at[0], self.recv_sem.at[sem], "seq", self.partner
        ).wait_recv()

    def finish(self):
        for copy in self.kept:
            copy.wait()
        for copy in self.sent:
            copy.wait_send()


def cut(at, size):
    return pl.ds(pl.multiple_of(at * size, size), size)


def heads_in_kernel(count, planes, qkv_ref, side_ref, q_ref, kv_ref, side_out, *sems):
    ways = Across(count, *sems[:3])
    greeted = ways.greet(True) + greet("mp", others_of("mp", planes))
    pl.semaphore_wait(pltpu.get_barrier_semaphore(), greeted)
    side = PlaneSpread(planes, side_ref, side_out, *sems[3:])
    side.start()
    rows, chips = qkv_ref.shape[0], ways.chips

    def places(chip):
        owner = 2 * chip + ways.core
        return (
            q_ref.at[cut(chip, rows)],
            kv_ref.at[cut(owner, rows), 0:HEAD_DIM],
            kv_ref.at[cut(owner, rows), HEAD_DIM : 2 * HEAD_DIM],
        )

    for d in list(range(1, chips)) + [0]:
        head = ways.chip_at(d)
        for kind, target in enumerate(places(ways.chip)):
            source = qkv_ref.at[:, cut(kind * chips + head, HEAD_DIM)]
            if d:
                ways.send(source, target, 3 * d + kind, 2 * head + ways.core)
            else:
                ways.keep(source, target)
    for copy in ways.kept:
        copy.wait()
    ways.kept = []
    for d in range(chips):
        chip = ways.chip_at(-d)
        if d:
            for kind, target in enumerate(places(chip)):
                ways.wait(target, 3 * d + kind)
        both = kv_ref.at[cut(2 * chip + ways.core, rows)]
        ways.send(both, both, 3 * chips + d, ways.partner)
    for d in range(chips):
        chip = ways.chip_at(-d)
        ways.wait(kv_ref.at[cut(2 * chip + 1 - ways.core, rows)], 3 * chips + d)
    ways.finish()
    side.finish()


def blocks_to_columns_kernel(count, source_ref, target_ref, *sems):
    ways = Across(count, *sems)
    pl.semaphore_wait(pltpu.get_barrier_semaphore(), ways.greet(False))
    rows = target_ref.shape[0]
    mine = target_ref.at[:, cut(ways.chip, HEAD_DIM)]
    for d in range(1, ways.chips):
        chip = ways.chip_at(d)
        ways.send(source_ref.at[cut(chip, rows)], mine, d, 2 * chip + ways.core)
    ways.keep(source_ref.at[cut(ways.chip, rows)], mine)
    for d in range(1, ways.chips):
        ways.wait(target_ref.at[:, cut(ways.chip_at(-d), HEAD_DIM)], d)
    ways.finish()


def columns_to_blocks_kernel(count, source_ref, target_ref, *sems):
    ways = Across(count, *sems)
    pl.semaphore_wait(pltpu.get_barrier_semaphore(), ways.greet(False))
    rows = source_ref.shape[0]
    mine = target_ref.at[cut(ways.chip, rows)]
    for d in range(1, ways.chips):
        chip = ways.chip_at(d)
        ways.send(source_ref.at[:, cut(chip, HEAD_DIM)], mine, d, 2 * chip + ways.core)
    ways.keep(source_ref.at[:, cut(ways.chip, HEAD_DIM)], mine)
    for d in range(1, ways.chips):
        ways.wait(target_ref.at[cut(ways.chip_at(-d), rows)], d)
    ways.finish()


def heads_grads_kernel(
    count, dq_ref, dk_ref, dv_ref, out_ref, got_k, got_v, low_k, low_v, send_sem, recv_sem, own_sem
):
    ways = Across(count, send_sem, recv_sem, own_sem)
    pl.semaphore_wait(pltpu.get_barrier_semaphore(), ways.greet(True))
    rows, chips = out_ref.shape[0], ways.chips
    pairs = ((dk_ref, got_k, low_k), (dv_ref, got_v, low_v))
    for i in range(chips):
        for kind, (ref, got, _) in enumerate(pairs):
            block = ref.at[cut(2 * i + 1 - ways.core, rows)]
            ways.send(block, got.at[i], 3 * chips + 2 * i + kind, ways.partner)

    def place(kind, chip):
        return out_ref.at[:, cut(kind * chips + chip, HEAD_DIM)]

    for d in range(1, chips):
        chip = ways.chip_at(d)
        ways.send(
            dq_ref.at[cut(chip, rows)], place(0, ways.chip), 3 * d, 2 * chip + ways.core
        )
    ways.keep(dq_ref.at[cut(ways.chip, rows)], place(0, ways.chip))
    for i in range(chips):
        for kind, (ref, got, low) in enumerate(pairs):
            ways.wait(got.at[i], 3 * chips + 2 * i + kind)
            total = ref[cut(2 * i + ways.core, rows), :] + got[i]
            low[i] = (total * (1.0, SCALE)[kind == 0]).astype(low.dtype)
    for d in range(1, chips):
        chip = ways.chip_at(d)
        for kind, (_, _, low) in enumerate(pairs):
            ways.send(
                low.at[chip], place(1 + kind, ways.chip), 3 * d + 1 + kind, 2 * chip + ways.core
            )
    for kind, (_, _, low) in enumerate(pairs):
        ways.keep(low.at[ways.chip], place(1 + kind, ways.chip))
    for d in range(1, chips):
        for kind in range(3):
            ways.wait(place(kind, ways.chip_at(-d)), 3 * d + kind)
    ways.finish()


def across_sems(sends, receives, keeps):
    return [
        pltpu.SemaphoreType.DMA((sends,)), pltpu.SemaphoreType.DMA((receives,)),
        pltpu.SemaphoreType.DMA((keeps,)),
    ]


def across_call(kernel, name, cid, sources, shapes, sems):
    hbm = pl.BlockSpec(memory_space=pl.ANY)
    return pl.pallas_call(
        functools.partial(kernel, lax.axis_size("seq")),
        out_shape=shapes,
        in_specs=[hbm] * len(sources),
        out_specs=[hbm] * len(shapes),
        scratch_shapes=across_sems(*sems),
        compiler_params=remote_params(cid),
        name=name,
    )(*sources)


def heads_in(cid, qkv, side):
    count, planes, rows = lax.axis_size("seq"), lax.axis_size("mp"), qkv.shape[0]
    chips = count // 2
    shape = jax.ShapeDtypeStruct
    hbm = pl.BlockSpec(memory_space=pl.ANY)
    return pl.pallas_call(
        functools.partial(heads_in_kernel, count, planes),
        out_shape=[
            shape((chips * rows, HEAD_DIM), qkv.dtype),
            shape((count * rows, 2 * HEAD_DIM), qkv.dtype),
            shape((count, planes) + side.shape[1:], side.dtype),
        ],
        in_specs=[hbm] * 2,
        out_specs=[hbm] * 3,
        scratch_shapes=across_sems(4 * chips, 4 * chips, 3)
        + [pltpu.SemaphoreType.DMA((planes,))] * 2 + [pltpu.SemaphoreType.DMA],
        compiler_params=remote_params(cid),
        name="heads_in",
    )(qkv, side)


def blocks_to_columns(name, cid, blocks):
    chips = lax.axis_size("seq") // 2
    shape = (blocks.shape[0] // chips, chips * HEAD_DIM)
    return across_call(
        blocks_to_columns_kernel, name, cid, [blocks],
        [jax.ShapeDtypeStruct(shape, blocks.dtype)], (chips, chips, 1),
    )[0]


def columns_to_blocks(name, cid, columns):
    chips = lax.axis_size("seq") // 2
    shape = (columns.shape[0] * chips, HEAD_DIM)
    return across_call(
        columns_to_blocks_kernel, name, cid, [columns],
        [jax.ShapeDtypeStruct(shape, columns.dtype)], (chips, chips, 1),
    )[0]


def heads_grads(cid, dq, dk, dv):
    count = lax.axis_size("seq")
    chips = count // 2
    rows = dq.shape[0] // chips
    f32, bf16 = jnp.float32, jnp.bfloat16
    vmem = pl.BlockSpec(memory_space=pltpu.VMEM)
    return pl.pallas_call(
        functools.partial(heads_grads_kernel, count),
        out_shape=jax.ShapeDtypeStruct((rows, 3 * chips * HEAD_DIM), bf16),
        in_specs=[vmem] * 3,
        out_specs=pl.BlockSpec(memory_space=pl.ANY),
        scratch_shapes=[pltpu.VMEM((chips, rows, HEAD_DIM), f32)] * 2
        + [pltpu.VMEM((chips, rows, HEAD_DIM), bf16)] * 2
        + across_sems(2 * chips + 3 * (chips - 1), 5 * chips, 3),
        compiler_params=remote_params(cid),
        name="heads_grads",
    )(dq, dk, dv)


def tn(left, right):
    return lax.dot_general(
        left, right, (((0,), (0,)), ((), ())), preferred_element_type=jnp.float32
    )


def head_kernel(q_ref, k_ref, v_ref, low_ref, high_ref, pos_ref, out_ref, lse_ref):
    scores = nt(q_ref[...], k_ref[...]) * SCALE
    pos = pos_ref[...]
    scores = jnp.where((pos >= low_ref[...]) & (pos <= high_ref[...]), scores, -1e30)
    top = jnp.max(scores, axis=-1, keepdims=True)
    expo = jnp.exp(scores - top)
    mass = jnp.sum(expo, axis=-1, keepdims=True)
    probs = (expo / mass).astype(jnp.bfloat16)
    out_ref[...] = nn(probs, v_ref[...]).astype(jnp.bfloat16)
    lse_ref[...] = top + jnp.log(mass)


def head_back_kernel(q_ref, k_ref, v_ref, g_ref, low_ref, high_ref, pos_ref, lse_ref, dq_ref, dk_ref, dv_ref):
    queries, keys, grads = q_ref[...], k_ref[...], g_ref[...]
    scores = nt(queries, keys) * SCALE
    pos = pos_ref[...]
    scores = jnp.where((pos >= low_ref[...]) & (pos <= high_ref[...]), scores, -1e30)
    probs = jnp.exp(scores - lse_ref[...])
    prob_grad = nt(grads, v_ref[...])
    middle = jnp.sum(probs * prob_grad, axis=-1, keepdims=True)
    score_grad = (probs * (prob_grad - middle)).astype(jnp.bfloat16)
    dq_ref[...] = (nn(score_grad, keys) * SCALE).astype(jnp.bfloat16)
    dk = tn(score_grad, queries)
    dv = tn(probs.astype(jnp.bfloat16), grads)

    @pl.when(pl.program_id(0) == 0)
    def _():
        dk_ref[...] = dk
        dv_ref[...] = dv

    @pl.when(pl.program_id(0) > 0)
    def _():
        dk_ref[...] += dk
        dv_ref[...] += dv


def head_specs(rows, keys):
    block = pl.BlockSpec((rows, HEAD_DIM), lambda i: (i, 0))
    stat = pl.BlockSpec((rows, 1), lambda i: (i, 0))
    half = [pl.BlockSpec((keys, HEAD_DIM), lambda i, k=k: (0, k)) for k in range(2)]
    whole = pl.BlockSpec((keys, HEAD_DIM), lambda i: (0, 0))
    return block, stat, half, pl.BlockSpec((1, keys), lambda i: (0, 0)), whole


def head_call(q, kv, low, high, pos, rows):
    block, stat, half, line, _ = head_specs(rows, kv.shape[0])
    return pl.pallas_call(
        head_kernel,
        grid=(q.shape[0] // rows,),
        in_specs=[block, *half, stat, stat, line],
        out_specs=[block, stat],
        out_shape=[
            jax.ShapeDtypeStruct(q.shape, jnp.bfloat16),
            jax.ShapeDtypeStruct((q.shape[0], 1), jnp.float32),
        ],
        compiler_params=attend_params(),
        name="head",
    )(q, kv, kv, low, high, pos)


def head_back_call(q, kv, grad, low, high, pos, lse, rows):
    block, stat, half, line, whole = head_specs(rows, kv.shape[0])
    keys = jax.ShapeDtypeStruct((kv.shape[0], HEAD_DIM), jnp.float32)
    return pl.pallas_call(
        head_back_kernel,
        grid=(q.shape[0] // rows,),
        in_specs=[block, *half, block, stat, stat, line, stat],
        out_specs=[block, whole, whole],
        out_shape=[jax.ShapeDtypeStruct(q.shape, jnp.bfloat16), keys, keys],
        compiler_params=attend_params(),
        name="head_back",
    )(q, kv, kv, grad, low, high, pos, lse)


def shifted(value, axis, steps):
    count = lax.axis_size(axis)
    leading, last = (max(0, -steps), min(count, count - steps))
    return lax.ppermute(value, axis, [(source, source + steps) for source in range(leading, last)])


def matmul(left, right):
    return jnp.dot(left, right, preferred_element_type=jnp.float32)


def matmul_tn(left, right):
    return lax.dot_general(
        left, right, (((0,), (0,)), ((), ())), preferred_element_type=jnp.float32
    )


def matmul_nt(left, right):
    return lax.dot_general(
        left, right, (((1,), (1,)), ((), ())), preferred_element_type=jnp.float32
    )


def layout(lengths, positions, slot, total):
    starts = jnp.array([0, slot, 2 * slot, total - 2 * slot, total - slot], jnp.int32)
    seg = jnp.sum((positions[:, None] >= starts[None, :]).astype(jnp.int32), axis=1) - 1
    which = (seg[:, None] == jnp.arange(5, dtype=jnp.int32)[None, :]).astype(jnp.int32)
    start_of = jnp.sum(which * starts[None, :], axis=1)
    length_of = jnp.sum(which * lengths[None, :], axis=1)
    keep = (positions - start_of < length_of).astype(jnp.float32)
    first = (positions == start_of).astype(jnp.float32)
    return (start_of, keep, first)


def silu_slope(value):
    sigma = jax.nn.sigmoid(value)
    return sigma * (1.0 + value * (1.0 - sigma))


def gather_rows(array):
    return lax.all_gather(array, "seq", axis=0, tiled=True)


def gather_columns(array):
    return lax.all_gather(array, "seq", axis=1, tiled=True)


def after(value, *earlier):
    return lax.optimization_barrier((value,) + earlier)[0]


def by_chunk(value):
    rows = value.shape[0]
    return value.reshape((CHUNKS, rows // CHUNKS) + value.shape[1:]).swapaxes(0, 1)


def by_token(value):
    steps = value.shape[0]
    return value.swapaxes(0, 1).reshape((CHUNKS * steps,) + value.shape[2:])


def widened(gates, steps):
    gates = gates.reshape(STATE, steps, CHUNKS).swapaxes(0, 1)
    return jnp.broadcast_to(gates[..., None], (steps, STATE, CHUNKS, LANES))


def body(
    tokens,
    lengths,
    out_grad,
    mixer_gain,
    mixer_value,
    mixer_gate,
    conv_weight,
    conv_bias,
    select_proj,
    step_proj,
    step_bias,
    decay_log,
    skip_gain,
    mixer_out,
    first_gain,
    first_gate,
    first_lift,
    first_down,
    attend_gain,
    query_proj,
    key_proj,
    value_proj,
    attend_out,
    second_gain,
    second_gate,
    second_lift,
    second_down,
):
    f32, bf16 = jnp.float32, jnp.bfloat16
    length = tokens.shape[0]
    shards, planes = lax.axis_size("seq"), lax.axis_size("mp")
    me, plane = lax.axis_index("seq"), lax.axis_index("mp")
    total = length * shards
    slot = length // 4
    steps = length // CHUNKS
    share = length // planes
    positions = me * length + jnp.arange(length, dtype=jnp.int32)
    start_of, keep, first = layout(lengths, positions, slot, total)

    def mine(rows):
        return lax.dynamic_slice_in_dim(rows, plane * share, share)

    keep = keep[:, None]
    keep_share = jnp.broadcast_to(mine(keep), (share, LANES))
    x0 = tokens.astype(f32)
    x0_share = mine(x0)

    few = total <= tokens.shape[1]

    def collect(rows):
        return gather_rows(rows) if few else rows

    def hosted(*items):
        return list(items) if few else []

    def by_rows(result):
        if few:
            return result
        return lax.psum_scatter(
            result.astype(bf16), "seq", scatter_dimension=0, tiled=True
        ).astype(f32)

    def by_columns(result):
        if few:
            return result
        return lax.psum_scatter(
            result.astype(bf16), "seq", scatter_dimension=1, tiled=True
        ).astype(f32)

    def ffn_grads(u, e, acts):
        gate, lift, down = ffn_grads_call(u, e, acts, hidden)
        return by_rows(gate), by_rows(lift), by_columns(down)

    (value_w,) = carry("value_weights", 1, gathers=[(mixer_value, True)])
    gate_w = gather_rows(mixer_gate)
    hidden, head_width = first_gate.shape[1], query_proj.shape[1]
    first_both = gather_rows(
        after(
            jnp.concatenate([first_gate, first_lift], axis=1),
            value_w,
        )
    )

    u1 = by_chunk((x0 * rms_scale(x0) * mixer_gain).astype(bf16)).reshape(length, -1)
    inner = matmul(u1, value_w).reshape(steps, CHUNKS, -1)
    width = inner.shape[-1]
    zg = matmul(u1, gate_w)
    joined = 1.0 - first.reshape(CHUNKS, steps)[:, 0]
    prior = shifted(inner[steps - (CONV - 1) :, CHUNKS - 1], "seq", 1)
    halo = jnp.concatenate([prior[:, None], inner[steps - (CONV - 1) :, : CHUNKS - 1]], axis=1)
    padded = jnp.concatenate([halo * joined[None, :, None], inner], axis=0)
    conv = conv_bias[None, None, :]
    for tap in range(CONV):
        conv = conv + conv_weight[tap][None, None, :] * padded[tap : tap + steps]
    signal = jax.nn.silu(conv).astype(bf16)
    flat_signal = signal.reshape(length, width)
    select, (out_w,) = z_step(
        "select_sum", 2, sum_local, matmul_nt(select_proj, flat_signal), (), (), f32,
        gathers=[(mixer_out, False)],
    )
    step_low = select[:DT_RANK].astype(bf16)
    qkv_w = gather_rows(
        after(jnp.concatenate([query_proj, key_proj, value_proj], axis=1), select)
    )
    raised = (matmul_tn(step_low, step_proj) + step_bias[None, :]).reshape(steps, CHUNKS, width)
    dt = jax.nn.softplus(raised)
    signal_wide = signal.astype(f32)
    dx = dt * signal_wide
    rates = -jnp.exp(decay_log)
    rates2 = rates * LOG2E
    keep_chunk = jnp.broadcast_to(joined[:, None], (CHUNKS, LANES))
    ins = widened(select[DT_RANK : DT_RANK + STATE], steps)
    outs = widened(select[DT_RANK + STATE :], steps)
    order = jnp.arange(shards, dtype=jnp.int32)
    thr, off, summary = run_summary(dt, dx, ins, rates2, keep_chunk, False)
    (everyone,) = carry("state_spread", 3, spreads=[summary])
    states, enter = run_states(
        dt, dx, ins, outs, rates2, thr, off, everyone, (order < me).astype(jnp.int32)
    )
    ys = states + skip_gain[None, None, :] * signal_wide
    zg = zg.reshape(steps, CHUNKS, width)
    mix = by_token((ys * jax.nn.silu(zg)).astype(bf16))
    u2, x1_share, (first_w,) = z_step(
        "mixer_join", 4, forward_local, matmul(mix, out_w).astype(bf16),
        (x0_share, keep_share, first_gain[None]), ("share",), gathers=[(first_down, False)],
    )

    second_both = gather_rows(after(jnp.concatenate([second_gate, second_lift], axis=1), u2))

    gate1, lift1, part2 = ffn_forward_call(u2, first_both, first_w)
    heads = query_proj.shape[1] // HEAD_DIM
    by_head = few and shards == 2 * heads
    u3, x2_share, (attend_w, *u2_part) = z_step(
        "first_join", 5, forward_local, part2,
        (x1_share, keep_share, attend_gain[None]), ("share",),
        gathers=[(attend_out, False)], quarters=[u2] if by_head else [],
    )

    qkv = matmul(u3, qkv_w).astype(bf16)
    if by_head:
        head_q, head_kv, u2_all = heads_in(6, qkv, u2_part[0])
        u2_all = [u2_all.reshape(total, -1)]
        spot = jnp.arange(heads * length, dtype=jnp.int32)
        spot = (2 * (spot // length) + me % 2) * length + spot % length
        spot_start, _, _ = layout(lengths, spot, slot, total)
        low = jnp.maximum(spot_start, spot - (WINDOW - 1))[:, None]
        high = spot[:, None]
        key_pos = jnp.arange(total, dtype=jnp.int32)[None, :]
        head_att, lse = head_call(head_q, head_kv, low, high, key_pos, length)
        att = blocks_to_columns("heads_out", 12, head_att)
    else:
        query, pair = qkv[:, :head_width], qkv[:, head_width:]
        (pairs,) = carry("keys_values", 6, gathers=[(pair, True)])
        span = min(shards, WINDOW // length + 1) * length
        key_from = jnp.clip(positions[0] + length - span, 0, total - span)
        near_pairs = lax.dynamic_slice_in_dim(pairs, key_from, span)
        key_pos = (key_from + jnp.arange(span, dtype=jnp.int32))[None, :]
        low = jnp.maximum(start_of, positions - (WINDOW - 1))[:, None]
        high = positions[:, None]
        att, lse = attend_call(query, near_pairs, low, high, key_pos, heads)
    u4, x3_share, (second_w, *queries) = z_step(
        "attend_join", 7, forward_local, matmul(att, attend_w).astype(bf16),
        (x2_share, keep_share, second_gain[None]), ("share",),
        gathers=[(second_down, False)] + ([] if by_head else [(query, True)]),
        swaps=hosted(u1),
    )
    queries, u1_all = (queries[:-1], queries[-1:]) if few else (queries, [])
    early_all = collect(after(jnp.concatenate([mix, att], axis=1), u4))

    gate2, lift2, part4 = ffn_forward_call(u4, second_both, second_w)
    wide_grad = out_grad.astype(f32)
    e4 = (keep * wide_grad).astype(bf16)
    acts2, du4 = ffn_backward_call(e4, second_both, second_w, gate2, lift2)
    e3, g3_share, second_gain_part, ue4_all = z_step(
        "second_back", 8, backward_local, du4,
        (x3_share, keep_share, second_gain[None], mine(wide_grad)), ("share", "gain"),
        swaps=hosted(u4, e4),
    )
    acts2_all = collect(acts2)

    datt = matmul_nt(e3, attend_w).astype(bf16)
    if by_head:
        head_grad = columns_to_blocks("heads_grad_in", 9, datt)
        dq, dk, dv = head_back_call(head_q, head_kv, head_grad, low, high, key_pos, lse, length)
        dqkv = heads_grads(16, dq, dk, dv)
    else:
        dq, middle = query_back_call(query, near_pairs, datt, low, high, key_pos, lse, heads)
        stats = jnp.concatenate([lse, middle], axis=0).reshape(2 * heads, length)
        datts, all_stats = carry("query_grads", 9, gathers=[(datt, True), (stats, True)])
        all_stats = all_stats.reshape(shards, 2 * heads, length).swapaxes(0, 1).reshape(2 * heads, total)
        query_from = jnp.clip(positions[0], 0, total - span)
        every_pos = query_from + jnp.arange(span, dtype=jnp.int32)
        every_start, _, _ = layout(lengths, every_pos, slot, total)
        every_low = jnp.maximum(every_start, every_pos - (WINDOW - 1))[None, :]
        near_stats = lax.dynamic_slice_in_dim(all_stats, query_from, span, axis=1)[:, None]
        dk, dv = key_back_call(
            pair,
            lax.dynamic_slice_in_dim(queries[0], query_from, span),
            lax.dynamic_slice_in_dim(datts, query_from, span),
            high, every_low, every_pos[None, :], near_stats[:heads], near_stats[heads:], heads,
        )
        dqkv = jnp.concatenate([dq, dk, dv], axis=1)
    du3 = matmul_nt(dqkv, qkv_w)
    e2, g2_share, attend_gain_part, u3_all = z_step(
        "attend_back", 10, backward_local, after(du3.astype(bf16), early_all),
        (x2_share, keep_share, attend_gain[None], g3_share), ("share", "gain"),
        swaps=hosted(u3),
    )

    acts1, du2 = ffn_backward_call(e2, first_both, first_w, gate1, lift1, dqkv)
    e1, g1_share, first_gain_part, e2_all, *second_grads = z_step(
        "first_back", 11, backward_local, after(du2, acts2_all),
        (x1_share, keep_share, first_gain[None], g2_share), ("share", "gain"), swaps=hosted(e2) if by_head else hosted(u2, e2), work=(*ue4_all, acts2_all, hidden) if few else (),
    )
    acts1_all = collect(acts1)

    if few and not by_head:
        *u2_all, last = e2_all
        e2_all = [last]

    dmix = matmul_nt(by_chunk(e1).reshape(length, -1), out_w).reshape(steps, CHUNKS, width)
    dys = dmix * jax.nn.silu(zg)
    dzg = (dmix * ys * silu_slope(zg)).astype(bf16).reshape(length, width)
    skip_grad = jnp.sum(dys * signal_wide, axis=(0, 1))
    thr, off, summary = run_summary(dt, dys, outs, rates2, keep_chunk, True)
    everyone, *e1_part, sum4 = carry(
        "grad_spread", 13, spreads=[summary], quarters=[e1] if by_head else [], scatters=[part4],
    )
    ddt, prod, gate_grads, log_wide = run_grads(
        dt, dx, dys, ins, outs, rates2, rates, enter, thr, off, everyone,
        (order > me).astype(jnp.int32),
    )
    dpre = (ddt + prod * signal_wide) * jax.nn.sigmoid(raised)
    step_bias_grad = jnp.sum(dpre, axis=(0, 1))
    dpr = dpre.astype(bf16).reshape(length, width)
    step_grad = matmul(step_low, dpr)
    dsel, e31_all = z_step(
        "select_back", 14, sum_local,
        jnp.concatenate([matmul_nt(step_proj, dpr), gate_grads]),
        (), (), f32, swaps=hosted(e3) if by_head else hosted(e3, e1), planes=e1_part,
    )
    dsel = dsel.astype(bf16)
    select_grad = matmul(dsel, flat_signal)
    more = matmul_tn(dsel, select_proj).reshape(steps, CHUNKS, width)
    dconv, conv_sums = conv_back(prod, dys, dt, more, conv, padded, skip_gain)
    head = dconv[: CONV - 1] * joined[None, :, None]
    later = shifted(head[:, 0], "seq", -1)
    tail = jnp.concatenate([head[:, 1:], later[:, None]], axis=1)
    extended = jnp.concatenate([dconv, tail], axis=0)
    dxin = 0.0
    for tap in range(CONV):
        lag = CONV - 1 - tap
        dxin = dxin + conv_weight[tap][None, None, :] * extended[lag : lag + steps]
    dxin = dxin.astype(bf16).reshape(length, width)
    du1 = by_token(
        (matmul_nt(dxin, value_w) + matmul_nt(dzg, gate_w)).astype(bf16).reshape(steps, CHUNKS, -1)
    )
    few_rows = jnp.concatenate(
        [
            conv_sums[: CONV + 1],
            step_bias_grad[None],
            jnp.sum(log_wide, axis=1) * rates,
            skip_grad[None],
            jnp.zeros((9, width), f32),
        ]
    )
    pieces = []
    if few:
        e3_all, e1_all = e31_all
        e1_all = e1_all.reshape(total, -1)
        pieces = [
            (e1_all, early_all, 0, width), (e3_all, early_all, width, early_all.shape[1] - width)
        ]
    tokens_grad, gain_sums, (*dxz_all, small, mixed), *first_grads = z_step(
        "mixer_back", 15, last_backward_local, after(du1, acts1_all),
        (
            x0_share, keep_share, mixer_gain[None], g1_share,
            jnp.concatenate(
                [first_gain_part, attend_gain_part, second_gain_part, jnp.zeros_like(first_gain_part)]
            ),
        ),
        ("gains",), gain_at=4,
        gathers=hosted((dxin, True), (dzg, True)), sums=[(select_grad, step_grad, few_rows)],
        collects=[(x3_share + keep_share[:, 0:1] * sum4).astype(bf16)],
        work=(*u2_all, *e2_all, *u3_all, acts1_all, hidden) if few else (), pieces=pieces,
    )

    if few:
        (u1_all,), (dxin_all, dzg_all) = u1_all, dxz_all
        *first_grads, qkv_grad, mixer_out_grad, attend_out_grad = first_grads
    else:
        u1_all, dxin_all, dzg_all = u1, dxin, dzg
        qkv_grad = by_rows(side_grads_call(u3, acts1_all, hidden, False))
        mixer_out_grad = by_columns(matmul_tn(early_all[:, :width], e1))
        attend_out_grad = by_columns(matmul_tn(early_all[:, width:], e3))
    cuts = []
    at = 0
    for size in (2 * STATE + DT_RANK, DT_RANK, CONV, 1, 1, STATE, 1):
        cuts.append(small[at : at + size].astype(f32))
        at += size
    select_sum, step_sum, conv_w_sum, conv_b_sum, step_b_sum, decay_sum, skip_sum = cuts
    return (
        mixed,
        tokens_grad.astype(f32),
        gain_sums[3],
        by_rows(matmul_tn(u1_all, dxin_all)),
        by_rows(matmul_tn(u1_all, dzg_all)),
        conv_w_sum,
        conv_b_sum[0],
        select_sum,
        step_sum,
        step_b_sum[0],
        decay_sum,
        skip_sum[0],
        mixer_out_grad,
        gain_sums[0],
        *([grad.astype(f32) for grad in first_grads] or ffn_grads(u2, e2, acts1)),
        gain_sums[1],
        qkv_grad[:, :head_width],
        qkv_grad[:, head_width : 2 * head_width],
        qkv_grad[:, 2 * head_width :],
        attend_out_grad,
        gain_sums[2],
        *([grad.astype(f32) for grad in second_grads] or ffn_grads(u4, e4, acts2)),
    )


def solution(mesh):
    return jax.shard_map(
        body,
        mesh=mesh,
        in_specs=(
            P("seq", None),
            P(),
            P("seq", None),
            P(),
            P("seq", "mp"),
            P("seq", "mp"),
            P(None, "mp"),
            P("mp"),
            P(None, "mp"),
            P(None, "mp"),
            P("mp"),
            P(None, "mp"),
            P("mp"),
            P("mp", "seq"),
            P(),
            P("seq", "mp"),
            P("seq", "mp"),
            P("mp", "seq"),
            P(),
            P("seq", "mp"),
            P("seq", "mp"),
            P("seq", "mp"),
            P("mp", "seq"),
            P(),
            P("seq", "mp"),
            P("seq", "mp"),
            P("mp", "seq"),
        ),
        out_specs=(
            P("seq", None),
            P("seq", None),
            P(),
            P("seq", "mp"),
            P("seq", "mp"),
            P(None, "mp"),
            P("mp"),
            P(None, "mp"),
            P(None, "mp"),
            P("mp"),
            P(None, "mp"),
            P("mp"),
            P("mp", "seq"),
            P(),
            P("seq", "mp"),
            P("seq", "mp"),
            P("mp", "seq"),
            P(),
            P("seq", "mp"),
            P("seq", "mp"),
            P("seq", "mp"),
            P("mp", "seq"),
            P(),
            P("seq", "mp"),
            P("seq", "mp"),
            P("mp", "seq"),
        ),
        check_vma=False,
    )
```

```python
import functools
import math

import jax
import jax.numpy as jnp
from jax import lax
from jax.experimental import pallas as pl
from jax.experimental.pallas import tpu as pltpu
from jax.sharding import PartitionSpec as P

STATE = 16
CONV = 4
DT_RANK = 128
HEAD_DIM = 128
WINDOW = 2048
EPS = 1e-05
CHUNKS = 8
LANES = 128
LOG2E = 1.4426950408889634

VMEM = 48 * 1024 * 1024
MESH = pl.DeviceIdType.MESH


def chunk_scan(p, q, reverse):
    rows = p.shape[0]
    at = lax.broadcasted_iota(jnp.int32, p.shape, 0)
    d = 1
    while d < rows:
        move = (rows - d) if reverse else d
        ok = (at < rows - d) if reverse else (at >= d)
        ps = jnp.where(ok, pltpu.roll(p, move, 0), 1.0)
        qs = jnp.where(ok, pltpu.roll(q, move, 0), 0.0)
        q = p * qs + q
        p = p * ps
        d *= 2
    move = (rows - 1) if reverse else 1
    ok = (at < rows - 1) if reverse else (at >= 1)
    return p, q, jnp.where(ok, pltpu.roll(p, move, 0), 1.0), jnp.where(ok, pltpu.roll(q, move, 0), 0.0)

def spread(row, like):
    return jnp.broadcast_to(row, like.shape)

def ssm_summary(dt_ref, dx_ref, in_ref, rate_ref, keep_ref, thr_ref, off_ref, sum_ref):
    steps = dt_ref.shape[0]
    zero = jnp.zeros(dt_ref.shape[1:], jnp.float32)
    rates = [spread(rate_ref[n:n + 1, :], zero) for n in range(STATE)]
    def step(t, carry):
        total, states = carry
        dt, dx = dt_ref[t], dx_ref[t]
        states = tuple(jnp.exp2(dt * rates[n]) * states[n] + in_ref[t, n] * dx for n in range(STATE))
        return total + dt, states
    total, states = lax.fori_loop(0, steps, step, (zero, (zero,) * STATE), unroll=4)
    keep = keep_ref[...]
    reach, thru = [], []
    for n in range(STATE):
        p, q, pe, qe = chunk_scan(jnp.exp2(total * rates[n]) * keep, states[n], False)
        thr_ref[n] = pe * keep
        off_ref[n] = qe * keep
        reach.append(q[q.shape[0] - 1:, :])
        thru.append(p[p.shape[0] - 1:, :])
    sum_ref[...] = jnp.concatenate(reach + thru, axis=0).astype(sum_ref.dtype)

def entering_state(all_ref, pick_ref, backwards):
    count = all_ref.shape[0]
    running = jnp.zeros((STATE, LANES), jnp.float32)
    for k in range(count):
        j = count - 1 - k if backwards else k
        both = all_ref[j].astype(jnp.float32)
        new = both[STATE:] * running + both[:STATE]
        running = jnp.where(pick_ref[j] > 0, new, running)
    return running

def ssm_states(dt_ref, dx_ref, in_ref, out_ref, rate_ref, thr_ref, off_ref, all_ref, pick_ref, y_ref, enter_ref):
    steps = dt_ref.shape[0]
    zero = jnp.zeros(dt_ref.shape[1:], jnp.float32)
    rates = [spread(rate_ref[n:n + 1, :], zero) for n in range(STATE)]
    running = entering_state(all_ref, pick_ref, False)
    start = []
    for n in range(STATE):
        e = thr_ref[n] * spread(running[n:n + 1, :], zero) + off_ref[n]
        enter_ref[n] = e
        start.append(e)
    def step(t, states):
        dt, dx = dt_ref[t], dx_ref[t]
        states = tuple(jnp.exp2(dt * rates[n]) * states[n] + in_ref[t, n] * dx for n in range(STATE))
        parts = [out_ref[t, n] * states[n] for n in range(STATE)]
        while len(parts) > 1:
            parts = [a + b for a, b in zip(parts[::2], parts[1::2])]
        y_ref[t] = parts[0]
        return states
    lax.fori_loop(0, steps, step, tuple(start), unroll=4)

def ssm_back_summary(dt_ref, dy_ref, out_ref, rate_ref, keep_ref, thr_ref, off_ref, sum_ref):
    steps = dt_ref.shape[0]
    zero = jnp.zeros(dt_ref.shape[1:], jnp.float32)
    rates = [spread(rate_ref[n:n + 1, :], zero) for n in range(STATE)]
    def step(k, carry):
        t = steps - 1 - k
        total, back = carry
        dt, dy = dt_ref[t], dy_ref[t]
        back = tuple(jnp.exp2(dt * rates[n]) * (back[n] + out_ref[t, n] * dy) for n in range(STATE))
        return total + dt, back
    total, back = lax.fori_loop(0, steps, step, (zero, (zero,) * STATE), unroll=4)
    keep = keep_ref[...]
    reach, thru = [], []
    for n in range(STATE):
        p, q, pe, qe = chunk_scan(jnp.exp2(total * rates[n]) * keep, back[n] * keep, True)
        thr_ref[n] = pe
        off_ref[n] = qe
        reach.append(q[0:1, :])
        thru.append(p[0:1, :])
    sum_ref[...] = jnp.concatenate(reach + thru, axis=0).astype(sum_ref.dtype)

def ssm_grads(dt_ref, dx_ref, dy_ref, in_ref, out_ref, rate_ref, true_ref, enter_ref, thr_ref, off_ref, all_ref, pick_ref,
              ddt_ref, prod_ref, gate_ref, log_ref, h_ref, a_ref, ing_ref, outg_ref):
    steps = dt_ref.shape[0]
    zero = jnp.zeros(dt_ref.shape[1:], jnp.float32)
    rates = [spread(rate_ref[n:n + 1, :], zero) for n in range(STATE)]
    @pl.when(pl.program_id(0) == 0)
    def _():
        ing_ref[...] = jnp.zeros_like(ing_ref)
        outg_ref[...] = jnp.zeros_like(outg_ref)
    def forward(t, states):
        dt, dx, dy = dt_ref[t], dx_ref[t], dy_ref[t]
        new = []
        for n in range(STATE):
            h_ref[t, n] = states[n]
            a = jnp.exp2(dt * rates[n])
            a_ref[t, n] = a
            h = a * states[n] + in_ref[t, n] * dx
            outg_ref[t, n] += dy * h
            new.append(h)
        return tuple(new)
    lax.fori_loop(0, steps, forward, tuple(enter_ref[n] for n in range(STATE)), unroll=2)
    running = entering_state(all_ref, pick_ref, True)
    start = tuple(thr_ref[n] * spread(running[n:n + 1, :], zero) + off_ref[n] for n in range(STATE))
    true = [spread(true_ref[n:n + 1, :], zero) for n in range(STATE)]
    log_ref[...] = jnp.zeros_like(log_ref)
    def backward(k, back):
        t = steps - 1 - k
        dt, dx, dy = dt_ref[t], dx_ref[t], dy_ref[t]
        new, ddt, prod = [], [], []
        for n in range(STATE):
            lam = back[n] + out_ref[t, n] * dy
            q = lam * a_ref[t, n]
            dea = q * h_ref[t, n]
            ddt.append(dea * true[n])
            log_ref[n] += dea * dt
            prod.append(lam * in_ref[t, n])
            ing_ref[t, n] += lam * dx
            new.append(q)
        while len(ddt) > 1:
            ddt = [a + b for a, b in zip(ddt[::2], ddt[1::2])]
            prod = [a + b for a, b in zip(prod[::2], prod[1::2])]
        ddt_ref[t] = ddt[0]
        prod_ref[t] = prod[0]
        return tuple(new)
    lax.fori_loop(0, steps, backward, start, unroll=2)
    @pl.when(pl.program_id(0) == pl.num_programs(0) - 1)
    def _():
        ones = jnp.ones((8, LANES), jnp.float32)
        rows = steps * zero.shape[0]
        for k, wide_ref in enumerate((ing_ref, outg_ref)):
            for n in range(STATE):
                sums = lax.dot_general(
                    ones, wide_ref[:, n].reshape(rows, LANES), (((1,), (1,)), ((), ())),
                    precision=lax.Precision.HIGHEST, preferred_element_type=jnp.float32,
                )
                gate_ref[k * STATE + n:k * STATE + n + 1, :] = sums[0:1, :]


def specs(steps, rows):
    chan = pl.BlockSpec((steps, rows, LANES), lambda i: (0, 0, i))
    wide = pl.BlockSpec((steps, STATE, rows, LANES), lambda i: (0, 0, 0, 0))
    rate = pl.BlockSpec((STATE, LANES), lambda i: (0, i))
    per = pl.BlockSpec((STATE, rows, LANES), lambda i: (0, 0, i))
    summ = pl.BlockSpec((2 * STATE, LANES), lambda i: (0, i))
    keep = pl.BlockSpec((rows, LANES), lambda i: (0, 0))
    return chan, wide, rate, per, summ, keep

def params():
    return pltpu.CompilerParams(vmem_limit_bytes=VMEM, dimension_semantics=("arbitrary",))

def run_summary(dt, src, gates, rate2, keep, backwards):
    steps, rows, width = dt.shape
    chan, wide, rate, per, summ, kp = specs(steps, rows)
    f = jnp.float32
    return pl.pallas_call(
        ssm_back_summary if backwards else ssm_summary,
        grid=(width // LANES,),
        in_specs=[chan, chan, wide, rate, kp],
        out_specs=[per, per, summ],
        out_shape=[jax.ShapeDtypeStruct((STATE, rows, width), f)] * 2 + [jax.ShapeDtypeStruct((2 * STATE, width), jnp.bfloat16)],
        compiler_params=params(), name="ssm_back_summary" if backwards else "ssm_summary",
    )(dt, src, gates, rate2, keep)

def run_states(dt, dx, ins, outs, rate2, thr, off, everyone, pick):
    steps, rows, width = dt.shape
    chan, wide, rate, per, summ, kp = specs(steps, rows)
    count = everyone.shape[0]
    alls = pl.BlockSpec((count, 2 * STATE, LANES), lambda i: (0, 0, i))
    f = jnp.float32
    return pl.pallas_call(
        ssm_states, grid=(width // LANES,),
        in_specs=[chan, chan, wide, wide, rate, per, per, alls, pl.BlockSpec(memory_space=pltpu.SMEM)],
        out_specs=[chan, per],
        out_shape=[jax.ShapeDtypeStruct((steps, rows, width), f), jax.ShapeDtypeStruct((STATE, rows, width), f)],
        compiler_params=params(), name="ssm_states",
    )(dt, dx, ins, outs, rate2, thr, off, everyone, pick)

def run_grads(dt, dx, dy, ins, outs, rate2, rates, enter, thr, off, everyone, pick):
    steps, rows, width = dt.shape
    chan, wide, rate, per, summ, kp = specs(steps, rows)
    count = everyone.shape[0]
    alls = pl.BlockSpec((count, 2 * STATE, LANES), lambda i: (0, 0, i))
    f = jnp.float32
    s = jax.ShapeDtypeStruct
    return pl.pallas_call(
        ssm_grads, grid=(width // LANES,),
        in_specs=[chan, chan, chan, wide, wide, rate, rate, per, per, per, alls, pl.BlockSpec(memory_space=pltpu.SMEM)],
        out_specs=[chan, chan, pl.BlockSpec((2 * STATE, steps * rows), lambda i: (0, 0)), per],
        out_shape=[s((steps, rows, width), f)] * 2 + [s((2 * STATE, steps * rows), f), s((STATE, rows, width), f)],
        scratch_shapes=[pltpu.VMEM((steps, STATE, rows, LANES), f)] * 4,
        compiler_params=params(), name="ssm_grads",
    )(dt, dx, dy, ins, outs, rate2, rates, enter, thr, off, everyone, pick)


def conv_back_kernel(prod_ref, dy_ref, dt_ref, more_ref, conv_ref, padded_ref, skip_ref, dconv_ref, sums_ref):
    steps = conv_ref.shape[0]
    zero = jnp.zeros(conv_ref.shape[1:], jnp.float32)
    skip = spread(skip_ref[...], zero)

    def step(t, sums):
        value = conv_ref[t]
        sigma = jax.nn.sigmoid(value)
        grad = prod_ref[t] * dt_ref[t] + dy_ref[t] * skip + more_ref[t]
        grad = grad * (sigma * (1.0 + value * (1.0 - sigma)))
        dconv_ref[t] = grad
        taps = tuple(sums[k] + grad * padded_ref[t + k] for k in range(CONV))
        return taps + (sums[CONV] + grad,)

    sums = lax.fori_loop(0, steps, step, (zero,) * (CONV + 1), unroll=2)
    sums_ref[...] = jnp.zeros_like(sums_ref)
    for k in range(CONV + 1):
        sums_ref[k : k + 1, :] = jnp.sum(sums[k], axis=0, keepdims=True)


def conv_back(prod, dys, dt, more, conv, padded, skip):
    steps, rows, width = conv.shape
    chan = pl.BlockSpec((steps, rows, LANES), lambda i: (0, 0, i))
    longer = pl.BlockSpec((padded.shape[0], rows, LANES), lambda i: (0, 0, i))
    f32 = jnp.float32
    return pl.pallas_call(
        conv_back_kernel,
        grid=(width // LANES,),
        in_specs=[chan] * 5 + [longer, pl.BlockSpec((1, LANES), lambda i: (0, i))],
        out_specs=[chan, pl.BlockSpec((8, LANES), lambda i: (0, i))],
        out_shape=[
            jax.ShapeDtypeStruct((steps, rows, width), f32), jax.ShapeDtypeStruct((8, width), f32)
        ],
        compiler_params=params(),
        name="conv_back",
    )(prod, dys, dt, more, conv, padded, skip[None])


FFN_TILE = 512


def mm(left, right):
    return jnp.dot(left, right, preferred_element_type=jnp.float32)


def mm_nt(left, right):
    return lax.dot_general(
        left, right, (((1,), (1,)), ((), ())), preferred_element_type=jnp.float32
    )


def ffn_forward_kernel(u_ref, gate_w_ref, lift_w_ref, down_ref, gate_ref, lift_ref, part_ref, total):
    at = pl.program_id(0)
    u = u_ref[...]
    gate = mm(u, gate_w_ref[...])
    lift = mm(u, lift_w_ref[...])
    gate_ref[...] = gate
    lift_ref[...] = lift
    hidden = (gate * jax.nn.sigmoid(gate) * lift).astype(jnp.bfloat16)
    piece = mm(hidden, down_ref[...])

    @pl.when(at == 0)
    def _():
        total[...] = piece

    @pl.when(at > 0)
    def _():
        total[...] += piece

    @pl.when(at == pl.num_programs(0) - 1)
    def _():
        part_ref[...] = total[...].astype(part_ref.dtype)


def ffn_forward_call(u, both_w, down_w):
    rows, feat = u.shape
    hidden = down_w.shape[0]
    tile = min(FFN_TILE, hidden)
    count = hidden // tile
    f32, bf16 = jnp.float32, jnp.bfloat16
    shape = jax.ShapeDtypeStruct
    whole = pl.BlockSpec((rows, feat), lambda i: (0, 0))
    act = pl.BlockSpec((rows, tile), lambda i: (0, i))
    return pl.pallas_call(
        ffn_forward_kernel,
        grid=(count,),
        in_specs=[
            whole,
            pl.BlockSpec((feat, tile), lambda i: (0, i)),
            pl.BlockSpec((feat, tile), lambda i: (0, count + i)),
            pl.BlockSpec((tile, feat), lambda i: (i, 0)),
        ],
        out_specs=[act, act, whole],
        out_shape=[shape((rows, hidden), f32), shape((rows, hidden), f32), shape((rows, feat), bf16)],
        scratch_shapes=[pltpu.VMEM((rows, feat), f32)],
        compiler_params=params(),
        name="ffn_forward",
    )(u, both_w, both_w, down_w)


def ffn_backward_kernel(e_ref, gate_w_ref, lift_w_ref, down_ref, gate_ref, lift_ref, *rest):
    *side_ref, acts_ref, part_ref, total = rest
    at = pl.program_id(0)
    tile = gate_ref.shape[1]
    grad = mm_nt(e_ref[...], down_ref[...])
    gate, lift = gate_ref[...], lift_ref[...]
    sigma = jax.nn.sigmoid(gate)
    silu = gate * sigma
    gate_low = (grad * lift * (sigma * (1.0 + gate * (1.0 - sigma)))).astype(jnp.bfloat16)
    lift_low = (grad * silu).astype(jnp.bfloat16)
    acts_ref[:, 0:tile] = (silu * lift).astype(jnp.bfloat16)
    acts_ref[:, tile : 2 * tile] = gate_low
    acts_ref[:, 2 * tile : 3 * tile] = lift_low
    if side_ref:
        acts_ref[:, 3 * tile :] = side_ref[0][...]
    piece = mm_nt(gate_low, gate_w_ref[...]) + mm_nt(lift_low, lift_w_ref[...])

    @pl.when(at == 0)
    def _():
        total[...] = piece

    @pl.when(at > 0)
    def _():
        total[...] += piece

    @pl.when(at == pl.num_programs(0) - 1)
    def _():
        part_ref[...] = total[...].astype(part_ref.dtype)


def ffn_backward_call(e, both_w, down_w, gate, lift, *side):
    more = side[0].shape[1] if side else 0
    rows, feat = e.shape
    hidden = down_w.shape[0]
    tile = min(FFN_TILE, hidden)
    count = hidden // tile
    f32, bf16 = jnp.float32, jnp.bfloat16
    shape = jax.ShapeDtypeStruct
    whole = pl.BlockSpec((rows, feat), lambda i: (0, 0))
    act = pl.BlockSpec((rows, tile), lambda i: (0, i))
    return pl.pallas_call(
        ffn_backward_kernel,
        grid=(count,),
        in_specs=[
            whole,
            pl.BlockSpec((feat, tile), lambda i: (0, i)),
            pl.BlockSpec((feat, tile), lambda i: (0, count + i)),
            pl.BlockSpec((tile, feat), lambda i: (i, 0)),
            act, act,
        ]
        + [pl.BlockSpec((rows, more // count), lambda i: (0, i)) for _ in side],
        out_specs=[pl.BlockSpec((rows, 3 * tile + more // count), lambda i: (0, i)), whole],
        out_shape=[shape((rows, 3 * hidden + more), bf16), shape((rows, feat), bf16)],
        scratch_shapes=[pltpu.VMEM((rows, feat), f32)],
        compiler_params=params(),
        name="ffn_backward",
    )(e, both_w, both_w, down_w, gate, lift, *side)


def ffn_grads_tile(u_t, e_t, acts_ref, gate_ref, lift_ref, down_ref):
    tile = gate_ref.shape[1]
    down_ref[...] = mm(e_t[...], acts_ref[:, 0:tile]).T.astype(down_ref.dtype)
    gate_ref[...] = mm(u_t[...], acts_ref[:, tile : 2 * tile]).astype(gate_ref.dtype)
    lift_ref[...] = mm(u_t[...], acts_ref[:, 2 * tile : 3 * tile]).astype(lift_ref.dtype)


def ffn_grads_specs(rows, feat, hidden, wide):
    tile = min(FFN_TILE, hidden)
    count = hidden // tile
    out = pl.BlockSpec((feat, tile), lambda i: (0, i))
    return (
        (count,), pl.BlockSpec((rows, wide // count), lambda i: (0, i)),
        [out, out, pl.BlockSpec((tile, feat), lambda i: (i, 0))],
    )


def ffn_grads_kernel(u_ref, e_ref, acts_ref, gate_ref, lift_ref, down_ref, u_t, e_t):
    @pl.when(pl.program_id(0) == 0)
    def _():
        u_t[...] = u_ref[...].T
        e_t[...] = e_ref[...].T

    ffn_grads_tile(u_t, e_t, acts_ref, gate_ref, lift_ref, down_ref)


def ffn_grads_call(u, e, acts, hidden):
    rows, feat = u.shape
    grid, block, outs = ffn_grads_specs(rows, feat, hidden, acts.shape[1])
    shape = jax.ShapeDtypeStruct
    whole = pl.BlockSpec((rows, feat), lambda i: (0, 0))
    return pl.pallas_call(
        ffn_grads_kernel,
        grid=grid,
        in_specs=[whole, whole, block],
        out_specs=outs,
        out_shape=[shape((feat, hidden), jnp.float32)] * 2 + [shape((hidden, feat), jnp.float32)],
        scratch_shapes=[pltpu.VMEM((feat, rows), u.dtype)] * 2,
        compiler_params=params(),
        name="ffn_grads",
    )(u, e, acts)


def ffn_grads_beside(sources, outs, turned):
    *sources, acts_ref = sources
    for source, target in zip(sources, turned):
        target[...] = source[...].T
    rows, feat = sources[0].shape
    grid, block, specs = ffn_grads_specs(rows, feat, outs[0].shape[1], acts_ref.shape[1])

    def tiles(acts, gate, lift, down, *side):
        ffn_grads_tile(turned[0], turned[1], acts, gate, lift, down)
        for o_t, out in zip(turned[2:], side):
            out[...] = mm(o_t[...], acts[:, acts.shape[1] - out.shape[1] :])

    specs = specs + [
        pl.BlockSpec((feat, out.shape[1] // grid[0]), lambda i: (0, i)) for out in outs[3:]
    ]
    pltpu.emit_pipeline(tiles, grid=grid, in_specs=[block], out_specs=specs)(acts_ref, *outs)


def columns_grad_beside(o_ref, source_ref, out_ref, o_t, first):
    o_t[...] = o_ref[...].T
    rows, feat = o_ref.shape
    tile = min(FFN_TILE, out_ref.shape[0])

    def tiles(source, out):
        out[...] = mm(o_t[...], source[...]).T

    pltpu.emit_pipeline(
        tiles,
        grid=(out_ref.shape[0] // tile,),
        in_specs=[pl.BlockSpec((rows, tile), lambda i: (0, first // tile + i))],
        out_specs=[pl.BlockSpec((tile, feat), lambda i: (i, 0))],
    )(source_ref, out_ref)


def side_grads_kernel(turned, o_ref, side_ref, out_ref, o_t):
    @pl.when(pl.program_id(0) == 0)
    def _():
        o_t[...] = o_ref[...].T

    result = mm(o_t[...], side_ref[...])
    out_ref[...] = result.T if turned else result


def side_grads_call(o, acts, hidden, turned):
    rows, feat = o.shape
    count = hidden // min(FFN_TILE, hidden)
    side = (acts.shape[1] - 3 * hidden) // count
    step = acts.shape[1] // count // side
    out = (count * side, feat) if turned else (feat, count * side)
    return pl.pallas_call(
        functools.partial(side_grads_kernel, turned),
        grid=(count,),
        in_specs=[
            pl.BlockSpec((rows, feat), lambda i: (0, 0)),
            pl.BlockSpec((rows, side), lambda i: (0, step * i + step - 1)),
        ],
        out_specs=pl.BlockSpec((side, feat), lambda i: (i, 0)) if turned
        else pl.BlockSpec((feat, side), lambda i: (0, i)),
        out_shape=jax.ShapeDtypeStruct(out, jnp.float32),
        scratch_shapes=[pltpu.VMEM((feat, rows), o.dtype)],
        compiler_params=params(),
        name="side_grads",
    )(o, acts)


class Ring:
    def __init__(self, count):
        self.count = count
        self.chips = count // 2
        self.side = math.isqrt(self.chips)
        self.long = self.chips // 2
        self.short = self.chips - 1 - self.long
        self.me = lax.axis_index("seq")
        self.core = self.me % 2
        self.way = 1 - 2 * self.core
        self.at = self.flip(self.me // 2)
        self.partner = self.me + self.way
        self.long_next = self.device(1, self.core)
        self.short_next = self.device(-1, self.core)

    def flip(self, chip):
        row, column = chip // self.side, chip % self.side
        return row * self.side + column + (row % 2) * (self.side - 1 - 2 * column)

    def device(self, hops, core):
        place = (self.at + hops * self.way + 2 * self.chips) % self.chips
        return self.flip(place) * 2 + core


def remote(source, target, send_sem, recv_sem, axis, to):
    return pltpu.make_async_remote_copy(
        src_ref=source,
        dst_ref=target,
        send_sem=send_sem,
        recv_sem=recv_sem,
        device_id={axis: to},
        device_id_type=MESH,
    )


def greet(axis, devices):
    barrier = pltpu.get_barrier_semaphore()
    for to in devices:
        pl.semaphore_signal(barrier, inc=1, device_id={axis: to}, device_id_type=MESH)
    return len(devices)


def others_of(axis, count):
    me = lax.axis_index(axis)
    return [lax.rem(me + d, count) for d in range(1, count)]


class Gather:
    def __init__(self, ring, shard, full, by_rows, send_sem, recv_sem, own_sem):
        self.ring, self.shard, self.full, self.by_rows = ring, shard, full, by_rows
        self.send_sem, self.recv_sem = send_sem, recv_sem
        self.size = shard.shape[0 if by_rows else 1]
        self.own = pltpu.make_async_copy(shard, self.slot(ring.me), own_sem)
        self.sent = []

    def slot(self, device):
        part = pl.ds(pl.multiple_of(device * self.size, self.size), self.size)
        return self.full.at[part] if self.by_rows else self.full.at[:, part]

    def send(self, source, device, sem, to):
        copy = remote(
            source, self.slot(device), self.send_sem.at[len(self.sent)], self.recv_sem.at[sem],
            "seq", to,
        )
        copy.start()
        self.sent.append(copy)

    def wait(self, device, sem):
        slot = self.slot(device)
        remote(
            slot, slot, self.send_sem.at[0], self.recv_sem.at[sem], "seq", self.ring.partner
        ).wait_recv()

    def start(self):
        ring = self.ring
        self.send(self.shard, ring.me, 0, ring.long_next)
        if ring.short:
            self.send(self.shard, ring.me, ring.long, ring.short_next)
        self.send(self.shard, ring.me, ring.long + ring.short, ring.partner)
        self.own.start()

    def hop(self, i):
        ring = self.ring
        base = ring.long + ring.short + 1
        if i <= ring.long:
            device = ring.device(-i, ring.core)
            self.wait(device, i - 1)
            if i < ring.long:
                self.send(self.slot(device), device, i, ring.long_next)
            self.send(self.slot(device), device, base + i - 1, ring.partner)
        if i <= ring.short:
            device = ring.device(i, ring.core)
            self.wait(device, ring.long + i - 1)
            if i < ring.short:
                self.send(self.slot(device), device, ring.long + i, ring.short_next)
            self.send(self.slot(device), device, base + ring.long + i - 1, ring.partner)

    def finish(self):
        ring = self.ring
        base = ring.long + ring.short + 1
        other = 1 - ring.core
        self.wait(ring.partner, base - 1)
        for i in range(1, ring.long + 1):
            self.wait(ring.device(i, other), base + i - 1)
        for i in range(1, ring.short + 1):
            self.wait(ring.device(-i, other), base + ring.long + i - 1)
        self.own.wait()
        for copy in self.sent:
            copy.wait_send()


class Swap:
    def __init__(self, count, source, target, send_sem, recv_sem, own_sem):
        self.count, self.source, self.target = count, source, target
        self.send_sem, self.recv_sem = send_sem, recv_sem
        self.me = lax.axis_index("seq")
        self.rows = target.shape[0] // count
        self.width = target.shape[1]
        self.own = pltpu.make_async_copy(self.block(self.me), self.slot(self.me), own_sem)
        self.sent = []

    def block(self, to):
        if len(self.source.shape) == 3:
            return self.source.at[to]
        return self.source.at[:, pl.ds(pl.multiple_of(to * self.width, self.width), self.width)]

    def slot(self, device):
        return self.target.at[pl.ds(pl.multiple_of(device * self.rows, self.rows), self.rows)]

    def start(self):
        for d in range(1, self.count):
            to = lax.rem(self.me + d, self.count)
            copy = remote(
                self.block(to), self.slot(self.me), self.send_sem.at[d - 1],
                self.recv_sem.at[d - 1], "seq", to,
            )
            copy.start()
            self.sent.append(copy)
        self.own.start()

    def finish(self):
        for d in range(1, self.count):
            slot = self.slot(lax.rem(self.me + self.count - d, self.count))
            remote(
                slot, slot, self.send_sem.at[0], self.recv_sem.at[d - 1], "seq",
                lax.rem(self.me + d, self.count),
            ).wait_recv()
        self.own.wait()
        for copy in self.sent:
            copy.wait_send()


def rms_scale(x):
    return lax.rsqrt(jnp.mean(x * x, axis=-1, keepdims=True) + EPS)


def forward_local(ins, outs, total):
    x_ref, keep_ref, gain_ref = ins
    new = x_ref[...] + keep_ref[:, 0:1] * total
    outs[0][...] = new
    return new * rms_scale(new) * gain_ref[...], None


def norm_back(ins, total):
    x_ref, keep_ref, gain_ref, grad_ref = ins[:4]
    x = x_ref[...]
    scale = rms_scale(x)
    weighted = gain_ref[...] * total
    middle = jnp.mean(weighted * x, axis=-1, keepdims=True)
    row = jnp.sum(total * x * scale, axis=0, keepdims=True)
    return grad_ref[...] + scale * weighted - x * (scale * scale * scale) * middle, row


def backward_local(ins, outs, total):
    new, row = norm_back(ins, total)
    outs[0][...] = new
    outs[1][...] = row
    return ins[1][:, 0:1] * new, None


def last_backward_local(ins, outs, total):
    return norm_back(ins, total)


def sum_local(ins, outs, total):
    return total, None


class Quarter(Swap):
    def __init__(self, count, planes, source, target, send_sem, recv_sem, own_sem):
        self.count, self.source, self.target = count, source, target
        self.send_sem, self.recv_sem = send_sem, recv_sem
        self.me = lax.axis_index("seq")
        self.rows, self.width = target.shape[1:]
        self.share = pl.ds(
            pl.multiple_of(lax.axis_index("mp") * self.rows, self.rows), self.rows
        )
        self.own = pltpu.make_async_copy(self.block(self.me), self.slot(self.me), own_sem)
        self.sent = []

    def block(self, to):
        columns = pl.ds(pl.multiple_of(to * self.width, self.width), self.width)
        return self.source.at[self.share, columns]

    def slot(self, device):
        return self.target.at[device]


class PlaneSpread:
    def __init__(self, planes, source, target, send_sem, recv_sem, own_sem):
        self.planes, self.source, self.target = planes, source, target
        self.send_sem, self.recv_sem = send_sem, recv_sem
        self.me = lax.axis_index("mp")
        self.own = pltpu.make_async_copy(source, target.at[:, self.me], own_sem)
        self.sent = []

    def start(self):
        for d in range(1, self.planes):
            copy = remote(
                self.source, self.target.at[:, self.me], self.send_sem.at[d - 1],
                self.recv_sem.at[d - 1], "mp", lax.rem(self.me + d, self.planes),
            )
            copy.start()
            self.sent.append(copy)
        self.own.start()

    def finish(self):
        for d in range(1, self.planes):
            slot = self.target.at[:, lax.rem(self.me + self.planes - d, self.planes)]
            remote(
                slot, slot, self.send_sem.at[0], self.recv_sem.at[d - 1], "mp",
                lax.rem(self.me + d, self.planes),
            ).wait_recv()
        self.own.wait()
        for copy in self.sent:
            copy.wait_send()


class Spread:
    def __init__(self, count, source, target, send_sem, recv_sem, own_sem):
        self.count, self.source, self.target = count, source, target
        self.send_sem, self.recv_sem = send_sem, recv_sem
        self.me = lax.axis_index("seq")
        self.own = pltpu.make_async_copy(source, target.at[self.me], own_sem)
        self.sent = []

    def start(self):
        for d in range(1, self.count):
            copy = remote(
                self.source, self.target.at[self.me], self.send_sem.at[d - 1],
                self.recv_sem.at[d - 1], "seq", lax.rem(self.me + d, self.count),
            )
            copy.start()
            self.sent.append(copy)
        self.own.start()

    def finish(self):
        for d in range(1, self.count):
            slot = self.target.at[lax.rem(self.me + self.count - d, self.count)]
            remote(
                slot, slot, self.send_sem.at[0], self.recv_sem.at[d - 1], "seq",
                lax.rem(self.me + d, self.count),
            ).wait_recv()
        self.own.wait()
        for copy in self.sent:
            copy.wait_send()


class PlaneScatter:
    def __init__(self, planes, part, target, got, send_sem, recv_sem):
        self.planes, self.part, self.target, self.got = planes, part, target, got
        self.send_sem, self.recv_sem = send_sem, recv_sem
        self.me = lax.axis_index("mp")
        self.sent = []

    def block(self, to):
        rows = self.part.shape[0] // self.planes
        return pl.ds(pl.multiple_of(to * rows, rows), rows)

    def start(self):
        for d in range(1, self.planes):
            to = lax.rem(self.me + d, self.planes)
            copy = remote(
                self.part.at[self.block(to)], self.got.at[d - 1], self.send_sem.at[d - 1],
                self.recv_sem.at[d - 1], "mp", to,
            )
            copy.start()
            self.sent.append(copy)

    def total(self):
        total = self.part[self.block(self.me), :].astype(jnp.float32)
        for d in range(1, self.planes):
            self.sent[d - 1].wait_recv()
            total = total + self.got[d - 1].astype(jnp.float32)
        return total

    def finish(self):
        self.target[...] = self.total()
        for copy in self.sent:
            copy.wait_send()


class PlaneCollect:
    def __init__(self, planes, source, target, send_sem, recv_sem):
        self.planes, self.source, self.target = planes, source, target
        self.send_sem, self.recv_sem = send_sem, recv_sem
        self.me = lax.axis_index("mp")
        rows = source.shape[0]
        self.own = target.at[pl.ds(pl.multiple_of(self.me * rows, rows), rows)]
        self.sent = []

    def start(self):
        for d in range(1, self.planes):
            copy = remote(
                self.source, self.own, self.send_sem.at[d - 1], self.recv_sem.at[d - 1],
                "mp", lax.rem(self.me + d, self.planes),
            )
            copy.start()
            self.sent.append(copy)
        self.own[...] = self.source[...]

    def finish(self):
        for copy in self.sent:
            copy.wait_recv()
        for copy in self.sent:
            copy.wait_send()


class LineSum:
    def __init__(self, part, got, stage, mine, full, sems):
        self.part, self.got, self.stage, self.mine, self.full = part, got, stage, mine, full
        self.sems = sems
        me = lax.axis_index("mp")
        self.me = me
        half = me // 2
        self.outer = (me == 0) | (me == 3)
        self.inner = (me == 1) | (me == 2)
        self.partner = 4 * half + 1 - me
        self.far_inner, self.far_outer = 2 - half, 3 - 3 * half

    def block(self, plane):
        rows = self.mine.shape[0]
        return pl.ds(pl.multiple_of(plane * rows, rows), rows)

    def toward(self, source, slot, sem, to):
        return remote(
            source, self.got.at[slot], self.sems[0].at[sem], self.sems[1].at[slot], "mp", to
        )

    def out(self, source, plane, sem, slot, to):
        return remote(
            source, self.full.at[self.block(plane)], self.sems[2].at[sem], self.sems[3].at[slot],
            "mp", to,
        )

    def start(self):
        part, partner = self.part, self.partner

        @pl.when(self.outer)
        def _():
            self.toward(part.at[self.block(self.far_outer)], 2, 0, partner).start()
            self.toward(part.at[self.block(self.far_inner)], 3, 1, partner).start()
            self.toward(part.at[self.block(partner)], 0, 2, partner).start()

        @pl.when(self.inner)
        def _():
            self.toward(part.at[self.block(partner)], 0, 2, partner).start()

    def relay(self):
        @pl.when(self.inner)
        def _():
            for slot, to in ((2, self.far_outer), (3, self.far_inner)):
                block = self.part.at[self.block(to)]
                self.toward(block, slot, slot - 2, self.partner).wait_recv()
                joined = block[...].astype(jnp.float32) + self.got[slot].astype(jnp.float32)
                self.stage[slot - 2] = joined.astype(self.stage.dtype)
                self.toward(self.stage.at[slot - 2], 1, slot - 2, to).start()

    def total(self):
        block = self.part.at[self.block(self.me)]
        total = block[...].astype(jnp.float32)
        for slot in (0, 1):
            self.toward(block, slot, 0, self.partner).wait_recv()
            total = total + self.got[slot].astype(jnp.float32)
        return total

    def collect(self):
        @pl.when(self.inner)
        def _():
            self.out(self.mine, self.me, 1, 1, self.far_inner).start()
            self.out(self.mine, self.me, 0, 0, self.partner).start()

        @pl.when(self.outer)
        def _():
            self.out(self.mine, self.me, 1, 2, self.far_inner).start()
            self.out(self.mine, self.me, 0, 0, self.partner).start()

        self.full[self.block(self.me), :] = self.mine[...]

    def arrive(self, plane, slot):
        block = self.full.at[self.block(plane)]
        self.out(block, plane, 0, slot, self.partner).wait_recv()
        return block

    def forward(self):
        @pl.when(self.inner)
        def _():
            block = self.arrive(self.far_inner, 1)
            self.out(block, self.far_inner, 2, 1, self.partner).start()
            block = self.arrive(self.far_outer, 2)
            self.out(block, self.far_outer, 3, 2, self.partner).start()

    def finish(self):
        self.arrive(self.partner, 0)

        @pl.when(self.outer)
        def _():
            self.arrive(self.far_inner, 1)
            self.arrive(self.far_outer, 2)

        block = self.part.at[self.block(self.me)]
        for sem in range(3):
            self.toward(block, 0, sem, self.partner).wait_send()
        for sem in range(2):
            self.out(self.mine, self.me, sem, 0, self.partner).wait_send()

        @pl.when(self.inner)
        def _():
            for sem in (2, 3):
                self.out(self.mine, self.me, sem, 0, self.partner).wait_send()


class DirectSum:
    def __init__(self, planes, part, got, mine, full, sems):
        self.scatter = PlaneScatter(planes, part, None, got, sems[0], sems[1])
        self.result = PlaneCollect(planes, mine, full, sems[2], sems[3])

    def start(self):
        self.scatter.start()

    def relay(self):
        pass

    def total(self):
        return self.scatter.total()

    def collect(self):
        self.result.start()

    def forward(self):
        pass

    def finish(self):
        self.result.finish()
        for copy in self.scatter.sent:
            copy.wait_send()


class LineCollect(LineSum):
    def __init__(self, source, target, send_sem, recv_sem):
        sems = (None, None, send_sem, recv_sem)
        super().__init__(None, None, None, source, target, sems)

    def start(self):
        self.collect()

    def finish(self):
        self.arrive(self.partner, 0)

        @pl.when(self.outer)
        def _():
            self.arrive(self.far_inner, 1)
            self.arrive(self.far_outer, 2)

        for sem in range(2):
            self.out(self.mine, self.me, sem, 0, self.partner).wait_send()

        @pl.when(self.inner)
        def _():
            for sem in (2, 3):
                self.out(self.mine, self.me, sem, 0, self.partner).wait_send()


class SeqSum:
    def __init__(self, count, parts, out, low, got, mine, send_sem, recv_sem):
        self.count, self.parts, self.out = count, parts, out
        self.low, self.got, self.mine = low, got, mine
        self.send_sem, self.recv_sem = send_sem, recv_sem
        self.me = lax.axis_index("seq")
        self.rows = low.shape[0] // count
        self.first, self.second = [], []

    def block(self, device):
        return pl.ds(pl.multiple_of(device * self.rows, self.rows), self.rows)

    def start(self):
        at = 0
        for part in self.parts:
            size = part.shape[0]
            self.low[at : at + size, :] = part[...].astype(self.low.dtype)
            at += size
        if at < self.low.shape[0]:
            self.low[at:, :] = jnp.zeros((self.low.shape[0] - at, self.low.shape[1]), self.low.dtype)
        for d in range(1, self.count):
            to = lax.rem(self.me + d, self.count)
            copy = remote(
                self.low.at[self.block(to)], self.got.at[d - 1],
                self.send_sem.at[d - 1], self.recv_sem.at[d - 1], "seq", to,
            )
            copy.start()
            self.first.append(copy)

    def middle(self):
        own = self.block(self.me)
        total = self.low[own, :].astype(jnp.float32)
        for d in range(1, self.count):
            self.first[d - 1].wait_recv()
            total = total + self.got[d - 1].astype(jnp.float32)
        self.mine[...] = total.astype(self.mine.dtype)
        for d in range(1, self.count):
            copy = remote(
                self.mine, self.out.at[own], self.send_sem.at[self.count + d - 1],
                self.recv_sem.at[self.count + d - 1], "seq", lax.rem(self.me + d, self.count),
            )
            copy.start()
            self.second.append(copy)
        self.out[own, :] = self.mine[...]

    def finish(self):
        for d in range(1, self.count):
            slot = self.out.at[self.block(lax.rem(self.me + self.count - d, self.count))]
            remote(
                slot, slot, self.send_sem.at[self.count], self.recv_sem.at[self.count + d - 1],
                "seq", lax.rem(self.me + d, self.count),
            ).wait_recv()
        for copy in self.first + self.second:
            copy.wait_send()


class GainSum:
    def __init__(self, planes, count, rows, out, across, along, sems):
        self.planes, self.count, self.rows, self.out = planes, count, rows, out
        self.across, self.along, self.sems = across, along, sems
        self.me, self.plane = lax.axis_index("seq"), lax.axis_index("mp")
        self.first, self.second = [], []

    def start(self, row):
        held = self.rows.shape[0]
        self.out[...] = self.rows[...]
        self.out[held - 1 : held, :] = row
        for d in range(1, self.planes):
            copy = remote(
                self.out, self.across.at[d - 1], self.sems[0].at[d - 1], self.sems[1].at[d - 1],
                "mp", lax.rem(self.plane + d, self.planes),
            )
            copy.start()
            self.first.append(copy)

    def middle(self):
        total = self.out[...]
        for d in range(1, self.planes):
            self.first[d - 1].wait_recv()
            total = total + self.across[d - 1]
        for copy in self.first:
            copy.wait_send()
        self.out[...] = total
        for d in range(1, self.count):
            copy = remote(
                self.out, self.along.at[d - 1], self.sems[2].at[d - 1], self.sems[3].at[d - 1],
                "seq", lax.rem(self.me + d, self.count),
            )
            copy.start()
            self.second.append(copy)

    def finish(self):
        total = self.out[...]
        for d in range(1, self.count):
            self.second[d - 1].wait_recv()
            total = total + self.along[d - 1]
        for copy in self.second:
            copy.wait_send()
        self.out[...] = total


class Plan:
    def __init__(self, gathers=(), swaps=(), spreads=(), sums=(), quarters=(), planes=(), collects=()):
        self.count = lax.axis_size("seq")
        self.planes = lax.axis_size("mp")
        self.upright = bool(planes or collects)
        count = self.count
        vmem = pl.BlockSpec(memory_space=pltpu.VMEM)
        hbm = pl.BlockSpec(memory_space=pl.ANY)
        shape = jax.ShapeDtypeStruct
        self.sources, self.in_specs, self.shapes, self.out_specs, self.scratch = [], [], [], [], []
        self.kinds, self.after = [], []
        sems = [
            pltpu.SemaphoreType.DMA((2 * count,)), pltpu.SemaphoreType.DMA((2 * count,)),
            pltpu.SemaphoreType.DMA,
        ]
        for array, rows in gathers:
            height, width = array.shape
            by_rows = rows or width % LANES != 0
            self.add("rows" if by_rows else "columns", [array], hbm, hbm, sems, shape(
                (count * height, width) if by_rows else (height, count * width), array.dtype
            ))
            self.after[-1] = (height, width) if by_rows and not rows else None
        for array in swaps:
            height, width = array.shape[0], array.shape[1] // count
            if width % LANES:
                array = array.reshape(height, count, width).swapaxes(0, 1)
            self.add("swap", [array], hbm, hbm, sems, shape((count * height, width), array.dtype))
        for array in spreads:
            self.add("spread", [array], vmem, vmem, sems, shape((count,) + array.shape, array.dtype))
        for parts in sums:
            have, width = sum(part.shape[0] for part in parts), parts[0].shape[1]
            rows = -(-have // (16 * count)) * 16
            bf16 = jnp.bfloat16
            self.add("sum", list(parts), vmem, vmem, sems + [
                pltpu.VMEM((rows * count, width), bf16),
                pltpu.VMEM((count - 1, rows, width), bf16),
                pltpu.VMEM((rows, width), bf16),
            ], shape((rows * count, width), bf16))

        for array in quarters:
            rows, width = array.shape
            self.add("quarter", [array], hbm, hbm, sems, shape(
                (count, rows // self.planes, width // count), array.dtype
            ))
        for array in planes:
            self.add("plane", [array], hbm, hbm, sems, shape(
                (array.shape[0], self.planes) + array.shape[1:], array.dtype
            ))
        for array in collects:
            self.add("collect", [array], vmem, vmem, sems[:2], shape(
                (self.planes * array.shape[0], array.shape[1]), array.dtype
            ))

    def add(self, kind, arrays, in_spec, out_spec, scratch, shape):
        self.kinds.append((kind, len(arrays), len(scratch)))
        self.sources += arrays
        self.in_specs += [in_spec] * len(arrays)
        self.shapes.append(shape)
        self.out_specs.append(out_spec)
        self.scratch += scratch
        self.after.append(None)

    def results(self, targets):
        return [
            t if cut is None
            else t.reshape((self.count,) + cut).swapaxes(0, 1).reshape(cut[0], self.count * cut[1])
            for t, cut in zip(targets, self.after)
        ]

    def bind(self, sources, targets, scratch):
        count = self.count
        self.ring = None
        self.items = []
        self.wide = False
        for (kind, many, held), target in zip(self.kinds, targets):
            mine, sources = sources[:many], sources[many:]
            sems, scratch = scratch[:held], scratch[held:]
            if kind in ("rows", "columns"):
                if self.ring is None:
                    self.ring = Ring(count)
                self.items.append(Gather(self.ring, mine[0], target, kind == "rows", *sems))
                continue
            if kind == "plane":
                self.items.append(PlaneSpread(self.planes, mine[0], target, *sems))
                continue
            if kind == "collect":
                if self.planes == 4:
                    self.items.append(LineCollect(mine[0], target, *sems))
                else:
                    self.items.append(PlaneCollect(self.planes, mine[0], target, *sems))
                continue
            self.wide = True
            if kind == "quarter":
                self.items.append(Quarter(count, self.planes, mine[0], target, *sems))
            elif kind == "swap":
                self.items.append(Swap(count, mine[0], target, *sems))
            elif kind == "spread":
                self.items.append(Spread(count, mine[0], target, *sems))
            else:
                self.items.append(SeqSum(count, mine, target, *sems[3:], *sems[:2]))

    def greet(self, wide=False):
        if self.wide or wide:
            return greet("seq", others_of("seq", self.count))
        if self.ring is not None:
            near = [self.ring.long_next, self.ring.partner]
            if self.ring.short:
                near.append(self.ring.short_next)
            return greet("seq", near)
        return 0

    def start(self):
        for item in self.items:
            item.start()

    def pass_on(self):
        for item in self.items:
            if isinstance(item, LineCollect):
                item.forward()

    def hops(self):
        gathers = [item for item in self.items if isinstance(item, Gather)]
        if gathers:
            for i in range(1, self.ring.long + 1):
                for item in gathers:
                    item.hop(i)
        for item in self.items:
            if isinstance(item, SeqSum):
                item.middle()

    def finish(self):
        for item in self.items:
            item.finish()


def step_kernel(planes, plan, local, n_ins, n_outs, gain_at, work, pieces, *refs):
    part_ref, refs = refs[0], refs[1:]
    ins, refs = refs[:n_ins], refs[n_ins:]
    sources, refs = refs[: len(plan.sources)], refs[len(plan.sources) :]
    work_ins, refs = refs[:work], refs[work:]
    piece_ins, refs = refs[: 2 * len(pieces)], refs[2 * len(pieces) :]
    full_ref, refs = refs[0], refs[1:]
    outs, refs = refs[:n_outs], refs[n_outs:]
    targets, refs = refs[: len(plan.shapes)], refs[len(plan.shapes) :]
    work_outs, refs = refs[:work], refs[work:]
    piece_outs, refs = refs[: len(pieces)], refs[len(pieces) :]
    got, mine, stage = refs[:3]
    sems, refs = refs[3:7], refs[7:]
    plan.bind(sources, targets, refs[: len(plan.scratch)])
    refs = refs[len(plan.scratch) :]
    turned, refs = refs[: work - 1 if work else 0], refs[work - 1 if work else 0 :]
    piece_turned, refs = refs[: len(pieces)], refs[len(pieces) :]
    gains = None
    if gain_at is not None:
        gains = GainSum(planes, plan.count, ins[gain_at], outs[0], refs[0], refs[1], refs[2:])
    greeted = greet("mp", others_of("mp", planes)) + plan.greet(gains is not None)
    pl.semaphore_wait(pltpu.get_barrier_semaphore(), greeted)
    if planes == 4:
        line = LineSum(part_ref, got, stage, mine, full_ref, sems)
    else:
        line = DirectSum(planes, part_ref, got, mine, full_ref, sems)
    line.start()
    plan.start()
    line.relay()
    if work:
        ffn_grads_beside(work_ins, work_outs, turned)
    for i, first in enumerate(pieces):
        columns_grad_beside(*piece_ins[2 * i : 2 * i + 2], piece_outs[i], piece_turned[i], first)
    plan.pass_on()
    value, row = local(ins, outs, line.total())
    mine[...] = value.astype(mine.dtype)
    line.collect()
    if gains is not None:
        gains.start(row)
    line.forward()
    plan.hops()
    if gains is not None:
        gains.middle()
    line.finish()
    plan.finish()
    if gains is not None:
        gains.finish()


def remote_params(cid):
    return pltpu.CompilerParams(
        collective_id=cid, has_side_effects=True, vmem_limit_bytes=VMEM
    )


def z_step(name, cid, local, part, others, extra, out_dtype=jnp.bfloat16, gain_at=None, work=(), pieces=(), **carried):
    planes = lax.axis_size("mp")
    plan = Plan(**carried)
    rows, width = part.shape
    share = rows // planes
    f32 = jnp.float32
    shape = jax.ShapeDtypeStruct
    held = 0 if gain_at is None else others[gain_at].shape[0]
    kinds = {
        "share": shape((share, width), f32),
        "gain": shape((1, width), f32),
        "gains": shape((held, width), f32),
    }
    gain_scratch = [] if gain_at is None else [
        pltpu.VMEM((planes - 1, held, width), f32),
        pltpu.VMEM((plan.count - 1, held, width), f32),
        pltpu.SemaphoreType.DMA((planes,)),
        pltpu.SemaphoreType.DMA((planes,)),
        pltpu.SemaphoreType.DMA((plan.count,)),
        pltpu.SemaphoreType.DMA((plan.count,)),
    ]
    vmem = pl.BlockSpec(memory_space=pltpu.VMEM)
    hbm = pl.BlockSpec(memory_space=pl.ANY)
    work_shapes, turned = [], []
    if work:
        u, e, *side, acts, hidden = work
        low = jnp.bfloat16
        work_shapes = [shape((u.shape[1], hidden), low)] * 2 + [shape((hidden, e.shape[1]), low)]
        for o in side:
            work_shapes.append(shape((o.shape[1], acts.shape[1] - 3 * hidden), f32))
        turned = [pltpu.VMEM((u.shape[1], u.shape[0]), u.dtype)] * (2 + len(side))
    piece_ins, piece_shapes, piece_turned = [], [], []
    for o, source, _, size in pieces:
        piece_ins += [o, source]
        piece_shapes.append(shape((size, o.shape[1]), f32))
        piece_turned.append(pltpu.VMEM((o.shape[1], o.shape[0]), o.dtype))
    result = pl.pallas_call(
        functools.partial(
            step_kernel, planes, plan, local, len(others), len(extra), gain_at, len(work_shapes),
            tuple(first for _, _, first, _ in pieces),
        ),
        out_shape=[shape((rows, width), out_dtype)] + [kinds[kind] for kind in extra]
        + plan.shapes + work_shapes + piece_shapes,
        in_specs=[vmem] * (1 + len(others)) + plan.in_specs + ([vmem] * (len(work) - 2) + [hbm] if work else [])
        + [vmem, hbm] * len(pieces),
        out_specs=[vmem] * (1 + len(extra)) + plan.out_specs + [hbm] * len(work_shapes + piece_shapes),
        scratch_shapes=[
            pltpu.VMEM((max(planes, 4), share, width), part.dtype),
            pltpu.VMEM((share, width), out_dtype),
            pltpu.VMEM((2, share, width), part.dtype),
        ]
        + [pltpu.SemaphoreType.DMA((max(planes, 4),))] * 4
        + plan.scratch + turned + piece_turned + gain_scratch,
        compiler_params=remote_params(cid),
        name=name,
    )(part, *others, *plan.sources, *work[:-1], *piece_ins)
    cut = 1 + len(extra)
    rest = cut + len(plan.shapes)
    return list(result[:cut]) + [plan.results(result[cut:rest])] + list(result[rest:])


def carry_kernel(planes, plan, scatters, *refs):
    sources, refs = refs[: len(plan.sources)], refs[len(plan.sources) :]
    parts, refs = refs[:scatters], refs[scatters:]
    targets, refs = refs[: len(plan.shapes)], refs[len(plan.shapes) :]
    sums, refs = refs[:scatters], refs[scatters:]
    plan.bind(sources, targets, refs[: len(plan.scratch)])
    refs = refs[len(plan.scratch) :]
    items = []
    for part, total in zip(parts, sums):
        items.append(PlaneScatter(planes, part, total, *refs[:3]))
        refs = refs[3:]
    greeted = plan.greet()
    if items or plan.upright:
        greeted += greet("mp", others_of("mp", planes))
    pl.semaphore_wait(pltpu.get_barrier_semaphore(), greeted)
    plan.start()
    for item in items:
        item.start()
    plan.pass_on()
    plan.hops()
    plan.finish()
    for item in items:
        item.finish()


def carry(name, cid, scatters=(), **carried):
    planes = lax.axis_size("mp")
    plan = Plan(**carried)
    vmem = pl.BlockSpec(memory_space=pltpu.VMEM)
    shape = jax.ShapeDtypeStruct
    sems = [pltpu.SemaphoreType.DMA((planes,))] * 2
    shapes, scratch = [], []
    for part in scatters:
        share = (part.shape[0] // planes, part.shape[1])
        shapes.append(shape(share, jnp.float32))
        scratch += [pltpu.VMEM((planes - 1,) + share, part.dtype)] + sems
    result = pl.pallas_call(
        functools.partial(carry_kernel, planes, plan, len(scatters)),
        out_shape=plan.shapes + shapes,
        in_specs=plan.in_specs + [vmem] * len(scatters),
        out_specs=plan.out_specs + [vmem] * len(shapes),
        scratch_shapes=plan.scratch + scratch,
        compiler_params=remote_params(cid),
        name=name,
    )(*plan.sources, *scatters)
    cut = len(plan.shapes)
    return plan.results(result[:cut]) + list(result[cut:])


SCALE = 1.0 / math.sqrt(HEAD_DIM)


def nt(left, right):
    return lax.dot_general(
        left, right, (((1,), (1,)), ((), ())), preferred_element_type=jnp.float32
    )


def nn(left, right):
    return jnp.dot(left, right, preferred_element_type=jnp.float32)


def attend_kernel(q_ref, k_ref, v_ref, low_ref, high_ref, pos_ref, out_ref, lse_ref):
    scores = nt(q_ref[...], k_ref[...]) * SCALE
    pos = pos_ref[...]
    scores = jnp.where((pos >= low_ref[...]) & (pos <= high_ref[...]), scores, -1e30)
    top = jnp.max(scores, axis=-1, keepdims=True)
    expo = jnp.exp(scores - top)
    mass = jnp.sum(expo, axis=-1, keepdims=True)
    probs = (expo / mass).astype(jnp.bfloat16)
    out_ref[...] = nn(probs, v_ref[...]).astype(jnp.bfloat16)
    lse_ref[0] = top + jnp.log(mass)


def query_back_kernel(q_ref, k_ref, v_ref, g_ref, low_ref, high_ref, pos_ref, lse_ref, dq_ref, mid_ref):
    keys = k_ref[...]
    scores = nt(q_ref[...], keys) * SCALE
    pos = pos_ref[...]
    scores = jnp.where((pos >= low_ref[...]) & (pos <= high_ref[...]), scores, -1e30)
    probs = jnp.exp(scores - lse_ref[0])
    prob_grad = nt(g_ref[...], v_ref[...])
    middle = jnp.sum(probs * prob_grad, axis=-1, keepdims=True)
    score_grad = (probs * (prob_grad - middle)).astype(jnp.bfloat16)
    dq_ref[...] = (nn(score_grad, keys) * SCALE).astype(jnp.bfloat16)
    mid_ref[0] = middle


def key_back_kernel(k_ref, v_ref, q_ref, g_ref, pos_ref, low_ref, high_ref, lse_ref, mid_ref, dk_ref, dv_ref):
    queries, grads = q_ref[...], g_ref[...]
    scores = nt(k_ref[...], queries) * SCALE
    pos = pos_ref[...]
    scores = jnp.where((pos >= low_ref[...]) & (pos <= high_ref[...]), scores, -1e30)
    probs = jnp.exp(scores - lse_ref[0])
    prob_grad = nt(v_ref[...], grads)
    score_grad = (probs * (prob_grad - mid_ref[0])).astype(jnp.bfloat16)
    dk_ref[...] = (nn(score_grad, queries) * SCALE).astype(jnp.bfloat16)
    dv_ref[...] = nn(probs.astype(jnp.bfloat16), grads).astype(jnp.bfloat16)


def head_block(rows, first):
    return pl.BlockSpec((rows, HEAD_DIM), lambda h: (0, first + h))


def whole_block(*shape):
    return pl.BlockSpec(shape, lambda h: (0,) * len(shape))


def attend_params():
    return pltpu.CompilerParams(vmem_limit_bytes=VMEM, dimension_semantics=("arbitrary",))


def attend_call(q, pair, low, high, pos, heads):
    rows, keys = q.shape[0], pair.shape[0]
    return pl.pallas_call(
        attend_kernel,
        grid=(heads,),
        in_specs=[
            head_block(rows, 0), head_block(keys, 0), head_block(keys, heads),
            whole_block(rows, 1), whole_block(rows, 1), whole_block(1, keys),
        ],
        out_specs=[head_block(rows, 0), pl.BlockSpec((1, rows, 1), lambda h: (h, 0, 0))],
        out_shape=[
            jax.ShapeDtypeStruct(q.shape, jnp.bfloat16),
            jax.ShapeDtypeStruct((heads, rows, 1), jnp.float32),
        ],
        compiler_params=attend_params(),
        name="attend",
    )(q, pair, pair, low, high, pos)


def query_back_call(q, pair, grad, low, high, pos, lse, heads):
    rows, keys = q.shape[0], pair.shape[0]
    stat = pl.BlockSpec((1, rows, 1), lambda h: (h, 0, 0))
    return pl.pallas_call(
        query_back_kernel,
        grid=(heads,),
        in_specs=[
            head_block(rows, 0), head_block(keys, 0), head_block(keys, heads),
            head_block(rows, 0),
            whole_block(rows, 1), whole_block(rows, 1), whole_block(1, keys), stat,
        ],
        out_specs=[head_block(rows, 0), stat],
        out_shape=[
            jax.ShapeDtypeStruct(q.shape, jnp.bfloat16),
            jax.ShapeDtypeStruct((heads, rows, 1), jnp.float32),
        ],
        compiler_params=attend_params(),
        name="query_back",
    )(q, pair, pair, grad, low, high, pos, lse)


def key_back_call(pair, queries, grads, pos, low, high, lse, mid, heads):
    rows, many = pair.shape[0], queries.shape[0]
    stat = pl.BlockSpec((1, 1, many), lambda h: (h, 0, 0))
    shape = jax.ShapeDtypeStruct((rows, heads * HEAD_DIM), jnp.bfloat16)
    return pl.pallas_call(
        key_back_kernel,
        grid=(heads,),
        in_specs=[
            head_block(rows, 0), head_block(rows, heads), head_block(many, 0), head_block(many, 0),
            whole_block(rows, 1), whole_block(1, many), whole_block(1, many), stat, stat,
        ],
        out_specs=[head_block(rows, 0)] * 2,
        out_shape=[shape, shape],
        compiler_params=attend_params(),
        name="key_back",
    )(pair, pair, queries, grads, pos, low, high, lse, mid)


class Across:
    def __init__(self, count, send_sem, recv_sem, own_sem):
        self.chips = count // 2
        me = lax.axis_index("seq")
        self.me, self.chip, self.core = me, me // 2, me % 2
        self.partner = me + 1 - 2 * self.core
        self.send_sem, self.recv_sem, self.own_sem = send_sem, recv_sem, own_sem
        self.sent, self.kept = [], []

    def chip_at(self, hops):
        return lax.rem(self.chip + hops + self.chips, self.chips)

    def greet(self, with_partner):
        near = [self.chip_at(d) * 2 + self.core for d in range(1, self.chips)]
        return greet("seq", near + ([self.partner] if with_partner else []))

    def send(self, source, target, sem, to):
        copy = remote(
            source, target, self.send_sem.at[len(self.sent)], self.recv_sem.at[sem], "seq", to
        )
        copy.start()
        self.sent.append(copy)

    def keep(self, source, target):
        copy = pltpu.make_async_copy(source, target, self.own_sem.at[len(self.kept)])
        copy.start()
        self.kept.append(copy)

    def wait(self, target, sem):
        remote(
            target, target, self.send_sem.at[0], self.recv_sem.at[sem], "seq", self.partner
        ).wait_recv()

    def finish(self):
        for copy in self.kept:
            copy.wait()
        for copy in self.sent:
            copy.wait_send()


def cut(at, size):
    return pl.ds(pl.multiple_of(at * size, size), size)


def heads_in_kernel(count, planes, qkv_ref, side_ref, q_ref, kv_ref, side_out, *sems):
    ways = Across(count, *sems[:3])
    greeted = ways.greet(True) + greet("mp", others_of("mp", planes))
    pl.semaphore_wait(pltpu.get_barrier_semaphore(), greeted)
    side = PlaneSpread(planes, side_ref, side_out, *sems[3:])
    side.start()
    rows, chips = qkv_ref.shape[0], ways.chips

    def places(chip):
        owner = 2 * chip + ways.core
        return (
            q_ref.at[cut(chip, rows)],
            kv_ref.at[cut(owner, rows), 0:HEAD_DIM],
            kv_ref.at[cut(owner, rows), HEAD_DIM : 2 * HEAD_DIM],
        )

    for d in list(range(1, chips)) + [0]:
        head = ways.chip_at(d)
        for kind, target in enumerate(places(ways.chip)):
            source = qkv_ref.at[:, cut(kind * chips + head, HEAD_DIM)]
            if d:
                ways.send(source, target, 3 * d + kind, 2 * head + ways.core)
            else:
                ways.keep(source, target)
    for copy in ways.kept:
        copy.wait()
    ways.kept = []
    for d in range(chips):
        chip = ways.chip_at(-d)
        if d:
            for kind, target in enumerate(places(chip)):
                ways.wait(target, 3 * d + kind)
        both = kv_ref.at[cut(2 * chip + ways.core, rows)]
        ways.send(both, both, 3 * chips + d, ways.partner)
    for d in range(chips):
        chip = ways.chip_at(-d)
        ways.wait(kv_ref.at[cut(2 * chip + 1 - ways.core, rows)], 3 * chips + d)
    ways.finish()
    side.finish()


def blocks_to_columns_kernel(count, source_ref, target_ref, *sems):
    ways = Across(count, *sems)
    pl.semaphore_wait(pltpu.get_barrier_semaphore(), ways.greet(False))
    rows = target_ref.shape[0]
    mine = target_ref.at[:, cut(ways.chip, HEAD_DIM)]
    for d in range(1, ways.chips):
        chip = ways.chip_at(d)
        ways.send(source_ref.at[cut(chip, rows)], mine, d, 2 * chip + ways.core)
    ways.keep(source_ref.at[cut(ways.chip, rows)], mine)
    for d in range(1, ways.chips):
        ways.wait(target_ref.at[:, cut(ways.chip_at(-d), HEAD_DIM)], d)
    ways.finish()


def columns_to_blocks_kernel(count, source_ref, target_ref, *sems):
    ways = Across(count, *sems)
    pl.semaphore_wait(pltpu.get_barrier_semaphore(), ways.greet(False))
    rows = source_ref.shape[0]
    mine = target_ref.at[cut(ways.chip, rows)]
    for d in range(1, ways.chips):
        chip = ways.chip_at(d)
        ways.send(source_ref.at[:, cut(chip, HEAD_DIM)], mine, d, 2 * chip + ways.core)
    ways.keep(source_ref.at[:, cut(ways.chip, HEAD_DIM)], mine)
    for d in range(1, ways.chips):
        ways.wait(target_ref.at[cut(ways.chip_at(-d), rows)], d)
    ways.finish()


def heads_grads_kernel(
    count, dq_ref, dk_ref, dv_ref, out_ref, got_k, got_v, low_k, low_v, send_sem, recv_sem, own_sem
):
    ways = Across(count, send_sem, recv_sem, own_sem)
    pl.semaphore_wait(pltpu.get_barrier_semaphore(), ways.greet(True))
    rows, chips = out_ref.shape[0], ways.chips
    pairs = ((dk_ref, got_k, low_k), (dv_ref, got_v, low_v))
    for i in range(chips):
        for kind, (ref, got, _) in enumerate(pairs):
            block = ref.at[cut(2 * i + 1 - ways.core, rows)]
            ways.send(block, got.at[i], 3 * chips + 2 * i + kind, ways.partner)

    def place(kind, chip):
        return out_ref.at[:, cut(kind * chips + chip, HEAD_DIM)]

    for d in range(1, chips):
        chip = ways.chip_at(d)
        ways.send(
            dq_ref.at[cut(chip, rows)], place(0, ways.chip), 3 * d, 2 * chip + ways.core
        )
    ways.keep(dq_ref.at[cut(ways.chip, rows)], place(0, ways.chip))
    for i in range(chips):
        for kind, (ref, got, low) in enumerate(pairs):
            ways.wait(got.at[i], 3 * chips + 2 * i + kind)
            total = ref[cut(2 * i + ways.core, rows), :] + got[i]
            low[i] = (total * (1.0, SCALE)[kind == 0]).astype(low.dtype)
    for d in range(1, chips):
        chip = ways.chip_at(d)
        for kind, (_, _, low) in enumerate(pairs):
            ways.send(
                low.at[chip], place(1 + kind, ways.chip), 3 * d + 1 + kind, 2 * chip + ways.core
            )
    for kind, (_, _, low) in enumerate(pairs):
        ways.keep(low.at[ways.chip], place(1 + kind, ways.chip))
    for d in range(1, chips):
        for kind in range(3):
            ways.wait(place(kind, ways.chip_at(-d)), 3 * d + kind)
    ways.finish()


def across_sems(sends, receives, keeps):
    return [
        pltpu.SemaphoreType.DMA((sends,)), pltpu.SemaphoreType.DMA((receives,)),
        pltpu.SemaphoreType.DMA((keeps,)),
    ]


def across_call(kernel, name, cid, sources, shapes, sems):
    hbm = pl.BlockSpec(memory_space=pl.ANY)
    return pl.pallas_call(
        functools.partial(kernel, lax.axis_size("seq")),
        out_shape=shapes,
        in_specs=[hbm] * len(sources),
        out_specs=[hbm] * len(shapes),
        scratch_shapes=across_sems(*sems),
        compiler_params=remote_params(cid),
        name=name,
    )(*sources)


def heads_in(cid, qkv, side):
    count, planes, rows = lax.axis_size("seq"), lax.axis_size("mp"), qkv.shape[0]
    chips = count // 2
    shape = jax.ShapeDtypeStruct
    hbm = pl.BlockSpec(memory_space=pl.ANY)
    return pl.pallas_call(
        functools.partial(heads_in_kernel, count, planes),
        out_shape=[
            shape((chips * rows, HEAD_DIM), qkv.dtype),
            shape((count * rows, 2 * HEAD_DIM), qkv.dtype),
            shape((count, planes) + side.shape[1:], side.dtype),
        ],
        in_specs=[hbm] * 2,
        out_specs=[hbm] * 3,
        scratch_shapes=across_sems(4 * chips, 4 * chips, 3)
        + [pltpu.SemaphoreType.DMA((planes,))] * 2 + [pltpu.SemaphoreType.DMA],
        compiler_params=remote_params(cid),
        name="heads_in",
    )(qkv, side)


def blocks_to_columns(name, cid, blocks):
    chips = lax.axis_size("seq") // 2
    shape = (blocks.shape[0] // chips, chips * HEAD_DIM)
    return across_call(
        blocks_to_columns_kernel, name, cid, [blocks],
        [jax.ShapeDtypeStruct(shape, blocks.dtype)], (chips, chips, 1),
    )[0]


def columns_to_blocks(name, cid, columns):
    chips = lax.axis_size("seq") // 2
    shape = (columns.shape[0] * chips, HEAD_DIM)
    return across_call(
        columns_to_blocks_kernel, name, cid, [columns],
        [jax.ShapeDtypeStruct(shape, columns.dtype)], (chips, chips, 1),
    )[0]


def heads_grads(cid, dq, dk, dv):
    count = lax.axis_size("seq")
    chips = count // 2
    rows = dq.shape[0] // chips
    f32, bf16 = jnp.float32, jnp.bfloat16
    vmem = pl.BlockSpec(memory_space=pltpu.VMEM)
    return pl.pallas_call(
        functools.partial(heads_grads_kernel, count),
        out_shape=jax.ShapeDtypeStruct((rows, 3 * chips * HEAD_DIM), bf16),
        in_specs=[vmem] * 3,
        out_specs=pl.BlockSpec(memory_space=pl.ANY),
        scratch_shapes=[pltpu.VMEM((chips, rows, HEAD_DIM), f32)] * 2
        + [pltpu.VMEM((chips, rows, HEAD_DIM), bf16)] * 2
        + across_sems(2 * chips + 3 * (chips - 1), 5 * chips, 3),
        compiler_params=remote_params(cid),
        name="heads_grads",
    )(dq, dk, dv)


def tn(left, right):
    return lax.dot_general(
        left, right, (((0,), (0,)), ((), ())), preferred_element_type=jnp.float32
    )


def head_kernel(q_ref, k_ref, v_ref, low_ref, high_ref, pos_ref, out_ref, lse_ref):
    scores = nt(q_ref[...], k_ref[...]) * SCALE
    pos = pos_ref[...]
    scores = jnp.where((pos >= low_ref[...]) & (pos <= high_ref[...]), scores, -1e30)
    top = jnp.max(scores, axis=-1, keepdims=True)
    expo = jnp.exp(scores - top)
    mass = jnp.sum(expo, axis=-1, keepdims=True)
    probs = (expo / mass).astype(jnp.bfloat16)
    out_ref[...] = nn(probs, v_ref[...]).astype(jnp.bfloat16)
    lse_ref[...] = top + jnp.log(mass)


def head_back_kernel(q_ref, k_ref, v_ref, g_ref, low_ref, high_ref, pos_ref, lse_ref, dq_ref, dk_ref, dv_ref):
    queries, keys, grads = q_ref[...], k_ref[...], g_ref[...]
    scores = nt(queries, keys) * SCALE
    pos = pos_ref[...]
    scores = jnp.where((pos >= low_ref[...]) & (pos <= high_ref[...]), scores, -1e30)
    probs = jnp.exp(scores - lse_ref[...])
    prob_grad = nt(grads, v_ref[...])
    middle = jnp.sum(probs * prob_grad, axis=-1, keepdims=True)
    score_grad = (probs * (prob_grad - middle)).astype(jnp.bfloat16)
    dq_ref[...] = (nn(score_grad, keys) * SCALE).astype(jnp.bfloat16)
    dk = tn(score_grad, queries)
    dv = tn(probs.astype(jnp.bfloat16), grads)

    @pl.when(pl.program_id(0) == 0)
    def _():
        dk_ref[...] = dk
        dv_ref[...] = dv

    @pl.when(pl.program_id(0) > 0)
    def _():
        dk_ref[...] += dk
        dv_ref[...] += dv


def head_specs(rows, keys):
    block = pl.BlockSpec((rows, HEAD_DIM), lambda i: (i, 0))
    stat = pl.BlockSpec((rows, 1), lambda i: (i, 0))
    half = [pl.BlockSpec((keys, HEAD_DIM), lambda i, k=k: (0, k)) for k in range(2)]
    whole = pl.BlockSpec((keys, HEAD_DIM), lambda i: (0, 0))
    return block, stat, half, pl.BlockSpec((1, keys), lambda i: (0, 0)), whole


def head_call(q, kv, low, high, pos, rows):
    block, stat, half, line, _ = head_specs(rows, kv.shape[0])
    return pl.pallas_call(
        head_kernel,
        grid=(q.shape[0] // rows,),
        in_specs=[block, *half, stat, stat, line],
        out_specs=[block, stat],
        out_shape=[
            jax.ShapeDtypeStruct(q.shape, jnp.bfloat16),
            jax.ShapeDtypeStruct((q.shape[0], 1), jnp.float32),
        ],
        compiler_params=attend_params(),
        name="head",
    )(q, kv, kv, low, high, pos)


def head_back_call(q, kv, grad, low, high, pos, lse, rows):
    block, stat, half, line, whole = head_specs(rows, kv.shape[0])
    keys = jax.ShapeDtypeStruct((kv.shape[0], HEAD_DIM), jnp.float32)
    return pl.pallas_call(
        head_back_kernel,
        grid=(q.shape[0] // rows,),
        in_specs=[block, *half, block, stat, stat, line, stat],
        out_specs=[block, whole, whole],
        out_shape=[jax.ShapeDtypeStruct(q.shape, jnp.bfloat16), keys, keys],
        compiler_params=attend_params(),
        name="head_back",
    )(q, kv, kv, grad, low, high, pos, lse)


def shifted(value, axis, steps):
    count = lax.axis_size(axis)
    leading, last = (max(0, -steps), min(count, count - steps))
    return lax.ppermute(value, axis, [(source, source + steps) for source in range(leading, last)])


def matmul(left, right):
    return jnp.dot(left, right, preferred_element_type=jnp.float32)


def matmul_tn(left, right):
    return lax.dot_general(
        left, right, (((0,), (0,)), ((), ())), preferred_element_type=jnp.float32
    )


def matmul_nt(left, right):
    return lax.dot_general(
        left, right, (((1,), (1,)), ((), ())), preferred_element_type=jnp.float32
    )


def layout(lengths, positions, slot, total):
    starts = jnp.array([0, slot, 2 * slot, total - 2 * slot, total - slot], jnp.int32)
    seg = jnp.sum((positions[:, None] >= starts[None, :]).astype(jnp.int32), axis=1) - 1
    which = (seg[:, None] == jnp.arange(5, dtype=jnp.int32)[None, :]).astype(jnp.int32)
    start_of = jnp.sum(which * starts[None, :], axis=1)
    length_of = jnp.sum(which * lengths[None, :], axis=1)
    keep = (positions - start_of < length_of).astype(jnp.float32)
    first = (positions == start_of).astype(jnp.float32)
    return (start_of, keep, first)


def silu_slope(value):
    sigma = jax.nn.sigmoid(value)
    return sigma * (1.0 + value * (1.0 - sigma))


def gather_rows(array):
    return lax.all_gather(array, "seq", axis=0, tiled=True)


def gather_columns(array):
    return lax.all_gather(array, "seq", axis=1, tiled=True)


def after(value, *earlier):
    return lax.optimization_barrier((value,) + earlier)[0]


def by_chunk(value):
    rows = value.shape[0]
    return value.reshape((CHUNKS, rows // CHUNKS) + value.shape[1:]).swapaxes(0, 1)


def by_token(value):
    steps = value.shape[0]
    return value.swapaxes(0, 1).reshape((CHUNKS * steps,) + value.shape[2:])


def widened(gates, steps):
    gates = gates.reshape(STATE, steps, CHUNKS).swapaxes(0, 1)
    return jnp.broadcast_to(gates[..., None], (steps, STATE, CHUNKS, LANES))


def body(
    tokens,
    lengths,
    out_grad,
    mixer_gain,
    mixer_value,
    mixer_gate,
    conv_weight,
    conv_bias,
    select_proj,
    step_proj,
    step_bias,
    decay_log,
    skip_gain,
    mixer_out,
    first_gain,
    first_gate,
    first_lift,
    first_down,
    attend_gain,
    query_proj,
    key_proj,
    value_proj,
    attend_out,
    second_gain,
    second_gate,
    second_lift,
    second_down,
):
    f32, bf16 = jnp.float32, jnp.bfloat16
    length = tokens.shape[0]
    shards, planes = lax.axis_size("seq"), lax.axis_size("mp")
    me, plane = lax.axis_index("seq"), lax.axis_index("mp")
    total = length * shards
    slot = length // 4
    steps = length // CHUNKS
    share = length // planes
    positions = me * length + jnp.arange(length, dtype=jnp.int32)
    start_of, keep, first = layout(lengths, positions, slot, total)

    def mine(rows):
        return lax.dynamic_slice_in_dim(rows, plane * share, share)

    keep = keep[:, None]
    keep_share = jnp.broadcast_to(mine(keep), (share, LANES))
    x0 = tokens.astype(f32)
    x0_share = mine(x0)

    few = total <= tokens.shape[1]

    def collect(rows):
        return gather_rows(rows) if few else rows

    def hosted(*items):
        return list(items) if few else []

    def by_rows(result):
        if few:
            return result
        return lax.psum_scatter(
            result.astype(bf16), "seq", scatter_dimension=0, tiled=True
        ).astype(f32)

    def by_columns(result):
        if few:
            return result
        return lax.psum_scatter(
            result.astype(bf16), "seq", scatter_dimension=1, tiled=True
        ).astype(f32)

    def ffn_grads(u, e, acts):
        gate, lift, down = ffn_grads_call(u, e, acts, hidden)
        return by_rows(gate), by_rows(lift), by_columns(down)

    (value_w,) = carry("value_weights", 1, gathers=[(mixer_value, True)])
    gate_w = gather_rows(mixer_gate)
    hidden, head_width = first_gate.shape[1], query_proj.shape[1]
    first_both = gather_rows(
        after(
            jnp.concatenate([first_gate, first_lift], axis=1),
            value_w,
        )
    )

    u1 = by_chunk((x0 * rms_scale(x0) * mixer_gain).astype(bf16)).reshape(length, -1)
    inner = matmul(u1, value_w).reshape(steps, CHUNKS, -1)
    width = inner.shape[-1]
    zg = matmul(u1, gate_w)
    joined = 1.0 - first.reshape(CHUNKS, steps)[:, 0]
    prior = shifted(inner[steps - (CONV - 1) :, CHUNKS - 1], "seq", 1)
    halo = jnp.concatenate([prior[:, None], inner[steps - (CONV - 1) :, : CHUNKS - 1]], axis=1)
    padded = jnp.concatenate([halo * joined[None, :, None], inner], axis=0)
    conv = conv_bias[None, None, :]
    for tap in range(CONV):
        conv = conv + conv_weight[tap][None, None, :] * padded[tap : tap + steps]
    signal = jax.nn.silu(conv).astype(bf16)
    flat_signal = signal.reshape(length, width)
    select, (out_w,) = z_step(
        "select_sum", 2, sum_local, matmul_nt(select_proj, flat_signal), (), (), f32,
        gathers=[(mixer_out, False)],
    )
    step_low = select[:DT_RANK].astype(bf16)
    qkv_w = gather_rows(
        after(jnp.concatenate([query_proj, key_proj, value_proj], axis=1), select)
    )
    raised = (matmul_tn(step_low, step_proj) + step_bias[None, :]).reshape(steps, CHUNKS, width)
    dt = jax.nn.softplus(raised)
    signal_wide = signal.astype(f32)
    dx = dt * signal_wide
    rates = -jnp.exp(decay_log)
    rates2 = rates * LOG2E
    keep_chunk = jnp.broadcast_to(joined[:, None], (CHUNKS, LANES))
    ins = widened(select[DT_RANK : DT_RANK + STATE], steps)
    outs = widened(select[DT_RANK + STATE :], steps)
    order = jnp.arange(shards, dtype=jnp.int32)
    thr, off, summary = run_summary(dt, dx, ins, rates2, keep_chunk, False)
    (everyone,) = carry("state_spread", 3, spreads=[summary])
    states, enter = run_states(
        dt, dx, ins, outs, rates2, thr, off, everyone, (order < me).astype(jnp.int32)
    )
    ys = states + skip_gain[None, None, :] * signal_wide
    zg = zg.reshape(steps, CHUNKS, width)
    mix = by_token((ys * jax.nn.silu(zg)).astype(bf16))
    u2, x1_share, (first_w,) = z_step(
        "mixer_join", 4, forward_local, matmul(mix, out_w).astype(bf16),
        (x0_share, keep_share, first_gain[None]), ("share",), gathers=[(first_down, False)],
    )

    second_both = gather_rows(after(jnp.concatenate([second_gate, second_lift], axis=1), u2))

    gate1, lift1, part2 = ffn_forward_call(u2, first_both, first_w)
    heads = query_proj.shape[1] // HEAD_DIM
    by_head = few and shards == 2 * heads
    u3, x2_share, (attend_w, *u2_part) = z_step(
        "first_join", 5, forward_local, part2,
        (x1_share, keep_share, attend_gain[None]), ("share",),
        gathers=[(attend_out, False)], quarters=[u2] if by_head else [],
    )

    qkv = matmul(u3, qkv_w).astype(bf16)
    if by_head:
        head_q, head_kv, u2_all = heads_in(6, qkv, u2_part[0])
        u2_all = [u2_all.reshape(total, -1)]
        spot = jnp.arange(heads * length, dtype=jnp.int32)
        spot = (2 * (spot // length) + me % 2) * length + spot % length
        spot_start, _, _ = layout(lengths, spot, slot, total)
        low = jnp.maximum(spot_start, spot - (WINDOW - 1))[:, None]
        high = spot[:, None]
        key_pos = jnp.arange(total, dtype=jnp.int32)[None, :]
        head_att, lse = head_call(head_q, head_kv, low, high, key_pos, length)
        att = blocks_to_columns("heads_out", 12, head_att)
    else:
        query, pair = qkv[:, :head_width], qkv[:, head_width:]
        (pairs,) = carry("keys_values", 6, gathers=[(pair, True)])
        span = min(shards, WINDOW // length + 1) * length
        key_from = jnp.clip(positions[0] + length - span, 0, total - span)
        near_pairs = lax.dynamic_slice_in_dim(pairs, key_from, span)
        key_pos = (key_from + jnp.arange(span, dtype=jnp.int32))[None, :]
        low = jnp.maximum(start_of, positions - (WINDOW - 1))[:, None]
        high = positions[:, None]
        att, lse = attend_call(query, near_pairs, low, high, key_pos, heads)
    u4, x3_share, (second_w, *queries) = z_step(
        "attend_join", 7, forward_local, matmul(att, attend_w).astype(bf16),
        (x2_share, keep_share, second_gain[None]), ("share",),
        gathers=[(second_down, False)] + ([] if by_head else [(query, True)]),
        swaps=hosted(u1),
    )
    queries, u1_all = (queries[:-1], queries[-1:]) if few else (queries, [])
    early_all = collect(after(jnp.concatenate([mix, att], axis=1), u4))

    gate2, lift2, part4 = ffn_forward_call(u4, second_both, second_w)
    wide_grad = out_grad.astype(f32)
    e4 = (keep * wide_grad).astype(bf16)
    acts2, du4 = ffn_backward_call(e4, second_both, second_w, gate2, lift2)
    e3, g3_share, second_gain_part, ue4_all = z_step(
        "second_back", 8, backward_local, du4,
        (x3_share, keep_share, second_gain[None], mine(wide_grad)), ("share", "gain"),
        swaps=hosted(u4, e4),
    )
    acts2_all = collect(acts2)

    datt = matmul_nt(e3, attend_w).astype(bf16)
    if by_head:
        head_grad = columns_to_blocks("heads_grad_in", 9, datt)
        dq, dk, dv = head_back_call(head_q, head_kv, head_grad, low, high, key_pos, lse, length)
        dqkv = heads_grads(16, dq, dk, dv)
    else:
        dq, middle = query_back_call(query, near_pairs, datt, low, high, key_pos, lse, heads)
        stats = jnp.concatenate([lse, middle], axis=0).reshape(2 * heads, length)
        datts, all_stats = carry("query_grads", 9, gathers=[(datt, True), (stats, True)])
        all_stats = all_stats.reshape(shards, 2 * heads, length).swapaxes(0, 1).reshape(2 * heads, total)
        query_from = jnp.clip(positions[0], 0, total - span)
        every_pos = query_from + jnp.arange(span, dtype=jnp.int32)
        every_start, _, _ = layout(lengths, every_pos, slot, total)
        every_low = jnp.maximum(every_start, every_pos - (WINDOW - 1))[None, :]
        near_stats = lax.dynamic_slice_in_dim(all_stats, query_from, span, axis=1)[:, None]
        dk, dv = key_back_call(
            pair,
            lax.dynamic_slice_in_dim(queries[0], query_from, span),
            lax.dynamic_slice_in_dim(datts, query_from, span),
            high, every_low, every_pos[None, :], near_stats[:heads], near_stats[heads:], heads,
        )
        dqkv = jnp.concatenate([dq, dk, dv], axis=1)
    du3 = matmul_nt(dqkv, qkv_w)
    e2, g2_share, attend_gain_part, u3_all = z_step(
        "attend_back", 10, backward_local, after(du3.astype(bf16), early_all),
        (x2_share, keep_share, attend_gain[None], g3_share), ("share", "gain"),
        swaps=hosted(u3),
    )

    acts1, du2 = ffn_backward_call(e2, first_both, first_w, gate1, lift1, dqkv)
    e1, g1_share, first_gain_part, e2_all, *second_grads = z_step(
        "first_back", 11, backward_local, after(du2, acts2_all),
        (x1_share, keep_share, first_gain[None], g2_share), ("share", "gain"), swaps=hosted(e2) if by_head else hosted(u2, e2), work=(*ue4_all, acts2_all, hidden) if few else (),
    )
    acts1_all = collect(acts1)

    if few and not by_head:
        *u2_all, last = e2_all
        e2_all = [last]

    dmix = matmul_nt(by_chunk(e1).reshape(length, -1), out_w).reshape(steps, CHUNKS, width)
    dys = dmix * jax.nn.silu(zg)
    dzg = (dmix * ys * silu_slope(zg)).astype(bf16).reshape(length, width)
    skip_grad = jnp.sum(dys * signal_wide, axis=(0, 1))
    thr, off, summary = run_summary(dt, dys, outs, rates2, keep_chunk, True)
    everyone, *e1_part, sum4 = carry(
        "grad_spread", 13, spreads=[summary], quarters=[e1] if by_head else [], scatters=[part4],
    )
    ddt, prod, gate_grads, log_wide = run_grads(
        dt, dx, dys, ins, outs, rates2, rates, enter, thr, off, everyone,
        (order > me).astype(jnp.int32),
    )
    dpre = (ddt + prod * signal_wide) * jax.nn.sigmoid(raised)
    step_bias_grad = jnp.sum(dpre, axis=(0, 1))
    dpr = dpre.astype(bf16).reshape(length, width)
    step_grad = matmul(step_low, dpr)
    dsel, e31_all = z_step(
        "select_back", 14, sum_local,
        jnp.concatenate([matmul_nt(step_proj, dpr), gate_grads]),
        (), (), f32, swaps=hosted(e3) if by_head else hosted(e3, e1), planes=e1_part,
    )
    dsel = dsel.astype(bf16)
    select_grad = matmul(dsel, flat_signal)
    more = matmul_tn(dsel, select_proj).reshape(steps, CHUNKS, width)
    dconv, conv_sums = conv_back(prod, dys, dt, more, conv, padded, skip_gain)
    head = dconv[: CONV - 1] * joined[None, :, None]
    later = shifted(head[:, 0], "seq", -1)
    tail = jnp.concatenate([head[:, 1:], later[:, None]], axis=1)
    extended = jnp.concatenate([dconv, tail], axis=0)
    dxin = 0.0
    for tap in range(CONV):
        lag = CONV - 1 - tap
        dxin = dxin + conv_weight[tap][None, None, :] * extended[lag : lag + steps]
    dxin = dxin.astype(bf16).reshape(length, width)
    du1 = by_token(
        (matmul_nt(dxin, value_w) + matmul_nt(dzg, gate_w)).astype(bf16).reshape(steps, CHUNKS, -1)
    )
    few_rows = jnp.concatenate(
        [
            conv_sums[: CONV + 1],
            step_bias_grad[None],
            jnp.sum(log_wide, axis=1) * rates,
            skip_grad[None],
            jnp.zeros((9, width), f32),
        ]
    )
    pieces = []
    if few:
        e3_all, e1_all = e31_all
        e1_all = e1_all.reshape(total, -1)
        pieces = [
            (e1_all, early_all, 0, width), (e3_all, early_all, width, early_all.shape[1] - width)
        ]
    tokens_grad, gain_sums, (*dxz_all, small, mixed), *first_grads = z_step(
        "mixer_back", 15, last_backward_local, after(du1, acts1_all),
        (
            x0_share, keep_share, mixer_gain[None], g1_share,
            jnp.concatenate(
                [first_gain_part, attend_gain_part, second_gain_part, jnp.zeros_like(first_gain_part)]
            ),
        ),
        ("gains",), gain_at=4,
        gathers=hosted((dxin, True), (dzg, True)), sums=[(select_grad, step_grad, few_rows)],
        collects=[(x3_share + keep_share[:, 0:1] * sum4).astype(bf16)],
        work=(*u2_all, *e2_all, *u3_all, acts1_all, hidden) if few else (), pieces=pieces,
    )

    if few:
        (u1_all,), (dxin_all, dzg_all) = u1_all, dxz_all
        *first_grads, qkv_grad, mixer_out_grad, attend_out_grad = first_grads
    else:
        u1_all, dxin_all, dzg_all = u1, dxin, dzg
        qkv_grad = by_rows(side_grads_call(u3, acts1_all, hidden, False))
        mixer_out_grad = by_columns(matmul_tn(early_all[:, :width], e1))
        attend_out_grad = by_columns(matmul_tn(early_all[:, width:], e3))
    cuts = []
    at = 0
    for size in (2 * STATE + DT_RANK, DT_RANK, CONV, 1, 1, STATE, 1):
        cuts.append(small[at : at + size].astype(f32))
        at += size
    select_sum, step_sum, conv_w_sum, conv_b_sum, step_b_sum, decay_sum, skip_sum = cuts
    return (
        mixed,
        tokens_grad.astype(f32),
        gain_sums[3],
        by_rows(matmul_tn(u1_all, dxin_all)),
        by_rows(matmul_tn(u1_all, dzg_all)),
        conv_w_sum,
        conv_b_sum[0],
        select_sum,
        step_sum,
        step_b_sum[0],
        decay_sum,
        skip_sum[0],
        mixer_out_grad,
        gain_sums[0],
        *([grad.astype(f32) for grad in first_grads] or ffn_grads(u2, e2, acts1)),
        gain_sums[1],
        qkv_grad[:, :head_width],
        qkv_grad[:, head_width : 2 * head_width],
        qkv_grad[:, 2 * head_width :],
        attend_out_grad,
        gain_sums[2],
        *([grad.astype(f32) for grad in second_grads] or ffn_grads(u4, e4, acts2)),
    )


def solution(mesh):
    return jax.shard_map(
        body,
        mesh=mesh,
        in_specs=(
            P("seq", None),
            P(),
            P("seq", None),
            P(),
            P("seq", "mp"),
            P("seq", "mp"),
            P(None, "mp"),
            P("mp"),
            P(None, "mp"),
            P(None, "mp"),
            P("mp"),
            P(None, "mp"),
            P("mp"),
            P("mp", "seq"),
            P(),
            P("seq", "mp"),
            P("seq", "mp"),
            P("mp", "seq"),
            P(),
            P("seq", "mp"),
            P("seq", "mp"),
            P("seq", "mp"),
            P("mp", "seq"),
            P(),
            P("seq", "mp"),
            P("seq", "mp"),
            P("mp", "seq"),
        ),
        out_specs=(
            P("seq", None),
            P("seq", None),
            P(),
            P("seq", "mp"),
            P("seq", "mp"),
            P(None, "mp"),
            P("mp"),
            P(None, "mp"),
            P(None, "mp"),
            P("mp"),
            P(None, "mp"),
            P("mp"),
            P("mp", "seq"),
            P(),
            P("seq", "mp"),
            P("seq", "mp"),
            P("mp", "seq"),
            P(),
            P("seq", "mp"),
            P("seq", "mp"),
            P("seq", "mp"),
            P("mp", "seq"),
            P(),
            P("seq", "mp"),
            P("seq", "mp"),
            P("mp", "seq"),
        ),
        check_vma=False,
    )
```
